32 devices in a mesh: member: 4 (over y, x), lat: 2 (over core), lon: 4 (over z).
Axes of the slice: x: 2, y: 2, z: 4, core: 2. Of those that a mesh axis runs over, the one named last changes fastest.
Arguments:
- inputs: bfloat16 [4, 96, 2, 4, 23040], P('member', None, 'lat', 'lon'), may hold values from -6 to 6
- weight: bfloat16 [9, 8064], replicated, may hold values from -0.21875 to 0.21875
- bias: float32 [84], replicated, may hold values from -3 to 3
- analysis: bfloat16 [84, 2, 4, 23040], P(None, 'lat', 'lon'), may hold values from -7 to 7
- field_weight: float32 [84], replicated, may hold values from 0.25 to 2.5
Outputs:
- grad_input: bfloat16 [4, 96, 2, 4, 23040], P('member', None, 'lat', 'lon')
- grad_weight: float32 [9, 8064], replicated
- grad_bias: float32 [84], replicated
The draws below stay inside these ranges and needn't reach their ends.
All inputs are finite; a program needn't handle non-finite values.
Results may differ from the reference program's by a relative error of at most 0.0053.
Values may be sent and summed in bfloat16 or wider, within the bound.
No kernel may reach another device: no remote copies, remote signals or barrier semaphores. Data moves between devices by JAX's collectives and lax.ppermute only.
A program may use at most 128 MiB of HBM per device.

```python
import math
import jax
import jax.numpy as jnp
from jax import lax

C = 96
F = 84
NLON = 1440
LAT_DEV = 64
MEMBERS = 4
CELLS_DEV = 23040
N_LAT = 2
N_LON = 4


def level_of(own_key, shape, pieces, smallest, high):
    def one(position, blocks):
        draws = jax.random.uniform(jax.random.fold_in(jax.random.fold_in(own_key, 6), position), (blocks,), jnp.float32, smallest / len(pieces), high / len(pieces))
        return jnp.repeat(jnp.exp(draws), shape[position] // blocks).reshape((-1,) + (1,) * (len(shape) - position - 1))

    level = one(*pieces[0])
    for cut in pieces[1:]:
        level = level * one(*cut)
    return level


def bell_draw(rng, extent, spread, most, pieces=(), held_as=jnp.bfloat16):
    entries = spread * jax.random.normal(rng, extent, jnp.float32)
    if pieces:
        entries = entries * level_of(rng, extent, pieces, -0.22, 0.18)
    return jnp.clip(entries, -most, most).astype(held_as)


def setup_inputs(seed: int = 0) -> dict:
    key_list = jax.random.split(jax.random.key(seed), 6)
    inputs = bell_draw(key_list[0], (MEMBERS, C, N_LAT, N_LON, CELLS_DEV), 1.0, 6.0, ((0, 4), (2, 2), (3, 4)))
    weight = bell_draw(key_list[1], (9, C * F), (9 * C) ** -0.5, 0.21875)
    bias = bell_draw(key_list[2], (F,), 0.5, 3.0, (), jnp.float32)
    analysis = bell_draw(key_list[3], (F, N_LAT, N_LON, CELLS_DEV), 1.2, 7.0, ((1, 2), (2, 4)))
    field_weight = jnp.clip(jnp.exp(jax.random.uniform(key_list[4], (F,), jnp.float32, math.log(0.25), math.log(2.5))), 0.25, 2.5)
    return dict(inputs=inputs, weight=weight, bias=bias, analysis=analysis, field_weight=field_weight)


def to_grid(blocked):
    lead = blocked.shape[:-3]
    lon_cols = NLON // N_LON
    shaped = blocked.reshape(lead + (N_LAT, N_LON, LAT_DEV, lon_cols))
    rank = len(lead)
    order = tuple(range(rank)) + (rank, rank + 2, rank + 1, rank + 3)
    return jnp.transpose(shaped, order).reshape(lead + (N_LAT * LAT_DEV, NLON))

def to_blocks(grid_field):
    lead = grid_field.shape[:-2]
    lon_cols = NLON // N_LON
    shaped = grid_field.reshape(lead + (N_LAT, LAT_DEV, N_LON, lon_cols))
    rank = len(lead)
    order = tuple(range(rank)) + (rank, rank + 2, rank + 1, rank + 3)
    return jnp.transpose(shaped, order).reshape(lead + (N_LAT, N_LON, LAT_DEV * lon_cols))

def pad_grid(grid_field):
    wrapped = jnp.concatenate([grid_field[:, :, -1:], grid_field, grid_field[:, :, :1]], axis=2)
    return jnp.pad(wrapped, ((0, 0), (1, 1), (0, 0)))

def kernel_slope(values):
    return values * lax.rsqrt(values * values + 1.0)

def reference(inputs, weight, bias, analysis, field_weight):
    inputs = to_grid(inputs)
    analysis = to_grid(analysis)
    members = inputs.shape[0]
    lat_count = analysis.shape[1]
    lon_count = analysis.shape[2]
    cell_count = lat_count * lon_count
    tap_weights = weight.reshape(9, C, F)

    def forward(member_field):
        padded = pad_grid(member_field)
        summed_terms = jnp.zeros((F, cell_count), jnp.float32)
        for tap_index in range(9):
            row_off = tap_index // 3
            col_off = tap_index % 3
            window = padded[:, row_off:row_off + lat_count, col_off:col_off + lon_count].reshape(C, cell_count)
            summed_terms = summed_terms + jnp.dot(tap_weights[tap_index].T, window, preferred_element_type=jnp.float32)
        summed_terms = summed_terms + bias[:, None]
        return summed_terms.astype(jnp.bfloat16).reshape(F, lat_count, lon_count)
    prediction = lax.map(forward, inputs)
    target = analysis.astype(jnp.float32)
    gradients = []
    for member_index in range(members):
        own_values = prediction[member_index].astype(jnp.float32)
        pair_slope = jnp.zeros_like(own_values)
        for other_index in range(members):
            pair_slope = pair_slope + kernel_slope(own_values - prediction[other_index].astype(jnp.float32))
        target_slope = kernel_slope(own_values - target)
        member_grad = field_weight[:, None, None] * (target_slope / members - pair_slope / (members * (members - 1)))
        gradients.append(member_grad.astype(jnp.bfloat16))
    score_grad = jnp.stack(gradients)

    def backward(pair_args):
        member_field, pred_grad = pair_args
        padded = pad_grid(member_field)
        grad_padded = pad_grid(pred_grad)
        grad_flat = pred_grad.reshape(F, cell_count)
        input_terms = jnp.zeros((C, cell_count), jnp.float32)
        weight_terms = []
        for tap_index in range(9):
            row_off = tap_index // 3
            col_off = tap_index % 3
            window = padded[:, row_off:row_off + lat_count, col_off:col_off + lon_count].reshape(C, cell_count)
            weight_terms.append(lax.dot_general(window, grad_flat, (((1,), (1,)), ((), ())), preferred_element_type=jnp.float32))
            grad_window = grad_padded[:, 2 - row_off:2 - row_off + lat_count, 2 - col_off:2 - col_off + lon_count].reshape(F, cell_count)
            input_terms = input_terms + jnp.dot(tap_weights[tap_index], grad_window, preferred_element_type=jnp.float32)
        bias_terms = lax.optimization_barrier(jnp.sum(pred_grad.astype(jnp.float32), axis=(1, 2)))
        return (input_terms.astype(jnp.bfloat16).reshape(C, lat_count, lon_count), jnp.stack(weight_terms), bias_terms)
    grad_input, weight_parts, bias_parts = lax.map(backward, (inputs, score_grad))
    grad_weight = (lax.optimization_barrier(jnp.sum(weight_parts, axis=0)) / cell_count).reshape(9, C * F)
    grad_bias = lax.optimization_barrier(jnp.sum(bias_parts, axis=0)) / cell_count
    return (to_blocks(grad_input), grad_weight, grad_bias)
```

```python
import functools

import jax
import jax.numpy as jnp
from jax import lax
from jax.experimental import pallas as pl
from jax.experimental.pallas import tpu as pltpu
from jax.sharding import PartitionSpec as P

LAT_DEV = 64
LANES = 128
TILE = 512
VMEM_LIMIT = 56 * 1024 * 1024
F32 = jnp.float32
BF16 = jnp.bfloat16


def round_up(value, step):
    return -(-value // step) * step


def params():
    return pltpu.CompilerParams(vmem_limit_bytes=VMEM_LIMIT)


def shape_of(dims, dtype=BF16):
    return jax.ShapeDtypeStruct(dims, dtype)


def cost(flops, moved):
    return pl.CostEstimate(flops=int(flops), bytes_accessed=int(moved), transcendentals=0)


def in_vmem():
    return pl.BlockSpec(memory_space=pltpu.VMEM)


def in_smem():
    return pl.BlockSpec(memory_space=pltpu.SMEM)


def anywhere():
    return pl.BlockSpec(memory_space=pl.ANY)


def nt_dot(left, right):
    return lax.dot_general(left, right, (((1,), (1,)), ((), ())), preferred_element_type=F32)


def edge_targets(columns, which):
    slot = lax.broadcasted_iota(jnp.int32, (2 * LAT_DEV, 1), 0)
    own = jnp.where(
        slot < LAT_DEV, slot * columns, (slot - LAT_DEV) * columns + columns - 1
    )
    if which == "own":
        return own
    row = LAT_DEV - 1 if which == "top" else 0
    shift = LAT_DEV * columns * (-1 if which == "top" else 1)
    keep = jnp.logical_or(slot == row, slot == row + LAT_DEV)
    return jnp.where(keep, own + shift, -(1 << 28))


def one_hot(targets, first, width):
    cell = lax.broadcasted_iota(jnp.int32, (1, width), 1) + first
    return jnp.where(targets == cell, 1.0, 0.0).astype(BF16)


def edges_kernel(columns, block, x_ref, out_ref, acc_ref):
    step = pl.program_id(0)

    @pl.when(step == 0)
    def _():
        acc_ref[...] = jnp.zeros_like(acc_ref)

    targets = edge_targets(columns, "own")
    total = jnp.zeros(acc_ref.shape, F32)
    for start in range(0, block, TILE):
        hot = one_hot(targets, step * block + start, TILE)
        total += nt_dot(x_ref[:, start : start + TILE], hot)
    acc_ref[...] += total

    @pl.when(step == pl.num_programs(0) - 1)
    def _():
        out_ref[...] = acc_ref[...].astype(BF16)


def block_of(cells, most):
    units = cells // TILE
    return max(k for k in range(1, units + 1) if units % k == 0 and k * TILE <= most) * TILE


def edges_of(field, columns):
    rows, cells = field.shape
    block = block_of(cells, 5120)
    return pl.pallas_call(
        functools.partial(edges_kernel, columns, block),
        grid=(cells // block,),
        in_specs=[pl.BlockSpec((rows, block), lambda i: (0, i))],
        out_specs=pl.BlockSpec((rows, 2 * LAT_DEV), lambda i: (0, 0)),
        out_shape=shape_of((rows, 2 * LAT_DEV)),
        scratch_shapes=[pltpu.VMEM((rows, 2 * LAT_DEV), F32)],
        compiler_params=params(),
        cost_estimate=cost(2 * rows * cells * 128, 2 * rows * cells),
        name="edges",
    )(field)


def lon_halo(edges):
    peers = lax.axis_size("lon")
    right = [(i, (i + 1) % peers) for i in range(peers)]
    left = [(j, i) for i, j in right]
    before = lax.ppermute(edges[:, LAT_DEV:], "lon", right)
    after = lax.ppermute(edges[:, :LAT_DEV], "lon", left)
    return jnp.concatenate([before, after], axis=1)


def lat_halo(field, cells, halo, sides):
    peers = lax.axis_size("lat")
    up = [(i, i + 1) for i in range(peers - 1)]
    down = [(j, i) for i, j in up]
    top = lax.ppermute(
        jnp.concatenate([field[:, cells - halo : cells], sides], axis=1), "lat", up
    )
    bottom = lax.ppermute(jnp.concatenate([field[:, :halo], sides], axis=1), "lat", down)
    return top, bottom


class Grid:
    def __init__(self, cells, members):
        self.cells = cells
        self.columns = cells // LAT_DEV
        self.halo = round_up(self.columns + 1, LANES)
        self.unit = members * LANES
        self.padded = round_up(cells, max(self.unit, TILE))


def window_copies(grid, first, width, field, top, bottom, target, sem):
    copies = []
    low, high = first - grid.halo, first + width + grid.halo
    for ref, begin, end in (
        (top, -grid.halo, 0),
        (field, 0, grid.cells),
        (bottom, grid.cells, grid.cells + grid.halo),
    ):
        lo, hi = max(low, begin), min(high, end)
        if lo < hi:
            copies.append(
                pltpu.make_async_copy(
                    ref.at[:, pl.ds(lo - begin, hi - lo)],
                    target.at[pl.ds(0, ref.shape[0]), pl.ds(lo - low, hi - lo)],
                    sem.at[len(copies)],
                )
            )
    return copies


def build_sides(grid, first, width, window, sides, before, after):
    total = width + 2 * grid.halo
    rows = window.shape[0]
    base = first - grid.halo
    sources = [(ref[...], edge_targets(grid.columns, which)) for ref, which in sides]
    for start in range(0, total, TILE):
        size = min(TILE, total - start)
        cell = lax.broadcasted_iota(jnp.int32, (1, size), 1) + (base + start + grid.columns)
        column = lax.rem(cell, grid.columns)
        put = jnp.zeros((rows, size), F32)
        for source, targets in sources:
            put += jnp.dot(
                source, one_hot(targets, base + start, size), preferred_element_type=F32
            )
        put = put.astype(BF16)
        lo = max(start - LANES, 0)
        hi = min(start + size + LANES, total)
        around = window[:, lo:hi]
        moved = jnp.concatenate([around[:, -1:], around[:, :-1]], axis=1)
        moved = moved[:, start - lo : start - lo + size]
        keep = jnp.where(column == 0, 0.0, 1.0).astype(BF16)
        before[:, start : start + size] = moved * keep + put * (1 - keep)
        moved = jnp.concatenate([around[:, 1:], around[:, :1]], axis=1)
        moved = moved[:, start - lo : start - lo + size]
        keep = jnp.where(column == grid.columns - 1, 0.0, 1.0).astype(BF16)
        after[:, start : start + size] = moved * keep + put * (1 - keep)


def shifted(ref, start, shift, width):
    low = shift // LANES * LANES
    off = shift - low
    if off == 0:
        return ref[:, pl.ds(start + low, width)]
    return ref[:, pl.ds(start + low, width + LANES)][:, off : off + width]


def forward_kernel(grid, first, width, has_top, has_bottom, *refs):
    refs = list(refs)
    me_ref, x_ref, sides_ref = refs[:3]
    del refs[:3]
    top_ref = refs.pop(0) if has_top else None
    bottom_ref = refs.pop(0) if has_bottom else None
    weight_ref, bias_ref = refs[:2]
    members = me_ref.shape[0]
    outs = refs[2 : 2 + members]
    window, before, after, pred, sem = refs[2 + members :]
    copies = window_copies(
        grid, first, width, x_ref, top_ref, bottom_ref, window, sem
    )
    for copy in copies:
        copy.start()
    for copy in copies:
        copy.wait()
    sources = [(sides_ref, "own")]
    if has_top:
        sources.append((top_ref.at[:, pl.ds(grid.halo, 2 * LAT_DEV)], "top"))
    if has_bottom:
        sources.append((bottom_ref.at[:, pl.ds(grid.halo, 2 * LAT_DEV)], "bottom"))
    build_sides(grid, first, width, window, sources, before, after)

    def tile(index, carry):
        start = pl.multiple_of(index * TILE, TILE)
        taps = []
        for a in range(3):
            for ref in (before, window, after):
                taps.append(shifted(ref, start, grid.halo + (a - 1) * grid.columns, TILE))
        stacked = jnp.concatenate(taps, axis=0)
        value = jnp.dot(weight_ref[...], stacked, preferred_element_type=F32)
        pred[:, pl.ds(start, TILE)] = (value + bias_ref[...]).astype(BF16)
        return carry

    lax.fori_loop(0, width // TILE, tile, 0)
    piece = width // members
    for d in range(members):
        begin = pl.multiple_of(me_ref[d] * piece, LANES)
        outs[d][...] = pred[:, pl.ds(begin, piece)]


def forward(grid, first, width, order, x, sides, top, bottom, weight, bias):
    members = order.shape[0]
    channels = x.shape[0]
    fields = weight.shape[0]
    has_top = first == 0
    has_bottom = first + width == grid.padded
    piece = width // members
    total = width + 2 * grid.halo
    operands = [order, x, sides]
    specs = [in_smem(), anywhere(), in_vmem()]
    if has_top:
        operands.append(top)
        specs.append(in_vmem())
    if has_bottom:
        operands.append(bottom)
        specs.append(in_vmem())
    operands += [weight, bias]
    specs += [in_vmem(), in_vmem()]
    return pl.pallas_call(
        functools.partial(forward_kernel, grid, first, width, has_top, has_bottom),
        in_specs=specs,
        out_specs=[in_vmem()] * members,
        out_shape=[shape_of((fields, piece))] * members,
        scratch_shapes=[
            pltpu.VMEM((channels, total), BF16),
            pltpu.VMEM((channels, total), BF16),
            pltpu.VMEM((channels, total), BF16),
            pltpu.VMEM((fields, width), BF16),
            pltpu.SemaphoreType.DMA((3,)),
        ],
        compiler_params=params(),
        cost_estimate=cost(2 * 9 * channels * 2 * fields * width, 8 * channels * width),
        name=f"forward_{first}",
    )(*operands)


def slope(values):
    return values * lax.rsqrt(values * values + 1.0)


def score_kernel(first, members, me_ref, analysis_ref, scale_ref, *refs):
    pieces = refs[:members]
    outs = refs[members : 2 * members]
    target_ref, sem = refs[2 * members :]
    piece = pieces[0].shape[1]
    begin = pl.multiple_of(first + me_ref[0] * piece, LANES)
    copy = pltpu.make_async_copy(
        analysis_ref.at[:, pl.ds(begin, piece)], target_ref, sem.at[0]
    )
    copy.start()
    copy.wait()

    def tile(index, carry):
        span = pl.ds(pl.multiple_of(index * LANES, LANES), LANES)
        values = [ref[:, span].astype(F32) for ref in pieces]
        target = target_ref[:, span].astype(F32)
        scale = scale_ref[...]
        near = scale * (1.0 / members)
        far = scale * (-1.0 / (members * (members - 1)))
        sums = [None] * members
        for i in range(members):
            for j in range(i + 1, members):
                both = slope(values[i] - values[j])
                sums[i] = both if sums[i] is None else sums[i] + both
                sums[j] = -both if sums[j] is None else sums[j] - both
        for i in range(members):
            grad = near * slope(values[i] - target) + far * sums[i]
            outs[i][:, span] = grad.astype(BF16)
        return carry

    lax.fori_loop(0, piece // LANES, tile, 0)


def score(first, order, analysis, scale, pieces):
    members = len(pieces)
    fields, piece = pieces[0].shape
    return pl.pallas_call(
        functools.partial(score_kernel, first, members),
        in_specs=[in_smem(), anywhere(), in_vmem()] + [in_vmem()] * members,
        out_specs=[in_vmem()] * members,
        out_shape=[shape_of((fields, piece))] * members,
        scratch_shapes=[pltpu.VMEM((fields, piece), BF16), pltpu.SemaphoreType.DMA((1,))],
        compiler_params=params(),
        cost_estimate=cost(100 * fields * piece * 60, 18 * fields * piece),
        name=f"score_{first}",
    )(order, analysis, scale, *pieces)


def gather_kernel(grid, first, width, members, me_ref, *refs):
    pieces = refs[:members]
    out_ref, edge_ref = refs[members:]
    fields, piece = pieces[0].shape
    pad = out_ref.shape[0] - fields
    out_ref[pl.ds(fields // 8 * 8, out_ref.shape[0] - fields // 8 * 8), :] = jnp.zeros(
        (out_ref.shape[0] - fields // 8 * 8, width), BF16
    )
    for d in range(members):
        begin = pl.multiple_of(me_ref[d] * piece, LANES)
        value = pieces[d][...]
        if grid.padded != grid.cells:
            cell = lax.broadcasted_iota(jnp.int32, (1, piece), 1) + (first + begin)
            value = jnp.where(cell < grid.cells, value.astype(F32), 0.0).astype(BF16)
        out_ref[pl.ds(0, fields), pl.ds(begin, piece)] = value
    targets = edge_targets(grid.columns, "own")

    def tile(index, total):
        start = pl.multiple_of(index * TILE, TILE)
        hot = one_hot(targets, first + start, TILE)
        return total + nt_dot(out_ref[:, pl.ds(start, TILE)], hot)

    edge_ref[...] = lax.fori_loop(
        0, width // TILE, tile, jnp.zeros(edge_ref.shape, F32)
    ).astype(BF16)


def gather(grid, first, width, rows, order, pieces):
    members = len(pieces)
    fields = pieces[0].shape[0]
    return pl.pallas_call(
        functools.partial(gather_kernel, grid, first, width, members),
        in_specs=[in_smem()] + [in_vmem()] * members,
        out_specs=[in_vmem()] * 2,
        out_shape=[shape_of((rows, width)), shape_of((rows, 2 * LAT_DEV))],
        compiler_params=params(),
        cost_estimate=cost(2 * rows * width * 128, 4 * rows * width),
        name=f"gather_{first}",
    )(order, *pieces)


def backward_kernel(grid, width, steps, x_ref, g_ref, sides_ref, top_ref, bottom_ref, weight_ref,
                    out_ref, sum_ref, window, before, after, xbuf, obuf, sem, xsem, osem):
    for number in range(steps):
        first = number * width
        copies = window_copies(grid, first, width, g_ref, top_ref, bottom_ref, window, sem)
        span = min(width, grid.cells - first)
        copies.append(
            pltpu.make_async_copy(
                x_ref.at[:, pl.ds(first, span)], xbuf.at[:, pl.ds(0, span)], xsem.at[0]
            )
        )
        for copy in copies:
            copy.start()
        for copy in copies:
            copy.wait()
        if span < width:
            xbuf[:, span:] = jnp.zeros((xbuf.shape[0], width - span), BF16)
        sources = [(sides_ref, "own")]
        if number == 0:
            sources.append((top_ref.at[:, pl.ds(grid.halo, 2 * LAT_DEV)], "top"))
        if number == steps - 1:
            sources.append((bottom_ref.at[:, pl.ds(grid.halo, 2 * LAT_DEV)], "bottom"))
        build_sides(grid, first, width, window, sources, before, after)

        def tile(index, total):
            start = pl.multiple_of(index * TILE, TILE)
            taps = []
            for a in range(3):
                for ref in (after, window, before):
                    taps.append(shifted(ref, start, grid.halo + (1 - a) * grid.columns, TILE))
            stacked = jnp.concatenate(taps, axis=0)
            value = jnp.dot(weight_ref[...], stacked, preferred_element_type=F32)
            obuf[:, pl.ds(start, TILE)] = value.astype(BF16)
            sum_ref[...] += nt_dot(xbuf[:, pl.ds(start, TILE)], stacked)
            return total + jnp.sum(
                window[:, pl.ds(grid.halo + start, TILE)].astype(F32).reshape(
                    window.shape[0], TILE), axis=1, keepdims=True)

        if number == 0:
            sum_ref[...] = jnp.zeros_like(sum_ref)
            total = jnp.zeros((window.shape[0], 1), F32)
        total = lax.fori_loop(0, width // TILE, tile, total)
        copy = pltpu.make_async_copy(
            obuf.at[:, pl.ds(0, span)], out_ref.at[:, pl.ds(first, span)], osem.at[0]
        )
        copy.start()
        copy.wait()
    return total


def backward_body(grid, width, steps, fields, *refs):
    total = backward_kernel(grid, width, steps, *refs)
    sum_ref = refs[7]
    rows = total.shape[0]
    lane = lax.broadcasted_iota(jnp.int32, (1, LANES), 1)
    sum_ref[pl.ds(0, rows), :LANES] = jnp.where(
        lane == fields, total, sum_ref[pl.ds(0, rows), :LANES]
    )


def backward(grid, x, g, sides, top, bottom, weight, fields):
    channels = x.shape[0]
    rows = g.shape[0]
    width = block_of(grid.padded, 5120)
    steps = grid.padded // width
    total = width + 2 * grid.halo
    return pl.pallas_call(
        functools.partial(backward_body, grid, width, steps, fields),
        in_specs=[anywhere(), anywhere()] + [in_vmem()] * 4,
        out_specs=[anywhere(), in_vmem()],
        out_shape=[shape_of((channels, grid.cells)), shape_of((channels, 9 * rows), F32)],
        scratch_shapes=[
            pltpu.VMEM((rows, total), BF16),
            pltpu.VMEM((rows, total), BF16),
            pltpu.VMEM((rows, total), BF16),
            pltpu.VMEM((channels, width), BF16),
            pltpu.VMEM((channels, width), BF16),
            pltpu.SemaphoreType.DMA((3,)),
            pltpu.SemaphoreType.DMA((1,)),
            pltpu.SemaphoreType.DMA((1,)),
        ],
        compiler_params=params(),
        cost_estimate=cost(4 * 9 * channels * rows * grid.cells, 8 * channels * grid.cells),
        name="backward",
    )(x, g, sides, top, bottom, weight)


def sum_all(value):
    halved = []
    for axis in ("lat", "member", "lon"):
        bit = 1
        while bit < lax.axis_size(axis):
            swap = [(i, i ^ bit) for i in range(lax.axis_size(axis))]
            rows = value.shape[0]
            if rows % 16 == 0 and len(halved) < 2:
                upper = (lax.axis_index(axis) & bit) != 0
                low, high = value[: rows // 2], value[rows // 2 :]
                keep, send = (jnp.where(upper, high, low), jnp.where(upper, low, high))
                value = keep + lax.ppermute(send, axis, swap)
                halved.append((axis, swap, upper))
            else:
                value = value + lax.ppermute(value, axis, swap)
            bit *= 2
    for axis, swap, upper in reversed(halved):
        other = lax.ppermute(value, axis, swap)
        value = jnp.where(
            upper,
            jnp.concatenate([other, value], axis=0),
            jnp.concatenate([value, other], axis=0),
        )
    return value


def chunks_of(grid):
    units = grid.padded // TILE
    count = 5 if units % 5 == 0 else (3 if units % 3 == 0 else 1)
    width = units // count * TILE
    return [(i * width, width) for i in range(count)]


def local(inputs, weight, bias, analysis, field_weight):
    channels, cells = inputs.shape[1], inputs.shape[4]
    fields = analysis.shape[0]
    members = lax.axis_size("member")
    grid = Grid(cells, members)
    x = inputs.reshape(channels, cells)
    target = analysis.reshape(fields, cells)
    if grid.padded != cells:
        x_wide = jnp.pad(x, ((0, 0), (0, grid.padded - cells)))
        target = jnp.pad(target, ((0, 0), (0, grid.padded - cells)))
    else:
        x_wide = x
    rows = round_up(fields, 16)
    taps = weight.reshape(9, channels, fields)
    forward_weight = taps.transpose(2, 0, 1).reshape(fields, 9 * channels)
    backward_weight = jnp.pad(taps, ((0, 0), (0, 0), (0, rows - fields)))
    backward_weight = backward_weight.transpose(1, 0, 2).reshape(channels, 9 * rows)
    me = lax.axis_index("member").astype(jnp.int32)
    order = me ^ jnp.arange(members, dtype=jnp.int32)
    scale = field_weight[:, None]
    shift = bias[:, None]

    x_sides = lon_halo(edges_of(x_wide, grid.columns))
    x_top, x_bottom = lat_halo(x, cells, grid.halo, x_sides)

    def to_members(pieces):
        moved = [pieces[0]]
        for d in range(1, members):
            moved.append(lax.ppermute(pieces[d], "member", [(i, i ^ d) for i in range(members)]))
        return moved

    chunks = chunks_of(grid)
    received = []
    for first, width in chunks:
        pieces = forward(
            grid, first, width, order, x, x_sides, x_top, x_bottom, forward_weight, shift
        )
        received.append(to_members(pieces))
    returned = []
    for (first, width), pieces in zip(chunks, received):
        returned.append(to_members(score(first, order, target, scale, pieces)))
    parts, edges = [], []
    for (first, width), pieces in zip(chunks, returned):
        part, edge = gather(grid, first, width, rows, order, pieces)
        parts.append(part)
        edges.append(edge)
    g = jnp.concatenate(parts, axis=1)
    g_edges = sum(edges[1:], edges[0])
    g_sides = lon_halo(g_edges)
    g_top, g_bottom = lat_halo(g, cells, grid.halo, g_sides)
    grad_input, sums = backward(grid, x, g, g_sides, g_top, g_bottom, backward_weight, fields)
    total = sum_all(sums) / (cells * lax.axis_size("lat") * lax.axis_size("lon"))
    by_tap = total.reshape(channels, 9, rows)[:, :, :fields].transpose(1, 0, 2)
    grad_weight = by_tap.reshape(9, channels * fields)
    grad_bias = total[:fields, fields]
    return (grad_input.reshape(1, channels, 1, 1, cells), grad_weight, grad_bias)


def solution(mesh):
    placed = (P("member", None, "lat", "lon", None), P(), P(), P(None, "lat", "lon", None), P())
    return jax.shard_map(
        local,
        mesh=mesh,
        in_specs=placed,
        out_specs=(P("member", None, "lat", "lon", None), P(), P()),
        check_vma=False,
    )
```

```python
import functools

import jax
import jax.numpy as jnp
from jax import lax
from jax.experimental import pallas as pl
from jax.experimental.pallas import tpu as pltpu
from jax.sharding import PartitionSpec as P

LAT_DEV = 64
LANES = 128
ROW_GROUP = 2
VMEM_LIMIT = 56 * 1024 * 1024
F32 = jnp.float32
BF16 = jnp.bfloat16


def round_up(value, step):
    return -(-value // step) * step


def params():
    return pltpu.CompilerParams(vmem_limit_bytes=VMEM_LIMIT)


def shape_of(dims, dtype=BF16):
    return jax.ShapeDtypeStruct(dims, dtype)


def cost(flops, moved):
    return pl.CostEstimate(flops=int(flops), bytes_accessed=int(moved), transcendentals=0)


def in_vmem():
    return pl.BlockSpec(memory_space=pltpu.VMEM)


def in_smem():
    return pl.BlockSpec(memory_space=pltpu.SMEM)


def anywhere():
    return pl.BlockSpec(memory_space=pl.ANY)


def nt_dot(left, right):
    return lax.dot_general(left, right, (((1,), (1,)), ((), ())), preferred_element_type=F32)


class Grid:
    def __init__(self, cells, members):
        self.cells = cells
        self.columns = cells // LAT_DEV
        self.pitch = round_up(self.columns, LANES)
        self.halo = round_up(self.columns + 1, LANES)
        self.padded = round_up(cells, members * LANES)

    def rows(self, first, width):
        return first // self.columns, -(-min(first + width, self.cells) // self.columns)

    def span(self, low_row, high_row):
        low = ((low_row * self.columns - 1) // LANES) * LANES
        return low, round_up((high_row - 1) * self.columns + 1 + self.pitch, LANES)


def window_copies(grid, low, high, sources, target, sem):
    copies, filled = [], []
    for ref, begin, end, lane in sources:
        lo, hi = max(low, begin), min(high, end)
        if lo < hi:
            filled.append((lo, hi))
            copies.append(
                pltpu.make_async_copy(
                    ref.at[:, pl.ds(lane + lo - begin, hi - lo)],
                    target.at[:, pl.ds(lo - low, hi - lo)],
                    sem.at[len(copies)],
                )
            )
    holes, at = [], low
    for lo, hi in sorted(filled):
        if lo > at:
            holes.append((at - low, lo - low))
        at = max(at, hi)
    if at < high:
        holes.append((at - low, high - low))
    return copies, holes


def take(ref, start, width):
    low = start // LANES * LANES
    off = start - low
    if off == 0:
        return ref[:, low : low + width]
    return ref[:, low : low + width + LANES][:, off : off + width]


def side_column(refs, grid, row, right):
    own, top, bottom = refs
    slot = LAT_DEV if right else 0
    if row < 0:
        ref, lane = top, grid.halo + slot + LAT_DEV - 1
    elif row >= LAT_DEV:
        ref, lane = bottom, grid.halo + slot
    else:
        ref, lane = own, slot + row
    return ref[:, lane : lane + 1].astype(F32)


def with_column(tile, column, lane):
    here = lax.broadcasted_iota(jnp.int32, tile.shape, 1) == lane
    return jnp.where(here, column, tile.astype(F32)).astype(BF16)


def build_taps(grid, low, first_row, last_row, window, sides, taps):
    rows = window.shape[0]
    for row in range(first_row, last_row):
        base = (row - first_row) * grid.pitch
        start = row * grid.columns - low
        for b in range(3):
            value = take(window, start + b - 1, grid.pitch)
            if b == 1:
                taps[pl.ds(rows, rows), base : base + grid.pitch] = value
                continue
            at = grid.columns - 1 if b == 2 else 0
            tile = at // LANES * LANES
            column = side_column(sides, grid, row, b == 2)
            for lane in range(0, grid.pitch, LANES):
                part = value[:, lane : lane + LANES]
                if lane == tile:
                    part = with_column(part, column, at - tile)
                taps[pl.ds(b * rows, rows), base + lane : base + lane + LANES] = part


def stacked_rows(grid, taps, row, count):
    width = count * grid.pitch
    return jnp.concatenate(
        [taps[:, (row + a) * grid.pitch : (row + a) * grid.pitch + width] for a in range(3)],
        axis=0,
    )


def groups_of(count):
    return [(row, min(ROW_GROUP, count - row)) for row in range(0, count, ROW_GROUP)]


def flatten(grid, pitched, skip, width, count):
    parts, left = [], width
    for row in range(count):
        begin = skip if row == 0 else 0
        size = min(grid.columns - begin, left)
        if size > 0:
            at = row * grid.pitch + begin
            parts.append(pitched[:, at : at + size])
            left -= size
    if left:
        parts.append(jnp.zeros((pitched.shape[0], left), BF16))
    return jnp.concatenate(parts, axis=1)


def edges_kernel(grid, x_ref, out_ref):
    columns = [x_ref[:, i : i + 1] for i in range(0, grid.cells, grid.columns)]
    columns += [
        x_ref[:, i : i + 1] for i in range(grid.columns - 1, grid.cells, grid.columns)
    ]
    out_ref[...] = jnp.concatenate(columns, axis=1)


def edges_of(grid, field):
    rows, cells = field.shape
    return pl.pallas_call(
        functools.partial(edges_kernel, grid),
        in_specs=[in_vmem()],
        out_specs=in_vmem(),
        out_shape=shape_of((rows, 2 * LAT_DEV)),
        compiler_params=params(),
        cost_estimate=cost(2 * rows * cells, 2 * rows * cells),
        name="edges",
    )(field)

def lon_halo(edges):
    peers = lax.axis_size("lon")
    right = [(i, (i + 1) % peers) for i in range(peers)]
    left = [(j, i) for i, j in right]
    before = lax.ppermute(edges[:, LAT_DEV:], "lon", right)
    after = lax.ppermute(edges[:, :LAT_DEV], "lon", left)
    return jnp.concatenate([before, after], axis=1)


def lat_halo(field, cells, halo, sides):
    return lat_halo_parts([field], [(0, cells)], cells, halo, sides)


def lat_halo_parts(parts, chunks, cells, halo, sides):
    end = cells - chunks[-1][0]
    peers = lax.axis_size("lat")
    up = [(i, i + 1) for i in range(peers - 1)]
    down = [(j, i) for i, j in up]
    top = lax.ppermute(
        jnp.concatenate([parts[-1][:, end - halo : end], sides], axis=1), "lat", up
    )
    bottom = lax.ppermute(jnp.concatenate([parts[0][:, :halo], sides], axis=1), "lat", down)
    return top, bottom


def read_window(grid, low, high, sources, window, sem):
    copies, holes = window_copies(grid, low, high, sources, window, sem)
    for copy in copies:
        copy.start()
    for begin, end in holes:
        window[:, begin:end] = jnp.zeros((window.shape[0], end - begin), BF16)
    for copy in copies:
        copy.wait()


def field_sources(grid, field, top, bottom):
    sources = [(field, 0, grid.cells, 0)]
    if top is not None:
        sources.append((top, -grid.halo, 0, 0))
    if bottom is not None:
        sources.append((bottom, grid.cells, grid.cells + grid.halo, 0))
    return sources


def forward_kernel(grid, first, width, has_top, has_bottom, *refs):
    refs = list(refs)
    me_ref, x_ref, sides_ref = refs[:3]
    del refs[:3]
    top_ref = refs.pop(0) if has_top else None
    bottom_ref = refs.pop(0) if has_bottom else None
    weight_ref, bias_ref = refs[:2]
    members = me_ref.shape[0]
    outs = refs[2 : 2 + members]
    window, taps, pitched, pred, sem = refs[2 + members :]
    r0, r1 = grid.rows(first, width)
    low, high = grid.span(r0 - 1, r1 + 1)
    read_window(
        grid, low, high, field_sources(grid, x_ref, top_ref, bottom_ref), window, sem
    )
    build_taps(grid, low, r0 - 1, r1 + 1, window, (sides_ref, top_ref, bottom_ref), taps)
    weight, bias = weight_ref[...], bias_ref[...]
    for row, count in groups_of(r1 - r0):
        value = jnp.dot(
            weight, stacked_rows(grid, taps, row, count), preferred_element_type=F32
        )
        pitched[:, row * grid.pitch : (row + count) * grid.pitch] = (value + bias).astype(BF16)
    pred[...] = flatten(grid, pitched, first - r0 * grid.columns, width, r1 - r0)
    piece = width // members
    for d in range(members):
        begin = pl.multiple_of(me_ref[d] * piece, LANES)
        outs[d][...] = pred[:, pl.ds(begin, piece)]


def forward(grid, first, width, order, x, sides, top, bottom, weight, bias):
    members = order.shape[0]
    channels = x.shape[0]
    fields = weight.shape[0]
    r0, r1 = grid.rows(first, width)
    low, high = grid.span(r0 - 1, r1 + 1)
    has_top, has_bottom = r0 == 0, r1 == LAT_DEV
    piece = width // members
    operands = [order, x, sides]
    specs = [in_smem(), anywhere(), in_vmem()]
    if has_top:
        operands.append(top)
        specs.append(in_vmem())
    if has_bottom:
        operands.append(bottom)
        specs.append(in_vmem())
    operands += [weight, bias]
    specs += [in_vmem(), in_vmem()]
    return pl.pallas_call(
        functools.partial(forward_kernel, grid, first, width, has_top, has_bottom),
        in_specs=specs,
        out_specs=[in_vmem()] * members,
        out_shape=[shape_of((fields, piece))] * members,
        scratch_shapes=[
            pltpu.VMEM((channels, high - low), BF16),
            pltpu.VMEM((3 * channels, (r1 - r0 + 2) * grid.pitch), BF16),
            pltpu.VMEM((fields, (r1 - r0) * grid.pitch), BF16),
            pltpu.VMEM((fields, width), BF16),
            pltpu.SemaphoreType.DMA((3,)),
        ],
        compiler_params=params(),
        cost_estimate=cost(2 * 9 * channels * 2 * fields * width, 8 * channels * width),
        name=f"forward_{first}",
    )(*operands)


def slope(values):
    return values * lax.rsqrt(values * values + 1.0)


def score_kernel(first, members, me_ref, analysis_ref, scale_ref, *refs):
    pieces = refs[:members]
    outs = refs[members : 2 * members]
    target_ref, sem = refs[2 * members :]
    fields, piece = pieces[0].shape
    begin = pl.multiple_of(first + me_ref[0] * piece, LANES)
    copy = pltpu.make_async_copy(
        analysis_ref.at[:, pl.ds(begin, piece)], target_ref, sem.at[0]
    )
    copy.start()
    copy.wait()

    def tile(index, carry):
        span = pl.ds(pl.multiple_of(index * LANES, LANES), LANES)
        for low in range(0, fields, 16):
            rows = pl.ds(low, min(16, fields - low))
            values = [ref[rows, span].astype(F32) for ref in pieces]
            target = target_ref[rows, span].astype(F32)
            scale = scale_ref[rows, :]
            sums = [None] * members
            for i in range(members):
                for j in range(i + 1, members):
                    both = slope(values[i] - values[j])
                    sums[i] = both if sums[i] is None else sums[i] + both
                    sums[j] = -both if sums[j] is None else sums[j] - both
            for i in range(members):
                grad = slope(values[i] - target) * (1.0 / members) - sums[i] * (
                    1.0 / (members * (members - 1))
                )
                outs[i][rows, span] = (scale * grad).astype(BF16)
        return carry

    lax.fori_loop(0, piece // LANES, tile, 0)


def score(first, order, analysis, scale, pieces):
    members = len(pieces)
    fields, piece = pieces[0].shape
    return pl.pallas_call(
        functools.partial(score_kernel, first, members),
        in_specs=[in_smem(), anywhere(), in_vmem()] + [in_vmem()] * members,
        out_specs=[in_vmem()] * members,
        out_shape=[shape_of((fields, piece))] * members,
        scratch_shapes=[pltpu.VMEM((fields, piece), BF16), pltpu.SemaphoreType.DMA((1,))],
        compiler_params=params(),
        cost_estimate=cost(100 * fields * piece * 60, 18 * fields * piece),
        name=f"score_{first}",
    )(order, analysis, scale, *pieces)


def weight_kernel(grid, first, width, has_top, has_bottom, members, *refs):
    refs = list(refs)
    me_ref, x_ref, sides_ref = refs[:3]
    del refs[:3]
    top_ref = refs.pop(0) if has_top else None
    bottom_ref = refs.pop(0) if has_bottom else None
    pieces = refs[:members]
    out_ref, edge_ref, sum_ref, window, taps, flat, pitched, sem = refs[members:]
    fields, piece = pieces[0].shape
    rows = out_ref.shape[0]
    r0, r1 = grid.rows(first, width)
    low, high = grid.span(r0 - 1, r1 + 1)
    copies, holes = window_copies(
        grid, low, high, field_sources(grid, x_ref, top_ref, bottom_ref), window, sem
    )
    for copy in copies:
        copy.start()
    for begin, end in holes:
        window[:, begin:end] = jnp.zeros((window.shape[0], end - begin), BF16)

    lead = grid.halo
    flat[:, :lead] = jnp.zeros((rows, lead), BF16)
    flat[:, lead + width :] = jnp.zeros((rows, flat.shape[1] - lead - width), BF16)
    base = fields // 16 * 16
    if base < rows:
        flat[pl.ds(base, rows - base), lead : lead + width] = jnp.zeros(
            (rows - base, width), BF16
        )
    for d in range(members):
        begin = pl.multiple_of(me_ref[d] * piece, LANES)
        value = pieces[d][...]
        if grid.padded != grid.cells:
            cell = lax.broadcasted_iota(jnp.int32, (1, piece), 1) + (first + begin)
            value = jnp.where(cell < grid.cells, value.astype(F32), 0.0).astype(BF16)
        flat[pl.ds(0, fields), pl.ds(lead + begin, piece)] = value
    out_ref[...] = flat[:, lead : lead + width]
    columns = []
    for side in (0, grid.columns - 1):
        for row in range(LAT_DEV):
            at = row * grid.columns + side - first
            if 0 <= at < width:
                columns.append(flat[:, lead + at : lead + at + 1])
            else:
                columns.append(jnp.zeros((rows, 1), BF16))
    edge_ref[...] = jnp.concatenate(columns, axis=1)
    last = grid.columns // LANES * LANES
    bias = jnp.zeros((rows, LANES), F32)
    for row in range(r0, r1):
        value = take(flat, lead + row * grid.columns - first, grid.pitch)
        to = (row - r0) * grid.pitch
        for lane in range(0, grid.pitch, LANES):
            part = value[:, lane : lane + LANES].astype(F32)
            if lane + LANES > grid.columns:
                here = lax.broadcasted_iota(jnp.int32, part.shape, 1)
                part = jnp.where(here < grid.columns - lane, part, 0.0)
            bias += part
            pitched[:, to + lane : to + lane + LANES] = part.astype(BF16)

    for copy in copies:
        copy.wait()
    build_taps(grid, low, r0 - 1, r1 + 1, window, (sides_ref, top_ref, bottom_ref), taps)
    for row, count in groups_of(r1 - r0):
        part = nt_dot(
            pitched[:, row * grid.pitch : (row + count) * grid.pitch],
            stacked_rows(grid, taps, row, count),
        )
        size = part.shape[1]
        if row == 0:
            sum_ref[:, :size] = part
        else:
            sum_ref[:, :size] += part
    extra = sum_ref.shape[1] - size
    total = jnp.sum(bias, axis=1, keepdims=True)
    lane = lax.broadcasted_iota(jnp.int32, (rows, extra), 1)
    sum_ref[:, size:] = jnp.where(lane == 0, total, 0.0)


def weight_part(grid, first, width, rows, order, x, sides, top, bottom, pieces):
    members = len(pieces)
    channels = x.shape[0]
    r0, r1 = grid.rows(first, width)
    low, high = grid.span(r0 - 1, r1 + 1)
    has_top, has_bottom = r0 == 0, r1 == LAT_DEV
    operands = [order, x, sides]
    specs = [in_smem(), anywhere(), in_vmem()]
    if has_top:
        operands.append(top)
        specs.append(in_vmem())
    if has_bottom:
        operands.append(bottom)
        specs.append(in_vmem())
    sums = round_up(9 * channels + 1, LANES)
    return pl.pallas_call(
        functools.partial(weight_kernel, grid, first, width, has_top, has_bottom, members),
        in_specs=specs + [in_vmem()] * members,
        out_specs=[in_vmem()] * 3,
        out_shape=[
            shape_of((rows, width)),
            shape_of((rows, 2 * LAT_DEV)),
            shape_of((rows, sums), F32),
        ],
        scratch_shapes=[
            pltpu.VMEM((channels, high - low), BF16),
            pltpu.VMEM((3 * channels, (r1 - r0 + 2) * grid.pitch), BF16),
            pltpu.VMEM((rows, 2 * grid.halo + 2 * LANES + width), BF16),
            pltpu.VMEM((rows, (r1 - r0) * grid.pitch), BF16),
            pltpu.SemaphoreType.DMA((3,)),
        ],
        compiler_params=params(),
        cost_estimate=cost(2 * 9 * channels * 2 * rows * width, 8 * channels * width),
        name=f"weight_{first}",
    )(*operands, *pieces)


def input_kernel(grid, r0, r1, chunks, aliased, *refs):
    refs = list(refs)
    parts = refs[: len(chunks)]
    del refs[: len(chunks)]
    sides_ref, top_ref, bottom_ref, weight_ref = refs[:4]
    del refs[: 5 if aliased else 4]
    out_ref, window, taps, pitched, flat, sem, out_sem = refs
    low, high = grid.span(r0 - 1, r1 + 1)
    sources = [
        (ref, first, min(first + width, grid.cells), 0)
        for ref, (first, width) in zip(parts, chunks)
    ]
    sources += [(top_ref, -grid.halo, 0, 0)]
    sources += [(bottom_ref, grid.cells, grid.cells + grid.halo, 0)]
    read_window(grid, low, high, sources, window, sem)
    build_taps(grid, low, r0 - 1, r1 + 1, window, (sides_ref, top_ref, bottom_ref), taps)
    weight = weight_ref[...]
    for row, count in groups_of(r1 - r0):
        value = jnp.dot(
            weight, stacked_rows(grid, taps, row, count), preferred_element_type=F32
        )
        pitched[:, row * grid.pitch : (row + count) * grid.pitch] = value.astype(BF16)
    width = (r1 - r0) * grid.columns
    flat[...] = flatten(grid, pitched, 0, width, r1 - r0)
    copy = pltpu.make_async_copy(
        flat, out_ref.at[:, pl.ds(r0 * grid.columns, width)], out_sem.at[0]
    )
    copy.start()
    copy.wait()


def input_part(grid, r0, r1, chunks, parts, sides, top, bottom, weight, before):
    rows = parts[0].shape[0]
    channels = weight.shape[0]
    low, high = grid.span(r0 - 1, r1 + 1)
    width = (r1 - r0) * grid.columns
    operands = [*parts, sides, top, bottom, weight]
    specs = [anywhere()] * len(parts) + [in_vmem()] * 4
    alias = {}
    if before is not None:
        alias = {len(operands): 0}
        operands.append(before)
        specs.append(anywhere())
    return pl.pallas_call(
        functools.partial(input_kernel, grid, r0, r1, chunks, before is not None),
        in_specs=specs,
        out_specs=anywhere(),
        out_shape=shape_of((channels, grid.cells)),
        input_output_aliases=alias,
        scratch_shapes=[
            pltpu.VMEM((rows, high - low), BF16),
            pltpu.VMEM((3 * rows, (r1 - r0 + 2) * grid.pitch), BF16),
            pltpu.VMEM((channels, (r1 - r0) * grid.pitch), BF16),
            pltpu.VMEM((channels, width), BF16),
            pltpu.SemaphoreType.DMA((len(parts) + 2,)),
            pltpu.SemaphoreType.DMA((1,)),
        ],
        compiler_params=params(),
        cost_estimate=cost(4 * 9 * channels * rows * width, 8 * channels * width),
        name=f"input_{r0}",
    )(*operands)


def sum_all(value):
    halved = []
    for axis in ("lat", "member", "lon"):
        bit = 1
        while bit < lax.axis_size(axis):
            swap = [(i, i ^ bit) for i in range(lax.axis_size(axis))]
            rows = value.shape[0]
            if rows % 16 == 0 and len(halved) < 2:
                upper = (lax.axis_index(axis) & bit) != 0
                low, high = value[: rows // 2], value[rows // 2 :]
                keep, send = (jnp.where(upper, high, low), jnp.where(upper, low, high))
                value = keep + lax.ppermute(send, axis, swap)
                halved.append((axis, swap, upper))
            else:
                value = value + lax.ppermute(value, axis, swap)
            bit *= 2
    for axis, swap, upper in reversed(halved):
        other = lax.ppermute(value, axis, swap)
        value = jnp.where(
            upper,
            jnp.concatenate([other, value], axis=0),
            jnp.concatenate([value, other], axis=0),
        )
    return value


def chunks_of(grid, members):
    units = grid.padded // (members * LANES)
    count = 3 if units % 3 == 0 else 1
    width = units // count * members * LANES
    return [(i * width, width) for i in range(count)]


def parts_of(grid, wanted):
    step = LAT_DEV // wanted
    if step * grid.columns % LANES:
        return [(0, LAT_DEV)]
    return [(row, row + step) for row in range(0, LAT_DEV, step)]


def local(inputs, weight, bias, analysis, field_weight):
    channels, cells = inputs.shape[1], inputs.shape[4]
    fields = analysis.shape[0]
    members = lax.axis_size("member")
    grid = Grid(cells, members)
    x = inputs.reshape(channels, cells)
    target = analysis.reshape(fields, cells)
    if grid.padded != cells:
        target = jnp.pad(target, ((0, 0), (0, grid.padded - cells)))
    rows = round_up(fields, 16)
    taps = weight.reshape(9, channels, fields)
    forward_weight = taps.transpose(2, 0, 1).reshape(fields, 9 * channels)
    backward_weight = jnp.pad(taps[::-1], ((0, 0), (0, 0), (0, rows - fields)))
    backward_weight = backward_weight.transpose(1, 0, 2).reshape(channels, 9 * rows)
    me = lax.axis_index("member").astype(jnp.int32)
    order = me ^ jnp.arange(members, dtype=jnp.int32)
    scale = jnp.broadcast_to(field_weight[:, None], (fields, LANES))
    shift = bias[:, None]

    x_sides = lon_halo(edges_of(grid, x))
    x_top, x_bottom = lat_halo(x, cells, grid.halo, x_sides)

    def to_members(pieces):
        moved = [pieces[0]]
        for d in range(1, members):
            moved.append(lax.ppermute(pieces[d], "member", [(i, i ^ d) for i in range(members)]))
        return moved

    chunks = chunks_of(grid, members)
    turn = sorted(range(len(chunks)), key=lambda i: i != len(chunks) // 2)
    received, returned, parts, edges, sums = {}, {}, {}, {}, {}
    for i in turn:
        first, width = chunks[i]
        received[i] = to_members(
            forward(grid, first, width, order, x, x_sides, x_top, x_bottom, forward_weight, shift)
        )
    for i in turn:
        returned[i] = to_members(score(chunks[i][0], order, target, scale, received[i]))
    for i in turn:
        first, width = chunks[i]
        parts[i], edges[i], sums[i] = weight_part(
            grid, first, width, rows, order, x, x_sides, x_top, x_bottom, returned[i]
        )
    parts = [parts[i] for i in range(len(chunks))]
    total = sum_all(functools.reduce(jnp.add, [sums[i] for i in turn]))
    g_sides = lon_halo(functools.reduce(jnp.add, [edges[i] for i in turn]))
    g_top, g_bottom = lat_halo_parts(parts, chunks, cells, grid.halo, g_sides)
    grad_input = None
    for r0, r1 in parts_of(grid, 2):
        grad_input = input_part(
            grid, r0, r1, chunks, parts, g_sides, g_top, g_bottom, backward_weight, grad_input
        )
    total = total / (cells * lax.axis_size("lat") * lax.axis_size("lon"))
    grad_weight = total[:fields, : 9 * channels].T.reshape(9, channels * fields)
    grad_bias = total[:fields, 9 * channels]
    return (grad_input.reshape(1, channels, 1, 1, cells), grad_weight, grad_bias)


def solution(mesh):
    placed = (P("member", None, "lat", "lon", None), P(), P(), P(None, "lat", "lon", None), P())
    return jax.shard_map(
        local,
        mesh=mesh,
        in_specs=placed,
        out_specs=(P("member", None, "lat", "lon", None), P(), P()),
        check_vma=False,
    )
```

```python
import functools

import jax
import jax.numpy as jnp
from jax import lax
from jax.experimental import pallas as pl
from jax.experimental.pallas import tpu as pltpu
from jax.sharding import PartitionSpec as P

LAT_DEV = 64
LANES = 128
ROW_GROUP = 2
VMEM_LIMIT = 22 * 1024 * 1024
F32 = jnp.float32
BF16 = jnp.bfloat16


def round_up(value, step):
    return -(-value // step) * step


def params():
    return pltpu.CompilerParams(vmem_limit_bytes=VMEM_LIMIT)


def shape_of(dims, dtype=BF16):
    return jax.ShapeDtypeStruct(dims, dtype)


def cost(flops, moved):
    return pl.CostEstimate(flops=int(flops), bytes_accessed=int(moved), transcendentals=0)


def in_vmem():
    return pl.BlockSpec(memory_space=pltpu.VMEM)


def in_smem():
    return pl.BlockSpec(memory_space=pltpu.SMEM)


def anywhere():
    return pl.BlockSpec(memory_space=pl.ANY)


def nt_dot(left, right):
    return lax.dot_general(left, right, (((1,), (1,)), ((), ())), preferred_element_type=F32)


class Grid:
    def __init__(self, cells, members):
        self.cells = cells
        self.columns = cells // LAT_DEV
        self.pitch = round_up(self.columns, LANES)
        self.halo = round_up(self.columns + 1, LANES)
        self.padded = round_up(cells, members * LANES)

    def rows(self, first, width):
        return first // self.columns, -(-min(first + width, self.cells) // self.columns)

    def span(self, low_row, high_row):
        low = ((low_row * self.columns - 1) // LANES) * LANES
        return low, round_up((high_row - 1) * self.columns + 1 + self.pitch, LANES)


def window_copies(grid, low, high, sources, target, sem):
    copies, filled = [], []
    for ref, begin, end, lane in sources:
        lo, hi = max(low, begin), min(high, end)
        if lo < hi:
            filled.append((lo, hi))
            copies.append(
                pltpu.make_async_copy(
                    ref.at[:, pl.ds(lane + lo - begin, hi - lo)],
                    target.at[:, pl.ds(lo - low, hi - lo)],
                    sem.at[len(copies)],
                )
            )
    holes, at = [], low
    for lo, hi in sorted(filled):
        if lo > at:
            holes.append((at - low, lo - low))
        at = max(at, hi)
    if at < high:
        holes.append((at - low, high - low))
    return copies, holes


def take(ref, start, width):
    low = start // LANES * LANES
    off = start - low
    if off == 0:
        return ref[:, low : low + width]
    return ref[:, low : low + width + LANES][:, off : off + width]


def side_column(refs, grid, row, right):
    own, top, bottom = refs
    slot = LAT_DEV if right else 0
    if row < 0:
        ref, lane = top, grid.halo + slot + LAT_DEV - 1
    elif row >= LAT_DEV:
        ref, lane = bottom, grid.halo + slot
    else:
        ref, lane = own, slot + row
    return ref[:, lane : lane + 1].astype(F32)


def with_column(tile, column, lane):
    here = lax.broadcasted_iota(jnp.int32, tile.shape, 1).astype(BF16) == lane
    return jnp.where(here, jnp.broadcast_to(column, tile.shape).astype(BF16), tile)


def build_taps(grid, low, first_row, last_row, window, sides, taps):
    rows = window.shape[0]
    for row in range(first_row, last_row):
        base = (row - first_row) * grid.pitch
        start = row * grid.columns - low
        for b in range(3):
            value = take(window, start + b - 1, grid.pitch)
            if b == 1:
                taps[pl.ds(rows, rows), base : base + grid.pitch] = value
                continue
            at = grid.columns - 1 if b == 2 else 0
            tile = at // LANES * LANES
            column = side_column(sides, grid, row, b == 2)
            for lane in range(0, grid.pitch, LANES):
                part = value[:, lane : lane + LANES]
                if lane == tile:
                    part = with_column(part, column, at - tile)
                taps[pl.ds(b * rows, rows), base + lane : base + lane + LANES] = part


def stacked_rows(grid, taps, row, count):
    width = count * grid.pitch
    return jnp.concatenate(
        [taps[:, (row + a) * grid.pitch : (row + a) * grid.pitch + width] for a in range(3)],
        axis=0,
    )


def groups_of(count):
    return [(row, min(ROW_GROUP, count - row)) for row in range(0, count, ROW_GROUP)]


def flatten(grid, pitched, skip, width, count):
    parts, left = [], width
    for row in range(count):
        begin = skip if row == 0 else 0
        size = min(grid.columns - begin, left)
        if size > 0:
            at = row * grid.pitch + begin
            parts.append(pitched[:, at : at + size])
            left -= size
    if left:
        parts.append(jnp.zeros((pitched.shape[0], left), BF16))
    return jnp.concatenate(parts, axis=1)


def edges_kernel(grid, x_ref, out_ref):
    columns = [x_ref[:, i : i + 1] for i in range(0, grid.cells, grid.columns)]
    columns += [
        x_ref[:, i : i + 1] for i in range(grid.columns - 1, grid.cells, grid.columns)
    ]
    out_ref[...] = jnp.concatenate(columns, axis=1)


def edges_of(grid, field):
    rows, cells = field.shape
    return pl.pallas_call(
        functools.partial(edges_kernel, grid),
        in_specs=[in_vmem()],
        out_specs=in_vmem(),
        out_shape=shape_of((rows, 2 * LAT_DEV)),
        compiler_params=params(),
        cost_estimate=cost(2 * rows * cells, 2 * rows * cells),
        name="edges",
    )(field)

def lon_halo(edges):
    peers = lax.axis_size("lon")
    right = [(i, (i + 1) % peers) for i in range(peers)]
    left = [(j, i) for i, j in right]
    before = lax.ppermute(edges[:, LAT_DEV:], "lon", right)
    after = lax.ppermute(edges[:, :LAT_DEV], "lon", left)
    return jnp.concatenate([before, after], axis=1)


def lat_halo(field, cells, halo, sides):
    return lat_halo_parts([field], [(0, cells)], cells, halo, sides)


def lat_halo_parts(parts, chunks, cells, halo, sides):
    end = cells - chunks[-1][0]
    peers = lax.axis_size("lat")
    up = [(i, i + 1) for i in range(peers - 1)]
    down = [(j, i) for i, j in up]
    top = lax.ppermute(
        jnp.concatenate([parts[-1][:, end - halo : end], sides], axis=1), "lat", up
    )
    bottom = lax.ppermute(jnp.concatenate([parts[0][:, :halo], sides], axis=1), "lat", down)
    return top, bottom


def read_window(grid, low, high, sources, window, sem):
    copies, holes = window_copies(grid, low, high, sources, window, sem)
    for copy in copies:
        copy.start()
    for begin, end in holes:
        window[:, begin:end] = jnp.zeros((window.shape[0], end - begin), BF16)
    for copy in copies:
        copy.wait()


def field_sources(grid, field, top, bottom):
    sources = [(field, 0, grid.cells, 0)]
    if top is not None:
        sources.append((top, -grid.halo, 0, 0))
    if bottom is not None:
        sources.append((bottom, grid.cells, grid.cells + grid.halo, 0))
    return sources


def forward_kernel(grid, first, width, has_top, has_bottom, members, *refs):
    refs = list(refs)
    x_ref, sides_ref = refs[:2]
    del refs[:2]
    top_ref = refs.pop(0) if has_top else None
    bottom_ref = refs.pop(0) if has_bottom else None
    weight_ref, bias_ref, analysis_ref = refs[:3]
    outs = refs[3 : 3 + members]
    target_ref, window, taps, pitched, pred, sem, target_sem = refs[3 + members :]
    me = lax.axis_index("member")
    piece = width // members
    begin = pl.multiple_of(first + me * piece, LANES)
    target_copy = pltpu.make_async_copy(
        analysis_ref.at[:, pl.ds(begin, piece)], target_ref, target_sem.at[0]
    )
    target_copy.start()
    r0, r1 = grid.rows(first, width)
    low, high = grid.span(r0 - 1, r1 + 1)
    read_window(
        grid, low, high, field_sources(grid, x_ref, top_ref, bottom_ref), window, sem
    )
    build_taps(grid, low, r0 - 1, r1 + 1, window, (sides_ref, top_ref, bottom_ref), taps)
    weight, bias = weight_ref[...], bias_ref[...]
    for row, count in groups_of(r1 - r0):
        value = jnp.dot(
            weight, stacked_rows(grid, taps, row, count), preferred_element_type=F32
        )
        pitched[:, row * grid.pitch : (row + count) * grid.pitch] = (value + bias).astype(BF16)
    pred[...] = flatten(grid, pitched, first - r0 * grid.columns, width, r1 - r0)
    for d in range(members):
        begin = pl.multiple_of((me ^ d) * piece, LANES)
        outs[d][...] = pred[:, pl.ds(begin, piece)]
    target_copy.wait()


def forward(grid, first, width, members, x, sides, top, bottom, weight, bias, analysis):
    channels = x.shape[0]
    fields = weight.shape[0]
    r0, r1 = grid.rows(first, width)
    low, high = grid.span(r0 - 1, r1 + 1)
    has_top, has_bottom = r0 == 0, r1 == LAT_DEV
    piece = width // members
    operands = [x, sides]
    specs = [anywhere(), in_vmem()]
    if has_top:
        operands.append(top)
        specs.append(in_vmem())
    if has_bottom:
        operands.append(bottom)
        specs.append(in_vmem())
    operands += [weight, bias, analysis]
    specs += [in_vmem(), in_vmem(), anywhere()]
    return pl.pallas_call(
        functools.partial(forward_kernel, grid, first, width, has_top, has_bottom, members),
        in_specs=specs,
        out_specs=[in_vmem()] * (members + 1),
        out_shape=[shape_of((fields, piece))] * (members + 1),
        scratch_shapes=[
            pltpu.VMEM((channels, high - low), BF16),
            pltpu.VMEM((3 * channels, (r1 - r0 + 2) * grid.pitch), BF16),
            pltpu.VMEM((fields, (r1 - r0) * grid.pitch), BF16),
            pltpu.VMEM((fields, width), BF16),
            pltpu.SemaphoreType.DMA((3,)),
            pltpu.SemaphoreType.DMA((1,)),
        ],
        compiler_params=params(),
        cost_estimate=cost(2 * 9 * channels * 2 * fields * width, 8 * channels * width),
        name=f"forward_{first}",
    )(*operands)


def slope(values):
    return values * lax.rsqrt(values * values + 1.0)


def score_kernel(members, target_ref, scale_ref, *refs):
    pieces = refs[:members]
    outs = refs[members : 2 * members]
    fields, piece = pieces[0].shape
    tiles = piece // LANES
    several = max(k for k in (1, 2, 3) if tiles % k == 0)

    def tile(index, carry):
        for part in range(several * -(-fields // 16)):
            low = part // several * 16
            at = (index * several + part % several) * LANES
            span = pl.ds(pl.multiple_of(at, LANES), LANES)
            rows = pl.ds(low, min(16, fields - low))
            values = [ref[rows, span].astype(F32) for ref in pieces]
            target = target_ref[rows, span].astype(F32)
            scale = scale_ref[rows, :]
            sums = [None] * members
            for i in range(members):
                for j in range(i + 1, members):
                    both = slope(values[i] - values[j])
                    sums[i] = both if sums[i] is None else sums[i] + both
                    sums[j] = -both if sums[j] is None else sums[j] - both
            for i in range(members):
                grad = slope(values[i] - target) * (1.0 / members) - sums[i] * (
                    1.0 / (members * (members - 1))
                )
                outs[i][rows, span] = (scale * grad).astype(BF16)
        return carry

    lax.fori_loop(0, tiles // several, tile, 0)


def score(first, target, scale, pieces):
    members = len(pieces)
    fields, piece = pieces[0].shape
    return pl.pallas_call(
        functools.partial(score_kernel, members),
        in_specs=[in_vmem(), in_vmem()] + [in_vmem()] * members,
        out_specs=[in_vmem()] * members,
        out_shape=[shape_of((fields, piece))] * members,
        compiler_params=params(),
        cost_estimate=cost(100 * fields * piece * 60, 18 * fields * piece),
        name=f"score_{first}",
    )(target, scale, *pieces)


def weight_kernel(grid, first, width, has_top, has_bottom, members, *refs):
    refs = list(refs)
    x_ref, sides_ref = refs[:2]
    del refs[:2]
    me = lax.axis_index("member")
    top_ref = refs.pop(0) if has_top else None
    bottom_ref = refs.pop(0) if has_bottom else None
    pieces = refs[:members]
    out_ref, edge_ref, sum_ref, window, taps, flat, pitched, sem = refs[members:]
    fields, piece = pieces[0].shape
    rows = out_ref.shape[0]
    r0, r1 = grid.rows(first, width)
    low, high = grid.span(r0 - 1, r1 + 1)
    copies, holes = window_copies(
        grid, low, high, field_sources(grid, x_ref, top_ref, bottom_ref), window, sem
    )
    for copy in copies:
        copy.start()
    for begin, end in holes:
        window[:, begin:end] = jnp.zeros((window.shape[0], end - begin), BF16)

    lead = grid.halo
    flat[:, :lead] = jnp.zeros((rows, lead), BF16)
    flat[:, lead + width :] = jnp.zeros((rows, flat.shape[1] - lead - width), BF16)
    base = fields // 16 * 16
    if base < rows:
        flat[pl.ds(base, rows - base), lead : lead + width] = jnp.zeros(
            (rows - base, width), BF16
        )
    for d in range(members):
        begin = pl.multiple_of((me ^ d) * piece, LANES)
        value = pieces[d][...]
        if grid.padded != grid.cells:
            cell = lax.broadcasted_iota(jnp.int32, (1, piece), 1) + (first + begin)
            value = jnp.where(cell < grid.cells, value.astype(F32), 0.0).astype(BF16)
        flat[pl.ds(0, fields), pl.ds(lead + begin, piece)] = value
    out_ref[...] = flat[:, lead : lead + width]
    columns = []
    for side in (0, grid.columns - 1):
        for row in range(LAT_DEV):
            at = row * grid.columns + side - first
            if 0 <= at < width:
                columns.append(flat[:, lead + at : lead + at + 1])
            else:
                columns.append(jnp.zeros((rows, 1), BF16))
    edge_ref[...] = jnp.concatenate(columns, axis=1)
    keep = jnp.where(
        lax.broadcasted_iota(jnp.int32, (1, LANES), 1) < grid.columns % LANES, 1.0, 0.0
    ).astype(BF16)
    for row in range(r0, r1):
        value = take(flat, lead + row * grid.columns - first, grid.pitch)
        to = (row - r0) * grid.pitch
        for lane in range(0, grid.pitch, LANES):
            part = value[:, lane : lane + LANES]
            if lane + LANES > grid.columns:
                part = part * keep
            pitched[:, to + lane : to + lane + LANES] = part

    for copy in copies:
        copy.wait()
    build_taps(grid, low, r0 - 1, r1 + 1, window, (sides_ref, top_ref, bottom_ref), taps)
    for row, count in groups_of(r1 - r0):
        stacked = stacked_rows(grid, taps, row, count)
        ones = jnp.ones((sum_ref.shape[1] - stacked.shape[0], stacked.shape[1]), BF16)
        part = nt_dot(
            pitched[:, row * grid.pitch : (row + count) * grid.pitch],
            jnp.concatenate([stacked, ones], axis=0),
        )
        if row == 0:
            sum_ref[...] = part
        else:
            sum_ref[...] += part


def weight_part(grid, first, width, rows, x, sides, top, bottom, pieces):
    members = len(pieces)
    channels = x.shape[0]
    r0, r1 = grid.rows(first, width)
    low, high = grid.span(r0 - 1, r1 + 1)
    has_top, has_bottom = r0 == 0, r1 == LAT_DEV
    operands = [x, sides]
    specs = [anywhere(), in_vmem()]
    if has_top:
        operands.append(top)
        specs.append(in_vmem())
    if has_bottom:
        operands.append(bottom)
        specs.append(in_vmem())
    sums = round_up(9 * channels + 1, LANES)
    return pl.pallas_call(
        functools.partial(weight_kernel, grid, first, width, has_top, has_bottom, members),
        in_specs=specs + [in_vmem()] * members,
        out_specs=[in_vmem()] * 3,
        out_shape=[
            shape_of((rows, width)),
            shape_of((rows, 2 * LAT_DEV)),
            shape_of((rows, sums), F32),
        ],
        scratch_shapes=[
            pltpu.VMEM((channels, high - low), BF16),
            pltpu.VMEM((3 * channels, (r1 - r0 + 2) * grid.pitch), BF16),
            pltpu.VMEM((rows, 2 * grid.halo + 2 * LANES + width), BF16),
            pltpu.VMEM((rows, (r1 - r0) * grid.pitch), BF16),
            pltpu.SemaphoreType.DMA((3,)),
        ],
        compiler_params=params(),
        cost_estimate=cost(2 * 9 * channels * 2 * rows * width, 8 * channels * width),
        name=f"weight_{first}",
    )(*operands, *pieces)


def input_kernel(grid, r0, r1, chunks, aliased, *refs):
    refs = list(refs)
    parts = refs[: len(chunks)]
    del refs[: len(chunks)]
    sides_ref, top_ref, bottom_ref, weight_ref = refs[:4]
    del refs[: 5 if aliased else 4]
    out_ref, window, taps, pitched, flat, sem, out_sem = refs
    low, high = grid.span(r0 - 1, r1 + 1)
    sources = [
        (ref, first, min(first + width, grid.cells), 0)
        for ref, (first, width) in zip(parts, chunks)
    ]
    sources += [(top_ref, -grid.halo, 0, 0)]
    sources += [(bottom_ref, grid.cells, grid.cells + grid.halo, 0)]
    read_window(grid, low, high, sources, window, sem)
    build_taps(grid, low, r0 - 1, r1 + 1, window, (sides_ref, top_ref, bottom_ref), taps)
    weight = weight_ref[...]
    for row, count in groups_of(r1 - r0):
        value = jnp.dot(
            weight, stacked_rows(grid, taps, row, count), preferred_element_type=F32
        )
        pitched[:, row * grid.pitch : (row + count) * grid.pitch] = value.astype(BF16)
    width = (r1 - r0) * grid.columns
    flat[...] = flatten(grid, pitched, 0, width, r1 - r0)
    copy = pltpu.make_async_copy(
        flat, out_ref.at[:, pl.ds(r0 * grid.columns, width)], out_sem.at[0]
    )
    copy.start()
    copy.wait()


def input_part(grid, r0, r1, chunks, parts, sides, top, bottom, weight, before):
    rows = parts[0].shape[0]
    channels = weight.shape[0]
    low, high = grid.span(r0 - 1, r1 + 1)
    width = (r1 - r0) * grid.columns
    operands = [*parts, sides, top, bottom, weight]
    specs = [anywhere()] * len(parts) + [in_vmem()] * 4
    alias = {}
    if before is not None:
        alias = {len(operands): 0}
        operands.append(before)
        specs.append(anywhere())
    return pl.pallas_call(
        functools.partial(input_kernel, grid, r0, r1, chunks, before is not None),
        in_specs=specs,
        out_specs=anywhere(),
        out_shape=shape_of((channels, grid.cells)),
        input_output_aliases=alias,
        scratch_shapes=[
            pltpu.VMEM((rows, high - low), BF16),
            pltpu.VMEM((3 * rows, (r1 - r0 + 2) * grid.pitch), BF16),
            pltpu.VMEM((channels, (r1 - r0) * grid.pitch), BF16),
            pltpu.VMEM((channels, width), BF16),
            pltpu.SemaphoreType.DMA((len(parts) + 2,)),
            pltpu.SemaphoreType.DMA((1,)),
        ],
        compiler_params=params(),
        cost_estimate=cost(4 * 9 * channels * rows * width, 8 * channels * width),
        name=f"input_{r0}",
    )(*operands)


def sum_all(value):
    halved = []
    for axis in ("lat", "member", "lon"):
        bit = 1
        while bit < lax.axis_size(axis):
            swap = [(i, i ^ bit) for i in range(lax.axis_size(axis))]
            rows = value.shape[0]
            if rows % 16 == 0 and len(halved) < 2:
                upper = (lax.axis_index(axis) & bit) != 0
                low, high = value[: rows // 2], value[rows // 2 :]
                keep, send = (jnp.where(upper, high, low), jnp.where(upper, low, high))
                value = keep + lax.ppermute(send, axis, swap)
                halved.append((axis, swap, upper))
            else:
                value = value + lax.ppermute(value, axis, swap)
            bit *= 2
    for axis, swap, upper in reversed(halved):
        other = lax.ppermute(value, axis, swap)
        value = jnp.where(
            upper,
            jnp.concatenate([other, value], axis=0),
            jnp.concatenate([value, other], axis=0),
        )
    return value


def chunks_of(grid, members):
    units = grid.padded // (members * LANES)
    count = 3 if units % 3 == 0 else 1
    width = units // count * members * LANES
    return [(i * width, width) for i in range(count)]


def parts_of(grid, wanted):
    step = LAT_DEV // wanted
    if step * grid.columns % LANES:
        return [(0, LAT_DEV)]
    return [(row, row + step) for row in range(0, LAT_DEV, step)]


def local(inputs, weight, bias, analysis, field_weight):
    channels, cells = inputs.shape[1], inputs.shape[4]
    fields = analysis.shape[0]
    members = lax.axis_size("member")
    grid = Grid(cells, members)
    x = inputs.reshape(channels, cells)
    target = analysis.reshape(fields, cells)
    if grid.padded != cells:
        target = jnp.pad(target, ((0, 0), (0, grid.padded - cells)))
    rows = round_up(fields, 16)
    taps = weight.reshape(9, channels, fields)
    forward_weight = taps.transpose(2, 0, 1).reshape(fields, 9 * channels)
    backward_weight = jnp.pad(taps[::-1], ((0, 0), (0, 0), (0, rows - fields)))
    backward_weight = backward_weight.transpose(1, 0, 2).reshape(channels, 9 * rows)
    scale = jnp.broadcast_to(field_weight[:, None], (fields, LANES))
    shift = bias[:, None]

    x_sides = lon_halo(edges_of(grid, x))
    x_top, x_bottom = lat_halo(x, cells, grid.halo, x_sides)

    def to_members(pieces):
        moved = [pieces[0]]
        for d in range(1, members):
            moved.append(lax.ppermute(pieces[d], "member", [(i, i ^ d) for i in range(members)]))
        return moved

    chunks = chunks_of(grid, members)
    turn = sorted(range(len(chunks)), key=lambda i: i != len(chunks) // 2)
    received, returned, targets, parts, edges, sums = {}, {}, {}, {}, {}, {}

    def weigh(i):
        first, width = chunks[i]
        parts[i], edges[i], sums[i] = weight_part(
            grid, first, width, rows, x, x_sides, x_top, x_bottom, returned[i]
        )

    for i in turn:
        first, width = chunks[i]
        *pieces, targets[i] = forward(
            grid, first, width, members, x, x_sides, x_top, x_bottom, forward_weight, shift,
            target,
        )
        received[i] = to_members(pieces)
    for at, i in enumerate(turn):
        if at >= 2:
            weigh(turn[at - 2])
            received[i], edges[turn[at - 2]] = lax.optimization_barrier(
                (received[i], edges[turn[at - 2]])
            )
        returned[i] = to_members(score(chunks[i][0], targets[i], scale, received[i]))
    for i in turn[-2:]:
        weigh(i)
    parts = [parts[i] for i in range(len(chunks))]
    total = sum_all(functools.reduce(jnp.add, [sums[i] for i in turn]))
    g_sides = lon_halo(functools.reduce(jnp.add, [edges[i] for i in turn]))
    g_top, g_bottom = lat_halo_parts(parts, chunks, cells, grid.halo, g_sides)
    grad_input = None
    for r0, r1 in parts_of(grid, 2):
        grad_input = input_part(
            grid, r0, r1, chunks, parts, g_sides, g_top, g_bottom, backward_weight, grad_input
        )
    total = total / (cells * lax.axis_size("lat") * lax.axis_size("lon"))
    grad_weight = total[:fields, : 9 * channels].T.reshape(9, channels * fields)
    grad_bias = total[:fields, 9 * channels]
    return (grad_input.reshape(1, channels, 1, 1, cells), grad_weight, grad_bias)


def solution(mesh):
    placed = (P("member", None, "lat", "lon", None), P(), P(), P(None, "lat", "lon", None), P())
    return jax.shard_map(
        local,
        mesh=mesh,
        in_specs=placed,
        out_specs=(P("member", None, "lat", "lon", None), P(), P()),
        check_vma=False,
    )
```

```python
import functools

import jax
import jax.numpy as jnp
from jax import lax
from jax.experimental import pallas as pl
from jax.experimental.pallas import tpu as pltpu
from jax.sharding import PartitionSpec as P

LAT_DEV = 64
LANES = 128
ROW_GROUP = 2
VMEM_LIMIT = 22 * 1024 * 1024
F32 = jnp.float32
BF16 = jnp.bfloat16


def round_up(value, step):
    return -(-value // step) * step


def params():
    return pltpu.CompilerParams(vmem_limit_bytes=VMEM_LIMIT)


def shape_of(dims, dtype=BF16):
    return jax.ShapeDtypeStruct(dims, dtype)


def cost(flops, moved):
    return pl.CostEstimate(flops=int(flops), bytes_accessed=int(moved), transcendentals=0)


def in_vmem():
    return pl.BlockSpec(memory_space=pltpu.VMEM)


def in_smem():
    return pl.BlockSpec(memory_space=pltpu.SMEM)


def in_hbm():
    return pl.BlockSpec(memory_space=pltpu.HBM)


def anywhere():
    return pl.BlockSpec(memory_space=pl.ANY)


def nt_dot(left, right):
    return lax.dot_general(left, right, (((1,), (1,)), ((), ())), preferred_element_type=F32)


class Grid:
    def __init__(self, cells, members):
        self.cells = cells
        self.columns = cells // LAT_DEV
        self.pitch = round_up(self.columns, LANES)
        self.halo = round_up(self.columns + 1, LANES)
        self.padded = round_up(cells, members * LANES)

    def rows(self, first, width):
        return first // self.columns, -(-min(first + width, self.cells) // self.columns)

    def span(self, low_row, high_row):
        low = ((low_row * self.columns - 1) // LANES) * LANES
        return low, round_up((high_row - 1) * self.columns + 1 + self.pitch, LANES)


def window_copies(grid, low, high, sources, target, sem):
    copies, filled = [], []
    for ref, begin, end, lane in sources:
        lo, hi = max(low, begin), min(high, end)
        if lo < hi:
            filled.append((lo, hi))
            copies.append(
                pltpu.make_async_copy(
                    ref.at[:, pl.ds(lane + lo - begin, hi - lo)],
                    target.at[:, pl.ds(lo - low, hi - lo)],
                    sem.at[len(copies)],
                )
            )
    holes, at = [], low
    for lo, hi in sorted(filled):
        if lo > at:
            holes.append((at - low, lo - low))
        at = max(at, hi)
    if at < high:
        holes.append((at - low, high - low))
    return copies, holes


def take(ref, start, width):
    low = start // LANES * LANES
    off = start - low
    if off == 0:
        return ref[:, low : low + width]
    return ref[:, low : low + width + LANES][:, off : off + width]


def side_column(refs, grid, row, right):
    own, top, bottom = refs
    slot = LAT_DEV if right else 0
    if row < 0:
        ref, lane = top, grid.halo + slot + LAT_DEV - 1
    elif row >= LAT_DEV:
        ref, lane = bottom, grid.halo + slot
    else:
        ref, lane = own, slot + row
    return ref[:, lane : lane + 1].astype(F32)


def with_column(tile, column, lane):
    here = lax.broadcasted_iota(jnp.int32, tile.shape, 1).astype(BF16) == lane
    return jnp.where(here, jnp.broadcast_to(column, tile.shape).astype(BF16), tile)


def build_taps(grid, low, first_row, last_row, window, sides, taps):
    rows = window.shape[0]
    for row in range(first_row, last_row):
        base = (row - first_row) * grid.pitch
        start = row * grid.columns - low
        for b in range(3):
            value = take(window, start + b - 1, grid.pitch)
            if b == 1:
                taps[pl.ds(rows, rows), base : base + grid.pitch] = value
                continue
            at = grid.columns - 1 if b == 2 else 0
            tile = at // LANES * LANES
            column = side_column(sides, grid, row, b == 2)
            for lane in range(0, grid.pitch, LANES):
                part = value[:, lane : lane + LANES]
                if lane == tile:
                    part = with_column(part, column, at - tile)
                taps[pl.ds(b * rows, rows), base + lane : base + lane + LANES] = part


def stacked_rows(grid, taps, row, count):
    width = count * grid.pitch
    return jnp.concatenate(
        [taps[:, (row + a) * grid.pitch : (row + a) * grid.pitch + width] for a in range(3)],
        axis=0,
    )


def groups_of(count):
    return [(row, min(ROW_GROUP, count - row)) for row in range(0, count, ROW_GROUP)]


def flatten(grid, pitched, skip, width, count):
    parts, left = [], width
    for row in range(count):
        begin = skip if row == 0 else 0
        size = min(grid.columns - begin, left)
        if size > 0:
            at = row * grid.pitch + begin
            parts.append(pitched[:, at : at + size])
            left -= size
    if left:
        parts.append(jnp.zeros((pitched.shape[0], left), BF16))
    return jnp.concatenate(parts, axis=1)


def edges_kernel(grid, places, tiles, x_ref, out_ref, held, sem):
    copies = [
        pltpu.make_async_copy(
            x_ref.at[:, pl.ds(tile * LANES, LANES)],
            held.at[:, pl.ds(number * LANES, LANES)],
            sem.at[number],
        )
        for number, tile in enumerate(tiles)
    ]
    for copy in copies:
        copy.start()
    for copy in copies:
        copy.wait()
    columns = []
    for cell in places:
        at = tiles.index(cell // LANES) * LANES + cell % LANES
        columns.append(held[:, at : at + 1])
    out_ref[...] = jnp.concatenate(columns, axis=1)


def edges_of(grid, field):
    rows, cells = field.shape
    places = [i for i in range(0, grid.cells, grid.columns)]
    places += [i for i in range(grid.columns - 1, grid.cells, grid.columns)]
    tiles = sorted({cell // LANES for cell in places})
    return pl.pallas_call(
        functools.partial(edges_kernel, grid, places, tiles),
        in_specs=[in_hbm()],
        out_specs=in_vmem(),
        out_shape=shape_of((rows, 2 * LAT_DEV)),
        scratch_shapes=[
            pltpu.VMEM((rows, len(tiles) * LANES), BF16),
            pltpu.SemaphoreType.DMA((len(tiles),)),
        ],
        compiler_params=params(),
        cost_estimate=cost(2 * rows * cells, 2 * rows * cells),
        name="edges",
    )(field)


def lon_halo(edges):
    peers = lax.axis_size("lon")
    right = [(i, (i + 1) % peers) for i in range(peers)]
    left = [(j, i) for i, j in right]
    before = lax.ppermute(edges[:, LAT_DEV:], "lon", right)
    after = lax.ppermute(edges[:, :LAT_DEV], "lon", left)
    return jnp.concatenate([before, after], axis=1)


def lat_halo(first_rows, last_rows, sides):
    peers = lax.axis_size("lat")
    if peers == 2:
        upper = lax.axis_index("lat") == 0
        sent = jnp.concatenate([jnp.where(upper, last_rows, first_rows), sides], axis=1)
        other = lax.ppermute(sent, "lat", [(0, 1), (1, 0)])
        none = jnp.zeros_like(other)
        return jnp.where(upper, none, other), jnp.where(upper, other, none)
    up = [(i, i + 1) for i in range(peers - 1)]
    down = [(j, i) for i, j in up]
    top = lax.ppermute(jnp.concatenate([last_rows, sides], axis=1), "lat", up)
    bottom = lax.ppermute(jnp.concatenate([first_rows, sides], axis=1), "lat", down)
    return top, bottom


def read_window(grid, low, high, sources, window, sem):
    copies, holes = window_copies(grid, low, high, sources, window, sem)
    for copy in copies:
        copy.start()
    for begin, end in holes:
        window[:, begin:end] = jnp.zeros((window.shape[0], end - begin), BF16)
    for copy in copies:
        copy.wait()


def field_sources(grid, field, top, bottom):
    sources = [(field, 0, grid.cells, 0)]
    if top is not None:
        sources.append((top, -grid.halo, 0, 0))
    if bottom is not None:
        sources.append((bottom, grid.cells, grid.cells + grid.halo, 0))
    return sources


def forward_kernel(grid, first, width, has_top, has_bottom, members, waits, *refs):
    refs = list(refs)
    x_ref, sides_ref = refs[:2]
    del refs[:2]
    top_ref = refs.pop(0) if has_top else None
    bottom_ref = refs.pop(0) if has_bottom else None
    weight_ref, bias_ref, analysis_ref = refs[:3]
    del refs[: 3 + waits]
    outs = refs[:members]
    target_ref, taps, window, pitched, pred, sem, target_sem = refs[members:]
    me = lax.axis_index("member")
    piece = width // members
    begin = pl.multiple_of(first + me * piece, LANES)
    target_copy = pltpu.make_async_copy(
        analysis_ref.at[:, pl.ds(begin, piece)], target_ref, target_sem.at[0]
    )
    target_copy.start()
    r0, r1 = grid.rows(first, width)
    low, high = grid.span(r0 - 1, r1 + 1)
    read_window(
        grid, low, high, field_sources(grid, x_ref, top_ref, bottom_ref), window, sem
    )
    build_taps(grid, low, r0 - 1, r1 + 1, window, (sides_ref, top_ref, bottom_ref), taps)
    weight, bias = weight_ref[...], bias_ref[...]
    for row, count in groups_of(r1 - r0):
        value = jnp.dot(
            weight, stacked_rows(grid, taps, row, count), preferred_element_type=F32
        )
        pitched[:, row * grid.pitch : (row + count) * grid.pitch] = (value + bias).astype(BF16)
    pred[...] = flatten(grid, pitched, first - r0 * grid.columns, width, r1 - r0)
    for d in range(members):
        begin = pl.multiple_of((me ^ d) * piece, LANES)
        outs[d][...] = pred[:, pl.ds(begin, piece)]
    target_copy.wait()


def forward(grid, first, width, members, x, sides, top, bottom, weight, bias, analysis, after):
    channels = x.shape[0]
    fields = weight.shape[0]
    r0, r1 = grid.rows(first, width)
    low, high = grid.span(r0 - 1, r1 + 1)
    has_top, has_bottom = r0 == 0, r1 == LAT_DEV
    piece = width // members
    operands = [x, sides]
    specs = [in_hbm(), in_vmem()]
    if has_top:
        operands.append(top)
        specs.append(in_vmem())
    if has_bottom:
        operands.append(bottom)
        specs.append(in_vmem())
    operands += [weight, bias, analysis, *after]
    specs += [in_vmem(), in_vmem(), in_hbm()] + [anywhere()] * len(after)
    return pl.pallas_call(
        functools.partial(
            forward_kernel, grid, first, width, has_top, has_bottom, members, len(after)
        ),
        in_specs=specs,
        out_specs=[in_vmem()] * (members + 2),
        out_shape=[shape_of((fields, piece))] * (members + 1)
        + [shape_of((3 * channels, (r1 - r0 + 2) * grid.pitch))],
        scratch_shapes=[
            pltpu.VMEM((channels, high - low), BF16),
            pltpu.VMEM((fields, (r1 - r0) * grid.pitch), BF16),
            pltpu.VMEM((fields, width), BF16),
            pltpu.SemaphoreType.DMA((3,)),
            pltpu.SemaphoreType.DMA((1,)),
        ],
        compiler_params=params(),
        cost_estimate=cost(2 * 9 * channels * 2 * fields * width, 8 * channels * width),
        name=f"forward_{first}",
    )(*operands)


def slope(values):
    return values * lax.rsqrt(values * values + 1.0)


def score_kernel(members, target_ref, scale_ref, *refs):
    pieces = refs[:members]
    outs = refs[-members:]
    fields, piece = pieces[0].shape
    tiles = piece // LANES
    several = max(k for k in (1, 2, 3) if tiles % k == 0)

    def tile(index, carry):
        for part in range(several * -(-fields // 16)):
            low = part // several * 16
            at = (index * several + part % several) * LANES
            span = pl.ds(pl.multiple_of(at, LANES), LANES)
            rows = pl.ds(low, min(16, fields - low))
            values = [ref[rows, span].astype(F32) for ref in pieces]
            target = target_ref[rows, span].astype(F32)
            scale = scale_ref[rows, :]
            sums = [None] * members
            for i in range(members):
                for j in range(i + 1, members):
                    both = slope(values[i] - values[j])
                    sums[i] = both if sums[i] is None else sums[i] + both
                    sums[j] = -both if sums[j] is None else sums[j] - both
            for i in range(members):
                grad = slope(values[i] - target) * (1.0 / members) - sums[i] * (
                    1.0 / (members * (members - 1))
                )
                outs[i][rows, span] = (scale * grad).astype(BF16)
        return carry

    lax.fori_loop(0, tiles // several, tile, 0)


def score(first, target, scale, pieces, after):
    members = len(pieces)
    fields, piece = pieces[0].shape
    return pl.pallas_call(
        functools.partial(score_kernel, members),
        in_specs=[in_vmem()] * (2 + members) + [anywhere()] * len(after),
        out_specs=[in_vmem()] * members,
        out_shape=[shape_of((fields, piece))] * members,
        compiler_params=params(),
        cost_estimate=cost(100 * fields * piece * 60, 18 * fields * piece),
        name=f"score_{first}",
    )(target, scale, *pieces, *after)


def weight_kernel(grid, first, width, members, chained, taps, *refs):
    me = lax.axis_index("member")
    pieces = refs[:members]
    before_ref = refs[members] if chained else None
    out_ref, edge_ref, sum_ref, flat, pitched = refs[members + chained :]
    fields, piece = pieces[0].shape
    rows = out_ref.shape[0]
    r0, r1 = grid.rows(first, width)
    lead = grid.halo
    flat[:, :lead] = jnp.zeros((rows, lead), BF16)
    flat[:, lead + width :] = jnp.zeros((rows, flat.shape[1] - lead - width), BF16)
    base = fields // 16 * 16
    if base < rows:
        flat[pl.ds(base, rows - base), lead : lead + width] = jnp.zeros(
            (rows - base, width), BF16
        )
    for d in range(members):
        begin = pl.multiple_of((me ^ d) * piece, LANES)
        value = pieces[d][...]
        if grid.padded != grid.cells:
            cell = lax.broadcasted_iota(jnp.int32, (1, piece), 1) + (first + begin)
            value = jnp.where(cell < grid.cells, value.astype(F32), 0.0).astype(BF16)
        flat[pl.ds(0, fields), pl.ds(lead + begin, piece)] = value
    out_ref[...] = flat[:, lead : lead + width]
    columns = []
    for side in (0, grid.columns - 1):
        for row in range(LAT_DEV):
            at = row * grid.columns + side - first
            if 0 <= at < width:
                columns.append(flat[:, lead + at : lead + at + 1])
            else:
                columns.append(jnp.zeros((rows, 1), BF16))
    edge_ref[...] = jnp.concatenate(columns, axis=1)
    keep = jnp.where(
        lax.broadcasted_iota(jnp.int32, (1, LANES), 1) < grid.columns % LANES, 1.0, 0.0
    ).astype(BF16)
    for row in range(r0, r1):
        value = take(flat, lead + row * grid.columns - first, grid.pitch)
        to = (row - r0) * grid.pitch
        for lane in range(0, grid.pitch, LANES):
            part = value[:, lane : lane + LANES]
            if lane + LANES > grid.columns:
                part = part * keep
            pitched[:, to + lane : to + lane + LANES] = part

    for row, count in groups_of(r1 - r0):
        stacked = stacked_rows(grid, taps, row, count)
        ones = jnp.ones((sum_ref.shape[1] - stacked.shape[0], stacked.shape[1]), BF16)
        part = nt_dot(
            pitched[:, row * grid.pitch : (row + count) * grid.pitch],
            jnp.concatenate([stacked, ones], axis=0),
        )
        if row == 0:
            sum_ref[...] = part + before_ref[...] if chained else part
        else:
            sum_ref[...] += part


def weight_part(grid, first, width, rows, taps, pieces, before):
    members = len(pieces)
    channels = taps.shape[0] // 3
    r0, r1 = grid.rows(first, width)
    sums = round_up(9 * channels + 1, LANES)
    chained = [] if before is None else [before]
    return pl.pallas_call(
        functools.partial(weight_kernel, grid, first, width, members, len(chained)),
        in_specs=[in_vmem()] * (1 + members + len(chained)),
        out_specs=[in_vmem()] * 3,
        out_shape=[
            shape_of((rows, width)),
            shape_of((rows, 2 * LAT_DEV)),
            shape_of((rows, sums), F32),
        ],
        scratch_shapes=[
            pltpu.VMEM((rows, 2 * grid.halo + 2 * LANES + width), BF16),
            pltpu.VMEM((rows, (r1 - r0) * grid.pitch), BF16),
        ],
        compiler_params=params(),
        cost_estimate=cost(2 * 9 * channels * 2 * rows * width, 8 * channels * width),
        name=f"weight_{first}",
    )(taps, *pieces, *chained)


def input_kernel(grid, r0, r1, chunks, aliased, *refs):
    refs = list(refs)
    parts = refs[: len(chunks)]
    del refs[: len(chunks)]
    sides_ref, weight_ref = refs[:2]
    del refs[:2]
    top_ref = refs.pop(0) if r0 == 0 else None
    bottom_ref = refs.pop(0) if r1 == LAT_DEV else None
    del refs[:aliased]
    out_ref, window, taps, pitched, flat, sem, out_sem = refs
    low, high = grid.span(r0 - 1, r1 + 1)
    sources = [
        (ref, first, min(first + width, grid.cells), 0)
        for ref, (first, width) in zip(parts, chunks)
    ]
    if r0 == 0:
        sources += [(top_ref, -grid.halo, 0, 0)]
    if r1 == LAT_DEV:
        sources += [(bottom_ref, grid.cells, grid.cells + grid.halo, 0)]
    read_window(grid, low, high, sources, window, sem)
    build_taps(grid, low, r0 - 1, r1 + 1, window, (sides_ref, top_ref, bottom_ref), taps)
    weight = weight_ref[...]
    for row, count in groups_of(r1 - r0):
        value = jnp.dot(
            weight, stacked_rows(grid, taps, row, count), preferred_element_type=F32
        )
        pitched[:, row * grid.pitch : (row + count) * grid.pitch] = value.astype(BF16)
    width = (r1 - r0) * grid.columns
    flat[...] = flatten(grid, pitched, 0, width, r1 - r0)
    copy = pltpu.make_async_copy(
        flat, out_ref.at[:, pl.ds(r0 * grid.columns, width)], out_sem.at[0]
    )
    copy.start()
    copy.wait()


def input_part(grid, r0, r1, chunks, parts, sides, top, bottom, weight, before):
    rows = parts[0].shape[0]
    channels = weight.shape[0]
    low, high = grid.span(r0 - 1, r1 + 1)
    width = (r1 - r0) * grid.columns
    operands = [*parts, sides, weight]
    specs = [anywhere()] * len(parts) + [in_vmem()] * 2
    if r0 == 0:
        operands.append(top)
        specs.append(in_vmem())
    if r1 == LAT_DEV:
        operands.append(bottom)
        specs.append(in_vmem())
    alias = {}
    if before is not None:
        alias = {len(operands): 0}
        operands.append(before)
        specs.append(anywhere())
    return pl.pallas_call(
        functools.partial(input_kernel, grid, r0, r1, chunks, int(before is not None)),
        in_specs=specs,
        out_specs=anywhere(),
        out_shape=shape_of((channels, grid.cells)),
        input_output_aliases=alias,
        scratch_shapes=[
            pltpu.VMEM((rows, high - low), BF16),
            pltpu.VMEM((3 * rows, (r1 - r0 + 2) * grid.pitch), BF16),
            pltpu.VMEM((channels, (r1 - r0) * grid.pitch), BF16),
            pltpu.VMEM((channels, width), BF16),
            pltpu.SemaphoreType.DMA((len(parts) + 2,)),
            pltpu.SemaphoreType.DMA((1,)),
        ],
        compiler_params=params(),
        cost_estimate=cost(4 * 9 * channels * rows * width, 8 * channels * width),
        name=f"input_{r0}",
    )(*operands)


def sum_all(value):
    halved = []
    for axis in ("lat", "member", "lon"):
        bit = 1
        while bit < lax.axis_size(axis):
            swap = [(i, i ^ bit) for i in range(lax.axis_size(axis))]
            rows = value.shape[0]
            if rows % 16 == 0 and len(halved) < 2:
                upper = (lax.axis_index(axis) & bit) != 0
                low, high = value[: rows // 2], value[rows // 2 :]
                keep, send = (jnp.where(upper, high, low), jnp.where(upper, low, high))
                value = keep + lax.ppermute(send, axis, swap)
                halved.append((axis, swap, upper))
            else:
                value = value + lax.ppermute(value, axis, swap)
            bit *= 2
    for axis, swap, upper in reversed(halved):
        other = lax.ppermute(value, axis, swap)
        value = jnp.where(
            upper,
            jnp.concatenate([other, value], axis=0),
            jnp.concatenate([value, other], axis=0),
        )
    return value


def chunks_of(grid, members):
    unit = members * LANES
    units = grid.padded // unit
    if units < 15:
        return [(0, grid.padded)], [0]
    sizes = [units * 2 // 5, units // 3]
    sizes.append(units - sum(sizes))
    first = [sum(sizes[:i]) for i in range(3)]
    return [(first[i] * unit, sizes[i] * unit) for i in range(3)], [1, 0, 2]


def parts_of(grid, wanted):
    step = LAT_DEV // wanted
    if step * grid.columns % LANES:
        return [(0, LAT_DEV)]
    ranges = [(row, row + step) for row in range(0, LAT_DEV, step)]
    return ranges[1:-1] + [ranges[0], ranges[-1]]


def local(inputs, weight, bias, analysis, field_weight):
    channels, cells = inputs.shape[1], inputs.shape[4]
    fields = analysis.shape[0]
    members = lax.axis_size("member")
    grid = Grid(cells, members)
    x = inputs.reshape(channels, cells)
    target = analysis.reshape(fields, cells)
    if grid.padded != cells:
        target = jnp.pad(target, ((0, 0), (0, grid.padded - cells)))
    rows = round_up(fields, 16)
    taps = weight.reshape(9, channels, fields)
    forward_weight = taps.transpose(2, 0, 1).reshape(fields, 9 * channels)
    backward_weight = jnp.pad(taps[::-1], ((0, 0), (0, 0), (0, rows - fields)))
    backward_weight = backward_weight.transpose(1, 0, 2).reshape(channels, 9 * rows)
    scale = jnp.broadcast_to(field_weight[:, None], (fields, LANES))
    shift = bias[:, None]

    x_sides = lon_halo(edges_of(grid, x))

    def to_members(pieces):
        moved = [pieces[0]]
        for d in range(1, members):
            moved.append(lax.ppermute(pieces[d], "member", [(i, i ^ d) for i in range(members)]))
        return moved

    chunks, turn = chunks_of(grid, members)
    received, returned, targets, taken = {}, {}, {}, {}
    parts, edges, sums = {}, {}, None
    x_top, x_bottom = None, None

    def x_lat_halo(sides):
        return lat_halo(x[:, : grid.halo], x[:, cells - grid.halo :], sides)

    def send(i, after):
        first, width = chunks[i]
        *pieces, targets[i], taken[i] = forward(
            grid, first, width, members, x, x_sides, x_top, x_bottom, forward_weight, shift,
            target, after,
        )
        received[i] = to_members(pieces)

    def answer(i, after):
        grads = score(chunks[i][0], targets[i], scale, received[i], after)
        returned[i] = to_members(grads)
        return grads[0]

    def weigh(i, before):
        first, width = chunks[i]
        parts[i], edges[i], total = weight_part(
            grid, first, width, rows, taken[i], returned[i], before
        )
        return total

    if len(turn) == 1:
        x_top, x_bottom = x_lat_halo(x_sides)
        send(0, [])
        answer(0, [])
        sums = weigh(0, None)
    else:
        a, b, c = turn
        send(a, [])
        late_sides, targets[a] = lax.optimization_barrier((x_sides, targets[a]))
        x_top, x_bottom = x_lat_halo(late_sides)
        send(b, [])
        done = answer(a, [targets[b]])
        send(c, [done])
        answer(b, [targets[c]])
        sums = weigh(a, None)
        answer(c, [edges[a]])
        sums = weigh(b, sums)
        sums = weigh(c, sums)
    parts = [parts[i] for i in range(len(chunks))]
    total = sum_all(sums)
    g_sides = lon_halo(functools.reduce(jnp.add, [edges[i] for i in turn]))
    end = cells - chunks[-1][0]
    g_top, g_bottom = lat_halo(
        parts[0][:, : grid.halo], parts[-1][:, end - grid.halo : end], g_sides
    )
    grad_input = None
    for r0, r1 in parts_of(grid, 4):
        grad_input = input_part(
            grid, r0, r1, chunks, parts, g_sides, g_top, g_bottom, backward_weight, grad_input
        )
    total = total / (cells * lax.axis_size("lat") * lax.axis_size("lon"))
    grad_weight = total[:fields, : 9 * channels].T.reshape(9, channels * fields)
    grad_bias = total[:fields, 9 * channels]
    return (grad_input.reshape(1, channels, 1, 1, cells), grad_weight, grad_bias)


def solution(mesh):
    placed = (P("member", None, "lat", "lon", None), P(), P(), P(None, "lat", "lon", None), P())
    return jax.shard_map(
        local,
        mesh=mesh,
        in_specs=placed,
        out_specs=(P("member", None, "lat", "lon", None), P(), P()),
        check_vma=False,
    )
```

```python
import functools

import jax
import jax.numpy as jnp
from jax import lax
from jax.experimental import pallas as pl
from jax.experimental.pallas import tpu as pltpu
from jax.sharding import PartitionSpec as P

LAT_DEV = 64
LANES = 128
ROW_GROUP = 2
SLACK = 3 * 1024 * 1024
F32 = jnp.float32
BF16 = jnp.bfloat16


def round_up(value, step):
    return -(-value // step) * step


def params(*held):
    total = sum(round_up(rows, 16) * round_up(lanes, LANES) * size for rows, lanes, size in held)
    return pltpu.CompilerParams(vmem_limit_bytes=total + SLACK)


def kept_in_hbm(value):
    return pltpu.with_memory_space_constraint(value, pltpu.HBM)


def shape_of(dims, dtype=BF16):
    return jax.ShapeDtypeStruct(dims, dtype)


def cost(flops, moved):
    return pl.CostEstimate(flops=int(flops), bytes_accessed=int(moved), transcendentals=0)


def in_vmem():
    return pl.BlockSpec(memory_space=pltpu.VMEM)


def in_smem():
    return pl.BlockSpec(memory_space=pltpu.SMEM)


def in_hbm():
    return pl.BlockSpec(memory_space=pltpu.HBM)


def anywhere():
    return pl.BlockSpec(memory_space=pl.ANY)


def nt_dot(left, right):
    return lax.dot_general(left, right, (((1,), (1,)), ((), ())), preferred_element_type=F32)


class Grid:
    def __init__(self, cells, members):
        self.cells = cells
        self.columns = cells // LAT_DEV
        self.pitch = round_up(self.columns, LANES)
        self.halo = round_up(self.columns + 1, LANES)
        self.padded = round_up(cells, members * LANES)

    def rows(self, first, width):
        return first // self.columns, -(-min(first + width, self.cells) // self.columns)

    def span(self, low_row, high_row):
        low = ((low_row * self.columns - 1) // LANES) * LANES
        return low, round_up((high_row - 1) * self.columns + 1 + self.pitch, LANES)


def window_copies(grid, low, high, sources, target, sem):
    copies, filled = [], []
    for ref, begin, end, lane in sources:
        lo, hi = max(low, begin), min(high, end)
        if lo < hi:
            filled.append((lo, hi))
            copies.append(
                pltpu.make_async_copy(
                    ref.at[:, pl.ds(lane + lo - begin, hi - lo)],
                    target.at[:, pl.ds(lo - low, hi - lo)],
                    sem.at[len(copies)],
                )
            )
    holes, at = [], low
    for lo, hi in sorted(filled):
        if lo > at:
            holes.append((at - low, lo - low))
        at = max(at, hi)
    if at < high:
        holes.append((at - low, high - low))
    return copies, holes


def take(ref, start, width):
    low = start // LANES * LANES
    off = start - low
    if off == 0:
        return ref[:, low : low + width]
    return ref[:, low : low + width + LANES][:, off : off + width]


def side_column(refs, grid, row, right):
    own, top, bottom = refs
    slot = LAT_DEV if right else 0
    if row < 0:
        ref, lane = top, grid.halo + slot + LAT_DEV - 1
    elif row >= LAT_DEV:
        ref, lane = bottom, grid.halo + slot
    else:
        ref, lane = own, slot + row
    return ref[:, lane : lane + 1].astype(F32)


def with_column(tile, column, lane):
    here = lax.broadcasted_iota(jnp.int32, tile.shape, 1).astype(BF16) == lane
    return jnp.where(here, jnp.broadcast_to(column, tile.shape).astype(BF16), tile)


def build_taps(grid, low, first_row, last_row, window, sides, taps):
    rows = window.shape[0]
    for row in range(first_row, last_row):
        base = (row - first_row) * grid.pitch
        start = row * grid.columns - low
        for b in range(3):
            value = take(window, start + b - 1, grid.pitch)
            if b == 1:
                taps[pl.ds(rows, rows), base : base + grid.pitch] = value
                continue
            at = grid.columns - 1 if b == 2 else 0
            tile = at // LANES * LANES
            column = side_column(sides, grid, row, b == 2)
            for lane in range(0, grid.pitch, LANES):
                part = value[:, lane : lane + LANES]
                if lane == tile:
                    part = with_column(part, column, at - tile)
                taps[pl.ds(b * rows, rows), base + lane : base + lane + LANES] = part


def stacked_rows(grid, taps, row, count):
    width = count * grid.pitch
    return jnp.concatenate(
        [taps[:, (row + a) * grid.pitch : (row + a) * grid.pitch + width] for a in range(3)],
        axis=0,
    )


def groups_of(count):
    return [(row, min(ROW_GROUP, count - row)) for row in range(0, count, ROW_GROUP)]


def flatten(grid, pitched, skip, width, count):
    parts, left = [], width
    for row in range(count):
        begin = skip if row == 0 else 0
        size = min(grid.columns - begin, left)
        if size > 0:
            at = row * grid.pitch + begin
            parts.append(pitched[:, at : at + size])
            left -= size
    if left:
        parts.append(jnp.zeros((pitched.shape[0], left), BF16))
    return jnp.concatenate(parts, axis=1)


def edges_kernel(grid, places, tiles, x_ref, out_ref, held, sem):
    copies = [
        pltpu.make_async_copy(
            x_ref.at[:, pl.ds(tile * LANES, LANES)],
            held.at[:, pl.ds(number * LANES, LANES)],
            sem.at[number],
        )
        for number, tile in enumerate(tiles)
    ]
    for copy in copies:
        copy.start()
    for copy in copies:
        copy.wait()
    columns = []
    for cell in places:
        at = tiles.index(cell // LANES) * LANES + cell % LANES
        columns.append(held[:, at : at + 1])
    out_ref[...] = jnp.concatenate(columns, axis=1)


def edges_of(grid, field):
    rows, cells = field.shape
    places = [i for i in range(0, grid.cells, grid.columns)]
    places += [i for i in range(grid.columns - 1, grid.cells, grid.columns)]
    tiles = sorted({cell // LANES for cell in places})
    return pl.pallas_call(
        functools.partial(edges_kernel, grid, places, tiles),
        in_specs=[in_hbm()],
        out_specs=in_vmem(),
        out_shape=shape_of((rows, 2 * LAT_DEV)),
        scratch_shapes=[
            pltpu.VMEM((rows, len(tiles) * LANES), BF16),
            pltpu.SemaphoreType.DMA((len(tiles),)),
        ],
        compiler_params=params((rows, (len(tiles) + 1) * LANES, 2)),
        cost_estimate=cost(2 * rows * cells, 2 * rows * cells),
        name="edges",
    )(kept_in_hbm(field))


def lon_halo(edges):
    peers = lax.axis_size("lon")
    right = [(i, (i + 1) % peers) for i in range(peers)]
    left = [(j, i) for i, j in right]
    before = lax.ppermute(edges[:, LAT_DEV:], "lon", right)
    after = lax.ppermute(edges[:, :LAT_DEV], "lon", left)
    return jnp.concatenate([before, after], axis=1)


def lat_halo(first_rows, last_rows, sides):
    peers = lax.axis_size("lat")
    if peers == 2:
        upper = lax.axis_index("lat") == 0
        sent = jnp.concatenate([jnp.where(upper, last_rows, first_rows), sides], axis=1)
        other = lax.ppermute(sent, "lat", [(0, 1), (1, 0)])
        none = jnp.zeros_like(other)
        return jnp.where(upper, none, other), jnp.where(upper, other, none)
    up = [(i, i + 1) for i in range(peers - 1)]
    down = [(j, i) for i, j in up]
    top = lax.ppermute(jnp.concatenate([last_rows, sides], axis=1), "lat", up)
    bottom = lax.ppermute(jnp.concatenate([first_rows, sides], axis=1), "lat", down)
    return top, bottom


def read_window(grid, low, high, sources, window, sem):
    copies, holes = window_copies(grid, low, high, sources, window, sem)
    for copy in copies:
        copy.start()
    for begin, end in holes:
        window[:, begin:end] = jnp.zeros((window.shape[0], end - begin), BF16)
    for copy in copies:
        copy.wait()


def field_sources(grid, field, top, bottom):
    sources = [(field, 0, grid.cells, 0)]
    if top is not None:
        sources.append((top, -grid.halo, 0, 0))
    if bottom is not None:
        sources.append((bottom, grid.cells, grid.cells + grid.halo, 0))
    return sources


def forward_kernel(grid, first, width, has_top, has_bottom, members, waits, *refs):
    refs = list(refs)
    x_ref, sides_ref = refs[:2]
    del refs[:2]
    top_ref = refs.pop(0) if has_top else None
    bottom_ref = refs.pop(0) if has_bottom else None
    weight_ref, bias_ref, analysis_ref = refs[:3]
    del refs[: 3 + waits]
    outs = refs[:members]
    target_ref, taps_out, taps, window, pitched, pred, sem, target_sem, taps_sem = refs[members:]
    me = lax.axis_index("member")
    piece = width // members
    begin = pl.multiple_of(first + me * piece, LANES)
    target_copy = pltpu.make_async_copy(
        analysis_ref.at[:, pl.ds(begin, piece)], target_ref, target_sem.at[0]
    )
    target_copy.start()
    r0, r1 = grid.rows(first, width)
    low, high = grid.span(r0 - 1, r1 + 1)
    read_window(
        grid, low, high, field_sources(grid, x_ref, top_ref, bottom_ref), window, sem
    )
    build_taps(grid, low, r0 - 1, r1 + 1, window, (sides_ref, top_ref, bottom_ref), taps)
    taps_copy = pltpu.make_async_copy(taps, taps_out, taps_sem.at[0])
    taps_copy.start()
    weight, bias = weight_ref[...], bias_ref[...]
    for row, count in groups_of(r1 - r0):
        value = jnp.dot(
            weight, stacked_rows(grid, taps, row, count), preferred_element_type=F32
        )
        pitched[:, row * grid.pitch : (row + count) * grid.pitch] = (value + bias).astype(BF16)
    pred[...] = flatten(grid, pitched, first - r0 * grid.columns, width, r1 - r0)
    for d in range(members):
        begin = pl.multiple_of((me ^ d) * piece, LANES)
        outs[d][...] = pred[:, pl.ds(begin, piece)]
    target_copy.wait()
    taps_copy.wait()


def forward(grid, first, width, members, x, sides, top, bottom, weight, bias, analysis, after):
    channels = x.shape[0]
    fields = weight.shape[0]
    r0, r1 = grid.rows(first, width)
    low, high = grid.span(r0 - 1, r1 + 1)
    has_top, has_bottom = r0 == 0, r1 == LAT_DEV
    piece = width // members
    operands = [kept_in_hbm(x), sides]
    specs = [in_hbm(), in_vmem()]
    if has_top:
        operands.append(top)
        specs.append(in_vmem())
    if has_bottom:
        operands.append(bottom)
        specs.append(in_vmem())
    operands += [weight, bias, kept_in_hbm(analysis), *after]
    specs += [in_vmem(), in_vmem(), in_hbm()] + [anywhere()] * len(after)
    return pl.pallas_call(
        functools.partial(
            forward_kernel, grid, first, width, has_top, has_bottom, members, len(after)
        ),
        in_specs=specs,
        out_specs=[in_vmem()] * (members + 1) + [in_hbm()],
        out_shape=[shape_of((fields, piece))] * (members + 1)
        + [pltpu.HBM((3 * channels, (r1 - r0 + 2) * grid.pitch), BF16)],
        scratch_shapes=[
            pltpu.VMEM((3 * channels, (r1 - r0 + 2) * grid.pitch), BF16),
            pltpu.VMEM((channels, high - low), BF16),
            pltpu.VMEM((fields, (r1 - r0) * grid.pitch), BF16),
            pltpu.VMEM((fields, width), BF16),
            pltpu.SemaphoreType.DMA((3,)),
            pltpu.SemaphoreType.DMA((1,)),
            pltpu.SemaphoreType.DMA((1,)),
        ],
        compiler_params=params(
            (3 * channels, (r1 - r0 + 2) * grid.pitch, 2),
            (channels, high - low + 3 * grid.halo, 2),
            (2 * fields, (r1 - r0) * grid.pitch, 2),
            (2 * fields, 2 * width, 2),
            (fields, 9 * channels, 2),
        ),
        cost_estimate=cost(width, width),
        name=f"forward_{first}",
    )(*operands)


def slope(values):
    return values * lax.rsqrt(values * values + 1.0)


def score_kernel(members, target_ref, scale_ref, *refs):
    pieces = refs[:members]
    outs = refs[-members:]
    fields, piece = pieces[0].shape
    tiles = piece // LANES
    several = max(k for k in (1, 2, 3) if tiles % k == 0)

    def tile(index, carry):
        for part in range(several * -(-fields // 16)):
            low = part // several * 16
            at = (index * several + part % several) * LANES
            span = pl.ds(pl.multiple_of(at, LANES), LANES)
            rows = pl.ds(low, min(16, fields - low))
            values = [ref[rows, span].astype(F32) for ref in pieces]
            target = target_ref[rows, span].astype(F32)
            scale = scale_ref[rows, :]
            sums = [None] * members
            for i in range(members):
                for j in range(i + 1, members):
                    both = slope(values[i] - values[j])
                    sums[i] = both if sums[i] is None else sums[i] + both
                    sums[j] = -both if sums[j] is None else sums[j] - both
            for i in range(members):
                grad = slope(values[i] - target) * (1.0 / members) - sums[i] * (
                    1.0 / (members * (members - 1))
                )
                outs[i][rows, span] = (scale * grad).astype(BF16)
        return carry

    lax.fori_loop(0, tiles // several, tile, 0)


def score(first, target, scale, pieces, after):
    members = len(pieces)
    fields, piece = pieces[0].shape
    return pl.pallas_call(
        functools.partial(score_kernel, members),
        in_specs=[in_vmem()] * (2 + members) + [anywhere()] * len(after),
        out_specs=[in_vmem()] * members,
        out_shape=[shape_of((fields, piece))] * members,
        compiler_params=params((9 * round_up(fields, 16), piece, 2), (fields, LANES, 4)),
        cost_estimate=cost(piece, piece),
        name=f"score_{first}",
    )(target, scale, *pieces, *after)


def weight_kernel(grid, first, width, members, chained, taps_ref, *refs):
    me = lax.axis_index("member")
    pieces = refs[:members]
    before_ref = refs[members] if chained else None
    out_ref, edge_ref, sum_ref, taps, flat, pitched, sem = refs[members + chained :]
    taps_copy = pltpu.make_async_copy(taps_ref, taps, sem.at[0])
    taps_copy.start()
    fields, piece = pieces[0].shape
    rows = out_ref.shape[0]
    r0, r1 = grid.rows(first, width)
    lead = grid.halo
    flat[:, :lead] = jnp.zeros((rows, lead), BF16)
    flat[:, lead + width :] = jnp.zeros((rows, flat.shape[1] - lead - width), BF16)
    base = fields // 16 * 16
    if base < rows:
        flat[pl.ds(base, rows - base), lead : lead + width] = jnp.zeros(
            (rows - base, width), BF16
        )
    for d in range(members):
        begin = pl.multiple_of((me ^ d) * piece, LANES)
        value = pieces[d][...]
        if grid.padded != grid.cells:
            cell = lax.broadcasted_iota(jnp.int32, (1, piece), 1) + (first + begin)
            value = jnp.where(cell < grid.cells, value.astype(F32), 0.0).astype(BF16)
        flat[pl.ds(0, fields), pl.ds(lead + begin, piece)] = value
    out_ref[...] = flat[:, lead : lead + width]
    columns = []
    for side in (0, grid.columns - 1):
        for row in range(LAT_DEV):
            at = row * grid.columns + side - first
            if 0 <= at < width:
                columns.append(flat[:, lead + at : lead + at + 1])
            else:
                columns.append(jnp.zeros((rows, 1), BF16))
    edge_ref[...] = jnp.concatenate(columns, axis=1)
    keep = jnp.where(
        lax.broadcasted_iota(jnp.int32, (1, LANES), 1) < grid.columns % LANES, 1.0, 0.0
    ).astype(BF16)
    for row in range(r0, r1):
        value = take(flat, lead + row * grid.columns - first, grid.pitch)
        to = (row - r0) * grid.pitch
        for lane in range(0, grid.pitch, LANES):
            part = value[:, lane : lane + LANES]
            if lane + LANES > grid.columns:
                part = part * keep
            pitched[:, to + lane : to + lane + LANES] = part

    taps_copy.wait()
    for row, count in groups_of(r1 - r0):
        stacked = stacked_rows(grid, taps, row, count)
        ones = jnp.ones((sum_ref.shape[1] - stacked.shape[0], stacked.shape[1]), BF16)
        part = nt_dot(
            pitched[:, row * grid.pitch : (row + count) * grid.pitch],
            jnp.concatenate([stacked, ones], axis=0),
        )
        if row == 0:
            sum_ref[...] = part + before_ref[...] if chained else part
        else:
            sum_ref[...] += part


def weight_part(grid, first, width, rows, taps, pieces, before):
    members = len(pieces)
    channels = taps.shape[0] // 3
    r0, r1 = grid.rows(first, width)
    sums = round_up(9 * channels + 1, LANES)
    chained = [] if before is None else [before]
    return pl.pallas_call(
        functools.partial(weight_kernel, grid, first, width, members, len(chained)),
        in_specs=[in_hbm()] + [in_vmem()] * (members + len(chained)),
        out_specs=[in_vmem()] * 3,
        out_shape=[
            shape_of((rows, width)),
            shape_of((rows, 2 * LAT_DEV)),
            shape_of((rows, sums), F32),
        ],
        scratch_shapes=[
            pltpu.VMEM(taps.shape, BF16),
            pltpu.VMEM((rows, 2 * grid.halo + 2 * LANES + width), BF16),
            pltpu.VMEM((rows, (r1 - r0) * grid.pitch), BF16),
            pltpu.SemaphoreType.DMA((1,)),
        ],
        compiler_params=params(
            (*taps.shape, 2),
            (rows, 2 * grid.halo + 2 * LANES + 3 * width, 2),
            (rows, (r1 - r0) * grid.pitch, 2),
            (rows, 3 * sums, 4),
        ),
        cost_estimate=cost(width, width),
        name=f"weight_{first}",
    )(kept_in_hbm(taps), *pieces, *chained)


def input_kernel(grid, r0, r1, chunks, aliased, *refs):
    refs = list(refs)
    parts = refs[: len(chunks)]
    del refs[: len(chunks)]
    sides_ref, weight_ref = refs[:2]
    del refs[:2]
    top_ref = refs.pop(0) if r0 == 0 else None
    bottom_ref = refs.pop(0) if r1 == LAT_DEV else None
    del refs[:aliased]
    out_ref, window, taps, pitched, flat, sem, out_sem = refs
    low, high = grid.span(r0 - 1, r1 + 1)
    sources = [
        (ref, first, min(first + width, grid.cells), 0)
        for ref, (first, width) in zip(parts, chunks)
    ]
    if r0 == 0:
        sources += [(top_ref, -grid.halo, 0, 0)]
    if r1 == LAT_DEV:
        sources += [(bottom_ref, grid.cells, grid.cells + grid.halo, 0)]
    read_window(grid, low, high, sources, window, sem)
    build_taps(grid, low, r0 - 1, r1 + 1, window, (sides_ref, top_ref, bottom_ref), taps)
    weight = weight_ref[...]
    for row, count in groups_of(r1 - r0):
        value = jnp.dot(
            weight, stacked_rows(grid, taps, row, count), preferred_element_type=F32
        )
        pitched[:, row * grid.pitch : (row + count) * grid.pitch] = value.astype(BF16)
    width = (r1 - r0) * grid.columns
    flat[...] = flatten(grid, pitched, 0, width, r1 - r0)
    copy = pltpu.make_async_copy(
        flat, out_ref.at[:, pl.ds(r0 * grid.columns, width)], out_sem.at[0]
    )
    copy.start()
    copy.wait()


def input_part(grid, r0, r1, chunks, parts, sides, top, bottom, weight, before):
    rows = parts[0].shape[0]
    channels = weight.shape[0]
    low, high = grid.span(r0 - 1, r1 + 1)
    width = (r1 - r0) * grid.columns
    operands = [*parts, sides, weight]
    specs = [anywhere()] * len(parts) + [in_vmem()] * 2
    if r0 == 0:
        operands.append(top)
        specs.append(in_vmem())
    if r1 == LAT_DEV:
        operands.append(bottom)
        specs.append(in_vmem())
    alias = {}
    if before is not None:
        alias = {len(operands): 0}
        operands.append(before)
        specs.append(anywhere())
    return pl.pallas_call(
        functools.partial(input_kernel, grid, r0, r1, chunks, int(before is not None)),
        in_specs=specs,
        out_specs=anywhere(),
        out_shape=shape_of((channels, grid.cells)),
        input_output_aliases=alias,
        scratch_shapes=[
            pltpu.VMEM((rows, high - low), BF16),
            pltpu.VMEM((3 * rows, (r1 - r0 + 2) * grid.pitch), BF16),
            pltpu.VMEM((channels, (r1 - r0) * grid.pitch), BF16),
            pltpu.VMEM((channels, width), BF16),
            pltpu.SemaphoreType.DMA((len(parts) + 2,)),
            pltpu.SemaphoreType.DMA((1,)),
        ],
        compiler_params=params(
            (rows, high - low + 3 * grid.halo, 2),
            (3 * rows, (r1 - r0 + 2) * grid.pitch, 2),
            (2 * channels, (r1 - r0) * grid.pitch, 2),
            (channels, 9 * rows, 2),
        ),
        cost_estimate=cost(4 * 9 * channels * rows * width, 8 * channels * width),
        name=f"input_{r0}",
    )(*operands)


def sum_all(value):
    halved = []
    for axis in ("lat", "member", "lon"):
        bit = 1
        while bit < lax.axis_size(axis):
            swap = [(i, i ^ bit) for i in range(lax.axis_size(axis))]
            rows = value.shape[0]
            if rows % 16 == 0 and len(halved) < 2:
                upper = (lax.axis_index(axis) & bit) != 0
                low, high = value[: rows // 2], value[rows // 2 :]
                keep, send = (jnp.where(upper, high, low), jnp.where(upper, low, high))
                value = keep + lax.ppermute(send, axis, swap)
                halved.append((axis, swap, upper))
            else:
                value = value + lax.ppermute(value, axis, swap)
            bit *= 2
    for axis, swap, upper in reversed(halved):
        other = lax.ppermute(value, axis, swap)
        value = jnp.where(
            upper,
            jnp.concatenate([other, value], axis=0),
            jnp.concatenate([value, other], axis=0),
        )
    return value


def chunks_of(grid, members):
    unit = members * LANES
    units = grid.padded // unit
    if units < 15:
        return [(0, grid.padded)], [0]
    sizes = [units * 3 // 8 + 1, units * 2 // 5]
    sizes.append(units - sum(sizes))
    first = [sum(sizes[:i]) for i in range(3)]
    return [(first[i] * unit, sizes[i] * unit) for i in range(3)], [1, 0, 2]


def parts_of(grid, wanted):
    step = LAT_DEV // wanted
    if step * grid.columns % LANES:
        return [(0, LAT_DEV)]
    ranges = [(row, row + step) for row in range(0, LAT_DEV, step)]
    return ranges[1:-1] + [ranges[0], ranges[-1]]


def local(inputs, weight, bias, analysis, field_weight):
    channels, cells = inputs.shape[1], inputs.shape[4]
    fields = analysis.shape[0]
    members = lax.axis_size("member")
    grid = Grid(cells, members)
    x = inputs.reshape(channels, cells)
    target = analysis.reshape(fields, cells)
    if grid.padded != cells:
        target = jnp.pad(target, ((0, 0), (0, grid.padded - cells)))
    rows = round_up(fields, 16)
    taps = weight.reshape(9, channels, fields)
    forward_weight = taps.transpose(2, 0, 1).reshape(fields, 9 * channels)
    backward_weight = jnp.pad(taps[::-1], ((0, 0), (0, 0), (0, rows - fields)))
    backward_weight = backward_weight.transpose(1, 0, 2).reshape(channels, 9 * rows)
    scale = jnp.broadcast_to(field_weight[:, None], (fields, LANES))
    shift = bias[:, None]

    x_sides = lon_halo(edges_of(grid, x))

    def to_members(pieces):
        moved = [pieces[0]]
        for d in range(1, members):
            moved.append(lax.ppermute(pieces[d], "member", [(i, i ^ d) for i in range(members)]))
        return moved

    chunks, turn = chunks_of(grid, members)
    received, returned, targets, taken = {}, {}, {}, {}
    parts, edges, sums = {}, {}, None
    x_top, x_bottom = None, None

    def x_lat_halo(sides):
        return lat_halo(x[:, : grid.halo], x[:, cells - grid.halo :], sides)

    def send(i, after):
        first, width = chunks[i]
        *pieces, targets[i], taken[i] = forward(
            grid, first, width, members, x, x_sides, x_top, x_bottom, forward_weight, shift,
            target, after,
        )
        received[i] = to_members(pieces)

    def answer(i, after):
        grads = score(chunks[i][0], targets[i], scale, received[i], after)
        returned[i] = to_members(grads)
        return grads[0]

    def weigh(i, before):
        first, width = chunks[i]
        parts[i], edges[i], total = weight_part(
            grid, first, width, rows, taken[i], returned[i], before
        )
        return total

    if len(turn) == 1:
        x_top, x_bottom = x_lat_halo(x_sides)
        send(0, [])
        answer(0, [])
        sums = weigh(0, None)
    else:
        a, b, c = turn
        send(a, [])
        late_sides, targets[a] = lax.optimization_barrier((x_sides, targets[a]))
        x_top, x_bottom = x_lat_halo(late_sides)
        send(b, [])
        done = answer(a, [targets[b]])
        send(c, [done])
        answer(b, [targets[c]])
        done = answer(c, [])
        returned[a][0], done = lax.optimization_barrier((returned[a][0], done))
        sums = weigh(a, None)
        sums = weigh(b, sums)
        sums = weigh(c, sums)
    ranges = parts_of(grid, 4)
    grad_input = None
    total = sum_all(sums)
    g_sides = lon_halo(functools.reduce(jnp.add, [edges[i] for i in turn]))
    parts = [parts[i] for i in range(len(chunks))]
    end = cells - chunks[-1][0]
    g_top, g_bottom = lat_halo(
        parts[0][:, : grid.halo], parts[-1][:, end - grid.halo : end], g_sides
    )
    for r0, r1 in ranges:
        grad_input = input_part(
            grid, r0, r1, chunks, parts, g_sides, g_top, g_bottom, backward_weight, grad_input
        )
    total = total / (cells * lax.axis_size("lat") * lax.axis_size("lon"))
    grad_weight = total[:fields, : 9 * channels].T.reshape(9, channels * fields)
    grad_bias = total[:fields, 9 * channels]
    return (grad_input.reshape(1, channels, 1, 1, cells), grad_weight, grad_bias)


def solution(mesh):
    placed = (P("member", None, "lat", "lon", None), P(), P(), P(None, "lat", "lon", None), P())
    return jax.shard_map(
        local,
        mesh=mesh,
        in_specs=placed,
        out_specs=(P("member", None, "lat", "lon", None), P(), P()),
        check_vma=False,
    )
```

```python
import functools

import jax
import jax.numpy as jnp
from jax import lax
from jax.experimental import pallas as pl
from jax.experimental.pallas import tpu as pltpu
from jax.sharding import PartitionSpec as P

LAT_DEV = 64
LANES = 128
ROW_GROUP = 2
SLACK = 3 * 1024 * 1024
F32 = jnp.float32
BF16 = jnp.bfloat16


def round_up(value, step):
    return -(-value // step) * step


def params(*held):
    total = sum(round_up(rows, 16) * round_up(lanes, LANES) * size for rows, lanes, size in held)
    return pltpu.CompilerParams(vmem_limit_bytes=total + SLACK)


def kept_in_hbm(value):
    return pltpu.with_memory_space_constraint(value, pltpu.HBM)


def kept_in_vmem(value):
    return pltpu.with_memory_space_constraint(value, pltpu.VMEM)


def shape_of(dims, dtype=BF16):
    return jax.ShapeDtypeStruct(dims, dtype)


def cost(flops, moved):
    return pl.CostEstimate(flops=int(flops), bytes_accessed=int(moved), transcendentals=0)


def in_vmem():
    return pl.BlockSpec(memory_space=pltpu.VMEM)


def in_smem():
    return pl.BlockSpec(memory_space=pltpu.SMEM)


def in_hbm():
    return pl.BlockSpec(memory_space=pltpu.HBM)


def anywhere():
    return pl.BlockSpec(memory_space=pl.ANY)


def nt_dot(left, right):
    return lax.dot_general(left, right, (((1,), (1,)), ((), ())), preferred_element_type=F32)


class Grid:
    def __init__(self, cells, members):
        self.cells = cells
        self.columns = cells // LAT_DEV
        self.pitch = round_up(self.columns, LANES)
        self.halo = round_up(self.columns + 1, LANES)
        self.padded = round_up(cells, members * LANES)

    def rows(self, first, width):
        return first // self.columns, -(-min(first + width, self.cells) // self.columns)

    def span(self, low_row, high_row):
        low = ((low_row * self.columns - 1) // LANES) * LANES
        return low, round_up((high_row - 1) * self.columns + 1 + self.pitch, LANES)


def window_copies(grid, low, high, sources, target, sem):
    copies, filled = [], []
    for ref, begin, end, lane in sources:
        lo, hi = max(low, begin), min(high, end)
        if lo < hi:
            filled.append((lo, hi))
            copies.append(
                pltpu.make_async_copy(
                    ref.at[:, pl.ds(lane + lo - begin, hi - lo)],
                    target.at[:, pl.ds(lo - low, hi - lo)],
                    sem.at[len(copies)],
                )
            )
    holes, at = [], low
    for lo, hi in sorted(filled):
        if lo > at:
            holes.append((at - low, lo - low))
        at = max(at, hi)
    if at < high:
        holes.append((at - low, high - low))
    return copies, holes


def take(ref, start, width):
    low = start // LANES * LANES
    off = start - low
    if off == 0:
        return ref[:, low : low + width]
    return ref[:, low : low + width + LANES][:, off : off + width]


def side_column(refs, grid, row, right):
    own, top, bottom = refs
    slot = LAT_DEV if right else 0
    if row < 0:
        ref, lane = top, grid.halo + slot + LAT_DEV - 1
    elif row >= LAT_DEV:
        ref, lane = bottom, grid.halo + slot
    else:
        ref, lane = own, slot + row
    return ref[:, lane : lane + 1].astype(F32)


def with_column(tile, column, lane):
    here = lax.broadcasted_iota(jnp.int32, tile.shape, 1).astype(BF16) == lane
    return jnp.where(here, jnp.broadcast_to(column, tile.shape).astype(BF16), tile)


def take_inside(ref, start, width, limit):
    low, high = max(start, 0), min(start + width, limit)
    base, top = low // LANES * LANES, min(round_up(high, LANES), ref.shape[1])
    if low == start and base + width + LANES <= limit:
        return take(ref, start, width)
    parts = [ref[:, base:top][:, low - base : high - base]]
    if low > start:
        parts.insert(0, jnp.zeros((ref.shape[0], low - start), BF16))
    if high < start + width:
        parts.append(jnp.zeros((ref.shape[0], start + width - high), BF16))
    return jnp.concatenate(parts, axis=1) if len(parts) > 1 else parts[0]


def row_taps(grid, row, b, field, low, limit, top, bottom):
    shift = b - 1
    if row < 0 and top is not None:
        return take_inside(top, grid.halo - grid.columns + shift, grid.pitch, top.shape[1])
    if row >= LAT_DEV and bottom is not None:
        return take_inside(bottom, shift, grid.pitch, bottom.shape[1])
    return take_inside(field, row * grid.columns + shift - low, grid.pitch, limit)


def build_taps(grid, low, limit, first_row, last_row, field, sides, taps):
    rows = field.shape[0]
    own, top, bottom = sides
    for row in range(first_row, last_row):
        base = (row - first_row) * grid.pitch
        for b in range(3):
            value = row_taps(grid, row, b, field, low, limit, top, bottom)
            if b == 1:
                taps[pl.ds(rows, rows), base : base + grid.pitch] = value
                continue
            at = grid.columns - 1 if b == 2 else 0
            tile = at // LANES * LANES
            column = side_column(sides, grid, row, b == 2)
            for lane in range(0, grid.pitch, LANES):
                part = value[:, lane : lane + LANES]
                if lane == tile:
                    part = with_column(part, column, at - tile)
                taps[pl.ds(b * rows, rows), base + lane : base + lane + LANES] = part


def stacked_rows(grid, taps, row, count):
    width = count * grid.pitch
    return jnp.concatenate(
        [taps[:, (row + a) * grid.pitch : (row + a) * grid.pitch + width] for a in range(3)],
        axis=0,
    )


def groups_of(count):
    return [(row, min(ROW_GROUP, count - row)) for row in range(0, count, ROW_GROUP)]


def flatten(grid, pitched, skip, width, count):
    parts, left = [], width
    for row in range(count):
        begin = skip if row == 0 else 0
        size = min(grid.columns - begin, left)
        if size > 0:
            at = row * grid.pitch + begin
            parts.append(pitched[:, at : at + size])
            left -= size
    if left:
        parts.append(jnp.zeros((pitched.shape[0], left), BF16))
    return jnp.concatenate(parts, axis=1)


def edges_kernel(grid, x_ref, held, out_ref, sem):
    rows, cells = x_ref.shape
    copies = []
    for low in range(0, rows, 16):
        span = pl.ds(low, min(16, rows - low))
        copies.append(
            pltpu.make_async_copy(x_ref.at[span, :], held.at[span, :], sem.at[len(copies)])
        )
    for copy in copies:
        copy.start()
    for low, copy in zip(range(0, rows, 16), copies):
        copy.wait()
        span = pl.ds(low, min(16, rows - low))
        columns = [held[span, i : i + 1] for i in range(0, grid.cells, grid.columns)]
        columns += [
            held[span, i : i + 1] for i in range(grid.columns - 1, grid.cells, grid.columns)
        ]
        out_ref[span, :] = jnp.concatenate(columns, axis=1)


def edges_of(grid, field):
    rows, cells = field.shape
    return pl.pallas_call(
        functools.partial(edges_kernel, grid),
        in_specs=[in_hbm()],
        out_specs=[in_vmem()] * 2,
        out_shape=[pltpu.VMEM((rows, cells), BF16), shape_of((rows, 2 * LAT_DEV))],
        scratch_shapes=[pltpu.SemaphoreType.DMA((-(-rows // 16),))],
        compiler_params=params((rows, LANES, 2)),
        cost_estimate=cost(rows, rows),
        name="edges",
    )(kept_in_hbm(field))


def lon_halo(edges):
    peers = lax.axis_size("lon")
    right = [(i, (i + 1) % peers) for i in range(peers)]
    left = [(j, i) for i, j in right]
    before = lax.ppermute(edges[:, LAT_DEV:], "lon", right)
    after = lax.ppermute(edges[:, :LAT_DEV], "lon", left)
    return jnp.concatenate([before, after], axis=1)


def lat_halo(first_rows, last_rows, sides):
    peers = lax.axis_size("lat")
    if peers == 2:
        upper = lax.axis_index("lat") == 0
        sent = jnp.concatenate([jnp.where(upper, last_rows, first_rows), sides], axis=1)
        other = lax.ppermute(sent, "lat", [(0, 1), (1, 0)])
        none = jnp.zeros_like(other)
        return jnp.where(upper, none, other), jnp.where(upper, other, none)
    up = [(i, i + 1) for i in range(peers - 1)]
    down = [(j, i) for i, j in up]
    top = lax.ppermute(jnp.concatenate([last_rows, sides], axis=1), "lat", up)
    bottom = lax.ppermute(jnp.concatenate([first_rows, sides], axis=1), "lat", down)
    return top, bottom


def read_window(grid, low, high, sources, window, sem):
    copies, holes = window_copies(grid, low, high, sources, window, sem)
    for copy in copies:
        copy.start()
    for begin, end in holes:
        window[:, begin:end] = jnp.zeros((window.shape[0], end - begin), BF16)
    for copy in copies:
        copy.wait()


def forward_kernel(grid, first, width, has_top, has_bottom, members, waits, *refs):
    refs = list(refs)
    x_ref, sides_ref = refs[:2]
    del refs[:2]
    top_ref = refs.pop(0) if has_top else None
    bottom_ref = refs.pop(0) if has_bottom else None
    weight_ref, bias_ref, analysis_ref = refs[:3]
    del refs[: 3 + waits]
    outs = refs[:members]
    target_ref, taps, pitched, pred, target_sem = refs[members:]
    me = lax.axis_index("member")
    piece = width // members
    begin = pl.multiple_of(first + me * piece, LANES)
    target_copy = pltpu.make_async_copy(
        analysis_ref.at[:, pl.ds(begin, piece)], target_ref, target_sem.at[0]
    )
    target_copy.start()
    r0, r1 = grid.rows(first, width)
    sides = (sides_ref, top_ref, bottom_ref)
    build_taps(grid, 0, grid.cells, r0 - 1, r1 + 1, x_ref, sides, taps)
    weight, bias = weight_ref[...], bias_ref[...]
    for row, count in groups_of(r1 - r0):
        value = jnp.dot(
            weight, stacked_rows(grid, taps, row, count), preferred_element_type=F32
        )
        pitched[:, row * grid.pitch : (row + count) * grid.pitch] = (value + bias).astype(BF16)
    pred[...] = flatten(grid, pitched, first - r0 * grid.columns, width, r1 - r0)
    for d in range(members):
        begin = pl.multiple_of((me ^ d) * piece, LANES)
        outs[d][...] = pred[:, pl.ds(begin, piece)]
    target_copy.wait()


def forward(
    grid, first, width, members, x, sides, top, bottom, weight, bias, analysis, after, keep
):
    channels = x.shape[0]
    fields = weight.shape[0]
    r0, r1 = grid.rows(first, width)
    has_top, has_bottom = r0 == 0, r1 == LAT_DEV
    piece = width // members
    held = (3 * channels, (r1 - r0 + 2) * grid.pitch)
    operands = [kept_in_vmem(x), sides]
    if has_top:
        operands.append(top)
    if has_bottom:
        operands.append(bottom)
    operands += [weight, bias]
    specs = [in_vmem()] * len(operands) + [in_hbm()] + [anywhere()] * len(after)
    operands += [kept_in_hbm(analysis), *after]
    return pl.pallas_call(
        functools.partial(
            forward_kernel, grid, first, width, has_top, has_bottom, members, len(after)
        ),
        in_specs=specs,
        out_specs=[in_vmem()] * (members + 1 + keep),
        out_shape=[shape_of((fields, piece))] * (members + 1) + [pltpu.VMEM(held, BF16)] * keep,
        scratch_shapes=[pltpu.VMEM(held, BF16)] * (1 - keep)
        + [
            pltpu.VMEM((fields, (r1 - r0) * grid.pitch), BF16),
            pltpu.VMEM((fields, width), BF16),
            pltpu.SemaphoreType.DMA((1,)),
        ],
        compiler_params=params(
            (*held, 2),
            (2 * fields, (r1 - r0) * grid.pitch, 2),
            (2 * fields, 2 * width, 2),
            (fields, 9 * channels, 2),
        ),
        cost_estimate=cost(width, width),
        name=f"forward_{first}",
    )(*operands)


def slope(values):
    return values * lax.rsqrt(values * values + 1.0)


def score_kernel(members, target_ref, scale_ref, *refs):
    pieces = refs[:members]
    outs = refs[-members:]
    fields, piece = pieces[0].shape
    tiles = piece // LANES
    several = max(k for k in (1, 2, 3) if tiles % k == 0)

    def tile(index, carry):
        for part in range(several * -(-fields // 16)):
            low = part // several * 16
            at = (index * several + part % several) * LANES
            span = pl.ds(pl.multiple_of(at, LANES), LANES)
            rows = pl.ds(low, min(16, fields - low))
            values = [ref[rows, span].astype(F32) for ref in pieces]
            target = target_ref[rows, span].astype(F32)
            scale = scale_ref[rows, :]
            sums = [None] * members
            for i in range(members):
                for j in range(i + 1, members):
                    both = slope(values[i] - values[j])
                    sums[i] = both if sums[i] is None else sums[i] + both
                    sums[j] = -both if sums[j] is None else sums[j] - both
            for i in range(members):
                grad = slope(values[i] - target) * (1.0 / members) - sums[i] * (
                    1.0 / (members * (members - 1))
                )
                outs[i][rows, span] = (scale * grad).astype(BF16)
        return carry

    lax.fori_loop(0, tiles // several, tile, 0)


def score(first, target, scale, pieces, after):
    members = len(pieces)
    fields, piece = pieces[0].shape
    return pl.pallas_call(
        functools.partial(score_kernel, members),
        in_specs=[in_vmem()] * (2 + members) + [anywhere()] * len(after),
        out_specs=[in_vmem()] * members,
        out_shape=[shape_of((fields, piece))] * members,
        compiler_params=params((9 * round_up(fields, 16), piece, 2), (fields, LANES, 4)),
        cost_estimate=cost(piece, piece),
        name=f"score_{first}",
    )(target, scale, *pieces, *after)


def weight_kernel(grid, first, width, members, chained, kept, has_top, has_bottom, *refs):
    me = lax.axis_index("member")
    refs = list(refs)
    if kept:
        taps = refs.pop(0)
    else:
        x_ref, sides_ref = refs[:2]
        del refs[:2]
        top_ref = refs.pop(0) if has_top else None
        bottom_ref = refs.pop(0) if has_bottom else None
    pieces = refs[:members]
    before_ref = refs[members] if chained else None
    out_ref, edge_ref, sum_ref, flat, pitched = refs[members + chained : members + chained + 5]
    if not kept:
        taps = refs[-1]
    fields, piece = pieces[0].shape
    rows = out_ref.shape[0]
    r0, r1 = grid.rows(first, width)
    lead = grid.halo
    flat[:, :lead] = jnp.zeros((rows, lead), BF16)
    flat[:, lead + width :] = jnp.zeros((rows, flat.shape[1] - lead - width), BF16)
    base = fields // 16 * 16
    if base < rows:
        flat[pl.ds(base, rows - base), lead : lead + width] = jnp.zeros(
            (rows - base, width), BF16
        )
    for d in range(members):
        begin = pl.multiple_of((me ^ d) * piece, LANES)
        value = pieces[d][...]
        if grid.padded != grid.cells:
            cell = lax.broadcasted_iota(jnp.int32, (1, piece), 1) + (first + begin)
            value = jnp.where(cell < grid.cells, value.astype(F32), 0.0).astype(BF16)
        flat[pl.ds(0, fields), pl.ds(lead + begin, piece)] = value
    out_ref[...] = flat[:, lead : lead + width]
    columns = []
    for side in (0, grid.columns - 1):
        for row in range(LAT_DEV):
            at = row * grid.columns + side - first
            if 0 <= at < width:
                columns.append(flat[:, lead + at : lead + at + 1])
            else:
                columns.append(jnp.zeros((rows, 1), BF16))
    edge_ref[...] = jnp.concatenate(columns, axis=1)
    keep = jnp.where(
        lax.broadcasted_iota(jnp.int32, (1, LANES), 1) < grid.columns % LANES, 1.0, 0.0
    ).astype(BF16)
    for row in range(r0, r1):
        value = take(flat, lead + row * grid.columns - first, grid.pitch)
        to = (row - r0) * grid.pitch
        for lane in range(0, grid.pitch, LANES):
            part = value[:, lane : lane + LANES]
            if lane + LANES > grid.columns:
                part = part * keep
            pitched[:, to + lane : to + lane + LANES] = part

    if not kept:
        sides = (sides_ref, top_ref, bottom_ref)
        build_taps(grid, 0, grid.cells, r0 - 1, r1 + 1, x_ref, sides, taps)
    for row, count in groups_of(r1 - r0):
        stacked = stacked_rows(grid, taps, row, count)
        ones = jnp.ones((sum_ref.shape[1] - stacked.shape[0], stacked.shape[1]), BF16)
        part = nt_dot(
            pitched[:, row * grid.pitch : (row + count) * grid.pitch],
            jnp.concatenate([stacked, ones], axis=0),
        )
        if row == 0:
            sum_ref[...] = part + before_ref[...] if chained else part
        else:
            sum_ref[...] += part


def weight_part(grid, first, width, rows, taps, x, sides, top, bottom, pieces, before):
    members = len(pieces)
    channels = x.shape[0]
    r0, r1 = grid.rows(first, width)
    sums = round_up(9 * channels + 1, LANES)
    chained = [] if before is None else [before]
    has_top, has_bottom = r0 == 0, r1 == LAT_DEV
    held = (3 * channels, (r1 - r0 + 2) * grid.pitch)
    kept = taps is not None
    if kept:
        operands = [kept_in_vmem(taps)]
    else:
        operands = [kept_in_vmem(x), sides] + [top] * has_top + [bottom] * has_bottom
    operands += [*pieces, *chained]
    return pl.pallas_call(
        functools.partial(
            weight_kernel, grid, first, width, members, len(chained), kept, has_top, has_bottom
        ),
        in_specs=[in_vmem()] * len(operands),
        out_specs=[in_vmem()] * 3,
        out_shape=[
            shape_of((rows, width)),
            shape_of((rows, 2 * LAT_DEV)),
            shape_of((rows, sums), F32),
        ],
        scratch_shapes=[
            pltpu.VMEM((rows, 2 * grid.halo + 2 * LANES + width), BF16),
            pltpu.VMEM((rows, (r1 - r0) * grid.pitch), BF16),
        ]
        + [pltpu.VMEM(held, BF16)] * (1 - kept),
        compiler_params=params(
            (*held, 2),
            (rows, 2 * grid.halo + 2 * LANES + 3 * width, 2),
            (rows, (r1 - r0) * grid.pitch, 2),
            (rows, 3 * sums, 4),
        ),
        cost_estimate=cost(width, width),
        name=f"weight_{first}",
    )(*operands)


def input_kernel(grid, r0, r1, chunks, aliased, *refs):
    refs = list(refs)
    parts = refs[: len(chunks)]
    del refs[: len(chunks)]
    sides_ref, weight_ref = refs[:2]
    del refs[:2]
    top_ref = refs.pop(0) if r0 == 0 else None
    bottom_ref = refs.pop(0) if r1 == LAT_DEV else None
    del refs[:aliased]
    out_ref, window, taps, pitched, flat, sem, out_sem = refs
    low, high = grid.span(r0 - 1, r1 + 1)
    sources = [
        (ref, first, min(first + width, grid.cells), 0)
        for ref, (first, width) in zip(parts, chunks)
    ]
    read_window(grid, low, high, sources, window, sem)
    sides = (sides_ref, top_ref, bottom_ref)
    build_taps(grid, low, high - low, r0 - 1, r1 + 1, window, sides, taps)
    weight = weight_ref[...]
    for row, count in groups_of(r1 - r0):
        value = jnp.dot(
            weight, stacked_rows(grid, taps, row, count), preferred_element_type=F32
        )
        pitched[:, row * grid.pitch : (row + count) * grid.pitch] = value.astype(BF16)
    width = (r1 - r0) * grid.columns
    flat[...] = flatten(grid, pitched, 0, width, r1 - r0)
    copy = pltpu.make_async_copy(
        flat, out_ref.at[:, pl.ds(r0 * grid.columns, width)], out_sem.at[0]
    )
    copy.start()
    copy.wait()


def input_part(grid, r0, r1, chunks, parts, sides, top, bottom, weight, before):
    rows = parts[0].shape[0]
    channels = weight.shape[0]
    low, high = grid.span(r0 - 1, r1 + 1)
    width = (r1 - r0) * grid.columns
    operands = [*parts, sides, weight]
    specs = [anywhere()] * len(parts) + [in_vmem()] * 2
    if r0 == 0:
        operands.append(top)
        specs.append(in_vmem())
    if r1 == LAT_DEV:
        operands.append(bottom)
        specs.append(in_vmem())
    alias = {}
    if before is not None:
        alias = {len(operands): 0}
        operands.append(before)
        specs.append(anywhere())
    return pl.pallas_call(
        functools.partial(input_kernel, grid, r0, r1, chunks, int(before is not None)),
        in_specs=specs,
        out_specs=anywhere(),
        out_shape=shape_of((channels, grid.cells)),
        input_output_aliases=alias,
        scratch_shapes=[
            pltpu.VMEM((rows, high - low), BF16),
            pltpu.VMEM((3 * rows, (r1 - r0 + 2) * grid.pitch), BF16),
            pltpu.VMEM((channels, (r1 - r0) * grid.pitch), BF16),
            pltpu.VMEM((channels, width), BF16),
            pltpu.SemaphoreType.DMA((len(parts) + 2,)),
            pltpu.SemaphoreType.DMA((1,)),
        ],
        compiler_params=params(
            (rows, high - low + 3 * grid.halo, 2),
            (3 * rows, (r1 - r0 + 2) * grid.pitch, 2),
            (2 * channels, (r1 - r0) * grid.pitch, 2),
            (channels, 9 * rows, 2),
        ),
        cost_estimate=cost(80 * channels * rows * width, 8 * channels * width),
        name=f"input_{r0}",
    )(*operands)


def sum_all(value, late):
    halved = []
    for axis in ("lat", "member", "lon"):
        bit = 1
        while bit < lax.axis_size(axis):
            swap = [(i, i ^ bit) for i in range(lax.axis_size(axis))]
            rows = value.shape[0]
            if rows % 16 == 0 and len(halved) < 2:
                upper = (lax.axis_index(axis) & bit) != 0
                low, high = value[: rows // 2], value[rows // 2 :]
                keep, send = (jnp.where(upper, high, low), jnp.where(upper, low, high))
                value = keep + lax.ppermute(send, axis, swap)
                if not halved:
                    value, late = lax.optimization_barrier((value, late))
                halved.append((axis, swap, upper))
            else:
                value = value + lax.ppermute(value, axis, swap)
            bit *= 2
    for axis, swap, upper in reversed(halved):
        other = lax.ppermute(value, axis, swap)
        value = jnp.where(
            upper,
            jnp.concatenate([other, value], axis=0),
            jnp.concatenate([value, other], axis=0),
        )
    return value, late


def chunks_of(grid, members):
    unit = members * LANES
    units = grid.padded // unit
    if units < 15:
        return [(0, grid.padded)], [0]
    sizes = [units * 3 // 8 + 1, units * 2 // 5]
    sizes.append(units - sum(sizes))
    first = [sum(sizes[:i]) for i in range(3)]
    return [(first[i] * unit, sizes[i] * unit) for i in range(3)], [1, 0, 2]


def parts_of(grid, wanted):
    step = LAT_DEV // wanted
    if step * grid.columns % LANES:
        return [(0, LAT_DEV)]
    ranges = [(row, row + step) for row in range(0, LAT_DEV, step)]
    return ranges[1:-1] + [ranges[0], ranges[-1]]


def local(inputs, weight, bias, analysis, field_weight):
    channels, cells = inputs.shape[1], inputs.shape[4]
    fields = analysis.shape[0]
    members = lax.axis_size("member")
    grid = Grid(cells, members)
    x = inputs.reshape(channels, cells)
    target = analysis.reshape(fields, cells)
    if grid.padded != cells:
        target = jnp.pad(target, ((0, 0), (0, grid.padded - cells)))
    rows = round_up(fields, 16)
    taps = weight.reshape(9, channels, fields)
    forward_weight = taps.transpose(2, 0, 1).reshape(fields, 9 * channels)
    backward_weight = jnp.pad(taps[::-1], ((0, 0), (0, 0), (0, rows - fields)))
    backward_weight = backward_weight.transpose(1, 0, 2).reshape(channels, 9 * rows)
    scale = jnp.broadcast_to(field_weight[:, None], (fields, LANES))
    shift = bias[:, None]

    x_in = x
    x, x_edges = edges_of(grid, x_in)
    x_sides = lon_halo(x_edges)

    def to_members(pieces):
        moved = [pieces[0]]
        for d in range(1, members):
            moved.append(lax.ppermute(pieces[d], "member", [(i, i ^ d) for i in range(members)]))
        return moved

    chunks, turn = chunks_of(grid, members)
    received, returned, targets, taken = {}, {}, {}, {}
    parts, edges, sums = {}, {}, None
    x_top, x_bottom = None, None

    def x_lat_halo(sides):
        return lat_halo(x_in[:, : grid.halo], x_in[:, cells - grid.halo :], sides)

    def send(i, after, keep):
        first, width = chunks[i]
        out = forward(
            grid, first, width, members, x, x_sides, x_top, x_bottom, forward_weight, shift,
            target, after, keep,
        )
        targets[i], taken[i] = out[members], out[-1] if keep else None
        received[i] = to_members(out[:members])

    def answer(i, after):
        grads = score(chunks[i][0], targets[i], scale, received[i], after)
        returned[i] = to_members(grads)
        return grads[0]

    def weigh(i, before):
        first, width = chunks[i]
        parts[i], edges[i], total = weight_part(
            grid, first, width, rows, taken[i], x, x_sides, x_top, x_bottom, returned[i], before
        )
        return total

    ranges = parts_of(grid, 4)
    grad_input = None
    if len(turn) == 1:
        x_top, x_bottom = x_lat_halo(x_sides)
        send(0, [], 0)
        answer(0, [])
        sums = weigh(0, None)
        early = []
        late_edges = edges[0]
    else:
        a, b, c = turn
        send(a, [], 0)
        late_sides, targets[a] = lax.optimization_barrier((x_sides, targets[a]))
        x_top, x_bottom = x_lat_halo(late_sides)
        send(b, [], 0)
        done = answer(a, [targets[b]])
        done = answer(b, [done])
        send(c, [done], 1)
        sums = weigh(a, None)
        answer(c, [edges[a]])
        sums = weigh(b, sums)
        early_sides = lon_halo(edges[a] + edges[b])
        sums = weigh(c, sums)
        done_rows = min(sum(chunks[a]) // grid.columns, LAT_DEV)
        early = [(r0, r1) for r0, r1 in ranges if r0 > 0 and r1 < done_rows]
        late_edges = edges[c]
    parts = [parts[i] for i in range(len(chunks))]
    for r0, r1 in early:
        grad_input = input_part(
            grid, r0, r1, chunks[:2], parts[:2], early_sides, None, None, backward_weight,
            grad_input,
        )
    total, late_edges = sum_all(sums, late_edges)
    g_sides = lon_halo(late_edges)
    if early:
        g_sides = g_sides + early_sides
    end = cells - chunks[-1][0]
    g_top, g_bottom = lat_halo(
        parts[0][:, : grid.halo], parts[-1][:, end - grid.halo : end], g_sides
    )
    for r0, r1 in ranges:
        if (r0, r1) in early:
            continue
        grad_input = input_part(
            grid, r0, r1, chunks, parts, g_sides, g_top, g_bottom, backward_weight, grad_input
        )
    total = total / (cells * lax.axis_size("lat") * lax.axis_size("lon"))
    grad_weight = total[:fields, : 9 * channels].T.reshape(9, channels * fields)
    grad_bias = total[:fields, 9 * channels]
    return (grad_input.reshape(1, channels, 1, 1, cells), grad_weight, grad_bias)


def solution(mesh):
    placed = (P("member", None, "lat", "lon", None), P(), P(), P(None, "lat", "lon", None), P())
    return jax.shard_map(
        local,
        mesh=mesh,
        in_specs=placed,
        out_specs=(P("member", None, "lat", "lon", None), P(), P()),
        check_vma=False,
    )
```

```python
import functools

import jax
import jax.numpy as jnp
from jax import lax
from jax.experimental import pallas as pl
from jax.experimental.pallas import tpu as pltpu
from jax.sharding import PartitionSpec as P

LAT_DEV = 64
LANES = 128
ROW_GROUP = 2
SLACK = 3 * 1024 * 1024
F32 = jnp.float32
BF16 = jnp.bfloat16


def round_up(value, step):
    return -(-value // step) * step


def params(*held):
    total = sum(round_up(rows, 16) * round_up(lanes, LANES) * size for rows, lanes, size in held)
    return pltpu.CompilerParams(vmem_limit_bytes=total + SLACK)


def kept_in_hbm(value):
    return pltpu.with_memory_space_constraint(value, pltpu.HBM)


def kept_in_vmem(value):
    return pltpu.with_memory_space_constraint(value, pltpu.VMEM)


def shape_of(dims, dtype=BF16):
    return jax.ShapeDtypeStruct(dims, dtype)


def cost(flops, moved):
    return pl.CostEstimate(flops=int(flops), bytes_accessed=int(moved), transcendentals=0)


def in_vmem():
    return pl.BlockSpec(memory_space=pltpu.VMEM)


def in_smem():
    return pl.BlockSpec(memory_space=pltpu.SMEM)


def in_hbm():
    return pl.BlockSpec(memory_space=pltpu.HBM)


def anywhere():
    return pl.BlockSpec(memory_space=pl.ANY)


def nt_dot(left, right):
    return lax.dot_general(left, right, (((1,), (1,)), ((), ())), preferred_element_type=F32)


class Grid:
    def __init__(self, cells, members):
        self.cells = cells
        self.columns = cells // LAT_DEV
        self.pitch = round_up(self.columns, LANES)
        self.halo = round_up(self.columns + 1, LANES)
        self.padded = round_up(cells, members * LANES)

    def rows(self, first, width):
        return first // self.columns, -(-min(first + width, self.cells) // self.columns)


def take(ref, start, width):
    low = start // LANES * LANES
    off = start - low
    if off == 0:
        return ref[:, low : low + width]
    return ref[:, low : low + width + LANES][:, off : off + width]


def side_column(refs, grid, row, right):
    own, top, bottom = refs
    slot = LAT_DEV if right else 0
    if row < 0:
        ref, lane = top, grid.halo + slot + LAT_DEV - 1
    elif row >= LAT_DEV:
        ref, lane = bottom, grid.halo + slot
    else:
        ref, lane = own, slot + row
    return ref[:, lane : lane + 1].astype(F32)


def with_column(tile, column, lane):
    here = lax.broadcasted_iota(jnp.int32, tile.shape, 1).astype(BF16) == lane
    return jnp.where(here, jnp.broadcast_to(column, tile.shape).astype(BF16), tile)


def take_cells(sources, start, width):
    parts, at, end = [], start, start + width
    for ref, begin, last in sources:
        base = (start - begin) // LANES * LANES
        if begin <= start and end <= last and base + width + LANES <= ref.shape[1]:
            return take(ref, start - begin, width)
        low, high = max(at, begin), min(end, last)
        if low < high:
            if low > at:
                parts.append(jnp.zeros((ref.shape[0], low - at), BF16))
            base = (low - begin) // LANES * LANES
            top = min(round_up(high - begin, LANES), ref.shape[1])
            parts.append(ref[:, base:top][:, low - begin - base : high - begin - base])
            at = high
    if at < end:
        parts.append(jnp.zeros((sources[0][0].shape[0], end - at), BF16))
    return jnp.concatenate(parts, axis=1) if len(parts) > 1 else parts[0]


def row_taps(grid, row, b, sources, top, bottom):
    shift = b - 1
    if row < 0 and top is not None:
        return take_cells([(top, 0, top.shape[1])], grid.halo - grid.columns + shift, grid.pitch)
    if row >= LAT_DEV and bottom is not None:
        return take_cells([(bottom, 0, bottom.shape[1])], shift, grid.pitch)
    return take_cells(sources, row * grid.columns + shift, grid.pitch)


def build_taps(grid, first_row, last_row, sources, sides, taps, backwards=False):
    rows = sources[0][0].shape[0]
    own, top, bottom = sides
    for row in range(first_row, last_row):
        base = (row - first_row) * grid.pitch
        for b in range(3):
            value = row_taps(grid, row, b, sources, top, bottom)
            block = pl.ds((2 - b if backwards else b) * rows, rows)
            if b == 1:
                taps[block, base : base + grid.pitch] = value
                continue
            at = grid.columns - 1 if b == 2 else 0
            tile = at // LANES * LANES
            column = side_column(sides, grid, row, b == 2)
            for lane in range(0, grid.pitch, LANES):
                part = value[:, lane : lane + LANES]
                if lane == tile:
                    part = with_column(part, column, at - tile)
                taps[block, base + lane : base + lane + LANES] = part


def stacked_rows(grid, taps, row, count, order=(0, 1, 2)):
    width = count * grid.pitch
    return jnp.concatenate(
        [taps[:, (row + a) * grid.pitch : (row + a) * grid.pitch + width] for a in order],
        axis=0,
    )


def groups_of(count):
    return [(row, min(ROW_GROUP, count - row)) for row in range(0, count, ROW_GROUP)]


def flatten(grid, pitched, skip, width, count):
    parts, left = [], width
    for row in range(count):
        begin = skip if row == 0 else 0
        size = min(grid.columns - begin, left)
        if size > 0:
            at = row * grid.pitch + begin
            parts.append(pitched[:, at : at + size])
            left -= size
    if left:
        parts.append(jnp.zeros((pitched.shape[0], left), BF16))
    return jnp.concatenate(parts, axis=1)


def edges_kernel(grid, places, tiles, x_ref, out_ref, held, sem):
    copies = [
        pltpu.make_async_copy(
            x_ref.at[:, pl.ds(tile * LANES, LANES)],
            held.at[:, pl.ds(number * LANES, LANES)],
            sem.at[number],
        )
        for number, tile in enumerate(tiles)
    ]
    for copy in copies:
        copy.start()
    for copy in copies:
        copy.wait()
    columns = []
    for cell in places:
        at = tiles.index(cell // LANES) * LANES + cell % LANES
        columns.append(held[:, at : at + 1])
    out_ref[...] = jnp.concatenate(columns, axis=1)


def edges_of(grid, field):
    rows = field.shape[0]
    places = [i for i in range(0, grid.cells, grid.columns)]
    places += [i for i in range(grid.columns - 1, grid.cells, grid.columns)]
    tiles = sorted({cell // LANES for cell in places})
    return pl.pallas_call(
        functools.partial(edges_kernel, grid, places, tiles),
        in_specs=[in_hbm()],
        out_specs=in_vmem(),
        out_shape=shape_of((rows, 2 * LAT_DEV)),
        scratch_shapes=[
            pltpu.VMEM((rows, len(tiles) * LANES), BF16),
            pltpu.SemaphoreType.DMA((len(tiles),)),
        ],
        compiler_params=params((rows, (len(tiles) + 1) * LANES, 2)),
        cost_estimate=cost(rows, rows),
        name="edges",
    )(kept_in_hbm(field))


def lon_halo(edges):
    peers = lax.axis_size("lon")
    right = [(i, (i + 1) % peers) for i in range(peers)]
    left = [(j, i) for i, j in right]
    before = lax.ppermute(edges[:, LAT_DEV:], "lon", right)
    after = lax.ppermute(edges[:, :LAT_DEV], "lon", left)
    return jnp.concatenate([before, after], axis=1)


def lat_halo(first_rows, last_rows, sides, upper):
    peers = lax.axis_size("lat")
    if peers == 2:
        sent = jnp.concatenate([jnp.where(upper, last_rows, first_rows), sides], axis=1)
        other = lax.ppermute(sent, "lat", [(0, 1), (1, 0)])
        none = jnp.zeros_like(other)
        return jnp.where(upper, none, other), jnp.where(upper, other, none)
    up = [(i, i + 1) for i in range(peers - 1)]
    down = [(j, i) for i, j in up]
    top = lax.ppermute(jnp.concatenate([last_rows, sides], axis=1), "lat", up)
    bottom = lax.ppermute(jnp.concatenate([first_rows, sides], axis=1), "lat", down)
    return top, bottom


def forward_kernel(grid, first, width, has_top, has_bottom, members, load, *refs):
    refs = list(refs)
    x_ref, sides_ref = refs[:2]
    del refs[:2]
    top_ref = refs.pop(0) if has_top else None
    bottom_ref = refs.pop(0) if has_bottom else None
    weight_ref, bias_ref, analysis_ref = refs[:3]
    del refs[:3]
    outs = refs[:members]
    target_ref, taps = refs[members : members + 2]
    pitched, pred, target_sem, load_sem = refs[-4:]
    me = lax.axis_index("member")
    piece = width // members
    r0, r1 = grid.rows(first, width)
    late = []
    if load:
        held = refs[members + 2]
        cut = min(round_up((r1 + 2) * grid.columns, LANES), grid.cells)
        copies = []
        for begin, end in ((0, cut), (cut, grid.cells)):
            for low in range(0, x_ref.shape[0], 16) if begin < end else ():
                at = (pl.ds(low, min(16, x_ref.shape[0] - low)), pl.ds(begin, end - begin))
                copies.append(
                    pltpu.make_async_copy(x_ref.at[at], held.at[at], load_sem.at[len(copies)])
                )
                copies[-1].start()
            if begin == 0:
                late = len(copies)
        for copy in copies[:late]:
            copy.wait()
        late = copies[late:]
        x_ref = held
    begin = pl.multiple_of(first + me * piece, LANES)
    target_copy = pltpu.make_async_copy(
        analysis_ref.at[:, pl.ds(begin, piece)], target_ref, target_sem.at[0]
    )
    target_copy.start()
    sides = (sides_ref, top_ref, bottom_ref)
    build_taps(grid, r0 - 1, r1 + 1, [(x_ref, 0, grid.cells)], sides, taps)
    weight, bias = weight_ref[...], bias_ref[...]
    for row, count in groups_of(r1 - r0):
        value = jnp.dot(
            weight, stacked_rows(grid, taps, row, count), preferred_element_type=F32
        )
        pitched[:, row * grid.pitch : (row + count) * grid.pitch] = (value + bias).astype(BF16)
    pred[...] = flatten(grid, pitched, first - r0 * grid.columns, width, r1 - r0)
    for d in range(members):
        begin = pl.multiple_of((me ^ d) * piece, LANES)
        outs[d][...] = pred[:, pl.ds(begin, piece)]
    target_copy.wait()
    for copy in late:
        copy.wait()


def forward(grid, first, width, members, x, load, sides, top, bottom, weight, bias, analysis):
    channels = x.shape[0]
    fields = weight.shape[0]
    r0, r1 = grid.rows(first, width)
    has_top, has_bottom = r0 == 0, r1 == LAT_DEV
    piece = width // members
    held = (3 * channels, (r1 - r0 + 2) * grid.pitch)
    operands = [kept_in_hbm(x) if load else kept_in_vmem(x), sides]
    if has_top:
        operands.append(top)
    if has_bottom:
        operands.append(bottom)
    operands += [weight, bias]
    specs = [in_hbm() if load else in_vmem()] + [in_vmem()] * (len(operands) - 1) + [in_hbm()]
    operands += [kept_in_hbm(analysis)]
    shapes = [shape_of((fields, piece))] * (members + 1) + [pltpu.VMEM(held, BF16)]
    if load:
        shapes.append(pltpu.VMEM((channels, grid.cells), BF16))
    return pl.pallas_call(
        functools.partial(
            forward_kernel, grid, first, width, has_top, has_bottom, members, load
        ),
        in_specs=specs,
        out_specs=[in_vmem()] * len(shapes),
        out_shape=shapes,
        scratch_shapes=[
            pltpu.VMEM((fields, (r1 - r0) * grid.pitch), BF16),
            pltpu.VMEM((fields, width), BF16),
            pltpu.SemaphoreType.DMA((1,)),
            pltpu.SemaphoreType.DMA((2 * -(-channels // 16),)),
        ],
        compiler_params=params(
            (2 * fields, (r1 - r0) * grid.pitch, 2),
            (2 * fields, 2 * width, 2),
            (fields, 9 * channels, 2),
        ),
        cost_estimate=cost(81 * channels * fields * width, 0),
        name=f"forward_{first}",
    )(*operands)


def slope(values):
    return values * lax.rsqrt(values * values + 1.0)


def score_kernel(members, target_ref, scale_ref, *refs):
    pieces = refs[:members]
    outs = refs[-members:]
    fields, piece = pieces[0].shape
    tiles = piece // LANES
    several = max(k for k in (1, 2, 3) if tiles % k == 0)

    def tile(index, carry):
        for part in range(several * -(-fields // 16)):
            low = part // several * 16
            at = (index * several + part % several) * LANES
            span = pl.ds(pl.multiple_of(at, LANES), LANES)
            rows = pl.ds(low, min(16, fields - low))
            values = [ref[rows, span].astype(F32) for ref in pieces]
            target = target_ref[rows, span].astype(F32)
            scale = scale_ref[rows, :]
            sums = [None] * members
            for i in range(members):
                for j in range(i + 1, members):
                    both = slope(values[i] - values[j])
                    sums[i] = both if sums[i] is None else sums[i] + both
                    sums[j] = -both if sums[j] is None else sums[j] - both
            for i in range(members):
                grad = slope(values[i] - target) * (1.0 / members) - sums[i] * (
                    1.0 / (members * (members - 1))
                )
                outs[i][rows, span] = (scale * grad).astype(BF16)
        return carry

    lax.fori_loop(0, tiles // several, tile, 0)


def score(first, target, scale, pieces, after):
    members = len(pieces)
    fields, piece = pieces[0].shape
    return pl.pallas_call(
        functools.partial(score_kernel, members),
        in_specs=[in_vmem()] * (2 + members) + [anywhere()] * len(after),
        out_specs=[in_vmem()] * members,
        out_shape=[shape_of((fields, piece))] * members,
        compiler_params=params((9 * round_up(fields, 16), piece, 2), (fields, LANES, 4)),
        cost_estimate=cost(13000 * fields * piece, 0),
        name=f"score_{first}",
    )(target, scale, *pieces, *after)


def weight_kernel(grid, first, width, members, chained, taps, *refs):
    me = lax.axis_index("member")
    pieces = refs[:members]
    before_ref = refs[members] if chained else None
    out_ref, edge_ref, sum_ref, flat, pitched = refs[members + chained :]
    fields, piece = pieces[0].shape
    rows = out_ref.shape[0]
    r0, r1 = grid.rows(first, width)
    lead = grid.halo
    flat[:, :lead] = jnp.zeros((rows, lead), BF16)
    flat[:, lead + width :] = jnp.zeros((rows, flat.shape[1] - lead - width), BF16)
    base = fields // 16 * 16
    if base < rows:
        flat[pl.ds(base, rows - base), lead : lead + width] = jnp.zeros(
            (rows - base, width), BF16
        )
    for d in range(members):
        begin = pl.multiple_of((me ^ d) * piece, LANES)
        value = pieces[d][...]
        if grid.padded != grid.cells:
            cell = lax.broadcasted_iota(jnp.int32, (1, piece), 1) + (first + begin)
            value = jnp.where(cell < grid.cells, value.astype(F32), 0.0).astype(BF16)
        flat[pl.ds(0, fields), pl.ds(lead + begin, piece)] = value
    out_ref[...] = flat[:, lead : lead + width]
    columns = []
    for side in (0, grid.columns - 1):
        for row in range(LAT_DEV):
            at = row * grid.columns + side - first
            if 0 <= at < width:
                columns.append(flat[:, lead + at : lead + at + 1])
            else:
                columns.append(jnp.zeros((rows, 1), BF16))
    edge_ref[...] = jnp.concatenate(columns, axis=1)
    keep = jnp.where(
        lax.broadcasted_iota(jnp.int32, (1, LANES), 1) < grid.columns % LANES, 1.0, 0.0
    ).astype(BF16)
    for row in range(r0, r1):
        value = take(flat, lead + row * grid.columns - first, grid.pitch)
        to = (row - r0) * grid.pitch
        for lane in range(0, grid.pitch, LANES):
            part = value[:, lane : lane + LANES]
            if lane + LANES > grid.columns:
                part = part * keep
            pitched[:, to + lane : to + lane + LANES] = part

    for row, count in groups_of(r1 - r0):
        stacked = stacked_rows(grid, taps, row, count)
        ones = jnp.ones((sum_ref.shape[1] - stacked.shape[0], stacked.shape[1]), BF16)
        part = nt_dot(
            pitched[:, row * grid.pitch : (row + count) * grid.pitch],
            jnp.concatenate([stacked, ones], axis=0),
        )
        if row == 0:
            sum_ref[...] = part + before_ref[...] if chained else part
        else:
            sum_ref[...] += part


def weight_part(grid, first, width, rows, taps, pieces, before):
    members = len(pieces)
    channels = taps.shape[0] // 3
    r0, r1 = grid.rows(first, width)
    sums = round_up(9 * channels + 1, LANES)
    chained = [] if before is None else [before]
    return pl.pallas_call(
        functools.partial(weight_kernel, grid, first, width, members, len(chained)),
        in_specs=[in_vmem()] * (1 + members + len(chained)),
        out_specs=[in_vmem()] * 3,
        out_shape=[
            shape_of((rows, width)),
            shape_of((rows, 2 * LAT_DEV)),
            shape_of((rows, sums), F32),
        ],
        scratch_shapes=[
            pltpu.VMEM((rows, 2 * grid.halo + 2 * LANES + width), BF16),
            pltpu.VMEM((rows, (r1 - r0) * grid.pitch), BF16),
        ],
        compiler_params=params(
            (rows, 2 * grid.halo + 2 * LANES + 3 * width, 2),
            (rows, (r1 - r0) * grid.pitch, 2),
            (rows, 3 * sums, 4),
        ),
        cost_estimate=cost(61 * channels * rows * width, 0),
        name=f"weight_{first}",
    )(kept_in_vmem(taps), *pieces, *chained)


def input_kernel(grid, r0, r1, chunks, aliased, *refs):
    refs = list(refs)
    parts = refs[: len(chunks)]
    del refs[: len(chunks)]
    sides_ref, weight_ref = refs[:2]
    del refs[:2]
    top_ref = refs.pop(0) if r0 == 0 else None
    bottom_ref = refs.pop(0) if r1 == LAT_DEV else None
    del refs[:aliased]
    out_ref, taps, pitched, flat, out_sem = refs
    sources = [
        (ref, first, min(first + width, grid.cells))
        for ref, (first, width) in zip(parts, chunks)
    ]
    sides = (sides_ref, top_ref, bottom_ref)
    build_taps(grid, r0 - 1, r1 + 1, sources, sides, taps, backwards=True)
    weight = weight_ref[...]
    for row, count in groups_of(r1 - r0):
        value = jnp.dot(
            weight,
            stacked_rows(grid, taps, row, count, (2, 1, 0)),
            preferred_element_type=F32,
        )
        pitched[:, row * grid.pitch : (row + count) * grid.pitch] = value.astype(BF16)
    width = (r1 - r0) * grid.columns
    flat[...] = flatten(grid, pitched, 0, width, r1 - r0)
    copy = pltpu.make_async_copy(
        flat, out_ref.at[:, pl.ds(r0 * grid.columns, width)], out_sem.at[0]
    )
    copy.start()
    copy.wait()


def input_part(grid, r0, r1, chunks, parts, sides, top, bottom, weight, before):
    rows = parts[0].shape[0]
    channels = weight.shape[0]
    width = (r1 - r0) * grid.columns
    held = (3 * rows, (r1 - r0 + 2) * grid.pitch)
    near = []
    for (first, size), part in zip(chunks, parts):
        if first < (r1 + 1) * grid.columns + 1 and first + size > (r0 - 1) * grid.columns - 1:
            near.append(((first, size), part))
    chunks, parts = [pair[0] for pair in near], [pair[1] for pair in near]
    operands = [*parts, sides, weight] + [top] * (r0 == 0) + [bottom] * (r1 == LAT_DEV)
    specs = [in_vmem()] * len(operands)
    alias = {}
    if before is not None:
        alias = {len(operands): 0}
        operands.append(before)
        specs.append(anywhere())
    return pl.pallas_call(
        functools.partial(input_kernel, grid, r0, r1, chunks, len(alias)),
        in_specs=specs,
        out_specs=anywhere(),
        out_shape=shape_of((channels, grid.cells)),
        input_output_aliases=alias,
        scratch_shapes=[
            pltpu.VMEM(held, BF16),
            pltpu.VMEM((channels, (r1 - r0) * grid.pitch), BF16),
            pltpu.VMEM((channels, width), BF16),
            pltpu.SemaphoreType.DMA((1,)),
        ],
        compiler_params=params(
            (rows, sum(part.shape[1] for part in parts), 2),
            (*held, 2),
            (2 * channels, (r1 - r0) * grid.pitch, 2),
            (channels, 9 * rows, 2),
        ),
        cost_estimate=cost(80 * channels * rows * width, 8 * channels * width),
        name=f"input_{r0}",
    )(*operands)


def steps_of_sum():
    steps = []
    for axis in ("lat", "member", "lon"):
        bit = 1
        while bit < lax.axis_size(axis):
            pairs = [(i, i ^ bit) for i in range(lax.axis_size(axis))]
            steps.append((axis, pairs, (lax.axis_index(axis) & bit) != 0))
            bit *= 2
    return steps


def sum_all(value, steps, flags, late):
    halved = []
    for (axis, pairs, _), upper in zip(steps, flags):
        rows = value.shape[0]
        if rows % 16 == 0 and len(halved) < 2:
            low, high = value[: rows // 2], value[rows // 2 :]
            keep, send = (jnp.where(upper, high, low), jnp.where(upper, low, high))
            value = keep + lax.ppermute(send, axis, pairs)
            if not halved:
                value, late = lax.optimization_barrier((value, late))
            halved.append((axis, pairs, upper))
        else:
            value = value + lax.ppermute(value, axis, pairs)
    for axis, pairs, upper in reversed(halved):
        other = lax.ppermute(value, axis, pairs)
        value = jnp.where(
            upper,
            jnp.concatenate([other, value], axis=0),
            jnp.concatenate([value, other], axis=0),
        )
    return value, late


def chunks_of(grid, members):
    unit = members * LANES
    units = grid.padded // unit
    if units < 15:
        return [(0, grid.padded)]
    head = units // 2 + 2
    return [(0, head * unit), (head * unit, (units - head) * unit)]


def parts_of(grid, wanted):
    step = LAT_DEV // wanted
    if step * grid.columns % LANES:
        return [(0, LAT_DEV)]
    ranges = [(row, row + step) for row in range(0, LAT_DEV, step)]
    return ranges[1:-1] + [ranges[0], ranges[-1]]


def local(inputs, weight, bias, analysis, field_weight):
    channels, cells = inputs.shape[1], inputs.shape[4]
    fields = analysis.shape[0]
    members = lax.axis_size("member")
    grid = Grid(cells, members)
    x = inputs.reshape(channels, cells)
    target = analysis.reshape(fields, cells)
    if grid.padded != cells:
        target = jnp.pad(target, ((0, 0), (0, grid.padded - cells)))
    rows = round_up(fields, 16)
    taps = weight.reshape(9, channels, fields)
    forward_weight = taps.transpose(2, 0, 1).reshape(fields, 9 * channels)
    backward_weight = jnp.pad(taps, ((0, 0), (0, 0), (0, rows - fields)))
    backward_weight = backward_weight.transpose(1, 0, 2).reshape(channels, 9 * rows)
    scale = jnp.broadcast_to(field_weight[:, None], (fields, LANES))
    shift = bias[:, None]
    steps = steps_of_sum()
    flags = [upper for _, _, upper in steps]
    x_sides = lon_halo(edges_of(grid, x))
    x_sides, forward_weight, backward_weight, scale, shift, flags = lax.optimization_barrier(
        (x_sides, forward_weight, backward_weight, scale, shift, flags)
    )
    first_lat = jnp.logical_not(flags[0])
    x_top, x_bottom = lat_halo(
        x[:, : grid.halo], x[:, cells - grid.halo :], x_sides, first_lat
    )

    def to_members(pieces):
        moved = [pieces[0]]
        for d in range(1, members):
            moved.append(lax.ppermute(pieces[d], "member", [(i, i ^ d) for i in range(members)]))
        return moved

    chunks = chunks_of(grid, members)
    received, returned, targets, taken = [], [], [], []
    parts, edges, sums = [], [], None
    held = None
    for first, width in chunks:
        out = forward(
            grid, first, width, members, x if held is None else held, held is None, x_sides,
            x_top, x_bottom, forward_weight, shift, target,
        )
        targets.append(out[members])
        taken.append(out[members + 1])
        if held is None:
            held = out[members + 2]
        received.append(to_members(out[:members]))
    for (first, width), pieces, goal in zip(chunks, received, targets):
        returned.append(to_members(score(first, goal, scale, pieces, [])))
    for number, (first, width) in enumerate(chunks):
        part, edge, sums = weight_part(
            grid, first, width, rows, taken[number], returned[number], sums
        )
        parts.append(part)
        edges.append(edge)
    ranges = parts_of(grid, 4)
    grad_input, early = None, []
    late_edges = edges[-1]
    if len(chunks) > 1:
        early_sides = lon_halo(edges[0])
        done_rows = chunks[0][1] // grid.columns
        early = [(r0, r1) for r0, r1 in ranges if r0 > 0 and r1 < done_rows]
    for r0, r1 in early:
        grad_input = input_part(
            grid, r0, r1, chunks[:1], parts[:1], early_sides, None, None, backward_weight,
            grad_input,
        )
    total, late_edges = sum_all(sums, steps, flags, late_edges)
    g_sides = lon_halo(late_edges)
    if len(chunks) > 1:
        g_sides = g_sides + early_sides
    end = cells - chunks[-1][0]
    g_top, g_bottom = lat_halo(
        parts[0][:, : grid.halo], parts[-1][:, end - grid.halo : end], g_sides, first_lat
    )
    for r0, r1 in ranges:
        if (r0, r1) in early:
            continue
        grad_input = input_part(
            grid, r0, r1, chunks, parts, g_sides, g_top, g_bottom, backward_weight, grad_input
        )
    total = total / (cells * lax.axis_size("lat") * lax.axis_size("lon"))
    grad_weight = total[:fields, : 9 * channels].T.reshape(9, channels * fields)
    grad_bias = total[:fields, 9 * channels]
    return (grad_input.reshape(1, channels, 1, 1, cells), grad_weight, grad_bias)


def solution(mesh):
    placed = (P("member", None, "lat", "lon", None), P(), P(), P(None, "lat", "lon", None), P())
    return jax.shard_map(
        local,
        mesh=mesh,
        in_specs=placed,
        out_specs=(P("member", None, "lat", "lon", None), P(), P()),
        check_vma=False,
    )
```

```python
import functools

import jax
import jax.numpy as jnp
from jax import lax
from jax.experimental import pallas as pl
from jax.experimental.pallas import tpu as pltpu
from jax.sharding import PartitionSpec as P

LAT_DEV = 64
LANES = 128
ROW_GROUP = 2
FLAT_LANES = 1024
SLACK = 3 * 1024 * 1024
F32 = jnp.float32
BF16 = jnp.bfloat16


def round_up(value, step):
    return -(-value // step) * step


def params(*held):
    total = sum(round_up(rows, 16) * round_up(lanes, LANES) * size for rows, lanes, size in held)
    return pltpu.CompilerParams(vmem_limit_bytes=total + SLACK)


def kept_in_hbm(value):
    return pltpu.with_memory_space_constraint(value, pltpu.HBM)


def kept_in_vmem(value):
    return pltpu.with_memory_space_constraint(value, pltpu.VMEM)


def shape_of(dims, dtype=BF16):
    return jax.ShapeDtypeStruct(dims, dtype)


def cost(flops, moved):
    return pl.CostEstimate(flops=int(flops), bytes_accessed=int(moved), transcendentals=0)


def in_vmem():
    return pl.BlockSpec(memory_space=pltpu.VMEM)


def in_smem():
    return pl.BlockSpec(memory_space=pltpu.SMEM)


def in_hbm():
    return pl.BlockSpec(memory_space=pltpu.HBM)


def anywhere():
    return pl.BlockSpec(memory_space=pl.ANY)


def nt_dot(left, right):
    return lax.dot_general(left, right, (((1,), (1,)), ((), ())), preferred_element_type=F32)


class Grid:
    def __init__(self, cells, members):
        self.cells = cells
        self.columns = cells // LAT_DEV
        self.pitch = round_up(self.columns, LANES)
        self.halo = round_up(self.columns + 1, LANES)
        self.padded = round_up(cells, members * LANES)

    def rows(self, first, width):
        return first // self.columns, -(-min(first + width, self.cells) // self.columns)


def take(ref, start, width):
    low = start // LANES * LANES
    off = start - low
    if off == 0:
        return ref[:, low : low + width]
    return ref[:, low : low + width + LANES][:, off : off + width]


def side_column(refs, grid, row, right):
    own, top, bottom = refs
    slot = LAT_DEV if right else 0
    if row < 0:
        ref, lane = top, grid.halo + slot + LAT_DEV - 1
    elif row >= LAT_DEV:
        ref, lane = bottom, grid.halo + slot
    else:
        ref, lane = own, slot + row
    return ref[:, lane : lane + 1].astype(F32)


def with_column(tile, column, lane):
    here = lax.broadcasted_iota(jnp.int32, tile.shape, 1).astype(BF16) == lane
    return jnp.where(here, jnp.broadcast_to(column, tile.shape).astype(BF16), tile)


def take_cells(sources, start, width):
    parts, at, end = [], start, start + width
    for ref, begin, last in sources:
        base = (start - begin) // LANES * LANES
        if begin <= start and end <= last and base + width + LANES <= ref.shape[1]:
            return take(ref, start - begin, width)
        low, high = max(at, begin), min(end, last)
        if low < high:
            if low > at:
                parts.append(jnp.zeros((ref.shape[0], low - at), BF16))
            base = (low - begin) // LANES * LANES
            top = min(round_up(high - begin, LANES), ref.shape[1])
            parts.append(ref[:, base:top][:, low - begin - base : high - begin - base])
            at = high
    if at < end:
        parts.append(jnp.zeros((sources[0][0].shape[0], end - at), BF16))
    return jnp.concatenate(parts, axis=1) if len(parts) > 1 else parts[0]


def row_taps(grid, row, b, sources, top, bottom):
    shift = b - 1
    if row < 0 and top is not None:
        return take_cells([(top, 0, top.shape[1])], grid.halo - grid.columns + shift, grid.pitch)
    if row >= LAT_DEV and bottom is not None:
        return take_cells([(bottom, 0, bottom.shape[1])], shift, grid.pitch)
    return take_cells(sources, row * grid.columns + shift, grid.pitch)


def build_taps(grid, origin, low, high, sources, sides, taps, backwards=False):
    rows = sources[0][0].shape[0]
    own, top, bottom = sides
    for row in range(low, high):
        base = (row - origin) * grid.pitch
        for b in range(3):
            value = row_taps(grid, row, b, sources, top, bottom)
            block = pl.ds((2 - b if backwards else b) * rows, rows)
            if b == 1:
                taps[block, base : base + grid.pitch] = value
                continue
            at = grid.columns - 1 if b == 2 else 0
            tile = at // LANES * LANES
            column = side_column(sides, grid, row, b == 2)
            for lane in range(0, grid.pitch, LANES):
                part = value[:, lane : lane + LANES]
                if lane == tile:
                    part = with_column(part, column, at - tile)
                taps[block, base + lane : base + lane + LANES] = part


def stacked_rows(grid, taps, row, count, order=(0, 1, 2)):
    width = count * grid.pitch
    return jnp.concatenate(
        [taps[:, (row + a) * grid.pitch : (row + a) * grid.pitch + width] for a in order],
        axis=0,
    )


def groups_of(count, size=ROW_GROUP):
    return [(row, min(size, count - row)) for row in range(0, count, size)]


def flat_piece(grid, pitched, skip, low, high, count):
    parts, at = [], low
    while at < high:
        row, column = divmod(at + skip, grid.columns)
        if row >= count:
            parts.append(jnp.zeros((pitched.shape[0], high - at), BF16))
            break
        size = min(grid.columns - column, high - at)
        begin = row * grid.pitch + column
        parts.append(pitched[:, begin : begin + size])
        at += size
    return jnp.concatenate(parts, axis=1) if len(parts) > 1 else parts[0]


def convolve(grid, r0, r1, skip, width, sources, sides, taps, weight, bias, pitched, flat,
             backwards=False, emit=None):
    built, done = r0 - 1, 0
    order = (2, 1, 0) if backwards else (0, 1, 2)
    for row, count in groups_of(r1 - r0):
        ready = min(r0 + row + count + 1 + ROW_GROUP, r1 + 1)
        build_taps(grid, r0 - 1, built, ready, sources, sides, taps, backwards)
        built = ready
        value = jnp.dot(
            weight, stacked_rows(grid, taps, row, count, order), preferred_element_type=F32
        )
        if bias is not None:
            value = value + bias
        pitched[:, row * grid.pitch : (row + count) * grid.pitch] = value.astype(BF16)
        last = row + count == r1 - r0
        while done < width:
            end = min(done + FLAT_LANES, width)
            if not last and end + skip > row * grid.columns:
                break
            flat[:, done:end] = flat_piece(grid, pitched, skip, done, end, r1 - r0)
            if emit is not None:
                emit(done, end)
            done = end


def edges_kernel(grid, places, tiles, x_ref, out_ref, held, sem):
    copies = [
        pltpu.make_async_copy(
            x_ref.at[:, pl.ds(tile * LANES, LANES)],
            held.at[:, pl.ds(number * LANES, LANES)],
            sem.at[number],
        )
        for number, tile in enumerate(tiles)
    ]
    for copy in copies:
        copy.start()
    for copy in copies:
        copy.wait()
    columns = []
    for cell in places:
        at = tiles.index(cell // LANES) * LANES + cell % LANES
        columns.append(held[:, at : at + 1])
    out_ref[...] = jnp.concatenate(columns, axis=1)


def edges_of(grid, field):
    rows = field.shape[0]
    places = [i for i in range(0, grid.cells, grid.columns)]
    places += [i for i in range(grid.columns - 1, grid.cells, grid.columns)]
    tiles = sorted({cell // LANES for cell in places})
    return pl.pallas_call(
        functools.partial(edges_kernel, grid, places, tiles),
        in_specs=[in_hbm()],
        out_specs=in_vmem(),
        out_shape=shape_of((rows, 2 * LAT_DEV)),
        scratch_shapes=[
            pltpu.VMEM((rows, len(tiles) * LANES), BF16),
            pltpu.SemaphoreType.DMA((len(tiles),)),
        ],
        compiler_params=params((rows, (len(tiles) + 1) * LANES, 2)),
        cost_estimate=cost(rows, rows),
        name="edges",
    )(kept_in_hbm(field))


def lon_halo(edges):
    peers = lax.axis_size("lon")
    right = [(i, (i + 1) % peers) for i in range(peers)]
    left = [(j, i) for i, j in right]
    before = lax.ppermute(edges[:, LAT_DEV:], "lon", right)
    after = lax.ppermute(edges[:, :LAT_DEV], "lon", left)
    return jnp.concatenate([before, after], axis=1)


def lat_halo(first_rows, last_rows, sides, upper):
    peers = lax.axis_size("lat")
    if peers == 2:
        sent = jnp.concatenate([jnp.where(upper, last_rows, first_rows), sides], axis=1)
        other = lax.ppermute(sent, "lat", [(0, 1), (1, 0)])
        none = jnp.zeros_like(other)
        return jnp.where(upper, none, other), jnp.where(upper, other, none)
    up = [(i, i + 1) for i in range(peers - 1)]
    down = [(j, i) for i, j in up]
    top = lax.ppermute(jnp.concatenate([last_rows, sides], axis=1), "lat", up)
    bottom = lax.ppermute(jnp.concatenate([first_rows, sides], axis=1), "lat", down)
    return top, bottom


def forward_kernel(grid, first, width, has_top, has_bottom, members, load, *refs):
    refs = list(refs)
    x_ref, sides_ref = refs[:2]
    del refs[:2]
    top_ref = refs.pop(0) if has_top else None
    bottom_ref = refs.pop(0) if has_bottom else None
    weight_ref, bias_ref, analysis_ref = refs[:3]
    del refs[:3]
    outs = refs[:members]
    target_ref, taps = refs[members : members + 2]
    pitched, pred, target_sem, load_sem = refs[-4:]
    me = lax.axis_index("member")
    piece = width // members
    r0, r1 = grid.rows(first, width)
    late = []
    if load:
        held = refs[members + 2]
        cut = min(round_up((r1 + 2) * grid.columns, LANES), grid.cells)
        copies = []
        for begin, end in ((0, cut), (cut, grid.cells)):
            for low in range(0, x_ref.shape[0], 16) if begin < end else ():
                at = (pl.ds(low, min(16, x_ref.shape[0] - low)), pl.ds(begin, end - begin))
                copies.append(
                    pltpu.make_async_copy(x_ref.at[at], held.at[at], load_sem.at[len(copies)])
                )
                copies[-1].start()
            if begin == 0:
                late = len(copies)
        for copy in copies[:late]:
            copy.wait()
        late = copies[late:]
        x_ref = held
    begin = pl.multiple_of(first + me * piece, LANES)
    target_copy = pltpu.make_async_copy(
        analysis_ref.at[:, pl.ds(begin, piece)], target_ref, target_sem.at[0]
    )
    target_copy.start()
    sides = (sides_ref, top_ref, bottom_ref)
    convolve(
        grid, r0, r1, first - r0 * grid.columns, width, [(x_ref, 0, grid.cells)], sides, taps,
        weight_ref[...], bias_ref[...], pitched, pred,
    )
    for d in range(members):
        begin = pl.multiple_of((me ^ d) * piece, LANES)
        outs[d][...] = pred[:, pl.ds(begin, piece)]
    target_copy.wait()
    for copy in late:
        copy.wait()


def forward(grid, first, width, members, x, load, sides, top, bottom, weight, bias, analysis):
    channels = x.shape[0]
    fields = weight.shape[0]
    r0, r1 = grid.rows(first, width)
    has_top, has_bottom = r0 == 0, r1 == LAT_DEV
    piece = width // members
    held = (3 * channels, (r1 - r0 + 2) * grid.pitch)
    operands = [kept_in_hbm(x) if load else kept_in_vmem(x), sides]
    if has_top:
        operands.append(top)
    if has_bottom:
        operands.append(bottom)
    operands += [weight, bias]
    specs = [in_hbm() if load else in_vmem()] + [in_vmem()] * (len(operands) - 1) + [in_hbm()]
    operands += [kept_in_hbm(analysis)]
    shapes = [shape_of((fields, piece))] * (members + 1) + [pltpu.VMEM(held, BF16)]
    if load:
        shapes.append(pltpu.VMEM((channels, grid.cells), BF16))
    return pl.pallas_call(
        functools.partial(
            forward_kernel, grid, first, width, has_top, has_bottom, members, load
        ),
        in_specs=specs,
        out_specs=[in_vmem()] * len(shapes),
        out_shape=shapes,
        scratch_shapes=[
            pltpu.VMEM((fields, (r1 - r0) * grid.pitch), BF16),
            pltpu.VMEM((fields, width), BF16),
            pltpu.SemaphoreType.DMA((1,)),
            pltpu.SemaphoreType.DMA((2 * -(-channels // 16),)),
        ],
        compiler_params=params(
            (2 * fields, (r1 - r0) * grid.pitch, 2),
            (2 * fields, 2 * width, 2),
            (fields, 9 * channels, 2),
        ),
        cost_estimate=cost(81 * channels * fields * width, 0),
        name=f"forward_{first}",
    )(*operands)


def slope(values):
    return values * lax.rsqrt(values * values + 1.0)


def score_kernel(members, target_ref, scale_ref, *refs):
    pieces = refs[:members]
    outs = refs[-members:]
    fields, piece = pieces[0].shape
    tiles = piece // LANES
    several = max(k for k in (1, 2, 3) if tiles % k == 0)

    def tile(index, carry):
        for part in range(several * -(-fields // 16)):
            low = part // several * 16
            at = (index * several + part % several) * LANES
            span = pl.ds(pl.multiple_of(at, LANES), LANES)
            rows = pl.ds(low, min(16, fields - low))
            values = [ref[rows, span].astype(F32) for ref in pieces]
            target = target_ref[rows, span].astype(F32)
            scale = scale_ref[rows, :]
            sums = [None] * members
            for i in range(members):
                for j in range(i + 1, members):
                    both = slope(values[i] - values[j])
                    sums[i] = both if sums[i] is None else sums[i] + both
                    sums[j] = -both if sums[j] is None else sums[j] - both
            for i in range(members):
                grad = slope(values[i] - target) * (1.0 / members) - sums[i] * (
                    1.0 / (members * (members - 1))
                )
                outs[i][rows, span] = (scale * grad).astype(BF16)
        return carry

    lax.fori_loop(0, tiles // several, tile, 0)


def score(first, target, scale, pieces, after):
    members = len(pieces)
    fields, piece = pieces[0].shape
    return pl.pallas_call(
        functools.partial(score_kernel, members),
        in_specs=[in_vmem()] * (2 + members) + [anywhere()] * len(after),
        out_specs=[in_vmem()] * members,
        out_shape=[shape_of((fields, piece))] * members,
        compiler_params=params((9 * round_up(fields, 16), piece, 2), (fields, LANES, 4)),
        cost_estimate=cost(13000 * fields * piece, 0),
        name=f"score_{first}",
    )(target, scale, *pieces, *after)


def weight_kernel(grid, first, width, members, chained, waits, halves, taps, *refs):
    me = lax.axis_index("member")
    pieces = refs[:members]
    before_ref = refs[members] if chained else None
    refs = refs[members + chained + waits :]
    out_ref, edge_ref = refs[:2]
    flat, pitched = refs[-2:]
    sum_ref = refs[-3]
    fields, piece = pieces[0].shape
    rows = out_ref.shape[0]
    r0, r1 = grid.rows(first, width)
    lead = grid.halo
    flat[:, :lead] = jnp.zeros((rows, lead), BF16)
    flat[:, lead + width :] = jnp.zeros((rows, flat.shape[1] - lead - width), BF16)
    base = fields // 16 * 16
    if base < rows:
        flat[pl.ds(base, rows - base), lead : lead + width] = jnp.zeros(
            (rows - base, width), BF16
        )
    for d in range(members):
        begin = pl.multiple_of((me ^ d) * piece, LANES)
        value = pieces[d][...]
        if grid.padded != grid.cells:
            cell = lax.broadcasted_iota(jnp.int32, (1, piece), 1) + (first + begin)
            value = jnp.where(cell < grid.cells, value.astype(F32), 0.0).astype(BF16)
        flat[pl.ds(0, fields), pl.ds(lead + begin, piece)] = value
    out_ref[...] = flat[:, lead : lead + width]
    columns = []
    for side in (0, grid.columns - 1):
        for row in range(LAT_DEV):
            at = row * grid.columns + side - first
            if 0 <= at < width:
                columns.append(flat[:, lead + at : lead + at + 1])
            else:
                columns.append(jnp.zeros((rows, 1), BF16))
    edge_ref[...] = jnp.concatenate(columns, axis=1)
    keep = jnp.where(
        lax.broadcasted_iota(jnp.int32, (1, LANES), 1) < grid.columns % LANES, 1.0, 0.0
    ).astype(BF16)
    for row, count in groups_of(r1 - r0, 2 * ROW_GROUP):
        for at in range(row, row + count):
            value = take(flat, lead + (r0 + at) * grid.columns - first, grid.pitch)
            to = at * grid.pitch
            for lane in range(0, grid.pitch, LANES):
                part = value[:, lane : lane + LANES]
                if lane + LANES > grid.columns:
                    part = part * keep
                pitched[:, to + lane : to + lane + LANES] = part
        stacked = stacked_rows(grid, taps, row, count)
        ones = jnp.ones((sum_ref.shape[1] - stacked.shape[0], stacked.shape[1]), BF16)
        part = nt_dot(
            pitched[:, row * grid.pitch : (row + count) * grid.pitch],
            jnp.concatenate([stacked, ones], axis=0),
        )
        if row == 0:
            sum_ref[...] = part + before_ref[...] if chained else part
        else:
            sum_ref[...] += part
    if halves:
        keep_ref, send_ref = refs[2:4]
        half = rows // 2
        upper = lax.axis_index("lat") & 1
        keep_ref[...] = sum_ref[pl.ds(pl.multiple_of(upper * half, 8), half), :]
        send_ref[...] = sum_ref[pl.ds(pl.multiple_of((1 - upper) * half, 8), half), :]


def weight_part(grid, first, width, rows, taps, pieces, before, after, halves):
    members = len(pieces)
    channels = taps.shape[0] // 3
    r0, r1 = grid.rows(first, width)
    sums = round_up(9 * channels + 1, members * LANES)
    chained = [] if before is None else [before]
    shapes = [shape_of((rows, width)), shape_of((rows, 2 * LAT_DEV))]
    whole = []
    if halves:
        shapes += [shape_of((rows // 2, sums), F32)] * 2
        whole = [pltpu.VMEM((rows, sums), F32)]
    else:
        shapes += [shape_of((rows, sums), F32)]
    return pl.pallas_call(
        functools.partial(
            weight_kernel, grid, first, width, members, len(chained), len(after), halves
        ),
        in_specs=[in_vmem()] * (1 + members + len(chained)) + [anywhere()] * len(after),
        out_specs=[in_vmem()] * len(shapes),
        out_shape=shapes,
        scratch_shapes=whole
        + [
            pltpu.VMEM((rows, 2 * grid.halo + 2 * LANES + width), BF16),
            pltpu.VMEM((rows, (r1 - r0) * grid.pitch), BF16),
        ],
        compiler_params=params(
            (rows, 2 * grid.halo + 2 * LANES + 3 * width, 2),
            (rows, (r1 - r0) * grid.pitch, 2),
            (rows, 3 * sums, 4),
        ),
        cost_estimate=cost(width, 0),
        name=f"weight_{first}",
    )(kept_in_vmem(taps), *pieces, *chained, *after)


def input_kernel(grid, r0, r1, chunks, aliased, *refs):
    refs = list(refs)
    parts = refs[: len(chunks)]
    del refs[: len(chunks)]
    sides_ref, weight_ref = refs[:2]
    del refs[:2]
    top_ref = refs.pop(0) if r0 == 0 else None
    bottom_ref = refs.pop(0) if r1 == LAT_DEV else None
    del refs[:aliased]
    out_ref, taps, pitched, flat, out_sem = refs
    sources = [
        (ref, first, min(first + width, grid.cells))
        for ref, (first, width) in zip(parts, chunks)
    ]
    sides = (sides_ref, top_ref, bottom_ref)
    copies = []

    def emit(low, high):
        at = r0 * grid.columns + low
        copies.append(
            pltpu.make_async_copy(
                flat.at[:, pl.ds(low, high - low)],
                out_ref.at[:, pl.ds(at, high - low)],
                out_sem.at[len(copies)],
            )
        )
        copies[-1].start()

    width = (r1 - r0) * grid.columns
    convolve(
        grid, r0, r1, 0, width, sources, sides, taps, weight_ref[...], None, pitched, flat,
        backwards=True, emit=emit,
    )
    for copy in copies:
        copy.wait()


def input_part(grid, r0, r1, chunks, parts, sides, top, bottom, weight, before):
    rows = parts[0].shape[0]
    channels = weight.shape[0]
    width = (r1 - r0) * grid.columns
    held = (3 * rows, (r1 - r0 + 2) * grid.pitch)
    near = []
    for (first, size), part in zip(chunks, parts):
        if first < (r1 + 1) * grid.columns + 1 and first + size > (r0 - 1) * grid.columns - 1:
            near.append(((first, size), part))
    chunks, parts = [pair[0] for pair in near], [pair[1] for pair in near]
    operands = [*parts, sides, weight] + [top] * (r0 == 0) + [bottom] * (r1 == LAT_DEV)
    specs = [in_vmem()] * len(operands)
    alias = {}
    if before is not None:
        alias = {len(operands): 0}
        operands.append(before)
        specs.append(anywhere())
    return pl.pallas_call(
        functools.partial(input_kernel, grid, r0, r1, chunks, len(alias)),
        in_specs=specs,
        out_specs=anywhere(),
        out_shape=shape_of((channels, grid.cells)),
        input_output_aliases=alias,
        scratch_shapes=[
            pltpu.VMEM(held, BF16),
            pltpu.VMEM((channels, (r1 - r0) * grid.pitch), BF16),
            pltpu.VMEM((channels, width), BF16),
            pltpu.SemaphoreType.DMA((-(-width // FLAT_LANES),)),
        ],
        compiler_params=params(
            (rows, sum(part.shape[1] for part in parts), 2),
            (*held, 2),
            (2 * channels, (r1 - r0) * grid.pitch, 2),
            (channels, 9 * rows, 2),
        ),
        cost_estimate=cost((80 if bottom is not None else 1) * channels * rows * width, width),
        name=f"input_{r0}",
    )(*operands)


def split_kernel(members, count, *refs):
    me = lax.axis_index("member")
    lanes = refs[count].shape[1]
    for d in range(members):
        span = pl.ds(pl.multiple_of((me ^ d) * lanes, LANES), lanes)
        total = refs[0][:, span]
        for ref in refs[1:count]:
            total += ref[:, span]
        refs[count + d][...] = total


def split_by_member(values, members):
    rows, lanes = values[0].shape
    return pl.pallas_call(
        functools.partial(split_kernel, members, len(values)),
        in_specs=[in_vmem()] * len(values),
        out_specs=[in_vmem()] * members,
        out_shape=[shape_of((rows, lanes // members), F32)] * members,
        compiler_params=params((rows, 3 * lanes, 4)),
        cost_estimate=cost(rows * lanes, 12 * rows * lanes),
        name="split",
    )(*values)


def join_kernel(members, *refs):
    me = lax.axis_index("member")
    lanes = refs[0].shape[1]
    for d in range(members):
        span = pl.ds(pl.multiple_of((me ^ d) * lanes, LANES), lanes)
        refs[members][:, span] = refs[d][...]


def join_members(pieces):
    members = len(pieces)
    rows, lanes = pieces[0].shape
    return pl.pallas_call(
        functools.partial(join_kernel, members),
        in_specs=[in_vmem()] * members,
        out_specs=in_vmem(),
        out_shape=shape_of((rows, members * lanes), F32),
        compiler_params=params((rows, 2 * members * lanes, 4)),
        cost_estimate=cost(rows * lanes, 12 * rows * lanes),
        name="join",
    )(*pieces)


def swap(value, axis, bits):
    return lax.ppermute(value, axis, [(i, i ^ bits) for i in range(lax.axis_size(axis))])


def sum_axis(value, axis, bit):
    size = lax.axis_size(axis)
    while bit < size:
        if 2 * bit < size:
            near, far, both = [swap(value, axis, k * bit) for k in (1, 2, 3)]
            value = (value + near) + (far + both)
        else:
            value = value + swap(value, axis, bit)
        bit *= 4
    return value


def sum_all(keep, send, upper, late):
    members = lax.axis_size("member")
    other = swap(send, "lat", 1)
    other, late = lax.optimization_barrier((other, late))
    values = [keep, other]
    if lax.axis_size("lat") > 2:
        values = [sum_axis(keep + other, "lat", 2)]
    pieces = split_by_member(values, members)
    moved = [swap(pieces[d], "member", d) for d in range(1, members)]
    value = functools.reduce(jnp.add, moved, pieces[0])
    value = sum_axis(value, "lon", 1)
    half = join_members([value] + [swap(value, "member", d) for d in range(1, members)])
    other = swap(half, "lat", 1)
    total = jnp.where(
        upper,
        jnp.concatenate([other, half], axis=0),
        jnp.concatenate([half, other], axis=0),
    )
    return total, late


def weights_kernel(taps_ref, forward_ref, backward_ref):
    count, channels, fields = taps_ref.shape
    rows = backward_ref.shape[1] // count
    taps = [taps_ref[t] for t in range(count)]
    forward_ref[...] = jnp.concatenate(
        [tap.astype(F32).T for tap in taps], axis=1
    ).astype(BF16)
    none = [jnp.zeros((channels, rows - fields), BF16)] * (rows > fields)
    backward_ref[...] = jnp.concatenate([part for tap in taps for part in (tap, *none)], axis=1)


def prepare_weights(taps, rows):
    count, channels, fields = taps.shape
    return pl.pallas_call(
        weights_kernel,
        in_specs=[in_vmem()],
        out_specs=[in_vmem()] * 2,
        out_shape=[shape_of((fields, count * channels)), shape_of((channels, count * rows))],
        compiler_params=params((4 * channels, count * LANES, 4)),
        cost_estimate=cost(channels, 8 * count * channels * rows),
        name="weights",
    )(taps)


def chunks_of(grid, members):
    unit = members * LANES
    units = grid.padded // unit
    if units < 15:
        return [(0, grid.padded)]
    head = units // 2 + 2
    return [(0, head * unit), (head * unit, (units - head) * unit)]


def parts_of(grid, wanted):
    step = LAT_DEV // wanted
    if step * grid.columns % LANES:
        return [(0, LAT_DEV)]
    ranges = [(row, row + step) for row in range(0, LAT_DEV, step)]
    return ranges[1:-1] + [ranges[0], ranges[-1]]


def local(inputs, weight, bias, analysis, field_weight):
    channels, cells = inputs.shape[1], inputs.shape[4]
    fields = analysis.shape[0]
    members = lax.axis_size("member")
    grid = Grid(cells, members)
    x = inputs.reshape(channels, cells)
    target = analysis.reshape(fields, cells)
    if grid.padded != cells:
        target = jnp.pad(target, ((0, 0), (0, grid.padded - cells)))
    rows = round_up(fields, 16)
    taps = weight.reshape(9, channels, fields)
    forward_weight, backward_weight = prepare_weights(taps, rows)
    scale = jnp.broadcast_to(field_weight[:, None], (fields, LANES))
    shift = bias[:, None]
    upper = (lax.axis_index("lat") & 1) != 0
    x_sides = lon_halo(edges_of(grid, x))
    x_sides, forward_weight, backward_weight, scale, shift, upper = lax.optimization_barrier(
        (x_sides, forward_weight, backward_weight, scale, shift, upper)
    )
    first_lat = jnp.logical_not(upper)
    x_top, x_bottom = lat_halo(
        x[:, : grid.halo], x[:, cells - grid.halo :], x_sides, first_lat
    )

    def to_members(pieces):
        moved = [pieces[0]]
        for d in range(1, members):
            moved.append(lax.ppermute(pieces[d], "member", [(i, i ^ d) for i in range(members)]))
        return moved

    chunks = chunks_of(grid, members)
    received, returned, targets, taken = [], [], [], []
    parts, edges, sums = [], [], None
    held = None
    for first, width in chunks:
        out = forward(
            grid, first, width, members, x if held is None else held, held is None, x_sides,
            x_top, x_bottom, forward_weight, shift, target,
        )
        targets.append(out[members])
        taken.append(out[members + 1])
        if held is None:
            held = out[members + 2]
        received.append(to_members(out[:members]))
    for (first, width), pieces, goal in zip(chunks, received, targets):
        returned.append(to_members(score(first, goal, scale, pieces, targets[-1:])))
    ranges = parts_of(grid, 4)
    grad_input, early = None, []
    for number, (first, width) in enumerate(chunks):
        final = number == len(chunks) - 1
        after = [returned[-1][0]] if grad_input is None else [kept_in_hbm(grad_input)]
        part, edge, *sums = weight_part(
            grid, first, width, rows, taken[number], returned[number],
            sums[0] if sums else None, after, final,
        )
        parts.append(part)
        edges.append(edge)
        if final:
            break
        early_sides = lon_halo(edge)
        done_rows = width // grid.columns
        early = [(r0, r1) for r0, r1 in ranges if r0 > 0 and r1 < done_rows]
        for r0, r1 in early:
            grad_input = input_part(
                grid, r0, r1, chunks[:1], parts[:1], early_sides, None, None, backward_weight,
                grad_input,
            )
    total, late_edges = sum_all(*sums, upper, edges[-1])
    g_sides = lon_halo(late_edges)
    if len(chunks) > 1:
        g_sides = g_sides + early_sides
    end = cells - chunks[-1][0]
    g_top, g_bottom = lat_halo(
        parts[0][:, : grid.halo], parts[-1][:, end - grid.halo : end], g_sides, first_lat
    )
    for r0, r1 in ranges:
        if (r0, r1) in early:
            continue
        grad_input = input_part(
            grid, r0, r1, chunks, parts, g_sides, g_top, g_bottom, backward_weight, grad_input
        )
    total = total / (cells * lax.axis_size("lat") * lax.axis_size("lon"))
    grad_weight = total[:fields, : 9 * channels].T.reshape(9, channels * fields)
    grad_bias = total[:fields, 9 * channels]
    return (grad_input.reshape(1, channels, 1, 1, cells), grad_weight, grad_bias)


def solution(mesh):
    placed = (P("member", None, "lat", "lon", None), P(), P(), P(None, "lat", "lon", None), P())
    return jax.shard_map(
        local,
        mesh=mesh,
        in_specs=placed,
        out_specs=(P("member", None, "lat", "lon", None), P(), P()),
        check_vma=False,
    )
```

```python
import functools

import jax
import jax.numpy as jnp
from jax import lax
from jax.experimental import pallas as pl
from jax.experimental.pallas import tpu as pltpu
from jax.sharding import PartitionSpec as P

LAT_DEV = 64
LANES = 128
ROW_GROUP = 2
FLAT_LANES = 1024
SLACK = 3 * 1024 * 1024
F32 = jnp.float32
BF16 = jnp.bfloat16


def round_up(value, step):
    return -(-value // step) * step


def params(*held):
    total = sum(round_up(rows, 16) * round_up(lanes, LANES) * size for rows, lanes, size in held)
    return pltpu.CompilerParams(vmem_limit_bytes=total + SLACK)


def kept_in_hbm(value):
    return pltpu.with_memory_space_constraint(value, pltpu.HBM)


def kept_in_vmem(value):
    return pltpu.with_memory_space_constraint(value, pltpu.VMEM)


def shape_of(dims, dtype=BF16):
    return jax.ShapeDtypeStruct(dims, dtype)


def cost(flops, moved):
    return pl.CostEstimate(flops=int(flops), bytes_accessed=int(moved), transcendentals=0)


def in_vmem():
    return pl.BlockSpec(memory_space=pltpu.VMEM)


def in_smem():
    return pl.BlockSpec(memory_space=pltpu.SMEM)


def in_hbm():
    return pl.BlockSpec(memory_space=pltpu.HBM)


def anywhere():
    return pl.BlockSpec(memory_space=pl.ANY)


def nt_dot(left, right):
    return lax.dot_general(left, right, (((1,), (1,)), ((), ())), preferred_element_type=F32)


class Grid:
    def __init__(self, cells, members):
        self.cells = cells
        self.columns = cells // LAT_DEV
        self.pitch = round_up(self.columns, LANES)
        self.halo = round_up(self.columns + 1, LANES)
        self.padded = round_up(cells, members * LANES)

    def rows(self, first, width):
        return first // self.columns, -(-min(first + width, self.cells) // self.columns)


def take(ref, start, width):
    low = start // LANES * LANES
    off = start - low
    if off == 0:
        return ref[:, low : low + width]
    return ref[:, low : low + width + LANES][:, off : off + width]


def side_column(refs, grid, row, right):
    own, top, bottom = refs
    slot = LAT_DEV if right else 0
    if row < 0:
        ref, lane = top, grid.halo + slot + LAT_DEV - 1
    elif row >= LAT_DEV:
        ref, lane = bottom, grid.halo + slot
    else:
        ref, lane = own, slot + row
    return ref[:, lane : lane + 1].astype(F32)


def with_column(tile, column, lane):
    here = lax.broadcasted_iota(jnp.int32, tile.shape, 1).astype(BF16) == lane
    return jnp.where(here, jnp.broadcast_to(column, tile.shape).astype(BF16), tile)


def take_cells(sources, start, width):
    parts, at, end = [], start, start + width
    for ref, begin, last in sources:
        base = (start - begin) // LANES * LANES
        if begin <= start and end <= last and base + width + LANES <= ref.shape[1]:
            return take(ref, start - begin, width)
        low, high = max(at, begin), min(end, last)
        if low < high:
            if low > at:
                parts.append(jnp.zeros((ref.shape[0], low - at), BF16))
            base = (low - begin) // LANES * LANES
            top = min(round_up(high - begin, LANES), ref.shape[1])
            parts.append(ref[:, base:top][:, low - begin - base : high - begin - base])
            at = high
    if at < end:
        parts.append(jnp.zeros((sources[0][0].shape[0], end - at), BF16))
    return jnp.concatenate(parts, axis=1) if len(parts) > 1 else parts[0]


def row_taps(grid, row, b, sources, top, bottom):
    shift = b - 1
    if row < 0 and top is not None:
        return take_cells([(top, 0, top.shape[1])], grid.halo - grid.columns + shift, grid.pitch)
    if row >= LAT_DEV and bottom is not None:
        return take_cells([(bottom, 0, bottom.shape[1])], shift, grid.pitch)
    return take_cells(sources, row * grid.columns + shift, grid.pitch)


def build_taps(grid, origin, low, high, sources, sides, taps, backwards=False):
    rows = sources[0][0].shape[0]
    own, top, bottom = sides
    for row in range(low, high):
        base = (row - origin) * grid.pitch
        for b in range(3):
            value = row_taps(grid, row, b, sources, top, bottom)
            block = pl.ds((2 - b if backwards else b) * rows, rows)
            if b == 1:
                taps[block, base : base + grid.pitch] = value
                continue
            at = grid.columns - 1 if b == 2 else 0
            tile = at // LANES * LANES
            column = side_column(sides, grid, row, b == 2)
            for lane in range(0, grid.pitch, LANES):
                part = value[:, lane : lane + LANES]
                if lane == tile:
                    part = with_column(part, column, at - tile)
                taps[block, base + lane : base + lane + LANES] = part


def stacked_rows(grid, taps, row, count, order=(0, 1, 2)):
    width = count * grid.pitch
    return jnp.concatenate(
        [taps[:, (row + a) * grid.pitch : (row + a) * grid.pitch + width] for a in order],
        axis=0,
    )


def groups_of(count, size=ROW_GROUP):
    return [(row, min(size, count - row)) for row in range(0, count, size)]


def flat_piece(grid, pitched, skip, low, high, count):
    parts, at = [], low
    while at < high:
        row, column = divmod(at + skip, grid.columns)
        if row >= count:
            parts.append(jnp.zeros((pitched.shape[0], high - at), BF16))
            break
        size = min(grid.columns - column, high - at)
        begin = row * grid.pitch + column
        parts.append(pitched[:, begin : begin + size])
        at += size
    return jnp.concatenate(parts, axis=1) if len(parts) > 1 else parts[0]


def convolve(grid, r0, r1, skip, width, sources, sides, taps, weight, bias, pitched, flat,
             backwards=False, emit=None, fetch=None):
    built, done = r0 - 1, 0
    order = (2, 1, 0) if backwards else (0, 1, 2)
    for row, count in groups_of(r1 - r0):
        ready = min(r0 + row + count + 1 + ROW_GROUP, r1 + 1)
        if fetch is not None:
            fetch(ready)
        build_taps(grid, r0 - 1, built, ready, sources, sides, taps, backwards)
        built = ready
        value = jnp.dot(
            weight, stacked_rows(grid, taps, row, count, order), preferred_element_type=F32
        )
        if bias is not None:
            value = value + bias
        pitched[:, row * grid.pitch : (row + count) * grid.pitch] = value.astype(BF16)
        last = row + count == r1 - r0
        while done < width:
            end = min(done + FLAT_LANES, width)
            if not last and end + skip > row * grid.columns:
                break
            flat[:, done:end] = flat_piece(grid, pitched, skip, done, end, r1 - r0)
            if emit is not None:
                emit(done, end)
            done = end


def edges_kernel(grid, places, tiles, x_ref, out_ref, held, sem):
    copies = [
        pltpu.make_async_copy(
            x_ref.at[:, pl.ds(tile * LANES, LANES)],
            held.at[:, pl.ds(number * LANES, LANES)],
            sem.at[number],
        )
        for number, tile in enumerate(tiles)
    ]
    for copy in copies:
        copy.start()
    for copy in copies:
        copy.wait()
    columns = []
    for cell in places:
        at = tiles.index(cell // LANES) * LANES + cell % LANES
        columns.append(held[:, at : at + 1])
    out_ref[...] = jnp.concatenate(columns, axis=1)


def edges_of(grid, field):
    rows = field.shape[0]
    places = [i for i in range(0, grid.cells, grid.columns)]
    places += [i for i in range(grid.columns - 1, grid.cells, grid.columns)]
    tiles = sorted({cell // LANES for cell in places})
    return pl.pallas_call(
        functools.partial(edges_kernel, grid, places, tiles),
        in_specs=[in_hbm()],
        out_specs=in_vmem(),
        out_shape=shape_of((rows, 2 * LAT_DEV)),
        scratch_shapes=[
            pltpu.VMEM((rows, len(tiles) * LANES), BF16),
            pltpu.SemaphoreType.DMA((len(tiles),)),
        ],
        compiler_params=params((rows, (len(tiles) + 1) * LANES, 2)),
        cost_estimate=cost(rows, rows),
        name="edges",
    )(kept_in_hbm(field))


def lon_halo(edges):
    peers = lax.axis_size("lon")
    right = [(i, (i + 1) % peers) for i in range(peers)]
    left = [(j, i) for i, j in right]
    before = lax.ppermute(edges[:, LAT_DEV:], "lon", right)
    after = lax.ppermute(edges[:, :LAT_DEV], "lon", left)
    return jnp.concatenate([before, after], axis=1)


def lat_halo(first_rows, last_rows, sides, upper):
    peers = lax.axis_size("lat")
    if peers == 2:
        sent = jnp.concatenate([jnp.where(upper, last_rows, first_rows), sides], axis=1)
        other = lax.ppermute(sent, "lat", [(0, 1), (1, 0)])
        none = jnp.zeros_like(other)
        return jnp.where(upper, none, other), jnp.where(upper, other, none)
    up = [(i, i + 1) for i in range(peers - 1)]
    down = [(j, i) for i, j in up]
    top = lax.ppermute(jnp.concatenate([last_rows, sides], axis=1), "lat", up)
    bottom = lax.ppermute(jnp.concatenate([first_rows, sides], axis=1), "lat", down)
    return top, bottom


def stages_of(grid, r0, r1):
    low = max((r0 - 1) * grid.columns - 1, 0) // LANES * LANES
    high = min(round_up((r1 + 1) * grid.columns + 1, LANES), grid.cells)
    step = round_up((high - low) // 4, LANES)
    stages = [(at, min(at + step, high)) for at in range(low, high, step)]
    if high < grid.cells:
        stages.append((high, grid.cells))
    if low > 0:
        stages.append((0, low))
    return stages


def forward_kernel(grid, first, width, has_top, has_bottom, members, load, waits, *refs):
    refs = list(refs)
    x_ref, sides_ref = refs[:2]
    del refs[:2]
    top_ref = refs.pop(0) if has_top else None
    bottom_ref = refs.pop(0) if has_bottom else None
    weight_ref, bias_ref, analysis_ref = refs[:3]
    del refs[: 3 + waits]
    outs = refs[:members]
    target_ref, taps = refs[members : members + 2]
    pitched, pred, target_sem, load_sem = refs[-4:]
    me = lax.axis_index("member")
    piece = width // members
    r0, r1 = grid.rows(first, width)
    pending = []
    if load:
        held = refs[members + 2]
        for begin, end in stages_of(grid, r0, r1):
            copies = []
            for low in range(0, x_ref.shape[0], 32):
                at = (pl.ds(low, min(32, x_ref.shape[0] - low)), pl.ds(begin, end - begin))
                sem = load_sem.at[len(pending), len(copies)]
                copies.append(pltpu.make_async_copy(x_ref.at[at], held.at[at], sem))
                copies[-1].start()
            pending.append((begin, end, copies))
        x_ref = held

    def fetch(row):
        while pending and (row is None or pending[0][0] < row * grid.columns + 1):
            for copy in pending.pop(0)[2]:
                copy.wait()

    begin = pl.multiple_of(first + me * piece, LANES)
    target_copy = pltpu.make_async_copy(
        analysis_ref.at[:, pl.ds(begin, piece)], target_ref, target_sem.at[0]
    )
    target_copy.start()
    sides = (sides_ref, top_ref, bottom_ref)
    convolve(
        grid, r0, r1, first - r0 * grid.columns, width, [(x_ref, 0, grid.cells)], sides, taps,
        weight_ref[...], bias_ref[...], pitched, pred, fetch=fetch,
    )
    for d in range(members):
        begin = pl.multiple_of((me ^ d) * piece, LANES)
        outs[d][...] = pred[:, pl.ds(begin, piece)]
    target_copy.wait()
    fetch(None)


def forward(
    grid, first, width, members, x, load, sides, top, bottom, weight, bias, analysis, after
):
    channels = x.shape[0]
    fields = weight.shape[0]
    r0, r1 = grid.rows(first, width)
    has_top, has_bottom = r0 == 0, r1 == LAT_DEV
    piece = width // members
    held = (3 * channels, (r1 - r0 + 2) * grid.pitch)
    operands = [kept_in_hbm(x) if load else kept_in_vmem(x), sides]
    if has_top:
        operands.append(top)
    if has_bottom:
        operands.append(bottom)
    operands += [weight, bias]
    specs = [in_hbm() if load else in_vmem()] + [in_vmem()] * (len(operands) - 1) + [in_hbm()]
    operands += [kept_in_hbm(analysis), *after]
    specs += [anywhere()] * len(after)
    shapes = [shape_of((fields, piece))] * (members + 1) + [pltpu.VMEM(held, BF16)]
    if load:
        shapes.append(pltpu.VMEM((channels, grid.cells), BF16))
    return pl.pallas_call(
        functools.partial(
            forward_kernel, grid, first, width, has_top, has_bottom, members, load, len(after)
        ),
        in_specs=specs,
        out_specs=[in_vmem()] * len(shapes),
        out_shape=shapes,
        scratch_shapes=[
            pltpu.VMEM((fields, (r1 - r0) * grid.pitch), BF16),
            pltpu.VMEM((fields, width), BF16),
            pltpu.SemaphoreType.DMA((1,)),
            pltpu.SemaphoreType.DMA((8, -(-channels // 32))),
        ],
        compiler_params=params(
            (2 * fields, (r1 - r0) * grid.pitch, 2),
            (2 * fields, 2 * width, 2),
            (fields, 9 * channels, 2),
        ),
        cost_estimate=cost(81 * channels * fields * width, 0),
        name=f"forward_{first}",
    )(*operands)


def slope(values):
    return values * lax.rsqrt(values * values + 1.0)


def score_kernel(members, target_ref, scale_ref, *refs):
    pieces = refs[:members]
    outs = refs[-members:]
    fields, piece = pieces[0].shape
    tiles = piece // LANES
    several = max(k for k in (1, 2, 3) if tiles % k == 0)

    def tile(index, carry):
        for part in range(several * -(-fields // 16)):
            low = part // several * 16
            at = (index * several + part % several) * LANES
            span = pl.ds(pl.multiple_of(at, LANES), LANES)
            rows = pl.ds(low, min(16, fields - low))
            values = [ref[rows, span].astype(F32) for ref in pieces]
            target = target_ref[rows, span].astype(F32)
            scale = scale_ref[rows, :]
            sums = [None] * members
            for i in range(members):
                for j in range(i + 1, members):
                    both = slope(values[i] - values[j])
                    sums[i] = both if sums[i] is None else sums[i] + both
                    sums[j] = -both if sums[j] is None else sums[j] - both
            for i in range(members):
                grad = slope(values[i] - target) * (1.0 / members) - sums[i] * (
                    1.0 / (members * (members - 1))
                )
                outs[i][rows, span] = (scale * grad).astype(BF16)
        return carry

    lax.fori_loop(0, tiles // several, tile, 0)


def score(first, target, scale, pieces, after):
    members = len(pieces)
    fields, piece = pieces[0].shape
    return pl.pallas_call(
        functools.partial(score_kernel, members),
        in_specs=[in_vmem()] * (2 + members) + [anywhere()] * len(after),
        out_specs=[in_vmem()] * members,
        out_shape=[shape_of((fields, piece))] * members,
        compiler_params=params((9 * round_up(fields, 16), piece, 2), (fields, LANES, 4)),
        cost_estimate=cost(13000 * fields * piece, 0),
        name=f"score_{first}",
    )(target, scale, *pieces, *after)


def weight_kernel(grid, first, width, members, chained, waits, halves, taps, *refs):
    me = lax.axis_index("member")
    pieces = refs[:members]
    before_ref = refs[members] if chained else None
    refs = refs[members + chained + waits :]
    out_ref, edge_ref = refs[:2]
    flat, pitched = refs[-2:]
    sum_ref = refs[-3]
    fields, piece = pieces[0].shape
    rows = out_ref.shape[0]
    r0, r1 = grid.rows(first, width)
    lead = grid.halo
    flat[:, :lead] = jnp.zeros((rows, lead), BF16)
    flat[:, lead + width :] = jnp.zeros((rows, flat.shape[1] - lead - width), BF16)
    base = fields // 16 * 16
    if base < rows:
        flat[pl.ds(base, rows - base), lead : lead + width] = jnp.zeros(
            (rows - base, width), BF16
        )
    for d in range(members):
        begin = pl.multiple_of((me ^ d) * piece, LANES)
        value = pieces[d][...]
        if grid.padded != grid.cells:
            cell = lax.broadcasted_iota(jnp.int32, (1, piece), 1) + (first + begin)
            value = jnp.where(cell < grid.cells, value.astype(F32), 0.0).astype(BF16)
        flat[pl.ds(0, fields), pl.ds(lead + begin, piece)] = value
    out_ref[...] = flat[:, lead : lead + width]
    columns = []
    for side in (0, grid.columns - 1):
        for row in range(LAT_DEV):
            at = row * grid.columns + side - first
            if 0 <= at < width:
                columns.append(flat[:, lead + at : lead + at + 1])
            else:
                columns.append(jnp.zeros((rows, 1), BF16))
    edge_ref[...] = jnp.concatenate(columns, axis=1)
    keep = jnp.where(
        lax.broadcasted_iota(jnp.int32, (1, LANES), 1) < grid.columns % LANES, 1.0, 0.0
    ).astype(BF16)
    for row, count in groups_of(r1 - r0, 2 * ROW_GROUP):
        for at in range(row, row + count):
            value = take(flat, lead + (r0 + at) * grid.columns - first, grid.pitch)
            to = at * grid.pitch
            for lane in range(0, grid.pitch, LANES):
                part = value[:, lane : lane + LANES]
                if lane + LANES > grid.columns:
                    part = part * keep
                pitched[:, to + lane : to + lane + LANES] = part
        stacked = stacked_rows(grid, taps, row, count)
        ones = jnp.ones((sum_ref.shape[1] - stacked.shape[0], stacked.shape[1]), BF16)
        part = nt_dot(
            pitched[:, row * grid.pitch : (row + count) * grid.pitch],
            jnp.concatenate([stacked, ones], axis=0),
        )
        if row == 0:
            sum_ref[...] = part + before_ref[...] if chained else part
        else:
            sum_ref[...] += part
    if halves:
        keep_ref, send_ref = refs[2:4]
        half = rows // 2
        upper = lax.axis_index("lat") & 1
        keep_ref[...] = sum_ref[pl.ds(pl.multiple_of(upper * half, 8), half), :]
        send_ref[...] = sum_ref[pl.ds(pl.multiple_of((1 - upper) * half, 8), half), :]


def weight_part(grid, first, width, rows, taps, pieces, before, after, halves):
    members = len(pieces)
    channels = taps.shape[0] // 3
    r0, r1 = grid.rows(first, width)
    sums = round_up(9 * channels + 1, members * LANES)
    chained = [] if before is None else [before]
    shapes = [shape_of((rows, width)), shape_of((rows, 2 * LAT_DEV))]
    whole = []
    if halves:
        shapes += [shape_of((rows // 2, sums), F32)] * 2
        whole = [pltpu.VMEM((rows, sums), F32)]
    else:
        shapes += [shape_of((rows, sums), F32)]
    return pl.pallas_call(
        functools.partial(
            weight_kernel, grid, first, width, members, len(chained), len(after), halves
        ),
        in_specs=[in_vmem()] * (1 + members + len(chained)) + [anywhere()] * len(after),
        out_specs=[in_vmem()] * len(shapes),
        out_shape=shapes,
        scratch_shapes=whole
        + [
            pltpu.VMEM((rows, 2 * grid.halo + 2 * LANES + width), BF16),
            pltpu.VMEM((rows, (r1 - r0) * grid.pitch), BF16),
        ],
        compiler_params=params(
            (rows, 2 * grid.halo + 2 * LANES + 3 * width, 2),
            (rows, (r1 - r0) * grid.pitch, 2),
            (rows, 3 * sums, 4),
        ),
        cost_estimate=cost(width, 0),
        name=f"weight_{first}",
    )(kept_in_vmem(taps), *pieces, *chained, *after)


def input_kernel(grid, r0, r1, chunks, aliased, *refs):
    refs = list(refs)
    parts = refs[: len(chunks)]
    del refs[: len(chunks)]
    sides_ref, weight_ref = refs[:2]
    del refs[:2]
    top_ref = refs.pop(0) if r0 == 0 else None
    bottom_ref = refs.pop(0) if r1 == LAT_DEV else None
    del refs[:aliased]
    out_ref, taps, pitched, flat, out_sem = refs
    sources = [
        (ref, first, min(first + width, grid.cells))
        for ref, (first, width) in zip(parts, chunks)
    ]
    sides = (sides_ref, top_ref, bottom_ref)
    copies = []

    def emit(low, high):
        at = r0 * grid.columns + low
        copies.append(
            pltpu.make_async_copy(
                flat.at[:, pl.ds(low, high - low)],
                out_ref.at[:, pl.ds(at, high - low)],
                out_sem.at[len(copies)],
            )
        )
        copies[-1].start()

    width = (r1 - r0) * grid.columns
    convolve(
        grid, r0, r1, 0, width, sources, sides, taps, weight_ref[...], None, pitched, flat,
        backwards=True, emit=emit,
    )
    for copy in copies:
        copy.wait()


def input_part(grid, r0, r1, chunks, parts, sides, top, bottom, weight, before, slow):
    rows = parts[0].shape[0]
    channels = weight.shape[0]
    width = (r1 - r0) * grid.columns
    held = (3 * rows, (r1 - r0 + 2) * grid.pitch)
    near = []
    for (first, size), part in zip(chunks, parts):
        if first < (r1 + 1) * grid.columns + 1 and first + size > (r0 - 1) * grid.columns - 1:
            near.append(((first, size), part))
    chunks, parts = [pair[0] for pair in near], [pair[1] for pair in near]
    operands = [*parts, sides, weight] + [top] * (r0 == 0) + [bottom] * (r1 == LAT_DEV)
    specs = [in_vmem()] * len(operands)
    alias = {}
    if before is not None:
        alias = {len(operands): 0}
        operands.append(before)
        specs.append(anywhere())
    return pl.pallas_call(
        functools.partial(input_kernel, grid, r0, r1, chunks, len(alias)),
        in_specs=specs,
        out_specs=anywhere(),
        out_shape=shape_of((channels, grid.cells)),
        input_output_aliases=alias,
        scratch_shapes=[
            pltpu.VMEM(held, BF16),
            pltpu.VMEM((channels, (r1 - r0) * grid.pitch), BF16),
            pltpu.VMEM((channels, width), BF16),
            pltpu.SemaphoreType.DMA((-(-width // FLAT_LANES),)),
        ],
        compiler_params=params(
            (rows, sum(part.shape[1] for part in parts), 2),
            (*held, 2),
            (2 * channels, (r1 - r0) * grid.pitch, 2),
            (channels, 9 * rows, 2),
        ),
        cost_estimate=cost((80 if slow else 1) * channels * rows * width, width),
        name=f"input_{r0}",
    )(*operands)


def split_kernel(members, count, *refs):
    me = lax.axis_index("member")
    lanes = refs[count].shape[1]
    for d in range(members):
        span = pl.ds(pl.multiple_of((me ^ d) * lanes, LANES), lanes)
        total = refs[0][:, span]
        for ref in refs[1:count]:
            total += ref[:, span]
        refs[count + d][...] = total


def split_by_member(values, members):
    rows, lanes = values[0].shape
    return pl.pallas_call(
        functools.partial(split_kernel, members, len(values)),
        in_specs=[in_vmem()] * len(values),
        out_specs=[in_vmem()] * members,
        out_shape=[shape_of((rows, lanes // members), F32)] * members,
        compiler_params=params((rows, 3 * lanes, 4)),
        cost_estimate=cost(rows * lanes, 12 * rows * lanes),
        name="split",
    )(*values)


def join_kernel(members, *refs):
    me = lax.axis_index("member")
    lanes = refs[0].shape[1]
    for d in range(members):
        span = pl.ds(pl.multiple_of((me ^ d) * lanes, LANES), lanes)
        refs[members][:, span] = refs[d][...]


def join_members(pieces):
    members = len(pieces)
    rows, lanes = pieces[0].shape
    return pl.pallas_call(
        functools.partial(join_kernel, members),
        in_specs=[in_vmem()] * members,
        out_specs=in_vmem(),
        out_shape=shape_of((rows, members * lanes), F32),
        compiler_params=params((rows, 2 * members * lanes, 4)),
        cost_estimate=cost(rows * lanes, 12 * rows * lanes),
        name="join",
    )(*pieces)


def swap(value, axis, bits):
    return lax.ppermute(value, axis, [(i, i ^ bits) for i in range(lax.axis_size(axis))])


def sum_axis(value, axis, bit):
    size = lax.axis_size(axis)
    while bit < size:
        if 2 * bit < size:
            near, far, both = [swap(value, axis, k * bit) for k in (1, 2, 3)]
            value = (value + near) + (far + both)
        else:
            value = value + swap(value, axis, bit)
        bit *= 4
    return value


def sum_all(keep, send, upper, late):
    members = lax.axis_size("member")
    other = swap(send, "lat", 1)
    other, late = lax.optimization_barrier((other, late))
    values = [keep, other]
    if lax.axis_size("lat") > 2:
        values = [sum_axis(keep + other, "lat", 2)]
    pieces = split_by_member(values, members)
    moved = [swap(pieces[d], "member", d) for d in range(1, members)]
    value = functools.reduce(jnp.add, moved, pieces[0])
    value = sum_axis(value, "lon", 1)
    half = join_members([value] + [swap(value, "member", d) for d in range(1, members)])
    other = swap(half, "lat", 1)
    total = jnp.where(
        upper,
        jnp.concatenate([other, half], axis=0),
        jnp.concatenate([half, other], axis=0),
    )
    return total, late


def weights_kernel(taps_ref, forward_ref, backward_ref):
    count, channels, fields = taps_ref.shape
    rows = backward_ref.shape[1] // count
    taps = [taps_ref[t] for t in range(count)]
    forward_ref[...] = jnp.concatenate(
        [tap.astype(F32).T for tap in taps], axis=1
    ).astype(BF16)
    none = [jnp.zeros((channels, rows - fields), BF16)] * (rows > fields)
    backward_ref[...] = jnp.concatenate([part for tap in taps for part in (tap, *none)], axis=1)


def prepare_weights(taps, rows):
    count, channels, fields = taps.shape
    return pl.pallas_call(
        weights_kernel,
        in_specs=[in_vmem()],
        out_specs=[in_vmem()] * 2,
        out_shape=[shape_of((fields, count * channels)), shape_of((channels, count * rows))],
        compiler_params=params((4 * channels, count * LANES, 4)),
        cost_estimate=cost(channels, 8 * count * channels * rows),
        name="weights",
    )(taps)


def chunks_of(grid, members):
    unit = members * LANES
    units = grid.padded // unit
    if units < 15:
        return [(0, grid.padded)], [0]
    sizes = [units * 3 // 8 + 1, units * 2 // 5]
    sizes.append(units - sum(sizes))
    first = [sum(sizes[:i]) for i in range(3)]
    return [(first[i] * unit, sizes[i] * unit) for i in range(3)], [1, 0, 2]


def parts_of(grid, wanted):
    step = LAT_DEV // wanted
    if step * grid.columns % LANES:
        return [(0, LAT_DEV)]
    ranges = [(row, row + step) for row in range(0, LAT_DEV, step)]
    return ranges[1:-1] + [ranges[0], ranges[-1]]


def local(inputs, weight, bias, analysis, field_weight):
    channels, cells = inputs.shape[1], inputs.shape[4]
    fields = analysis.shape[0]
    members = lax.axis_size("member")
    grid = Grid(cells, members)
    x = inputs.reshape(channels, cells)
    target = analysis.reshape(fields, cells)
    if grid.padded != cells:
        target = jnp.pad(target, ((0, 0), (0, grid.padded - cells)))
    rows = round_up(fields, 16)
    taps = weight.reshape(9, channels, fields)
    forward_weight, backward_weight = prepare_weights(taps, rows)
    scale = jnp.broadcast_to(field_weight[:, None], (fields, LANES))
    shift = bias[:, None]
    upper = (lax.axis_index("lat") & 1) != 0
    x_sides = lon_halo(edges_of(grid, x))
    x_sides, forward_weight, backward_weight, scale, shift, upper = lax.optimization_barrier(
        (x_sides, forward_weight, backward_weight, scale, shift, upper)
    )
    first_lat = jnp.logical_not(upper)
    def to_members(pieces):
        moved = [pieces[0]]
        for d in range(1, members):
            moved.append(lax.ppermute(pieces[d], "member", [(i, i ^ d) for i in range(members)]))
        return moved

    chunks, turn = chunks_of(grid, members)
    count = len(chunks)
    received, returned, targets, taken = [[None] * count for _ in range(4)]
    parts, edges = [[None] * count for _ in range(2)]

    def x_lat_halo(sides, first):
        return lat_halo(x[:, : grid.halo], x[:, cells - grid.halo :], sides, first)

    def send(i, field, load, halos, after):
        first, width = chunks[i]
        out = forward(
            grid, first, width, members, field, load, x_sides, *halos, forward_weight, shift,
            target, after,
        )
        targets[i], taken[i] = out[members : members + 2]
        received[i] = to_members(out[:members])
        return out[-1]

    def answer(i, after):
        grads = score(chunks[i][0], targets[i], scale, received[i], after)
        returned[i] = to_members(grads)
        return grads[0]

    def weigh(i, before, after, final):
        first, width = chunks[i]
        parts[i], edges[i], *sums = weight_part(
            grid, first, width, rows, taken[i], returned[i], before, after, final
        )
        return sums

    ranges = parts_of(grid, 4)
    grad_input, early = None, []
    if count == 1:
        send(0, x, True, x_lat_halo(x_sides, first_lat), [])
        answer(0, [])
        sums = weigh(0, None, [], True)
    else:
        a, b, c = turn
        held = send(a, x, True, (None, None), [])
        late_sides, late_first, targets[a] = lax.optimization_barrier(
            (x_sides, first_lat, targets[a])
        )
        halos = x_lat_halo(late_sides, late_first)
        send(b, held, False, halos, [])
        answer(a, [targets[b]])
        done = answer(b, [])
        send(c, held, False, halos, [done])
        sums = weigh(a, None, [targets[c]], False)
        done = answer(c, [edges[a]])
        sums = weigh(b, sums[0], [done], False)
        early_sides = lon_halo(edges[a] + edges[b])
        done_rows = min(sum(chunks[a]) // grid.columns, LAT_DEV)
        early = [(r0, r1) for r0, r1 in ranges if r0 > 0 and r1 < done_rows]
        for number, (r0, r1) in enumerate(early):
            grad_input = input_part(
                grid, r0, r1, chunks[:2], parts[:2], early_sides, None, None, backward_weight,
                grad_input, number > 0,
            )
            if number == 0:
                first_input = kept_in_hbm(grad_input)
        sums = weigh(c, sums[0], [first_input] if early else [], True)
    total, late_edges = sum_all(*sums, upper, edges[turn[-1]])
    g_sides = lon_halo(late_edges)
    if count > 1:
        g_sides = g_sides + early_sides
    end = cells - chunks[-1][0]
    g_top, g_bottom = lat_halo(
        parts[0][:, : grid.halo], parts[-1][:, end - grid.halo : end], g_sides, first_lat
    )
    for r0, r1 in ranges:
        if (r0, r1) in early:
            continue
        grad_input = input_part(
            grid, r0, r1, chunks, parts, g_sides, g_top, g_bottom, backward_weight, grad_input,
            True,
        )
    total = total / (cells * lax.axis_size("lat") * lax.axis_size("lon"))
    grad_weight = total[:fields, : 9 * channels].T.reshape(9, channels * fields)
    grad_bias = total[:fields, 9 * channels]
    return (grad_input.reshape(1, channels, 1, 1, cells), grad_weight, grad_bias)


def solution(mesh):
    placed = (P("member", None, "lat", "lon", None), P(), P(), P(None, "lat", "lon", None), P())
    return jax.shard_map(
        local,
        mesh=mesh,
        in_specs=placed,
        out_specs=(P("member", None, "lat", "lon", None), P(), P()),
        check_vma=False,
    )
```

```python
import functools

import jax
import jax.numpy as jnp
from jax import lax
from jax.experimental import pallas as pl
from jax.experimental.pallas import tpu as pltpu
from jax.sharding import PartitionSpec as P

LAT_DEV = 64
LANES = 128
ROW_GROUP = 2
FLAT_LANES = 1024
SLACK = 3 * 1024 * 1024
F32 = jnp.float32
BF16 = jnp.bfloat16


def round_up(value, step):
    return -(-value // step) * step


def params(*held):
    total = sum(round_up(rows, 16) * round_up(lanes, LANES) * size for rows, lanes, size in held)
    return pltpu.CompilerParams(vmem_limit_bytes=total + SLACK)


def kept_in_hbm(value):
    return pltpu.with_memory_space_constraint(value, pltpu.HBM)


def kept_in_vmem(value):
    return pltpu.with_memory_space_constraint(value, pltpu.VMEM)


def shape_of(dims, dtype=BF16):
    return jax.ShapeDtypeStruct(dims, dtype)


def cost(flops, moved):
    return pl.CostEstimate(flops=int(flops), bytes_accessed=int(moved), transcendentals=0)


def in_vmem():
    return pl.BlockSpec(memory_space=pltpu.VMEM)


def in_smem():
    return pl.BlockSpec(memory_space=pltpu.SMEM)


def in_hbm():
    return pl.BlockSpec(memory_space=pltpu.HBM)


def anywhere():
    return pl.BlockSpec(memory_space=pl.ANY)


def nt_dot(left, right):
    return lax.dot_general(left, right, (((1,), (1,)), ((), ())), preferred_element_type=F32)


class Grid:
    def __init__(self, cells, members):
        self.cells = cells
        self.columns = cells // LAT_DEV
        self.pitch = round_up(self.columns, LANES)
        self.halo = round_up(self.columns + 1, LANES)
        self.padded = round_up(cells, members * LANES)

    def rows(self, first, width):
        return first // self.columns, -(-min(first + width, self.cells) // self.columns)

    def layout(self, ranges):
        out, row, lane = [], 0, 0
        for first, width in ranges:
            r0, r1 = self.rows(first, width)
            out.append((first, width, r0, r1, row, lane))
            row, lane = row + r1 - r0 + 2, lane + width
        return out, row, lane


def take(ref, start, width):
    low = start // LANES * LANES
    off = start - low
    if off == 0:
        return ref[:, low : low + width]
    return ref[:, low : low + width + LANES][:, off : off + width]


def side_column(refs, grid, row, right):
    own, top, bottom = refs
    slot = LAT_DEV if right else 0
    if row < 0:
        ref, lane = top, grid.halo + slot + LAT_DEV - 1
    elif row >= LAT_DEV:
        ref, lane = bottom, grid.halo + slot
    else:
        ref, lane = own, slot + row
    return ref[:, lane : lane + 1].astype(F32)


def with_column(tile, column, lane):
    here = lax.broadcasted_iota(jnp.int32, tile.shape, 1).astype(BF16) == lane
    return jnp.where(here, jnp.broadcast_to(column, tile.shape).astype(BF16), tile)


def take_cells(sources, start, width):
    parts, at, end = [], start, start + width
    for ref, begin, last, lane in sorted(sources, key=lambda source: source[1]):
        shift = lane - begin
        base = (start + shift) // LANES * LANES
        if begin <= start and end <= last and base + width + LANES <= ref.shape[1]:
            return take(ref, start + shift, width)
        low, high = max(at, begin), min(end, last)
        if low < high:
            if low > at:
                parts.append(jnp.zeros((ref.shape[0], low - at), BF16))
            base = (low + shift) // LANES * LANES
            top = min(round_up(high + shift, LANES), ref.shape[1])
            parts.append(ref[:, base:top][:, low + shift - base : high + shift - base])
            at = high
    if at < end:
        parts.append(jnp.zeros((sources[0][0].shape[0], end - at), BF16))
    return jnp.concatenate(parts, axis=1) if len(parts) > 1 else parts[0]


def row_taps(grid, row, b, sources, top, bottom):
    shift = b - 1
    if row < 0 and top is not None:
        return take_cells([(top, 0, top.shape[1], 0)], grid.halo - grid.columns + shift, grid.pitch)
    if row >= LAT_DEV and bottom is not None:
        return take_cells([(bottom, 0, bottom.shape[1], 0)], shift, grid.pitch)
    return take_cells(sources, row * grid.columns + shift, grid.pitch)


def build_taps(grid, origin, low, high, sources, sides, taps, backwards=False):
    rows = sources[0][0].shape[0]
    own, top, bottom = sides
    for row in range(low, high):
        base = (row - origin) * grid.pitch
        for b in range(3):
            value = row_taps(grid, row, b, sources, top, bottom)
            block = pl.ds((2 - b if backwards else b) * rows, rows)
            if b == 1:
                taps[block, base : base + grid.pitch] = value
                continue
            at = grid.columns - 1 if b == 2 else 0
            tile = at // LANES * LANES
            column = side_column(sides, grid, row, b == 2)
            for lane in range(0, grid.pitch, LANES):
                part = value[:, lane : lane + LANES]
                if lane == tile:
                    part = with_column(part, column, at - tile)
                taps[block, base + lane : base + lane + LANES] = part


def stacked_rows(grid, taps, row, count, order=(0, 1, 2)):
    width = count * grid.pitch
    return jnp.concatenate(
        [taps[:, (row + a) * grid.pitch : (row + a) * grid.pitch + width] for a in order],
        axis=0,
    )


def groups_of(count, size=ROW_GROUP):
    return [(row, min(size, count - row)) for row in range(0, count, size)]


def flat_piece(grid, pitched, skip, low, high, count):
    parts, at = [], low
    while at < high:
        row, column = divmod(at + skip, grid.columns)
        if row >= count:
            parts.append(jnp.zeros((pitched.shape[0], high - at), BF16))
            break
        size = min(grid.columns - column, high - at)
        begin = row * grid.pitch + column
        parts.append(pitched[:, begin : begin + size])
        at += size
    return jnp.concatenate(parts, axis=1) if len(parts) > 1 else parts[0]


def convolve(grid, first, width, place, sources, sides, taps, weight, bias, pitched, flat,
             backwards=False, emit=None, fetch=None):
    r0, r1 = grid.rows(first, width)
    skip = first - r0 * grid.columns
    taps_row, lane = place
    built, done = r0 - 1, 0
    order = (2, 1, 0) if backwards else (0, 1, 2)
    for row, count in groups_of(r1 - r0):
        ready = min(r0 + row + count + 1 + ROW_GROUP, r1 + 1)
        if fetch is not None:
            fetch(ready)
        build_taps(
            grid, r0 - 1 - taps_row, built, ready, sources, sides, taps, backwards
        )
        built = ready
        stacked = stacked_rows(grid, taps, taps_row + row, count, order)
        value = jnp.dot(weight, stacked, preferred_element_type=F32)
        if bias is not None:
            value = value + bias
        pitched[:, row * grid.pitch : (row + count) * grid.pitch] = value.astype(BF16)
        last = row + count == r1 - r0
        while done < width:
            end = min(done + FLAT_LANES, width)
            if not last and end + skip > row * grid.columns:
                break
            piece = flat_piece(grid, pitched, skip, done, end, r1 - r0)
            flat[:, lane + done : lane + end] = piece
            if emit is not None:
                emit(done, end)
            done = end


def edges_kernel(grid, places, tiles, x_ref, out_ref, held, sem):
    copies = [
        pltpu.make_async_copy(
            x_ref.at[:, pl.ds(tile * LANES, LANES)],
            held.at[:, pl.ds(number * LANES, LANES)],
            sem.at[number],
        )
        for number, tile in enumerate(tiles)
    ]
    for copy in copies:
        copy.start()
    for copy in copies:
        copy.wait()
    columns = []
    for cell in places:
        at = tiles.index(cell // LANES) * LANES + cell % LANES
        columns.append(held[:, at : at + 1])
    out_ref[...] = jnp.concatenate(columns, axis=1)


def edges_of(grid, field):
    rows = field.shape[0]
    places = [i for i in range(0, grid.cells, grid.columns)]
    places += [i for i in range(grid.columns - 1, grid.cells, grid.columns)]
    tiles = sorted({cell // LANES for cell in places})
    return pl.pallas_call(
        functools.partial(edges_kernel, grid, places, tiles),
        in_specs=[in_hbm()],
        out_specs=in_vmem(),
        out_shape=shape_of((rows, 2 * LAT_DEV)),
        scratch_shapes=[
            pltpu.VMEM((rows, len(tiles) * LANES), BF16),
            pltpu.SemaphoreType.DMA((len(tiles),)),
        ],
        compiler_params=params((rows, (len(tiles) + 1) * LANES, 2)),
        cost_estimate=cost(rows, rows),
        name="edges",
    )(kept_in_hbm(field))


def lon_halo(edges):
    peers = lax.axis_size("lon")
    right = [(i, (i + 1) % peers) for i in range(peers)]
    left = [(j, i) for i, j in right]
    before = lax.ppermute(edges[:, LAT_DEV:], "lon", right)
    after = lax.ppermute(edges[:, :LAT_DEV], "lon", left)
    return jnp.concatenate([before, after], axis=1)


def lat_halo(first_rows, last_rows, sides, upper):
    peers = lax.axis_size("lat")
    if peers == 2:
        sent = jnp.concatenate([jnp.where(upper, last_rows, first_rows), sides], axis=1)
        other = lax.ppermute(sent, "lat", [(0, 1), (1, 0)])
        none = jnp.zeros_like(other)
        return jnp.where(upper, none, other), jnp.where(upper, other, none)
    up = [(i, i + 1) for i in range(peers - 1)]
    down = [(j, i) for i, j in up]
    top = lax.ppermute(jnp.concatenate([last_rows, sides], axis=1), "lat", up)
    bottom = lax.ppermute(jnp.concatenate([first_rows, sides], axis=1), "lat", down)
    return top, bottom


def stages_of(grid, ranges):
    stages, got = [], []
    for first, width in ranges:
        r0, r1 = grid.rows(first, width)
        low = max((r0 - 1) * grid.columns - 1, 0) // LANES * LANES
        high = min(round_up((r1 + 1) * grid.columns + 1, LANES), grid.cells)
        low = max([low] + [end for begin, end in got if begin <= low])
        step = round_up(max((high - low) // 3, LANES), LANES)
        stages += [(at, min(at + step, high)) for at in range(low, high, step)]
        got.append((low, high))
    at = 0
    for low, high in sorted(got) + [(grid.cells, grid.cells)]:
        if at < low:
            stages.append((at, low))
        at = max(at, high)
    return stages


def forward_kernel(grid, ranges, has_top, has_bottom, members, load, waits, *refs):
    refs = list(refs)
    x_ref, sides_ref = refs[:2]
    del refs[:2]
    top_ref = refs.pop(0) if has_top else None
    bottom_ref = refs.pop(0) if has_bottom else None
    weight_ref, bias_ref, analysis_ref = refs[:3]
    del refs[: 3 + waits]
    outs = refs[:members]
    target_ref, taps = refs[members : members + 2]
    pitched, pred, target_sem, load_sem = refs[-4:]
    me = lax.axis_index("member")
    places, _, width = grid.layout(ranges)
    piece = width // members
    pending = []
    if load:
        held = refs[members + 2]
        for begin, end in stages_of(grid, ranges):
            copies = []
            for low in range(0, x_ref.shape[0], 32):
                at = (pl.ds(low, min(32, x_ref.shape[0] - low)), pl.ds(begin, end - begin))
                sem = load_sem.at[len(pending), len(copies)]
                copies.append(pltpu.make_async_copy(x_ref.at[at], held.at[at], sem))
                copies[-1].start()
            pending.append((begin, end, copies))
        x_ref = held

    def fetch(low, high):
        for stage in list(pending):
            if stage[0] < high * grid.columns + 1 and stage[1] > low * grid.columns - 1:
                for copy in stage[2]:
                    copy.wait()
                pending.remove(stage)

    each = members // len(ranges)
    index = me // each
    begin = places[0][0] + me * piece
    if len(ranges) > 1:
        begin = jnp.where(index == 0, begin, places[1][0] + (me - each) * piece)
    begin = pl.multiple_of(begin, LANES)
    target_copy = pltpu.make_async_copy(
        analysis_ref.at[:, pl.ds(begin, piece)], target_ref, target_sem.at[0]
    )
    target_copy.start()
    sides = (sides_ref, top_ref, bottom_ref)
    weight, bias = weight_ref[...], bias_ref[...]
    for first, size, r0, r1, row, lane in places:
        convolve(
            grid, first, size, (row, lane), [(x_ref, 0, grid.cells, 0)], sides, taps, weight,
            bias, pitched, pred, fetch=lambda ready, r0=r0: fetch(r0 - 1, ready),
        )
    for d in range(members):
        begin = pl.multiple_of((me ^ d) * piece, LANES)
        outs[d][...] = pred[:, pl.ds(begin, piece)]
    target_copy.wait()
    fetch(0, LAT_DEV)


def forward(
    grid, ranges, members, x, load, sides, top, bottom, weight, bias, analysis, after
):
    channels = x.shape[0]
    fields = weight.shape[0]
    places, tap_rows, width = grid.layout(ranges)
    most = max(place[3] - place[2] for place in places)
    has_top = any(place[2] == 0 for place in places)
    has_bottom = any(place[3] == LAT_DEV for place in places)
    piece = width // members
    held = (3 * channels, tap_rows * grid.pitch)
    operands = [kept_in_hbm(x) if load else kept_in_vmem(x), sides]
    if has_top:
        operands.append(top)
    if has_bottom:
        operands.append(bottom)
    operands += [weight, bias]
    specs = [in_hbm() if load else in_vmem()] + [in_vmem()] * (len(operands) - 1) + [in_hbm()]
    operands += [kept_in_hbm(analysis), *after]
    specs += [anywhere()] * len(after)
    shapes = [shape_of((fields, piece))] * (members + 1) + [pltpu.VMEM(held, BF16)]
    if load:
        shapes.append(pltpu.VMEM((channels, grid.cells), BF16))
    return pl.pallas_call(
        functools.partial(
            forward_kernel, grid, ranges, has_top, has_bottom, members, load, len(after)
        ),
        in_specs=specs,
        out_specs=[in_vmem()] * len(shapes),
        out_shape=shapes,
        scratch_shapes=[
            pltpu.VMEM((fields, most * grid.pitch), BF16),
            pltpu.VMEM((fields, width), BF16),
            pltpu.SemaphoreType.DMA((1,)),
            pltpu.SemaphoreType.DMA((12, -(-channels // 32))),
        ],
        compiler_params=params(
            (2 * fields, most * grid.pitch, 2),
            (2 * fields, 2 * width, 2),
            (fields, 9 * channels, 2),
        ),
        cost_estimate=cost(81 * channels * fields * width, 0),
        name=f"forward_{ranges[0][0]}",
    )(*operands)


def slope(values):
    return values * lax.rsqrt(values * values + 1.0)


def score_kernel(members, target_ref, scale_ref, *refs):
    pieces = refs[:members]
    outs = refs[-members:]
    fields, piece = pieces[0].shape
    tiles = piece // LANES
    several = max(k for k in (1, 2, 3) if tiles % k == 0)

    def tile(index, carry):
        for part in range(several * -(-fields // 16)):
            low = part // several * 16
            at = (index * several + part % several) * LANES
            span = pl.ds(pl.multiple_of(at, LANES), LANES)
            rows = pl.ds(low, min(16, fields - low))
            values = [ref[rows, span].astype(F32) for ref in pieces]
            target = target_ref[rows, span].astype(F32)
            scale = scale_ref[rows, :]
            sums = [None] * members
            for i in range(members):
                for j in range(i + 1, members):
                    both = slope(values[i] - values[j])
                    sums[i] = both if sums[i] is None else sums[i] + both
                    sums[j] = -both if sums[j] is None else sums[j] - both
            for i in range(members):
                grad = slope(values[i] - target) * (1.0 / members) - sums[i] * (
                    1.0 / (members * (members - 1))
                )
                outs[i][rows, span] = (scale * grad).astype(BF16)
        return carry

    lax.fori_loop(0, tiles // several, tile, 0)


def score(first, target, scale, pieces, after):
    members = len(pieces)
    fields, piece = pieces[0].shape
    return pl.pallas_call(
        functools.partial(score_kernel, members),
        in_specs=[in_vmem()] * (2 + members) + [anywhere()] * len(after),
        out_specs=[in_vmem()] * members,
        out_shape=[shape_of((fields, piece))] * members,
        compiler_params=params((9 * round_up(fields, 16), piece, 2), (fields, LANES, 4)),
        cost_estimate=cost(13000 * fields * piece, 0),
        name=f"score_{first}",
    )(target, scale, *pieces, *after)


def weight_kernel(grid, ranges, members, chained, waits, halves, taps, *refs):
    me = lax.axis_index("member")
    pieces = refs[:members]
    before_ref = refs[members] if chained else None
    refs = refs[members + chained + waits :]
    out_ref, edge_ref = refs[:2]
    flat, pitched = refs[-2:]
    sum_ref = refs[-3]
    fields, piece = pieces[0].shape
    rows = out_ref.shape[0]
    places, _, _ = grid.layout(ranges)
    lead = grid.halo + 2 * LANES
    each = members // len(ranges)
    spots = [lead + lane + number * lead for number, (*_, lane) in enumerate(places)]
    at = 0
    for spot, (_, width, *_) in zip(spots, places):
        flat[:, at:spot] = jnp.zeros((rows, spot - at), BF16)
        at = spot + width
    flat[:, at:] = jnp.zeros((rows, flat.shape[1] - at), BF16)
    base = fields // 16 * 16
    if base < rows:
        for spot, (_, width, *_) in zip(spots, places):
            flat[pl.ds(base, rows - base), spot : spot + width] = jnp.zeros(
                (rows - base, width), BF16
            )
    for d in range(members):
        owner = me ^ d
        begin = pl.multiple_of(lead + owner * piece + owner // each * lead, LANES)
        value = pieces[d][...]
        if grid.padded != grid.cells:
            cell = lax.broadcasted_iota(jnp.int32, (1, piece), 1) + owner * piece
            value = jnp.where(cell < grid.cells, value.astype(F32), 0.0).astype(BF16)
        flat[pl.ds(0, fields), pl.ds(begin, piece)] = value
    for spot, (_, width, *_, lane) in zip(spots, places):
        out_ref[:, lane : lane + width] = flat[:, spot : spot + width]
    columns = []
    for side in (0, grid.columns - 1):
        for row in range(LAT_DEV):
            cell = row * grid.columns + side
            for spot, (first, width, *_) in zip(spots, places):
                if first <= cell < first + width:
                    at = spot + cell - first
                    columns.append(flat[:, at : at + 1])
                    break
            else:
                columns.append(jnp.zeros((rows, 1), BF16))
    edge_ref[...] = jnp.concatenate(columns, axis=1)
    keep = jnp.where(
        lax.broadcasted_iota(jnp.int32, (1, LANES), 1) < grid.columns % LANES, 1.0, 0.0
    ).astype(BF16)
    started = False
    for spot, (first, _, r0, r1, taps_row, _) in zip(spots, places):
        for row, count in groups_of(r1 - r0, 2 * ROW_GROUP):
            for at in range(row, row + count):
                value = take(flat, spot + (r0 + at) * grid.columns - first, grid.pitch)
                to = at * grid.pitch
                for lane in range(0, grid.pitch, LANES):
                    part = value[:, lane : lane + LANES]
                    if lane + LANES > grid.columns:
                        part = part * keep
                    pitched[:, to + lane : to + lane + LANES] = part
            stacked = stacked_rows(grid, taps, taps_row + row, count)
            ones = jnp.ones((sum_ref.shape[1] - stacked.shape[0], stacked.shape[1]), BF16)
            part = nt_dot(
                pitched[:, row * grid.pitch : (row + count) * grid.pitch],
                jnp.concatenate([stacked, ones], axis=0),
            )
            if started:
                sum_ref[...] += part
            else:
                sum_ref[...] = part + before_ref[...] if chained else part
            started = True
    if halves:
        keep_ref, send_ref = refs[2:4]
        half = rows // 2
        upper = lax.axis_index("lat") & 1
        keep_ref[...] = sum_ref[pl.ds(pl.multiple_of(upper * half, 8), half), :]
        send_ref[...] = sum_ref[pl.ds(pl.multiple_of((1 - upper) * half, 8), half), :]


def weight_part(grid, ranges, rows, taps, pieces, before, after, halves):
    members = len(pieces)
    channels = taps.shape[0] // 3
    places, _, width = grid.layout(ranges)
    most = max(place[3] - place[2] for place in places)
    room = width + (len(ranges) + 1) * (grid.halo + 2 * LANES)
    sums = round_up(9 * channels + 1, members * LANES)
    chained = [] if before is None else [before]
    shapes = [shape_of((rows, width)), shape_of((rows, 2 * LAT_DEV))]
    whole = []
    if halves:
        shapes += [shape_of((rows // 2, sums), F32)] * 2
        whole = [pltpu.VMEM((rows, sums), F32)]
    else:
        shapes += [shape_of((rows, sums), F32)]
    return pl.pallas_call(
        functools.partial(
            weight_kernel, grid, ranges, members, len(chained), len(after), halves
        ),
        in_specs=[in_vmem()] * (1 + members + len(chained)) + [anywhere()] * len(after),
        out_specs=[in_vmem()] * len(shapes),
        out_shape=shapes,
        scratch_shapes=whole
        + [pltpu.VMEM((rows, room), BF16), pltpu.VMEM((rows, most * grid.pitch), BF16)],
        compiler_params=params(
            (rows, room + 2 * width, 2),
            (rows, most * grid.pitch, 2),
            (rows, 3 * sums, 4),
        ),
        cost_estimate=cost(width, 0),
        name=f"weight_{ranges[0][0]}",
    )(kept_in_vmem(taps), *pieces, *chained, *after)


def input_kernel(grid, r0, r1, chunks, aliased, *refs):
    refs = list(refs)
    parts = refs[: len(chunks)]
    del refs[: len(chunks)]
    sides_ref, weight_ref = refs[:2]
    del refs[:2]
    top_ref = refs.pop(0) if r0 == 0 else None
    bottom_ref = refs.pop(0) if r1 == LAT_DEV else None
    del refs[:aliased]
    out_ref, taps, pitched, flat, out_sem = refs
    sources = []
    for ref, ranges in zip(parts, chunks):
        for first, width, *_, lane in grid.layout(ranges)[0]:
            sources.append((ref, first, min(first + width, grid.cells), lane))
    sides = (sides_ref, top_ref, bottom_ref)
    copies = []

    def emit(low, high):
        at = r0 * grid.columns + low
        copies.append(
            pltpu.make_async_copy(
                flat.at[:, pl.ds(low, high - low)],
                out_ref.at[:, pl.ds(at, high - low)],
                out_sem.at[len(copies)],
            )
        )
        copies[-1].start()

    width = (r1 - r0) * grid.columns
    convolve(
        grid, r0 * grid.columns, width, (0, 0), sources, sides, taps, weight_ref[...], None,
        pitched, flat, backwards=True, emit=emit,
    )
    for copy in copies:
        copy.wait()


def input_part(grid, r0, r1, chunks, parts, sides, top, bottom, weight, before, slow):
    rows = parts[0].shape[0]
    channels = weight.shape[0]
    width = (r1 - r0) * grid.columns
    held = (3 * rows, (r1 - r0 + 2) * grid.pitch)
    begin, end = (r0 - 1) * grid.columns - 1, (r1 + 1) * grid.columns + 1
    near = [
        (ranges, part)
        for ranges, part in zip(chunks, parts)
        if any(first < end and first + size > begin for first, size in ranges)
    ]
    chunks, parts = [pair[0] for pair in near], [pair[1] for pair in near]
    operands = [*parts, sides, weight] + [top] * (r0 == 0) + [bottom] * (r1 == LAT_DEV)
    specs = [in_vmem()] * len(operands)
    alias = {}
    if before is not None:
        alias = {len(operands): 0}
        operands.append(before)
        specs.append(anywhere())
    return pl.pallas_call(
        functools.partial(input_kernel, grid, r0, r1, chunks, len(alias)),
        in_specs=specs,
        out_specs=anywhere(),
        out_shape=shape_of((channels, grid.cells)),
        input_output_aliases=alias,
        scratch_shapes=[
            pltpu.VMEM(held, BF16),
            pltpu.VMEM((channels, (r1 - r0) * grid.pitch), BF16),
            pltpu.VMEM((channels, width), BF16),
            pltpu.SemaphoreType.DMA((-(-width // FLAT_LANES),)),
        ],
        compiler_params=params(
            (rows, sum(part.shape[1] for part in parts), 2),
            (*held, 2),
            (2 * channels, (r1 - r0) * grid.pitch, 2),
            (channels, 9 * rows, 2),
        ),
        cost_estimate=cost((80 if slow else 1) * channels * rows * width, width),
        name=f"input_{r0}",
    )(*operands)


def split_kernel(members, count, *refs):
    me = lax.axis_index("member")
    lanes = refs[count].shape[1]
    for d in range(members):
        span = pl.ds(pl.multiple_of((me ^ d) * lanes, LANES), lanes)
        total = refs[0][:, span]
        for ref in refs[1:count]:
            total += ref[:, span]
        refs[count + d][...] = total


def split_by_member(values, members):
    rows, lanes = values[0].shape
    return pl.pallas_call(
        functools.partial(split_kernel, members, len(values)),
        in_specs=[in_vmem()] * len(values),
        out_specs=[in_vmem()] * members,
        out_shape=[shape_of((rows, lanes // members), F32)] * members,
        compiler_params=params((rows, 3 * lanes, 4)),
        cost_estimate=cost(rows * lanes, 12 * rows * lanes),
        name="split",
    )(*values)


def join_kernel(members, *refs):
    me = lax.axis_index("member")
    lanes = refs[0].shape[1]
    for d in range(members):
        span = pl.ds(pl.multiple_of((me ^ d) * lanes, LANES), lanes)
        refs[members][:, span] = refs[d][...]


def join_members(pieces):
    members = len(pieces)
    rows, lanes = pieces[0].shape
    return pl.pallas_call(
        functools.partial(join_kernel, members),
        in_specs=[in_vmem()] * members,
        out_specs=in_vmem(),
        out_shape=shape_of((rows, members * lanes), F32),
        compiler_params=params((rows, 2 * members * lanes, 4)),
        cost_estimate=cost(rows * lanes, 12 * rows * lanes),
        name="join",
    )(*pieces)


def swap(value, axis, bits):
    return lax.ppermute(value, axis, [(i, i ^ bits) for i in range(lax.axis_size(axis))])


def sum_axis(value, axis, bit):
    size = lax.axis_size(axis)
    while bit < size:
        if 2 * bit < size:
            near, far, both = [swap(value, axis, k * bit) for k in (1, 2, 3)]
            value = (value + near) + (far + both)
        else:
            value = value + swap(value, axis, bit)
        bit *= 4
    return value


def sum_all(keep, send, upper, late):
    members = lax.axis_size("member")
    other = swap(send, "lat", 1)
    values = [keep, other]
    if lax.axis_size("lat") > 2:
        values = [sum_axis(keep + other, "lat", 2)]
    pieces = split_by_member(values, members)
    moved = [swap(pieces[d], "member", d) for d in range(1, members)]
    value = functools.reduce(jnp.add, moved, pieces[0])
    value, late = lax.optimization_barrier((value, late))
    value = sum_axis(value, "lon", 1)
    half = join_members([value] + [swap(value, "member", d) for d in range(1, members)])
    other = swap(half, "lat", 1)
    total = jnp.where(
        upper,
        jnp.concatenate([other, half], axis=0),
        jnp.concatenate([half, other], axis=0),
    )
    return total, late


def weights_kernel(taps_ref, forward_ref, backward_ref):
    count, channels, fields = taps_ref.shape
    rows = backward_ref.shape[1] // count
    taps = [taps_ref[t] for t in range(count)]
    forward_ref[...] = jnp.concatenate(
        [tap.astype(F32).T for tap in taps], axis=1
    ).astype(BF16)
    none = [jnp.zeros((channels, rows - fields), BF16)] * (rows > fields)
    backward_ref[...] = jnp.concatenate([part for tap in taps for part in (tap, *none)], axis=1)


def prepare_weights(taps, rows):
    count, channels, fields = taps.shape
    return pl.pallas_call(
        weights_kernel,
        in_specs=[in_vmem()],
        out_specs=[in_vmem()] * 2,
        out_shape=[shape_of((fields, count * channels)), shape_of((channels, count * rows))],
        compiler_params=params((4 * channels, count * LANES, 4)),
        cost_estimate=cost(channels, 8 * count * channels * rows),
        name="weights",
    )(taps)


def chunks_of(grid, members):
    unit = members * LANES
    units = grid.padded // unit
    if units < 15 or grid.padded != grid.cells or members % 2:
        return [[(0, grid.padded)]]
    outer = (units // 2 + 2) // 2 * unit
    return [
        [(0, outer), (grid.cells - outer, outer)],
        [(outer, grid.cells - 2 * outer)],
    ]


def parts_of(grid, wanted):
    step = LAT_DEV // wanted
    if step * grid.columns % LANES:
        return [(0, LAT_DEV)]
    ranges = [(row, row + step) for row in range(0, LAT_DEV, step)]
    return ranges[1:-1] + [ranges[0], ranges[-1]]


def local(inputs, weight, bias, analysis, field_weight):
    channels, cells = inputs.shape[1], inputs.shape[4]
    fields = analysis.shape[0]
    members = lax.axis_size("member")
    grid = Grid(cells, members)
    x = inputs.reshape(channels, cells)
    target = analysis.reshape(fields, cells)
    if grid.padded != cells:
        target = jnp.pad(target, ((0, 0), (0, grid.padded - cells)))
    rows = round_up(fields, 16)
    taps = weight.reshape(9, channels, fields)
    forward_weight, backward_weight = prepare_weights(taps, rows)
    scale = jnp.broadcast_to(field_weight[:, None], (fields, LANES))
    shift = bias[:, None]
    upper = (lax.axis_index("lat") & 1) != 0
    x_sides = lon_halo(edges_of(grid, x))
    x_sides, forward_weight, backward_weight, scale, shift, upper = lax.optimization_barrier(
        (x_sides, forward_weight, backward_weight, scale, shift, upper)
    )
    first_lat = jnp.logical_not(upper)
    def to_members(pieces):
        moved = {0: pieces[0]}
        for d in range(members - 1, 0, -1):
            moved[d] = swap(pieces[d], "member", d)
        return [moved[d] for d in range(members)]

    chunks = chunks_of(grid, members)
    x_top, x_bottom = lat_halo(
        x[:, : grid.halo], x[:, cells - grid.halo :], x_sides, first_lat
    )
    received, targets, taken, held = [], [], [], None
    for ranges in chunks:
        out = forward(
            grid, ranges, members, x if held is None else held, held is None, x_sides, x_top,
            x_bottom, forward_weight, shift, target, [],
        )
        targets.append(out[members])
        taken.append(out[members + 1])
        held = out[members + 2] if held is None else held
        received.append(to_members(out[:members]))
    returned = []
    for ranges, pieces, goal in zip(chunks, received, targets):
        grads = score(ranges[0][0], goal, scale, pieces, targets[-1:])
        returned.append(to_members(grads))

    blocks = parts_of(grid, 4)
    parts, edges, sums, grad_input = [], [], [None], None
    for number, ranges in enumerate(chunks):
        final = number == len(chunks) - 1
        after = [returned[-1][0]] if grad_input is None else [kept_in_hbm(grad_input)]
        part, edge, *sums = weight_part(
            grid, ranges, rows, taken[number], returned[number], sums[0], after, final
        )
        parts.append(part)
        edges.append(edge)
        if number == 0:
            end = part.shape[1] - grid.padded + cells
            outer_rows = (part[:, : grid.halo], part[:, end - grid.halo : end])
        if final:
            break
        g_sides = lon_halo(edge)
        g_top, g_bottom = lat_halo(*outer_rows, g_sides, first_lat)
        for r0, r1 in (blocks[-2], blocks[-1]):
            grad_input = input_part(
                grid, r0, r1, chunks[:1], parts[:1], g_sides, g_top, g_bottom, backward_weight,
                grad_input, False,
            )
        blocks = blocks[:-2]
    total, late_edges = sum_all(*sums, upper, edges[-1])
    late_sides = lon_halo(late_edges)
    if len(chunks) == 1:
        g_top, g_bottom = lat_halo(*outer_rows, late_sides, first_lat)
    else:
        late_sides = late_sides + g_sides
    for r0, r1 in blocks:
        grad_input = input_part(
            grid, r0, r1, chunks, parts, late_sides, g_top, g_bottom, backward_weight,
            grad_input, True,
        )
    total = total / (cells * lax.axis_size("lat") * lax.axis_size("lon"))
    grad_weight = total[:fields, : 9 * channels].T.reshape(9, channels * fields)
    grad_bias = total[:fields, 9 * channels]
    return (grad_input.reshape(1, channels, 1, 1, cells), grad_weight, grad_bias)


def solution(mesh):
    placed = (P("member", None, "lat", "lon", None), P(), P(), P(None, "lat", "lon", None), P())
    return jax.shard_map(
        local,
        mesh=mesh,
        in_specs=placed,
        out_specs=(P("member", None, "lat", "lon", None), P(), P()),
        check_vma=False,
    )
```

```python
import functools

import jax
import jax.numpy as jnp
from jax import lax
from jax.experimental import pallas as pl
from jax.experimental.pallas import tpu as pltpu
from jax.sharding import PartitionSpec as P

LAT_DEV = 64
LANES = 128
ROW_GROUP = 2
FLAT_LANES = 1024
SLACK = 3 * 1024 * 1024
F32 = jnp.float32
BF16 = jnp.bfloat16


def round_up(value, step):
    return -(-value // step) * step


def params(*held):
    total = sum(round_up(rows, 16) * round_up(lanes, LANES) * size for rows, lanes, size in held)
    return pltpu.CompilerParams(vmem_limit_bytes=total + SLACK)


def kept_in_hbm(value):
    return pltpu.with_memory_space_constraint(value, pltpu.HBM)


def kept_in_vmem(value):
    return pltpu.with_memory_space_constraint(value, pltpu.VMEM)


def shape_of(dims, dtype=BF16):
    return jax.ShapeDtypeStruct(dims, dtype)


def cost(flops, moved):
    return pl.CostEstimate(flops=int(flops), bytes_accessed=int(moved), transcendentals=0)


def in_vmem():
    return pl.BlockSpec(memory_space=pltpu.VMEM)


def in_smem():
    return pl.BlockSpec(memory_space=pltpu.SMEM)


def in_hbm():
    return pl.BlockSpec(memory_space=pltpu.HBM)


def anywhere():
    return pl.BlockSpec(memory_space=pl.ANY)


def nt_dot(left, right):
    return lax.dot_general(left, right, (((1,), (1,)), ((), ())), preferred_element_type=F32)


class Grid:
    def __init__(self, cells, members):
        self.cells = cells
        self.columns = cells // LAT_DEV
        self.pitch = round_up(self.columns, LANES)
        self.halo = round_up(self.columns + 1, LANES)
        self.padded = round_up(cells, members * LANES)

    def rows(self, first, width):
        return first // self.columns, -(-min(first + width, self.cells) // self.columns)

    def layout(self, ranges):
        out, row, lane = [], 0, 0
        for first, width in ranges:
            r0, r1 = self.rows(first, width)
            out.append((first, width, r0, r1, row, lane))
            row, lane = row + r1 - r0 + 2, lane + width
        return out, row, lane


def take(ref, start, width):
    low = start // LANES * LANES
    off = start - low
    if off == 0:
        return ref[:, low : low + width]
    return ref[:, low : low + width + LANES][:, off : off + width]


def side_column(refs, grid, row, right):
    own, top, bottom = refs
    slot = LAT_DEV if right else 0
    if row < 0:
        ref, lane = top, grid.halo + slot + LAT_DEV - 1
    elif row >= LAT_DEV:
        ref, lane = bottom, grid.halo + slot
    else:
        ref, lane = own, slot + row
    return ref[:, lane : lane + 1].astype(F32)


def with_column(tile, column, lane):
    here = lax.broadcasted_iota(jnp.int32, tile.shape, 1).astype(BF16) == lane
    return jnp.where(here, jnp.broadcast_to(column, tile.shape).astype(BF16), tile)


def take_cells(sources, start, width):
    parts, at, end = [], start, start + width
    for ref, begin, last, lane in sorted(sources, key=lambda source: source[1]):
        shift = lane - begin
        base = (start + shift) // LANES * LANES
        if begin <= start and end <= last and base + width + LANES <= ref.shape[1]:
            return take(ref, start + shift, width)
        low, high = max(at, begin), min(end, last)
        if low < high:
            if low > at:
                parts.append(jnp.zeros((ref.shape[0], low - at), BF16))
            base = (low + shift) // LANES * LANES
            top = min(round_up(high + shift, LANES), ref.shape[1])
            parts.append(ref[:, base:top][:, low + shift - base : high + shift - base])
            at = high
    if at < end:
        parts.append(jnp.zeros((sources[0][0].shape[0], end - at), BF16))
    return jnp.concatenate(parts, axis=1) if len(parts) > 1 else parts[0]


def row_taps(grid, row, b, sources, top, bottom):
    shift = b - 1
    if row < 0 and top is not None:
        return take_cells([(top, 0, top.shape[1], 0)], grid.halo - grid.columns + shift, grid.pitch)
    if row >= LAT_DEV and bottom is not None:
        return take_cells([(bottom, 0, bottom.shape[1], 0)], shift, grid.pitch)
    return take_cells(sources, row * grid.columns + shift, grid.pitch)


def build_taps(grid, origin, low, high, sources, sides, taps, backwards=False):
    rows = sources[0][0].shape[0]
    own, top, bottom = sides
    for row in range(low, high):
        base = (row - origin) * grid.pitch
        for b in range(3):
            value = row_taps(grid, row, b, sources, top, bottom)
            block = pl.ds((2 - b if backwards else b) * rows, rows)
            if b == 1:
                taps[block, base : base + grid.pitch] = value
                continue
            at = grid.columns - 1 if b == 2 else 0
            tile = at // LANES * LANES
            column = side_column(sides, grid, row, b == 2)
            for lane in range(0, grid.pitch, LANES):
                part = value[:, lane : lane + LANES]
                if lane == tile:
                    part = with_column(part, column, at - tile)
                taps[block, base + lane : base + lane + LANES] = part


def stacked_rows(grid, taps, row, count, order=(0, 1, 2)):
    width = count * grid.pitch
    return jnp.concatenate(
        [taps[:, (row + a) * grid.pitch : (row + a) * grid.pitch + width] for a in order],
        axis=0,
    )


def groups_of(count, size=ROW_GROUP):
    return [(row, min(size, count - row)) for row in range(0, count, size)]


def flat_piece(grid, pitched, skip, low, high, count):
    parts, at = [], low
    while at < high:
        row, column = divmod(at + skip, grid.columns)
        if row >= count:
            parts.append(jnp.zeros((pitched.shape[0], high - at), BF16))
            break
        size = min(grid.columns - column, high - at)
        begin = row * grid.pitch + column
        parts.append(pitched[:, begin : begin + size])
        at += size
    return jnp.concatenate(parts, axis=1) if len(parts) > 1 else parts[0]


def convolve(grid, first, width, place, sources, sides, taps, weight, bias, pitched, flat,
             backwards=False, emit=None, fetch=None):
    r0, r1 = grid.rows(first, width)
    skip = first - r0 * grid.columns
    taps_row, lane = place
    built, done = r0 - 1, 0
    order = (2, 1, 0) if backwards else (0, 1, 2)
    for row, count in groups_of(r1 - r0):
        ready = min(r0 + row + count + 1 + ROW_GROUP, r1 + 1)
        if fetch is not None:
            fetch(ready)
        build_taps(
            grid, r0 - 1 - taps_row, built, ready, sources, sides, taps, backwards
        )
        built = ready
        stacked = stacked_rows(grid, taps, taps_row + row, count, order)
        value = jnp.dot(weight, stacked, preferred_element_type=F32)
        if bias is not None:
            value = value + bias
        pitched[:, row * grid.pitch : (row + count) * grid.pitch] = value.astype(BF16)
        last = row + count == r1 - r0
        while done < width:
            end = min(done + FLAT_LANES, width)
            if not last and end + skip > row * grid.columns:
                break
            piece = flat_piece(grid, pitched, skip, done, end, r1 - r0)
            flat[:, lane + done : lane + end] = piece
            if emit is not None:
                emit(done, end)
            done = end


def edges_kernel(grid, places, tiles, x_ref, out_ref, row_ref, held, sem, row_sem):
    last = jnp.where(lax.axis_index("lat") == 0, (grid.cells - grid.halo) // LANES, 0)
    row_copy = pltpu.make_async_copy(
        x_ref.at[:, pl.ds(pl.multiple_of(last * LANES, LANES), grid.halo)],
        row_ref,
        row_sem.at[0],
    )
    row_copy.start()
    copies = [
        pltpu.make_async_copy(
            x_ref.at[:, pl.ds(tile * LANES, LANES)],
            held.at[:, pl.ds(number * LANES, LANES)],
            sem.at[number],
        )
        for number, tile in enumerate(tiles)
    ]
    for copy in copies:
        copy.start()
    for copy in copies:
        copy.wait()
    columns = []
    for cell in places:
        at = tiles.index(cell // LANES) * LANES + cell % LANES
        columns.append(held[:, at : at + 1])
    out_ref[...] = jnp.concatenate(columns, axis=1)
    row_copy.wait()


def edges_of(grid, field):
    rows = field.shape[0]
    places = [i for i in range(0, grid.cells, grid.columns)]
    places += [i for i in range(grid.columns - 1, grid.cells, grid.columns)]
    tiles = sorted({cell // LANES for cell in places})
    return pl.pallas_call(
        functools.partial(edges_kernel, grid, places, tiles),
        in_specs=[in_hbm()],
        out_specs=[in_vmem()] * 2,
        out_shape=[shape_of((rows, 2 * LAT_DEV)), shape_of((rows, grid.halo))],
        scratch_shapes=[
            pltpu.VMEM((rows, len(tiles) * LANES), BF16),
            pltpu.SemaphoreType.DMA((len(tiles),)),
            pltpu.SemaphoreType.DMA((1,)),
        ],
        compiler_params=params((rows, (len(tiles) + 1) * LANES + grid.halo, 2)),
        cost_estimate=cost(rows, rows),
        name="edges",
    )(kept_in_hbm(field))


def lon_halo(edges, odd):
    peers = lax.axis_size("lon")
    first, last = edges[:, :LAT_DEV], edges[:, LAT_DEV:]
    if peers % 2:
        right = [(i, (i + 1) % peers) for i in range(peers)]
        left = [(j, i) for i, j in right]
        before, after = lax.ppermute(last, "lon", right), lax.ppermute(first, "lon", left)
        return jnp.concatenate([before, after], axis=1)
    near = [(i, i ^ 1) for i in range(peers)]
    far = [(i, (i + 1 if i % 2 else i - 1) % peers) for i in range(peers)]
    inner = lax.ppermute(jnp.where(odd, first, last), "lon", near)
    outer = lax.ppermute(jnp.where(odd, last, first), "lon", far)
    return jnp.where(
        odd,
        jnp.concatenate([inner, outer], axis=1),
        jnp.concatenate([outer, inner], axis=1),
    )


def lat_halo(first_rows, last_rows, sides, upper, chosen=None):
    peers = lax.axis_size("lat")
    if peers == 2:
        if chosen is None:
            chosen = jnp.where(upper, last_rows, first_rows)
        sent = jnp.concatenate([chosen, sides], axis=1)
        other = lax.ppermute(sent, "lat", [(0, 1), (1, 0)])
        none = jnp.zeros_like(other)
        return jnp.where(upper, none, other), jnp.where(upper, other, none)
    up = [(i, i + 1) for i in range(peers - 1)]
    down = [(j, i) for i, j in up]
    top = lax.ppermute(jnp.concatenate([last_rows, sides], axis=1), "lat", up)
    bottom = lax.ppermute(jnp.concatenate([first_rows, sides], axis=1), "lat", down)
    return top, bottom


def stages_of(grid, ranges):
    stages, got = [], []
    for first, width in ranges:
        r0, r1 = grid.rows(first, width)
        low = max((r0 - 1) * grid.columns - 1, 0) // LANES * LANES
        high = min(round_up((r1 + 1) * grid.columns + 1, LANES), grid.cells)
        low = max([low] + [end for begin, end in got if begin <= low])
        step = round_up(max((high - low) // 3, LANES), LANES)
        stages += [(at, min(at + step, high)) for at in range(low, high, step)]
        got.append((low, high))
    at = 0
    for low, high in sorted(got) + [(grid.cells, grid.cells)]:
        if at < low:
            stages.append((at, low))
        at = max(at, high)
    return stages


def forward_kernel(grid, ranges, has_top, has_bottom, members, load, waits, *refs):
    refs = list(refs)
    x_ref, sides_ref = refs[:2]
    del refs[:2]
    top_ref = refs.pop(0) if has_top else None
    bottom_ref = refs.pop(0) if has_bottom else None
    weight_ref, bias_ref, analysis_ref = refs[:3]
    del refs[: 3 + waits]
    outs = refs[:members]
    target_ref, taps = refs[members : members + 2]
    pitched, pred, target_sem, load_sem = refs[-4:]
    me = lax.axis_index("member")
    places, _, width = grid.layout(ranges)
    piece = width // members
    pending = []
    if load:
        held = refs[members + 2]
        for begin, end in stages_of(grid, ranges):
            copies = []
            for low in range(0, x_ref.shape[0], 32):
                at = (pl.ds(low, min(32, x_ref.shape[0] - low)), pl.ds(begin, end - begin))
                sem = load_sem.at[len(pending), len(copies)]
                copies.append(pltpu.make_async_copy(x_ref.at[at], held.at[at], sem))
                copies[-1].start()
            pending.append((begin, end, copies))
        x_ref = held

    def fetch(low, high):
        for stage in list(pending):
            if stage[0] < high * grid.columns + 1 and stage[1] > low * grid.columns - 1:
                for copy in stage[2]:
                    copy.wait()
                pending.remove(stage)

    each = members // len(ranges)
    index = me // each
    begin = places[0][0] + me * piece
    if len(ranges) > 1:
        begin = jnp.where(index == 0, begin, places[1][0] + (me - each) * piece)
    begin = pl.multiple_of(begin, LANES)
    target_copy = pltpu.make_async_copy(
        analysis_ref.at[:, pl.ds(begin, piece)], target_ref, target_sem.at[0]
    )
    target_copy.start()
    sides = (sides_ref, top_ref, bottom_ref)
    weight, bias = weight_ref[...], bias_ref[...]
    for first, size, r0, r1, row, lane in places:
        convolve(
            grid, first, size, (row, lane), [(x_ref, 0, grid.cells, 0)], sides, taps, weight,
            bias, pitched, pred, fetch=lambda ready, r0=r0: fetch(r0 - 1, ready),
        )
    for d in range(members):
        begin = pl.multiple_of((me ^ d) * piece, LANES)
        outs[d][...] = pred[:, pl.ds(begin, piece)]
    target_copy.wait()
    fetch(0, LAT_DEV)


def forward(
    grid, ranges, members, x, load, sides, top, bottom, weight, bias, analysis, after
):
    channels = x.shape[0]
    fields = weight.shape[0]
    places, tap_rows, width = grid.layout(ranges)
    most = max(place[3] - place[2] for place in places)
    has_top = any(place[2] == 0 for place in places)
    has_bottom = any(place[3] == LAT_DEV for place in places)
    piece = width // members
    held = (3 * channels, tap_rows * grid.pitch)
    operands = [kept_in_hbm(x) if load else kept_in_vmem(x), sides]
    if has_top:
        operands.append(top)
    if has_bottom:
        operands.append(bottom)
    operands += [weight, bias]
    specs = [in_hbm() if load else in_vmem()] + [in_vmem()] * (len(operands) - 1) + [in_hbm()]
    operands += [kept_in_hbm(analysis), *after]
    specs += [anywhere()] * len(after)
    shapes = [shape_of((fields, piece))] * (members + 1) + [pltpu.VMEM(held, BF16)]
    if load:
        shapes.append(pltpu.VMEM((channels, grid.cells), BF16))
    return pl.pallas_call(
        functools.partial(
            forward_kernel, grid, ranges, has_top, has_bottom, members, load, len(after)
        ),
        in_specs=specs,
        out_specs=[in_vmem()] * len(shapes),
        out_shape=shapes,
        scratch_shapes=[
            pltpu.VMEM((fields, most * grid.pitch), BF16),
            pltpu.VMEM((fields, width), BF16),
            pltpu.SemaphoreType.DMA((1,)),
            pltpu.SemaphoreType.DMA((12, -(-channels // 32))),
        ],
        compiler_params=params(
            (2 * fields, most * grid.pitch, 2),
            (2 * fields, 2 * width, 2),
            (fields, 9 * channels, 2),
        ),
        cost_estimate=cost(81 * channels * fields * width, 0),
        name=f"forward_{ranges[0][0]}",
    )(*operands)


def slope(values):
    return values * lax.rsqrt(values * values + 1.0)


def score_kernel(members, target_ref, scale_ref, *refs):
    pieces = refs[:members]
    outs = refs[-members:]
    fields, piece = pieces[0].shape
    tiles = piece // LANES
    several = max(k for k in (1, 2, 3) if tiles % k == 0)

    def tile(index, carry):
        for part in range(several * -(-fields // 16)):
            low = part // several * 16
            at = (index * several + part % several) * LANES
            span = pl.ds(pl.multiple_of(at, LANES), LANES)
            rows = pl.ds(low, min(16, fields - low))
            values = [ref[rows, span].astype(F32) for ref in pieces]
            target = target_ref[rows, span].astype(F32)
            scale = scale_ref[rows, :]
            sums = [None] * members
            for i in range(members):
                for j in range(i + 1, members):
                    both = slope(values[i] - values[j])
                    sums[i] = both if sums[i] is None else sums[i] + both
                    sums[j] = -both if sums[j] is None else sums[j] - both
            for i in range(members):
                grad = slope(values[i] - target) * (1.0 / members) - sums[i] * (
                    1.0 / (members * (members - 1))
                )
                outs[i][rows, span] = (scale * grad).astype(BF16)
        return carry

    lax.fori_loop(0, tiles // several, tile, 0)


def score(first, target, scale, pieces, after):
    members = len(pieces)
    fields, piece = pieces[0].shape
    return pl.pallas_call(
        functools.partial(score_kernel, members),
        in_specs=[in_vmem()] * (2 + members) + [anywhere()] * len(after),
        out_specs=[in_vmem()] * members,
        out_shape=[shape_of((fields, piece))] * members,
        compiler_params=params((9 * round_up(fields, 16), piece, 2), (fields, LANES, 4)),
        cost_estimate=cost(13000 * fields * piece, 0),
        name=f"score_{first}",
    )(target, scale, *pieces, *after)


def weight_kernel(grid, ranges, members, chained, waits, halves, taps, *refs):
    me = lax.axis_index("member")
    pieces = refs[:members]
    before_ref = refs[members] if chained else None
    refs = refs[members + chained + waits :]
    out_ref, edge_ref = refs[:2]
    flat, pitched = refs[-2:]
    sum_ref = refs[-3]
    fields, piece = pieces[0].shape
    rows = out_ref.shape[0]
    places, _, _ = grid.layout(ranges)
    lead = grid.halo + 2 * LANES
    each = members // len(ranges)
    spots = [lead + lane + number * lead for number, (*_, lane) in enumerate(places)]
    at = 0
    for spot, (_, width, *_) in zip(spots, places):
        flat[:, at:spot] = jnp.zeros((rows, spot - at), BF16)
        at = spot + width
    flat[:, at:] = jnp.zeros((rows, flat.shape[1] - at), BF16)
    base = fields // 16 * 16
    if base < rows:
        for spot, (_, width, *_) in zip(spots, places):
            flat[pl.ds(base, rows - base), spot : spot + width] = jnp.zeros(
                (rows - base, width), BF16
            )
    for d in range(members):
        owner = me ^ d
        begin = pl.multiple_of(lead + owner * piece + owner // each * lead, LANES)
        value = pieces[d][...]
        if grid.padded != grid.cells:
            cell = lax.broadcasted_iota(jnp.int32, (1, piece), 1) + owner * piece
            value = jnp.where(cell < grid.cells, value.astype(F32), 0.0).astype(BF16)
        flat[pl.ds(0, fields), pl.ds(begin, piece)] = value
    for spot, (_, width, *_, lane) in zip(spots, places):
        out_ref[:, lane : lane + width] = flat[:, spot : spot + width]
    columns = []
    for side in (0, grid.columns - 1):
        for row in range(LAT_DEV):
            cell = row * grid.columns + side
            for spot, (first, width, *_) in zip(spots, places):
                if first <= cell < first + width:
                    at = spot + cell - first
                    columns.append(flat[:, at : at + 1])
                    break
            else:
                columns.append(jnp.zeros((rows, 1), BF16))
    edge_ref[...] = jnp.concatenate(columns, axis=1)
    keep = jnp.where(
        lax.broadcasted_iota(jnp.int32, (1, LANES), 1) < grid.columns % LANES, 1.0, 0.0
    ).astype(BF16)
    started = False
    for spot, (first, _, r0, r1, taps_row, _) in zip(spots, places):
        for row, count in groups_of(r1 - r0):
            for at in range(row, row + count):
                value = take(flat, spot + (r0 + at) * grid.columns - first, grid.pitch)
                to = at * grid.pitch
                for lane in range(0, grid.pitch, LANES):
                    part = value[:, lane : lane + LANES]
                    if lane + LANES > grid.columns:
                        part = part * keep
                    pitched[:, to + lane : to + lane + LANES] = part
            stacked = stacked_rows(grid, taps, taps_row + row, count)
            lanes = round_up(stacked.shape[0] + 1, LANES)
            ones = jnp.ones((lanes - stacked.shape[0], stacked.shape[1]), BF16)
            part = nt_dot(
                pitched[:, row * grid.pitch : (row + count) * grid.pitch],
                jnp.concatenate([stacked, ones], axis=0),
            )
            if started:
                sum_ref[:, :lanes] += part
            else:
                sum_ref[:, :lanes] = part + before_ref[:, :lanes] if chained else part
            started = True
    if lanes < sum_ref.shape[1]:
        sum_ref[:, lanes:] = jnp.zeros((rows, sum_ref.shape[1] - lanes), F32)
    if halves:
        keep_ref, send_ref = refs[2:4]
        half = rows // 2
        upper = lax.axis_index("lat") & 1
        keep_ref[...] = sum_ref[pl.ds(pl.multiple_of(upper * half, 8), half), :]
        send_ref[...] = sum_ref[pl.ds(pl.multiple_of((1 - upper) * half, 8), half), :]


def weight_part(grid, ranges, rows, taps, pieces, before, after, halves):
    members = len(pieces)
    channels = taps.shape[0] // 3
    places, _, width = grid.layout(ranges)
    most = max(place[3] - place[2] for place in places)
    room = width + (len(ranges) + 1) * (grid.halo + 2 * LANES)
    sums = round_up(9 * channels + 1, members * LANES)
    chained = [] if before is None else [before]
    shapes = [shape_of((rows, width)), shape_of((rows, 2 * LAT_DEV))]
    whole = []
    if halves:
        shapes += [shape_of((rows // 2, sums), F32)] * 2
        whole = [pltpu.VMEM((rows, sums), F32)]
    else:
        shapes += [shape_of((rows, sums), F32)]
    return pl.pallas_call(
        functools.partial(
            weight_kernel, grid, ranges, members, len(chained), len(after), halves
        ),
        in_specs=[in_vmem()] * (1 + members + len(chained)) + [anywhere()] * len(after),
        out_specs=[in_vmem()] * len(shapes),
        out_shape=shapes,
        scratch_shapes=whole
        + [pltpu.VMEM((rows, room), BF16), pltpu.VMEM((rows, most * grid.pitch), BF16)],
        compiler_params=params(
            (rows, room + 2 * width, 2),
            (rows, most * grid.pitch, 2),
            (rows, 3 * sums, 4),
        ),
        cost_estimate=cost(width, 0),
        name=f"weight_{ranges[0][0]}",
    )(kept_in_vmem(taps), *pieces, *chained, *after)


def input_kernel(grid, r0, r1, chunks, aliased, *refs):
    refs = list(refs)
    parts = refs[: len(chunks)]
    del refs[: len(chunks)]
    sides_ref, weight_ref = refs[:2]
    del refs[:2]
    top_ref = refs.pop(0) if r0 == 0 else None
    bottom_ref = refs.pop(0) if r1 == LAT_DEV else None
    del refs[:aliased]
    out_ref, taps, pitched, flat, out_sem = refs
    sources = []
    for ref, ranges in zip(parts, chunks):
        for first, width, *_, lane in grid.layout(ranges)[0]:
            sources.append((ref, first, min(first + width, grid.cells), lane))
    sides = (sides_ref, top_ref, bottom_ref)
    copies = []

    def emit(low, high):
        at = r0 * grid.columns + low
        copies.append(
            pltpu.make_async_copy(
                flat.at[:, pl.ds(low, high - low)],
                out_ref.at[:, pl.ds(at, high - low)],
                out_sem.at[len(copies)],
            )
        )
        copies[-1].start()

    width = (r1 - r0) * grid.columns
    convolve(
        grid, r0 * grid.columns, width, (0, 0), sources, sides, taps, weight_ref[...], None,
        pitched, flat, backwards=True, emit=emit,
    )
    for copy in copies:
        copy.wait()


def input_part(grid, r0, r1, chunks, parts, sides, top, bottom, weight, before, slow):
    rows = parts[0].shape[0]
    channels = weight.shape[0]
    width = (r1 - r0) * grid.columns
    held = (3 * rows, (r1 - r0 + 2) * grid.pitch)
    begin, end = (r0 - 1) * grid.columns - 1, (r1 + 1) * grid.columns + 1
    near = [
        (ranges, part)
        for ranges, part in zip(chunks, parts)
        if any(first < end and first + size > begin for first, size in ranges)
    ]
    chunks, parts = [pair[0] for pair in near], [pair[1] for pair in near]
    operands = [*parts, sides, weight] + [top] * (r0 == 0) + [bottom] * (r1 == LAT_DEV)
    specs = [in_vmem()] * len(operands)
    alias = {}
    if before is not None:
        alias = {len(operands): 0}
        operands.append(before)
        specs.append(anywhere())
    return pl.pallas_call(
        functools.partial(input_kernel, grid, r0, r1, chunks, len(alias)),
        in_specs=specs,
        out_specs=anywhere(),
        out_shape=shape_of((channels, grid.cells)),
        input_output_aliases=alias,
        scratch_shapes=[
            pltpu.VMEM(held, BF16),
            pltpu.VMEM((channels, (r1 - r0) * grid.pitch), BF16),
            pltpu.VMEM((channels, width), BF16),
            pltpu.SemaphoreType.DMA((-(-width // FLAT_LANES),)),
        ],
        compiler_params=params(
            (rows, sum(part.shape[1] for part in parts), 2),
            (*held, 2),
            (2 * channels, (r1 - r0) * grid.pitch, 2),
            (channels, 9 * rows, 2),
        ),
        cost_estimate=cost((80 if slow else 1) * channels * rows * width, width),
        name=f"input_{r0}",
    )(*operands)


def split_kernel(members, count, *refs):
    me = lax.axis_index("member")
    lanes = refs[count].shape[1]
    for d in range(members):
        span = pl.ds(pl.multiple_of((me ^ d) * lanes, LANES), lanes)
        total = refs[0][:, span]
        for ref in refs[1:count]:
            total += ref[:, span]
        refs[count + d][...] = total


def split_by_member(values, members):
    rows, lanes = values[0].shape
    return pl.pallas_call(
        functools.partial(split_kernel, members, len(values)),
        in_specs=[in_vmem()] * len(values),
        out_specs=[in_vmem()] * members,
        out_shape=[shape_of((rows, lanes // members), F32)] * members,
        compiler_params=params((rows, 3 * lanes, 4)),
        cost_estimate=cost(rows * lanes, 12 * rows * lanes),
        name="split",
    )(*values)


def join_kernel(members, *refs):
    me = lax.axis_index("member")
    lanes = refs[0].shape[1]
    for d in range(members):
        span = pl.ds(pl.multiple_of((me ^ d) * lanes, LANES), lanes)
        refs[members][:, span] = refs[d][...]


def join_members(pieces):
    members = len(pieces)
    rows, lanes = pieces[0].shape
    return pl.pallas_call(
        functools.partial(join_kernel, members),
        in_specs=[in_vmem()] * members,
        out_specs=in_vmem(),
        out_shape=shape_of((rows, members * lanes), F32),
        compiler_params=params((rows, 2 * members * lanes, 4)),
        cost_estimate=cost(rows * lanes, 12 * rows * lanes),
        name="join",
    )(*pieces)


def swap(value, axis, bits):
    return lax.ppermute(value, axis, [(i, i ^ bits) for i in range(lax.axis_size(axis))])


def sum_axis(value, axis, bit):
    size = lax.axis_size(axis)
    while bit < size:
        if 2 * bit < size:
            near, far, both = [swap(value, axis, k * bit) for k in (1, 2, 3)]
            value = (value + near) + (far + both)
        else:
            value = value + swap(value, axis, bit)
        bit *= 4
    return value


def sum_all(keep, send, upper, late):
    members = lax.axis_size("member")
    other = swap(send, "lat", 1)
    values = [keep, other]
    if lax.axis_size("lat") > 2:
        values = [sum_axis(keep + other, "lat", 2)]
    pieces = split_by_member(values, members)
    moved = [swap(pieces[d], "member", d) for d in range(1, members)]
    value = functools.reduce(jnp.add, moved, pieces[0])
    value, late = lax.optimization_barrier((value, late))
    value = sum_axis(value, "lon", 1)
    half = join_members([value] + [swap(value, "member", d) for d in range(1, members)])
    other = swap(half, "lat", 1)
    total = jnp.where(
        upper,
        jnp.concatenate([other, half], axis=0),
        jnp.concatenate([half, other], axis=0),
    )
    return total, late


def weights_kernel(taps_ref, forward_ref, backward_ref):
    count, channels, fields = taps_ref.shape
    rows = backward_ref.shape[1] // count
    taps = [taps_ref[t] for t in range(count)]
    forward_ref[...] = jnp.concatenate(
        [tap.astype(F32).T for tap in taps], axis=1
    ).astype(BF16)
    none = [jnp.zeros((channels, rows - fields), BF16)] * (rows > fields)
    backward_ref[...] = jnp.concatenate([part for tap in taps for part in (tap, *none)], axis=1)


def prepare_weights(taps, rows):
    count, channels, fields = taps.shape
    return pl.pallas_call(
        weights_kernel,
        in_specs=[in_vmem()],
        out_specs=[in_vmem()] * 2,
        out_shape=[shape_of((fields, count * channels)), shape_of((channels, count * rows))],
        compiler_params=params((4 * channels, count * LANES, 4)),
        cost_estimate=cost(channels, 8 * count * channels * rows),
        name="weights",
    )(taps)


def chunks_of(grid, members):
    unit = members * LANES
    units = grid.padded // unit
    if units < 15 or grid.padded != grid.cells or members % 2:
        return [[(0, grid.padded)]]
    outer = (units // 2 + 2) // 2 * unit
    return [
        [(0, outer), (grid.cells - outer, outer)],
        [(outer, grid.cells - 2 * outer)],
    ]


def parts_of(grid, wanted):
    step = LAT_DEV // wanted
    if step * grid.columns % LANES:
        return [(0, LAT_DEV)]
    ranges = [(row, row + step) for row in range(0, LAT_DEV, step)]
    return ranges[1:-1] + [ranges[0], ranges[-1]]


def local(inputs, weight, bias, analysis, field_weight):
    channels, cells = inputs.shape[1], inputs.shape[4]
    fields = analysis.shape[0]
    members = lax.axis_size("member")
    grid = Grid(cells, members)
    x = inputs.reshape(channels, cells)
    target = analysis.reshape(fields, cells)
    if grid.padded != cells:
        target = jnp.pad(target, ((0, 0), (0, grid.padded - cells)))
    rows = round_up(fields, 16)
    taps = weight.reshape(9, channels, fields)
    forward_weight, backward_weight = prepare_weights(taps, rows)
    scale = jnp.broadcast_to(field_weight[:, None], (fields, LANES))
    shift = bias[:, None]
    upper = (lax.axis_index("lat") & 1) != 0
    odd = (lax.axis_index("lon") & 1) != 0
    x_edges, x_row = edges_of(grid, x)
    x_sides = lon_halo(x_edges, odd)
    x_sides, forward_weight, backward_weight, scale, shift, upper, odd = (
        lax.optimization_barrier(
            (x_sides, forward_weight, backward_weight, scale, shift, upper, odd)
        )
    )
    first_lat = jnp.logical_not(upper)
    def to_members(pieces):
        moved = {0: pieces[0]}
        for d in range(members - 1, 0, -1):
            moved[d] = swap(pieces[d], "member", d)
        return [moved[d] for d in range(members)]

    chunks = chunks_of(grid, members)
    x_top, x_bottom = lat_halo(
        x[:, : grid.halo], x[:, cells - grid.halo :], x_sides, first_lat, x_row
    )
    received, targets, taken, held = [], [], [], None
    for ranges in chunks:
        out = forward(
            grid, ranges, members, x if held is None else held, held is None, x_sides, x_top,
            x_bottom, forward_weight, shift, target, [],
        )
        targets.append(out[members])
        taken.append(out[members + 1])
        held = out[members + 2] if held is None else held
        received.append(to_members(out[:members]))
    returned = []
    for ranges, pieces, goal in zip(chunks, received, targets):
        grads = score(ranges[0][0], goal, scale, pieces, targets[-1:])
        returned.append(to_members(grads))

    blocks = parts_of(grid, 4)
    parts, edges, sums, grad_input = [], [], [None], None
    for number, ranges in enumerate(chunks):
        final = number == len(chunks) - 1
        after = [returned[-1][0]] if number == 0 else [kept_in_hbm(first_input)]
        part, edge, *sums = weight_part(
            grid, ranges, rows, taken[number], returned[number], sums[0], after, final
        )
        parts.append(part)
        edges.append(edge)
        if number == 0:
            end = part.shape[1] - grid.padded + cells
            outer_rows = (part[:, : grid.halo], part[:, end - grid.halo : end])
        if final:
            break
        g_sides = lon_halo(edge, odd)
        g_top, g_bottom = lat_halo(*outer_rows, g_sides, first_lat)
        grad_input = first_input = input_part(
            grid, *blocks.pop(), chunks[:1], parts[:1], g_sides, g_top, g_bottom,
            backward_weight, None, False,
        )
        grad_input = input_part(
            grid, *blocks.pop(), chunks[:1], parts[:1], g_sides, g_top, g_bottom,
            backward_weight, grad_input, True,
        )
    total, late_edges = sum_all(*sums, upper, edges[-1])
    late_sides = lon_halo(late_edges, odd)
    if len(chunks) == 1:
        g_top, g_bottom = lat_halo(*outer_rows, late_sides, first_lat)
    else:
        late_sides = late_sides + g_sides
    for r0, r1 in blocks:
        grad_input = input_part(
            grid, r0, r1, chunks, parts, late_sides, g_top, g_bottom, backward_weight,
            grad_input, True,
        )
    total = total / (cells * lax.axis_size("lat") * lax.axis_size("lon"))
    grad_weight = total[:fields, : 9 * channels].T.reshape(9, channels * fields)
    grad_bias = total[:fields, 9 * channels]
    return (grad_input.reshape(1, channels, 1, 1, cells), grad_weight, grad_bias)


def solution(mesh):
    placed = (P("member", None, "lat", "lon", None), P(), P(), P(None, "lat", "lon", None), P())
    return jax.shard_map(
        local,
        mesh=mesh,
        in_specs=placed,
        out_specs=(P("member", None, "lat", "lon", None), P(), P()),
        check_vma=False,
    )
```

```python
import functools

import jax
import jax.numpy as jnp
from jax import lax
from jax.experimental import pallas as pl
from jax.experimental.pallas import tpu as pltpu
from jax.sharding import PartitionSpec as P

LAT_DEV = 64
LANES = 128
ROW_GROUP = 2
FLAT_LANES = 1024
SLACK = 3 * 1024 * 1024
F32 = jnp.float32
BF16 = jnp.bfloat16


def round_up(value, step):
    return -(-value // step) * step


def params(*held):
    total = sum(round_up(rows, 16) * round_up(lanes, LANES) * size for rows, lanes, size in held)
    return pltpu.CompilerParams(vmem_limit_bytes=total + SLACK)


def kept_in_hbm(value):
    return pltpu.with_memory_space_constraint(value, pltpu.HBM)


def kept_in_vmem(value):
    return pltpu.with_memory_space_constraint(value, pltpu.VMEM)


def shape_of(dims, dtype=BF16):
    return jax.ShapeDtypeStruct(dims, dtype)


def cost(flops, moved):
    return pl.CostEstimate(flops=int(flops), bytes_accessed=int(moved), transcendentals=0)


def in_vmem():
    return pl.BlockSpec(memory_space=pltpu.VMEM)


def in_smem():
    return pl.BlockSpec(memory_space=pltpu.SMEM)


def in_hbm():
    return pl.BlockSpec(memory_space=pltpu.HBM)


def anywhere():
    return pl.BlockSpec(memory_space=pl.ANY)


def nt_dot(left, right):
    return lax.dot_general(left, right, (((1,), (1,)), ((), ())), preferred_element_type=F32)


class Grid:
    def __init__(self, cells, members):
        self.cells = cells
        self.columns = cells // LAT_DEV
        self.pitch = round_up(self.columns, LANES)
        self.halo = round_up(self.columns + 1, LANES)
        self.padded = round_up(cells, members * LANES)

    def rows(self, first, width):
        return first // self.columns, -(-min(first + width, self.cells) // self.columns)

    def layout(self, ranges):
        out, row, lane = [], 0, 0
        for first, width in ranges:
            r0, r1 = self.rows(first, width)
            out.append((first, width, r0, r1, row, lane))
            row, lane = row + r1 - r0 + 2, lane + width
        return out, row, lane


def take(ref, start, width):
    low = start // LANES * LANES
    off = start - low
    if off == 0:
        return ref[:, low : low + width]
    return ref[:, low : low + width + LANES][:, off : off + width]


def side_column(refs, grid, row, right):
    own, top, bottom = refs
    slot = LAT_DEV if right else 0
    if row < 0:
        ref, lane = top, grid.halo + slot + LAT_DEV - 1
    elif row >= LAT_DEV:
        ref, lane = bottom, grid.halo + slot
    else:
        ref, lane = own, slot + row
    return ref[:, lane : lane + 1]


def take_cells(sources, start, width):
    parts, at, end = [], start, start + width
    for ref, begin, last, lane in sorted(sources, key=lambda source: source[1]):
        shift = lane - begin
        base = (start + shift) // LANES * LANES
        if begin <= start and end <= last and base + width + LANES <= ref.shape[1]:
            return take(ref, start + shift, width)
        low, high = max(at, begin), min(end, last)
        if low < high:
            if low > at:
                parts.append(jnp.zeros((ref.shape[0], low - at), BF16))
            base = (low + shift) // LANES * LANES
            top = min(round_up(high + shift, LANES), ref.shape[1])
            parts.append(ref[:, base:top][:, low + shift - base : high + shift - base])
            at = high
    if at < end:
        parts.append(jnp.zeros((sources[0][0].shape[0], end - at), BF16))
    return jnp.concatenate(parts, axis=1) if len(parts) > 1 else parts[0]


def row_cells(grid, row, sources, top, bottom):
    if row < 0 and top is not None:
        return take_cells([(top, 0, top.shape[1], 0)], grid.halo - grid.columns, grid.pitch)
    if row >= LAT_DEV and bottom is not None:
        return take_cells([(bottom, 0, bottom.shape[1], 0)], 0, grid.pitch)
    return take_cells(sources, row * grid.columns, grid.pitch)


def build_taps(grid, origin, low, high, sources, sides, taps, backwards=False):
    rows = sources[0][0].shape[0]
    own, top, bottom = sides
    for row in range(low, high):
        base = (row - origin) * grid.pitch
        value = row_cells(grid, row, sources, top, bottom)
        left = side_column(sides, grid, row, False)
        right = side_column(sides, grid, row, True)
        before = jnp.concatenate([left, value[:, : grid.pitch - 1]], axis=1)
        after = [value[:, 1 : grid.columns], right]
        if grid.columns < grid.pitch:
            after.append(jnp.zeros((rows, grid.pitch - grid.columns), BF16))
        for b, part in enumerate((before, value, jnp.concatenate(after, axis=1))):
            block = pl.ds((2 - b if backwards else b) * rows, rows)
            taps[block, base : base + grid.pitch] = part


def stacked_rows(grid, taps, row, count, order=(0, 1, 2)):
    width = count * grid.pitch
    return jnp.concatenate(
        [taps[:, (row + a) * grid.pitch : (row + a) * grid.pitch + width] for a in order],
        axis=0,
    )


def groups_of(count, size=ROW_GROUP):
    return [(row, min(size, count - row)) for row in range(0, count, size)]


def flat_piece(grid, pitched, skip, low, high, count):
    parts, at = [], low
    while at < high:
        row, column = divmod(at + skip, grid.columns)
        if row >= count:
            parts.append(jnp.zeros((pitched.shape[0], high - at), BF16))
            break
        size = min(grid.columns - column, high - at)
        begin = row * grid.pitch + column
        parts.append(pitched[:, begin : begin + size])
        at += size
    return jnp.concatenate(parts, axis=1) if len(parts) > 1 else parts[0]


def convolve(grid, first, width, place, sources, sides, taps, weight, bias, pitched, flat,
             backwards=False, emit=None, fetch=None):
    r0, r1 = grid.rows(first, width)
    skip = first - r0 * grid.columns
    taps_row, lane = place
    built, done = r0 - 1, 0
    order = (2, 1, 0) if backwards else (0, 1, 2)
    for row, count in groups_of(r1 - r0):
        ready = min(r0 + row + count + 1 + ROW_GROUP, r1 + 1)
        if fetch is not None:
            fetch(ready)
        build_taps(
            grid, r0 - 1 - taps_row, built, ready, sources, sides, taps, backwards
        )
        built = ready
        stacked = stacked_rows(grid, taps, taps_row + row, count, order)
        value = jnp.dot(weight, stacked, preferred_element_type=F32)
        if bias is not None:
            value = value + bias
        pitched[:, row * grid.pitch : (row + count) * grid.pitch] = value.astype(BF16)
        last = row + count == r1 - r0
        while done < width:
            end = min(done + FLAT_LANES, width)
            if not last and end + skip > row * grid.columns:
                break
            piece = flat_piece(grid, pitched, skip, done, end, r1 - r0)
            flat[:, lane + done : lane + end] = piece
            if emit is not None:
                emit(done, end)
            done = end


def edges_kernel(grid, places, tiles, x_ref, out_ref, row_ref, held, sem, row_sem):
    last = jnp.where(lax.axis_index("lat") == 0, (grid.cells - grid.halo) // LANES, 0)
    row_copy = pltpu.make_async_copy(
        x_ref.at[:, pl.ds(pl.multiple_of(last * LANES, LANES), grid.halo)],
        row_ref,
        row_sem.at[0],
    )
    row_copy.start()
    copies = [
        pltpu.make_async_copy(
            x_ref.at[:, pl.ds(tile * LANES, LANES)],
            held.at[:, pl.ds(number * LANES, LANES)],
            sem.at[number],
        )
        for number, tile in enumerate(tiles)
    ]
    for copy in copies:
        copy.start()
    for copy in copies:
        copy.wait()
    columns = []
    for cell in places:
        at = tiles.index(cell // LANES) * LANES + cell % LANES
        columns.append(held[:, at : at + 1])
    out_ref[...] = jnp.concatenate(columns, axis=1)
    row_copy.wait()


def edges_of(grid, field):
    rows = field.shape[0]
    places = [i for i in range(0, grid.cells, grid.columns)]
    places += [i for i in range(grid.columns - 1, grid.cells, grid.columns)]
    tiles = sorted({cell // LANES for cell in places})
    return pl.pallas_call(
        functools.partial(edges_kernel, grid, places, tiles),
        in_specs=[in_hbm()],
        out_specs=[in_vmem()] * 2,
        out_shape=[shape_of((rows, 2 * LAT_DEV)), shape_of((rows, grid.halo))],
        scratch_shapes=[
            pltpu.VMEM((rows, len(tiles) * LANES), BF16),
            pltpu.SemaphoreType.DMA((len(tiles),)),
            pltpu.SemaphoreType.DMA((1,)),
        ],
        compiler_params=params((rows, (len(tiles) + 1) * LANES + grid.halo, 2)),
        cost_estimate=cost(rows, rows),
        name="edges",
    )(kept_in_hbm(field))


def lon_halo(edges, odd):
    peers = lax.axis_size("lon")
    first, last = edges[:, :LAT_DEV], edges[:, LAT_DEV:]
    if peers % 2:
        right = [(i, (i + 1) % peers) for i in range(peers)]
        left = [(j, i) for i, j in right]
        before, after = lax.ppermute(last, "lon", right), lax.ppermute(first, "lon", left)
        return jnp.concatenate([before, after], axis=1)
    near = [(i, i ^ 1) for i in range(peers)]
    far = [(i, (i + 1 if i % 2 else i - 1) % peers) for i in range(peers)]
    inner = lax.ppermute(jnp.where(odd, first, last), "lon", near)
    outer = lax.ppermute(jnp.where(odd, last, first), "lon", far)
    return jnp.where(
        odd,
        jnp.concatenate([inner, outer], axis=1),
        jnp.concatenate([outer, inner], axis=1),
    )


def lat_halo(first_rows, last_rows, sides, upper, chosen=None):
    peers = lax.axis_size("lat")
    if peers == 2:
        if chosen is None:
            chosen = jnp.where(upper, last_rows, first_rows)
        sent = jnp.concatenate([chosen, sides], axis=1)
        other = lax.ppermute(sent, "lat", [(0, 1), (1, 0)])
        none = jnp.zeros_like(other)
        return jnp.where(upper, none, other), jnp.where(upper, other, none)
    up = [(i, i + 1) for i in range(peers - 1)]
    down = [(j, i) for i, j in up]
    top = lax.ppermute(jnp.concatenate([last_rows, sides], axis=1), "lat", up)
    bottom = lax.ppermute(jnp.concatenate([first_rows, sides], axis=1), "lat", down)
    return top, bottom


def stages_of(grid, ranges):
    stages, got = [], []
    for first, width in ranges:
        r0, r1 = grid.rows(first, width)
        low = max((r0 - 1) * grid.columns - 1, 0) // LANES * LANES
        high = min(round_up((r1 + 1) * grid.columns + 1, LANES), grid.cells)
        low = max([low] + [end for begin, end in got if begin <= low])
        step = round_up(max((high - low) // 3, LANES), LANES)
        stages += [(at, min(at + step, high)) for at in range(low, high, step)]
        got.append((low, high))
    at = 0
    for low, high in sorted(got) + [(grid.cells, grid.cells)]:
        if at < low:
            stages.append((at, low))
        at = max(at, high)
    return stages


def forward_kernel(grid, ranges, has_top, has_bottom, members, load, waits, *refs):
    refs = list(refs)
    x_ref, sides_ref = refs[:2]
    del refs[:2]
    top_ref = refs.pop(0) if has_top else None
    bottom_ref = refs.pop(0) if has_bottom else None
    weight_ref, bias_ref, analysis_ref = refs[:3]
    del refs[: 3 + waits]
    outs = refs[:members]
    target_ref, taps = refs[members : members + 2]
    pitched, pred, target_sem, load_sem = refs[-4:]
    me = lax.axis_index("member")
    places, _, width = grid.layout(ranges)
    piece = width // members
    pending = []
    if load:
        held = refs[members + 2]
        for begin, end in stages_of(grid, ranges):
            copies = []
            for low in range(0, x_ref.shape[0], 32):
                at = (pl.ds(low, min(32, x_ref.shape[0] - low)), pl.ds(begin, end - begin))
                sem = load_sem.at[len(pending), len(copies)]
                copies.append(pltpu.make_async_copy(x_ref.at[at], held.at[at], sem))
                copies[-1].start()
            pending.append((begin, end, copies))
        x_ref = held

    def fetch(low, high):
        for stage in list(pending):
            if stage[0] < high * grid.columns + 1 and stage[1] > low * grid.columns - 1:
                for copy in stage[2]:
                    copy.wait()
                pending.remove(stage)

    each = members // len(ranges)
    index = me // each
    begin = places[0][0] + me * piece
    if len(ranges) > 1:
        begin = jnp.where(index == 0, begin, places[1][0] + (me - each) * piece)
    begin = pl.multiple_of(begin, LANES)
    target_copy = pltpu.make_async_copy(
        analysis_ref.at[:, pl.ds(begin, piece)], target_ref, target_sem.at[0]
    )
    target_copy.start()
    sides = (sides_ref, top_ref, bottom_ref)
    weight, bias = weight_ref[...], bias_ref[...]
    for first, size, r0, r1, row, lane in places:
        convolve(
            grid, first, size, (row, lane), [(x_ref, 0, grid.cells, 0)], sides, taps, weight,
            bias, pitched, pred, fetch=lambda ready, r0=r0: fetch(r0 - 1, ready),
        )
    for d in range(members):
        begin = pl.multiple_of((me ^ d) * piece, LANES)
        outs[d][...] = pred[:, pl.ds(begin, piece)]
    target_copy.wait()
    fetch(0, LAT_DEV)


def forward(
    grid, ranges, members, x, load, sides, top, bottom, weight, bias, analysis, after
):
    channels = x.shape[0]
    fields = weight.shape[0]
    places, tap_rows, width = grid.layout(ranges)
    most = max(place[3] - place[2] for place in places)
    has_top = any(place[2] == 0 for place in places)
    has_bottom = any(place[3] == LAT_DEV for place in places)
    piece = width // members
    held = (3 * channels, tap_rows * grid.pitch)
    operands = [kept_in_hbm(x) if load else kept_in_vmem(x), sides]
    if has_top:
        operands.append(top)
    if has_bottom:
        operands.append(bottom)
    operands += [weight, bias]
    specs = [in_hbm() if load else in_vmem()] + [in_vmem()] * (len(operands) - 1) + [in_hbm()]
    operands += [kept_in_hbm(analysis), *after]
    specs += [anywhere()] * len(after)
    shapes = [shape_of((fields, piece))] * (members + 1) + [pltpu.VMEM(held, BF16)]
    if load:
        shapes.append(pltpu.VMEM((channels, grid.cells), BF16))
    return pl.pallas_call(
        functools.partial(
            forward_kernel, grid, ranges, has_top, has_bottom, members, load, len(after)
        ),
        in_specs=specs,
        out_specs=[in_vmem()] * len(shapes),
        out_shape=shapes,
        scratch_shapes=[
            pltpu.VMEM((fields, most * grid.pitch), BF16),
            pltpu.VMEM((fields, width), BF16),
            pltpu.SemaphoreType.DMA((1,)),
            pltpu.SemaphoreType.DMA((12, -(-channels // 32))),
        ],
        compiler_params=params(
            (2 * fields, most * grid.pitch, 2),
            (2 * fields, 2 * width, 2),
            (fields, 9 * channels, 2),
        ),
        cost_estimate=cost(81 * channels * fields * width, 0),
        name=f"forward_{ranges[0][0]}",
    )(*operands)


def slope(values):
    return values * lax.rsqrt(values * values + 1.0)


def score_kernel(members, target_ref, scale_ref, *refs):
    pieces = refs[:members]
    outs = refs[-members:]
    fields, piece = pieces[0].shape
    tiles = piece // LANES
    several = max(k for k in (1, 2, 3) if tiles % k == 0)

    def tile(index, carry):
        for part in range(several * -(-fields // 16)):
            low = part // several * 16
            at = (index * several + part % several) * LANES
            span = pl.ds(pl.multiple_of(at, LANES), LANES)
            rows = pl.ds(low, min(16, fields - low))
            values = [ref[rows, span].astype(F32) for ref in pieces]
            target = target_ref[rows, span].astype(F32)
            scale = scale_ref[rows, :]
            sums = [None] * members
            for i in range(members):
                for j in range(i + 1, members):
                    both = slope(values[i] - values[j])
                    sums[i] = both if sums[i] is None else sums[i] + both
                    sums[j] = -both if sums[j] is None else sums[j] - both
            for i in range(members):
                grad = slope(values[i] - target) * (1.0 / members) - sums[i] * (
                    1.0 / (members * (members - 1))
                )
                outs[i][rows, span] = (scale * grad).astype(BF16)
        return carry

    lax.fori_loop(0, tiles // several, tile, 0)


def score(first, target, scale, pieces, after):
    members = len(pieces)
    fields, piece = pieces[0].shape
    return pl.pallas_call(
        functools.partial(score_kernel, members),
        in_specs=[in_vmem()] * (2 + members) + [anywhere()] * len(after),
        out_specs=[in_vmem()] * members,
        out_shape=[shape_of((fields, piece))] * members,
        compiler_params=params((9 * round_up(fields, 16), piece, 2), (fields, LANES, 4)),
        cost_estimate=cost(13000 * fields * piece, 0),
        name=f"score_{first}",
    )(target, scale, *pieces, *after)


def gather_kernel(grid, ranges, members, *refs):
    me = lax.axis_index("member")
    pieces = refs[:members]
    out_ref, edge_ref = refs[members:]
    fields, piece = pieces[0].shape
    rows, width = out_ref.shape
    base = fields // 16 * 16
    if base < rows:
        out_ref[pl.ds(base, rows - base), :] = jnp.zeros((rows - base, width), BF16)
    for d in range(members):
        begin = pl.multiple_of((me ^ d) * piece, LANES)
        value = pieces[d][...]
        if grid.padded != grid.cells:
            cell = lax.broadcasted_iota(jnp.int32, (1, piece), 1) + begin
            value = jnp.where(cell < grid.cells, value.astype(F32), 0.0).astype(BF16)
        out_ref[pl.ds(0, fields), pl.ds(begin, piece)] = value
    columns = []
    for side in (0, grid.columns - 1):
        for row in range(LAT_DEV):
            cell = row * grid.columns + side
            for first, size, *_, lane in grid.layout(ranges)[0]:
                if first <= cell < first + size:
                    at = lane + cell - first
                    columns.append(out_ref[:, at : at + 1])
                    break
            else:
                columns.append(jnp.zeros((rows, 1), BF16))
    edge_ref[...] = jnp.concatenate(columns, axis=1)


def gather(grid, ranges, rows, pieces, after):
    members = len(pieces)
    width = members * pieces[0].shape[1]

    def kernel(*refs):
        gather_kernel(grid, ranges, members, *refs[:members], *refs[-2:])

    return pl.pallas_call(
        kernel,
        in_specs=[in_vmem()] * members + [anywhere()] * len(after),
        out_specs=[in_vmem()] * 2,
        out_shape=[shape_of((rows, width)), shape_of((rows, 2 * LAT_DEV))],
        compiler_params=params((rows, 2 * width + 2 * LAT_DEV, 2)),
        cost_estimate=cost(width, 0),
        name=f"gather_{ranges[0][0]}",
    )(*pieces, *after)


def weight_kernel(grid, ranges, chained, waits, halves, taps, part_ref, *refs):
    before_ref = refs[0] if chained else None
    refs = refs[chained + waits :]
    pitched, sum_ref = refs[-1], refs[-2]
    rows = part_ref.shape[0]
    keep = jnp.where(
        lax.broadcasted_iota(jnp.int32, (1, LANES), 1) < grid.columns % LANES, 1.0, 0.0
    ).astype(BF16)
    started = False
    for first, width, r0, r1, taps_row, place in grid.layout(ranges)[0]:
        source = [(part_ref, first, first + width, place)]
        for row, count in groups_of(r1 - r0):
            for at in range(row, row + count):
                value = take_cells(source, (r0 + at) * grid.columns, grid.pitch)
                to = at * grid.pitch
                for lane in range(0, grid.pitch, LANES):
                    part = value[:, lane : lane + LANES]
                    if lane + LANES > grid.columns:
                        part = part * keep
                    pitched[:, to + lane : to + lane + LANES] = part
            stacked = stacked_rows(grid, taps, taps_row + row, count)
            lanes = round_up(stacked.shape[0] + 1, LANES)
            ones = jnp.ones((lanes - stacked.shape[0], stacked.shape[1]), BF16)
            part = nt_dot(
                pitched[:, row * grid.pitch : (row + count) * grid.pitch],
                jnp.concatenate([stacked, ones], axis=0),
            )
            if started:
                sum_ref[:, :lanes] += part
            else:
                sum_ref[:, :lanes] = part + before_ref[:, :lanes] if chained else part
            started = True
    if lanes < sum_ref.shape[1]:
        sum_ref[:, lanes:] = jnp.zeros((rows, sum_ref.shape[1] - lanes), F32)
    if halves:
        keep_ref, send_ref = refs[:2]
        half = rows // 2
        upper = lax.axis_index("lat") & 1
        keep_ref[...] = sum_ref[pl.ds(pl.multiple_of(upper * half, 8), half), :]
        send_ref[...] = sum_ref[pl.ds(pl.multiple_of((1 - upper) * half, 8), half), :]


def weight_part(grid, ranges, members, taps, part, before, after, halves):
    rows = part.shape[0]
    channels = taps.shape[0] // 3
    places, _, width = grid.layout(ranges)
    most = max(place[3] - place[2] for place in places)
    sums = round_up(9 * channels + 1, members * LANES)
    chained = [] if before is None else [before]
    whole = []
    if halves:
        shapes = [shape_of((rows // 2, sums), F32)] * 2
        whole = [pltpu.VMEM((rows, sums), F32)]
    else:
        shapes = [shape_of((rows, sums), F32)]
    return pl.pallas_call(
        functools.partial(weight_kernel, grid, ranges, len(chained), len(after), halves),
        in_specs=[in_vmem()] * (2 + len(chained)) + [anywhere()] * len(after),
        out_specs=[in_vmem()] * len(shapes),
        out_shape=shapes,
        scratch_shapes=whole + [pltpu.VMEM((rows, most * grid.pitch), BF16)],
        compiler_params=params(
            (rows, width, 2),
            (rows, most * grid.pitch, 2),
            (rows, 3 * sums, 4),
        ),
        cost_estimate=cost(width, 0),
        name=f"weight_{ranges[0][0]}",
    )(kept_in_vmem(taps), part, *chained, *after)


def input_kernel(grid, r0, r1, chunks, aliased, *refs):
    refs = list(refs)
    parts = refs[: len(chunks)]
    del refs[: len(chunks)]
    sides_ref, weight_ref = refs[:2]
    del refs[:2]
    top_ref = refs.pop(0) if r0 == 0 else None
    bottom_ref = refs.pop(0) if r1 == LAT_DEV else None
    del refs[:aliased]
    out_ref, taps, pitched, flat, out_sem = refs
    sources = []
    for ref, ranges in zip(parts, chunks):
        for first, width, *_, lane in grid.layout(ranges)[0]:
            sources.append((ref, first, min(first + width, grid.cells), lane))
    sides = (sides_ref, top_ref, bottom_ref)
    copies = []

    def emit(low, high):
        at = r0 * grid.columns + low
        copies.append(
            pltpu.make_async_copy(
                flat.at[:, pl.ds(low, high - low)],
                out_ref.at[:, pl.ds(at, high - low)],
                out_sem.at[len(copies)],
            )
        )
        copies[-1].start()

    width = (r1 - r0) * grid.columns
    convolve(
        grid, r0 * grid.columns, width, (0, 0), sources, sides, taps, weight_ref[...], None,
        pitched, flat, backwards=True, emit=emit,
    )
    for copy in copies:
        copy.wait()


def input_part(grid, r0, r1, chunks, parts, sides, top, bottom, weight, before, slow):
    rows = parts[0].shape[0]
    channels = weight.shape[0]
    width = (r1 - r0) * grid.columns
    held = (3 * rows, (r1 - r0 + 2) * grid.pitch)
    begin, end = (r0 - 1) * grid.columns - 1, (r1 + 1) * grid.columns + 1
    near = [
        (ranges, part)
        for ranges, part in zip(chunks, parts)
        if any(first < end and first + size > begin for first, size in ranges)
    ]
    chunks, parts = [pair[0] for pair in near], [pair[1] for pair in near]
    operands = [*parts, sides, weight] + [top] * (r0 == 0) + [bottom] * (r1 == LAT_DEV)
    specs = [in_vmem()] * len(operands)
    alias = {}
    if before is not None:
        alias = {len(operands): 0}
        operands.append(before)
        specs.append(anywhere())
    return pl.pallas_call(
        functools.partial(input_kernel, grid, r0, r1, chunks, len(alias)),
        in_specs=specs,
        out_specs=anywhere(),
        out_shape=shape_of((channels, grid.cells)),
        input_output_aliases=alias,
        scratch_shapes=[
            pltpu.VMEM(held, BF16),
            pltpu.VMEM((channels, (r1 - r0) * grid.pitch), BF16),
            pltpu.VMEM((channels, width), BF16),
            pltpu.SemaphoreType.DMA((-(-width // FLAT_LANES),)),
        ],
        compiler_params=params(
            (rows, sum(part.shape[1] for part in parts), 2),
            (*held, 2),
            (2 * channels, (r1 - r0) * grid.pitch, 2),
            (channels, 9 * rows, 2),
        ),
        cost_estimate=cost((80 if slow else 1) * channels * rows * width, width),
        name=f"input_{r0}",
    )(*operands)


def split_kernel(members, count, *refs):
    me = lax.axis_index("member")
    lanes = refs[count].shape[1]
    for d in range(members):
        span = pl.ds(pl.multiple_of((me ^ d) * lanes, LANES), lanes)
        total = refs[0][:, span]
        for ref in refs[1:count]:
            total += ref[:, span]
        refs[count + d][...] = total


def split_by_member(values, members):
    rows, lanes = values[0].shape
    return pl.pallas_call(
        functools.partial(split_kernel, members, len(values)),
        in_specs=[in_vmem()] * len(values),
        out_specs=[in_vmem()] * members,
        out_shape=[shape_of((rows, lanes // members), F32)] * members,
        compiler_params=params((rows, 3 * lanes, 4)),
        cost_estimate=cost(rows * lanes, 12 * rows * lanes),
        name="split",
    )(*values)


def join_kernel(members, *refs):
    me = lax.axis_index("member")
    lanes = refs[0].shape[1]
    for d in range(members):
        span = pl.ds(pl.multiple_of((me ^ d) * lanes, LANES), lanes)
        refs[members][:, span] = refs[d][...]


def join_members(pieces):
    members = len(pieces)
    rows, lanes = pieces[0].shape
    return pl.pallas_call(
        functools.partial(join_kernel, members),
        in_specs=[in_vmem()] * members,
        out_specs=in_vmem(),
        out_shape=shape_of((rows, members * lanes), F32),
        compiler_params=params((rows, 2 * members * lanes, 4)),
        cost_estimate=cost(rows * lanes, 12 * rows * lanes),
        name="join",
    )(*pieces)


def swap(value, axis, bits):
    return lax.ppermute(value, axis, [(i, i ^ bits) for i in range(lax.axis_size(axis))])


def sum_axis(value, axis, bit):
    size = lax.axis_size(axis)
    while bit < size:
        if 2 * bit < size:
            near, far, both = [swap(value, axis, k * bit) for k in (1, 2, 3)]
            value = (value + near) + (far + both)
        else:
            value = value + swap(value, axis, bit)
        bit *= 4
    return value


def sum_all(keep, send, upper, late):
    members = lax.axis_size("member")
    other = swap(send, "lat", 1)
    values = [keep, other]
    if lax.axis_size("lat") > 2:
        values = [sum_axis(keep + other, "lat", 2)]
    pieces = split_by_member(values, members)
    moved = [swap(pieces[d], "member", d) for d in range(1, members)]
    value = functools.reduce(jnp.add, moved, pieces[0])
    value, late = lax.optimization_barrier((value, late))
    value = sum_axis(value, "lon", 1)
    half = join_members([value] + [swap(value, "member", d) for d in range(1, members)])
    other = swap(half, "lat", 1)
    total = jnp.where(
        upper,
        jnp.concatenate([other, half], axis=0),
        jnp.concatenate([half, other], axis=0),
    )
    return total, late


def weights_kernel(taps_ref, forward_ref, backward_ref):
    count, channels, fields = taps_ref.shape
    rows = backward_ref.shape[1] // count
    taps = [taps_ref[t] for t in range(count)]
    forward_ref[...] = jnp.concatenate(
        [tap.astype(F32).T for tap in taps], axis=1
    ).astype(BF16)
    none = [jnp.zeros((channels, rows - fields), BF16)] * (rows > fields)
    backward_ref[...] = jnp.concatenate([part for tap in taps for part in (tap, *none)], axis=1)


def prepare_weights(taps, rows):
    count, channels, fields = taps.shape
    return pl.pallas_call(
        weights_kernel,
        in_specs=[in_vmem()],
        out_specs=[in_vmem()] * 2,
        out_shape=[shape_of((fields, count * channels)), shape_of((channels, count * rows))],
        compiler_params=params((4 * channels, count * LANES, 4)),
        cost_estimate=cost(channels, 8 * count * channels * rows),
        name="weights",
    )(taps)


def chunks_of(grid, members):
    unit = members * LANES
    units = grid.padded // unit
    if units < 15 or grid.padded != grid.cells or members % 2:
        return [[(0, grid.padded)]]
    outer = (units // 2 + 2) // 2 * unit
    return [
        [(0, outer), (grid.cells - outer, outer)],
        [(outer, grid.cells - 2 * outer)],
    ]


def parts_of(grid, wanted):
    step = LAT_DEV // wanted
    if step * grid.columns % LANES:
        return [(0, LAT_DEV)]
    ranges = [(row, row + step) for row in range(0, LAT_DEV, step)]
    return ranges[1:-1] + [ranges[0], ranges[-1]]


def local(inputs, weight, bias, analysis, field_weight):
    channels, cells = inputs.shape[1], inputs.shape[4]
    fields = analysis.shape[0]
    members = lax.axis_size("member")
    grid = Grid(cells, members)
    x = inputs.reshape(channels, cells)
    target = analysis.reshape(fields, cells)
    if grid.padded != cells:
        target = jnp.pad(target, ((0, 0), (0, grid.padded - cells)))
    rows = round_up(fields, 16)
    taps = weight.reshape(9, channels, fields)
    forward_weight, backward_weight = prepare_weights(taps, rows)
    scale = jnp.broadcast_to(field_weight[:, None], (fields, LANES))
    shift = bias[:, None]
    upper = (lax.axis_index("lat") & 1) != 0
    odd = (lax.axis_index("lon") & 1) != 0
    x_edges, x_row = edges_of(grid, x)
    x_sides = lon_halo(x_edges, odd)
    x_sides, forward_weight, backward_weight, scale, shift, upper, odd = (
        lax.optimization_barrier(
            (x_sides, forward_weight, backward_weight, scale, shift, upper, odd)
        )
    )
    first_lat = jnp.logical_not(upper)
    def to_members(pieces):
        moved = {0: pieces[0]}
        for d in range(members - 1, 0, -1):
            moved[d] = swap(pieces[d], "member", d)
        return [moved[d] for d in range(members)]

    chunks = chunks_of(grid, members)
    x_top, x_bottom = lat_halo(
        x[:, : grid.halo], x[:, cells - grid.halo :], x_sides, first_lat, x_row
    )
    received, targets, taken, held = [], [], [], None
    for ranges in chunks:
        out = forward(
            grid, ranges, members, x if held is None else held, held is None, x_sides, x_top,
            x_bottom, forward_weight, shift, target, [],
        )
        targets.append(out[members])
        taken.append(out[members + 1])
        held = out[members + 2] if held is None else held
        received.append(to_members(out[:members]))
    returned = []
    for ranges, pieces, goal in zip(chunks, received, targets):
        grads = score(ranges[0][0], goal, scale, pieces, targets[-1:])
        returned.append(to_members(grads))

    blocks = parts_of(grid, 4)
    parts, edges, sums, grad_input = [], [], [None], None
    for number, ranges in enumerate(chunks):
        final = number == len(chunks) - 1
        after = [returned[-1][0]] if number == 0 else [kept_in_hbm(grad_input)]
        part, edge = gather(grid, ranges, rows, returned[number], after)
        sums = list(
            weight_part(grid, ranges, members, taken[number], part, sums[0], [], final)
        )
        parts.append(part)
        edges.append(edge)
        if number == 0:
            end = part.shape[1] - grid.padded + cells
            outer_rows = (part[:, : grid.halo], part[:, end - grid.halo : end])
        if final:
            break
        g_sides = lon_halo(edge, odd)
        g_sides, sums[0] = lax.optimization_barrier((g_sides, sums[0]))
        g_top, g_bottom = lat_halo(*outer_rows, g_sides, first_lat)
        for _ in range(2):
            grad_input = input_part(
                grid, *blocks.pop(), chunks[:1], parts[:1], g_sides, g_top, g_bottom,
                backward_weight, grad_input, False,
            )
    total, late_edges = sum_all(*sums, upper, edges[-1])
    late_sides = lon_halo(late_edges, odd)
    if len(chunks) == 1:
        g_top, g_bottom = lat_halo(*outer_rows, late_sides, first_lat)
    else:
        late_sides = late_sides + g_sides
    for r0, r1 in blocks:
        grad_input = input_part(
            grid, r0, r1, chunks, parts, late_sides, g_top, g_bottom, backward_weight,
            grad_input, True,
        )
    total = total / (cells * lax.axis_size("lat") * lax.axis_size("lon"))
    grad_weight = total[:fields, : 9 * channels].T.reshape(9, channels * fields)
    grad_bias = total[:fields, 9 * channels]
    return (grad_input.reshape(1, channels, 1, 1, cells), grad_weight, grad_bias)


def solution(mesh):
    placed = (P("member", None, "lat", "lon", None), P(), P(), P(None, "lat", "lon", None), P())
    return jax.shard_map(
        local,
        mesh=mesh,
        in_specs=placed,
        out_specs=(P("member", None, "lat", "lon", None), P(), P()),
        check_vma=False,
    )
```

```python
import functools

import jax
import jax.numpy as jnp
from jax import lax
from jax.experimental import pallas as pl
from jax.experimental.pallas import tpu as pltpu
from jax.sharding import PartitionSpec as P

LAT_DEV = 64
LANES = 128
ROW_GROUP = 2
FLAT_LANES = 1024
SLACK = 3 * 1024 * 1024
F32 = jnp.float32
BF16 = jnp.bfloat16


def round_up(value, step):
    return -(-value // step) * step


def params(*held):
    total = sum(round_up(rows, 16) * round_up(lanes, LANES) * size for rows, lanes, size in held)
    return pltpu.CompilerParams(vmem_limit_bytes=total + SLACK)


def kept_in_hbm(value):
    return pltpu.with_memory_space_constraint(value, pltpu.HBM)


def kept_in_vmem(value):
    return pltpu.with_memory_space_constraint(value, pltpu.VMEM)


def shape_of(dims, dtype=BF16):
    return jax.ShapeDtypeStruct(dims, dtype)


def cost(flops, moved):
    return pl.CostEstimate(flops=int(flops), bytes_accessed=int(moved), transcendentals=0)


def in_vmem():
    return pl.BlockSpec(memory_space=pltpu.VMEM)


def in_smem():
    return pl.BlockSpec(memory_space=pltpu.SMEM)


def in_hbm():
    return pl.BlockSpec(memory_space=pltpu.HBM)


def anywhere():
    return pl.BlockSpec(memory_space=pl.ANY)


def nt_dot(left, right):
    return lax.dot_general(left, right, (((1,), (1,)), ((), ())), preferred_element_type=F32)


class Grid:
    def __init__(self, cells, members):
        self.cells = cells
        self.columns = cells // LAT_DEV
        self.pitch = round_up(self.columns, LANES)
        self.halo = round_up(self.columns + 1, LANES)
        self.padded = round_up(cells, members * LANES)

    def rows(self, first, width):
        return first // self.columns, -(-min(first + width, self.cells) // self.columns)

    def layout(self, ranges):
        out, row, lane = [], 0, 0
        for first, width in ranges:
            r0, r1 = self.rows(first, width)
            out.append((first, width, r0, r1, row, lane))
            row, lane = row + r1 - r0 + 2, lane + width
        return out, row, lane


def take(ref, start, width):
    low = start // LANES * LANES
    off = start - low
    if off == 0:
        return ref[:, low : low + width]
    return ref[:, low : low + width + LANES][:, off : off + width]


def side_column(refs, grid, row, right):
    own, top, bottom = refs
    slot = LAT_DEV if right else 0
    if row < 0:
        ref, lane = top, grid.halo + slot + LAT_DEV - 1
    elif row >= LAT_DEV:
        ref, lane = bottom, grid.halo + slot
    else:
        ref, lane = own, slot + row
    return ref[:, lane : lane + 1]


def take_cells(sources, start, width):
    parts, at, end = [], start, start + width
    for ref, begin, last, lane in sorted(sources, key=lambda source: source[1]):
        shift = lane - begin
        base = (start + shift) // LANES * LANES
        if begin <= start and end <= last and base + width + LANES <= ref.shape[1]:
            return take(ref, start + shift, width)
        low, high = max(at, begin), min(end, last)
        if low < high:
            if low > at:
                parts.append(jnp.zeros((ref.shape[0], low - at), BF16))
            base = (low + shift) // LANES * LANES
            top = min(round_up(high + shift, LANES), ref.shape[1])
            parts.append(ref[:, base:top][:, low + shift - base : high + shift - base])
            at = high
    if at < end:
        parts.append(jnp.zeros((sources[0][0].shape[0], end - at), BF16))
    return jnp.concatenate(parts, axis=1) if len(parts) > 1 else parts[0]


def row_cells(grid, row, sources, top, bottom):
    if row < 0 and top is not None:
        return take_cells([(top, 0, top.shape[1], 0)], grid.halo - grid.columns, grid.pitch)
    if row >= LAT_DEV and bottom is not None:
        return take_cells([(bottom, 0, bottom.shape[1], 0)], 0, grid.pitch)
    return take_cells(sources, row * grid.columns, grid.pitch)


def build_taps(grid, origin, low, high, sources, sides, taps, backwards=False):
    rows = sources[0][0].shape[0]
    own, top, bottom = sides
    for row in range(low, high):
        base = (row - origin) * grid.pitch
        value = row_cells(grid, row, sources, top, bottom)
        left = side_column(sides, grid, row, False)
        right = side_column(sides, grid, row, True)
        before = jnp.concatenate([left, value[:, : grid.pitch - 1]], axis=1)
        after = [value[:, 1 : grid.columns], right]
        if grid.columns < grid.pitch:
            after.append(jnp.zeros((rows, grid.pitch - grid.columns), BF16))
        for b, part in enumerate((before, value, jnp.concatenate(after, axis=1))):
            block = pl.ds((2 - b if backwards else b) * rows, rows)
            taps[block, base : base + grid.pitch] = part


def stacked_rows(grid, taps, row, count, order=(0, 1, 2)):
    width = count * grid.pitch
    return jnp.concatenate(
        [taps[:, (row + a) * grid.pitch : (row + a) * grid.pitch + width] for a in order],
        axis=0,
    )


def groups_of(count, size=ROW_GROUP):
    return [(row, min(size, count - row)) for row in range(0, count, size)]


def flat_piece(grid, pitched, skip, low, high, count):
    parts, at = [], low
    while at < high:
        row, column = divmod(at + skip, grid.columns)
        if row >= count:
            parts.append(jnp.zeros((pitched.shape[0], high - at), BF16))
            break
        size = min(grid.columns - column, high - at)
        begin = row * grid.pitch + column
        parts.append(pitched[:, begin : begin + size])
        at += size
    return jnp.concatenate(parts, axis=1) if len(parts) > 1 else parts[0]


def convolve(grid, first, width, place, sources, sides, taps, weight, bias, pitched, flat,
             backwards=False, emit=None, fetch=None):
    r0, r1 = grid.rows(first, width)
    skip = first - r0 * grid.columns
    taps_row, lane = place
    built, done = r0 - 1, 0
    order = (2, 1, 0) if backwards else (0, 1, 2)
    for row, count in groups_of(r1 - r0):
        ready = min(r0 + row + count + 1 + ROW_GROUP, r1 + 1)
        if fetch is not None:
            fetch(ready)
        build_taps(
            grid, r0 - 1 - taps_row, built, ready, sources, sides, taps, backwards
        )
        built = ready
        stacked = stacked_rows(grid, taps, taps_row + row, count, order)
        value = jnp.dot(weight, stacked, preferred_element_type=F32)
        if bias is not None:
            value = value + bias
        pitched[:, row * grid.pitch : (row + count) * grid.pitch] = value.astype(BF16)
        last = row + count == r1 - r0
        while done < width:
            end = min(done + FLAT_LANES, width)
            if not last and end + skip > row * grid.columns:
                break
            piece = flat_piece(grid, pitched, skip, done, end, r1 - r0)
            flat[:, lane + done : lane + end] = piece
            if emit is not None:
                emit(done, end)
            done = end


def edges_kernel(grid, places, tiles, x_ref, out_ref, row_ref, held, sem, row_sem):
    last = jnp.where(lax.axis_index("lat") == 0, (grid.cells - grid.halo) // LANES, 0)
    row_copy = pltpu.make_async_copy(
        x_ref.at[:, pl.ds(pl.multiple_of(last * LANES, LANES), grid.halo)],
        row_ref,
        row_sem.at[0],
    )
    row_copy.start()
    copies = [
        pltpu.make_async_copy(
            x_ref.at[:, pl.ds(tile * LANES, LANES)],
            held.at[:, pl.ds(number * LANES, LANES)],
            sem.at[number],
        )
        for number, tile in enumerate(tiles)
    ]
    for copy in copies:
        copy.start()
    for copy in copies:
        copy.wait()
    columns = []
    for cell in places:
        at = tiles.index(cell // LANES) * LANES + cell % LANES
        columns.append(held[:, at : at + 1])
    out_ref[...] = jnp.concatenate(columns, axis=1)
    row_copy.wait()


def edges_of(grid, field):
    rows = field.shape[0]
    places = [i for i in range(0, grid.cells, grid.columns)]
    places += [i for i in range(grid.columns - 1, grid.cells, grid.columns)]
    tiles = sorted({cell // LANES for cell in places})
    return pl.pallas_call(
        functools.partial(edges_kernel, grid, places, tiles),
        in_specs=[in_hbm()],
        out_specs=[in_vmem()] * 2,
        out_shape=[shape_of((rows, 2 * LAT_DEV)), shape_of((rows, grid.halo))],
        scratch_shapes=[
            pltpu.VMEM((rows, len(tiles) * LANES), BF16),
            pltpu.SemaphoreType.DMA((len(tiles),)),
            pltpu.SemaphoreType.DMA((1,)),
        ],
        compiler_params=params((rows, (len(tiles) + 1) * LANES + grid.halo, 2)),
        cost_estimate=cost(rows, rows),
        name="edges",
    )(kept_in_hbm(field))


def lon_halo(edges, odd=None):
    peers = lax.axis_size("lon")
    first, last = edges[:, :LAT_DEV], edges[:, LAT_DEV:]
    if peers % 2 or odd is None:
        right = [(i, (i + 1) % peers) for i in range(peers)]
        left = [(j, i) for i, j in right]
        before, after = lax.ppermute(last, "lon", right), lax.ppermute(first, "lon", left)
        return jnp.concatenate([before, after], axis=1)
    near = [(i, i ^ 1) for i in range(peers)]
    far = [(i, (i + 1 if i % 2 else i - 1) % peers) for i in range(peers)]
    inner = lax.ppermute(jnp.where(odd, first, last), "lon", near)
    outer = lax.ppermute(jnp.where(odd, last, first), "lon", far)
    return jnp.where(
        odd,
        jnp.concatenate([inner, outer], axis=1),
        jnp.concatenate([outer, inner], axis=1),
    )


def lat_halo(first_rows, last_rows, sides, upper, chosen=None):
    peers = lax.axis_size("lat")
    if peers == 2:
        if chosen is None:
            chosen = jnp.where(upper, last_rows, first_rows)
        sent = jnp.concatenate([chosen, sides], axis=1)
        other = lax.ppermute(sent, "lat", [(0, 1), (1, 0)])
        none = jnp.zeros_like(other)
        return jnp.where(upper, none, other), jnp.where(upper, other, none)
    up = [(i, i + 1) for i in range(peers - 1)]
    down = [(j, i) for i, j in up]
    top = lax.ppermute(jnp.concatenate([last_rows, sides], axis=1), "lat", up)
    bottom = lax.ppermute(jnp.concatenate([first_rows, sides], axis=1), "lat", down)
    return top, bottom


def stages_of(grid, ranges):
    stages, got = [], []
    for first, width in ranges:
        r0, r1 = grid.rows(first, width)
        low = max((r0 - 1) * grid.columns - 1, 0) // LANES * LANES
        high = min(round_up((r1 + 1) * grid.columns + 1, LANES), grid.cells)
        low = max([low] + [end for begin, end in got if begin <= low])
        step = round_up(max((high - low) // 3, LANES), LANES)
        stages += [(at, min(at + step, high)) for at in range(low, high, step)]
        got.append((low, high))
    at = 0
    for low, high in sorted(got) + [(grid.cells, grid.cells)]:
        if at < low:
            stages.append((at, low))
        at = max(at, high)
    return stages


def forward_kernel(grid, ranges, has_top, has_bottom, members, load, waits, *refs):
    refs = list(refs)
    x_ref, sides_ref = refs[:2]
    del refs[:2]
    top_ref = refs.pop(0) if has_top else None
    bottom_ref = refs.pop(0) if has_bottom else None
    weight_ref, bias_ref, analysis_ref = refs[:3]
    del refs[: 3 + waits]
    outs = refs[:members]
    target_ref, taps = refs[members : members + 2]
    pitched, pred, target_sem, load_sem = refs[-4:]
    me = lax.axis_index("member")
    places, _, width = grid.layout(ranges)
    piece = width // members
    pending = []
    if load:
        held = refs[members + 2]
        for begin, end in stages_of(grid, ranges):
            copies = []
            for low in range(0, x_ref.shape[0], 32):
                at = (pl.ds(low, min(32, x_ref.shape[0] - low)), pl.ds(begin, end - begin))
                sem = load_sem.at[len(pending), len(copies)]
                copies.append(pltpu.make_async_copy(x_ref.at[at], held.at[at], sem))
                copies[-1].start()
            pending.append((begin, end, copies))
        x_ref = held

    def fetch(low, high):
        for stage in list(pending):
            if stage[0] < high * grid.columns + 1 and stage[1] > low * grid.columns - 1:
                for copy in stage[2]:
                    copy.wait()
                pending.remove(stage)

    each = members // len(ranges)
    index = me // each
    begin = places[0][0] + me * piece
    if len(ranges) > 1:
        begin = jnp.where(index == 0, begin, places[1][0] + (me - each) * piece)
    begin = pl.multiple_of(begin, LANES)
    target_copy = pltpu.make_async_copy(
        analysis_ref.at[:, pl.ds(begin, piece)], target_ref, target_sem.at[0]
    )
    target_copy.start()
    sides = (sides_ref, top_ref, bottom_ref)
    weight, bias = weight_ref[...], bias_ref[...]
    for first, size, r0, r1, row, lane in places:
        convolve(
            grid, first, size, (row, lane), [(x_ref, 0, grid.cells, 0)], sides, taps, weight,
            bias, pitched, pred, fetch=lambda ready, r0=r0: fetch(r0 - 1, ready),
        )
    for d in range(members):
        begin = pl.multiple_of((me ^ d) * piece, LANES)
        outs[d][...] = pred[:, pl.ds(begin, piece)]
    target_copy.wait()
    fetch(0, LAT_DEV)


def forward(
    grid, ranges, members, x, load, sides, top, bottom, weight, bias, analysis, after
):
    channels = x.shape[0]
    fields = weight.shape[0]
    places, tap_rows, width = grid.layout(ranges)
    most = max(place[3] - place[2] for place in places)
    has_top = any(place[2] == 0 for place in places)
    has_bottom = any(place[3] == LAT_DEV for place in places)
    piece = width // members
    held = (3 * channels, tap_rows * grid.pitch)
    operands = [kept_in_hbm(x) if load else kept_in_vmem(x), sides]
    if has_top:
        operands.append(top)
    if has_bottom:
        operands.append(bottom)
    operands += [weight, bias]
    specs = [in_hbm() if load else in_vmem()] + [in_vmem()] * (len(operands) - 1) + [in_hbm()]
    operands += [kept_in_hbm(analysis), *after]
    specs += [anywhere()] * len(after)
    shapes = [shape_of((fields, piece))] * (members + 1) + [pltpu.VMEM(held, BF16)]
    if load:
        shapes.append(pltpu.VMEM((channels, grid.cells), BF16))
    return pl.pallas_call(
        functools.partial(
            forward_kernel, grid, ranges, has_top, has_bottom, members, load, len(after)
        ),
        in_specs=specs,
        out_specs=[in_vmem()] * len(shapes),
        out_shape=shapes,
        scratch_shapes=[
            pltpu.VMEM((fields, most * grid.pitch), BF16),
            pltpu.VMEM((fields, width), BF16),
            pltpu.SemaphoreType.DMA((1,)),
            pltpu.SemaphoreType.DMA((12, -(-channels // 32))),
        ],
        compiler_params=params(
            (2 * fields, most * grid.pitch, 2),
            (2 * fields, 2 * width, 2),
            (fields, 9 * channels, 2),
        ),
        cost_estimate=cost(81 * channels * fields * width, 0),
        name=f"forward_{ranges[0][0]}",
    )(*operands)


def slope(values):
    return values * lax.rsqrt(values * values + 1.0)


def score_kernel(members, target_ref, scale_ref, *refs):
    pieces = refs[:members]
    outs = refs[-members:]
    fields, piece = pieces[0].shape
    tiles = piece // LANES
    several = max(k for k in (1, 2, 3) if tiles % k == 0)

    def tile(index, carry):
        for part in range(several * -(-fields // 16)):
            low = part // several * 16
            at = (index * several + part % several) * LANES
            span = pl.ds(pl.multiple_of(at, LANES), LANES)
            rows = pl.ds(low, min(16, fields - low))
            values = [ref[rows, span].astype(F32) for ref in pieces]
            target = target_ref[rows, span].astype(F32)
            scale = scale_ref[rows, :]
            sums = [None] * members
            for i in range(members):
                for j in range(i + 1, members):
                    both = slope(values[i] - values[j])
                    sums[i] = both if sums[i] is None else sums[i] + both
                    sums[j] = -both if sums[j] is None else sums[j] - both
            for i in range(members):
                grad = slope(values[i] - target) * (1.0 / members) - sums[i] * (
                    1.0 / (members * (members - 1))
                )
                outs[i][rows, span] = (scale * grad).astype(BF16)
        return carry

    lax.fori_loop(0, tiles // several, tile, 0)


def score(first, target, scale, pieces, after):
    members = len(pieces)
    fields, piece = pieces[0].shape
    return pl.pallas_call(
        functools.partial(score_kernel, members),
        in_specs=[in_vmem()] * (2 + members) + [anywhere()] * len(after),
        out_specs=[in_vmem()] * members,
        out_shape=[shape_of((fields, piece))] * members,
        compiler_params=params((9 * round_up(fields, 16), piece, 2), (fields, LANES, 4)),
        cost_estimate=cost(13000 * fields * piece, 0),
        name=f"score_{first}",
    )(target, scale, *pieces, *after)


def gather_kernel(grid, ranges, members, *refs):
    me = lax.axis_index("member")
    pieces = refs[:members]
    out_ref, edge_ref = refs[members:]
    fields, piece = pieces[0].shape
    rows, width = out_ref.shape
    base = fields // 16 * 16
    if base < rows:
        out_ref[pl.ds(base, rows - base), :] = jnp.zeros((rows - base, width), BF16)
    for d in range(members):
        begin = pl.multiple_of((me ^ d) * piece, LANES)
        value = pieces[d][...]
        if grid.padded != grid.cells:
            cell = lax.broadcasted_iota(jnp.int32, (1, piece), 1) + begin
            value = jnp.where(cell < grid.cells, value.astype(F32), 0.0).astype(BF16)
        out_ref[pl.ds(0, fields), pl.ds(begin, piece)] = value
    columns = []
    for side in (0, grid.columns - 1):
        for row in range(LAT_DEV):
            cell = row * grid.columns + side
            for first, size, *_, lane in grid.layout(ranges)[0]:
                if first <= cell < first + size:
                    at = lane + cell - first
                    columns.append(out_ref[:, at : at + 1])
                    break
            else:
                columns.append(jnp.zeros((rows, 1), BF16))
    edge_ref[...] = jnp.concatenate(columns, axis=1)


def gather(grid, ranges, rows, pieces, after):
    members = len(pieces)
    width = members * pieces[0].shape[1]

    def kernel(*refs):
        gather_kernel(grid, ranges, members, *refs[:members], *refs[-2:])

    return pl.pallas_call(
        kernel,
        in_specs=[in_vmem()] * members + [anywhere()] * len(after),
        out_specs=[in_vmem()] * 2,
        out_shape=[shape_of((rows, width)), shape_of((rows, 2 * LAT_DEV))],
        compiler_params=params((rows, 2 * width + 2 * LAT_DEV, 2)),
        cost_estimate=cost(width, 0),
        name=f"gather_{ranges[0][0]}",
    )(*pieces, *after)


def weight_kernel(grid, ranges, chained, waits, halves, taps, part_ref, *refs):
    before_ref = refs[0] if chained else None
    refs = refs[chained + waits :]
    pitched, sum_ref = refs[-1], refs[-2]
    rows = part_ref.shape[0]
    keep = jnp.where(
        lax.broadcasted_iota(jnp.int32, (1, LANES), 1) < grid.columns % LANES, 1.0, 0.0
    ).astype(BF16)
    started = False
    for first, width, r0, r1, taps_row, place in grid.layout(ranges)[0]:
        source = [(part_ref, first, first + width, place)]
        for row, count in groups_of(r1 - r0):
            for at in range(row, row + count):
                value = take_cells(source, (r0 + at) * grid.columns, grid.pitch)
                to = at * grid.pitch
                for lane in range(0, grid.pitch, LANES):
                    part = value[:, lane : lane + LANES]
                    if lane + LANES > grid.columns:
                        part = part * keep
                    pitched[:, to + lane : to + lane + LANES] = part
            stacked = stacked_rows(grid, taps, taps_row + row, count)
            lanes = round_up(stacked.shape[0] + 1, LANES)
            ones = jnp.ones((lanes - stacked.shape[0], stacked.shape[1]), BF16)
            part = nt_dot(
                pitched[:, row * grid.pitch : (row + count) * grid.pitch],
                jnp.concatenate([stacked, ones], axis=0),
            )
            if started:
                sum_ref[:, :lanes] += part
            else:
                sum_ref[:, :lanes] = part + before_ref[:, :lanes] if chained else part
            started = True
    if lanes < sum_ref.shape[1]:
        sum_ref[:, lanes:] = jnp.zeros((rows, sum_ref.shape[1] - lanes), F32)
    if halves:
        keep_ref, send_ref = refs[:2]
        half = rows // 2
        upper = lax.axis_index("lat") & 1
        keep_ref[...] = sum_ref[pl.ds(pl.multiple_of(upper * half, 8), half), :]
        send_ref[...] = sum_ref[pl.ds(pl.multiple_of((1 - upper) * half, 8), half), :]


def weight_part(grid, ranges, members, taps, part, before, after, halves):
    rows = part.shape[0]
    channels = taps.shape[0] // 3
    places, _, width = grid.layout(ranges)
    most = max(place[3] - place[2] for place in places)
    sums = round_up(9 * channels + 1, members * LANES)
    chained = [] if before is None else [before]
    whole = []
    if halves:
        shapes = [shape_of((rows // 2, sums), F32)] * 2
        whole = [pltpu.VMEM((rows, sums), F32)]
    else:
        shapes = [shape_of((rows, sums), F32)]
    return pl.pallas_call(
        functools.partial(weight_kernel, grid, ranges, len(chained), len(after), halves),
        in_specs=[in_vmem()] * (2 + len(chained)) + [anywhere()] * len(after),
        out_specs=[in_vmem()] * len(shapes),
        out_shape=shapes,
        scratch_shapes=whole + [pltpu.VMEM((rows, most * grid.pitch), BF16)],
        compiler_params=params(
            (rows, width, 2),
            (rows, most * grid.pitch, 2),
            (rows, 3 * sums, 4),
        ),
        cost_estimate=cost(width, 0),
        name=f"weight_{ranges[0][0]}",
    )(kept_in_vmem(taps), part, *chained, *after)


def input_kernel(grid, r0, r1, chunks, aliased, *refs):
    refs = list(refs)
    parts = refs[: len(chunks)]
    del refs[: len(chunks)]
    sides_ref, weight_ref = refs[:2]
    del refs[:2]
    top_ref = refs.pop(0) if r0 == 0 else None
    bottom_ref = refs.pop(0) if r1 == LAT_DEV else None
    del refs[:aliased]
    out_ref, taps, pitched, flat, out_sem = refs
    sources = []
    for ref, ranges in zip(parts, chunks):
        for first, width, *_, lane in grid.layout(ranges)[0]:
            sources.append((ref, first, min(first + width, grid.cells), lane))
    sides = (sides_ref, top_ref, bottom_ref)
    copies = []

    def emit(low, high):
        at = r0 * grid.columns + low
        copies.append(
            pltpu.make_async_copy(
                flat.at[:, pl.ds(low, high - low)],
                out_ref.at[:, pl.ds(at, high - low)],
                out_sem.at[len(copies)],
            )
        )
        copies[-1].start()

    width = (r1 - r0) * grid.columns
    convolve(
        grid, r0 * grid.columns, width, (0, 0), sources, sides, taps, weight_ref[...], None,
        pitched, flat, backwards=True, emit=emit,
    )
    for copy in copies:
        copy.wait()


def input_part(grid, r0, r1, chunks, parts, sides, top, bottom, weight, before, slow):
    rows = parts[0].shape[0]
    channels = weight.shape[0]
    width = (r1 - r0) * grid.columns
    held = (3 * rows, (r1 - r0 + 2) * grid.pitch)
    begin, end = (r0 - 1) * grid.columns - 1, (r1 + 1) * grid.columns + 1
    near = [
        (ranges, part)
        for ranges, part in zip(chunks, parts)
        if any(first < end and first + size > begin for first, size in ranges)
    ]
    chunks, parts = [pair[0] for pair in near], [pair[1] for pair in near]
    operands = [*parts, sides, weight] + [top] * (r0 == 0) + [bottom] * (r1 == LAT_DEV)
    specs = [in_vmem()] * len(operands)
    alias = {}
    if before is not None:
        alias = {len(operands): 0}
        operands.append(before)
        specs.append(anywhere())
    return pl.pallas_call(
        functools.partial(input_kernel, grid, r0, r1, chunks, len(alias)),
        in_specs=specs,
        out_specs=anywhere(),
        out_shape=shape_of((channels, grid.cells)),
        input_output_aliases=alias,
        scratch_shapes=[
            pltpu.VMEM(held, BF16),
            pltpu.VMEM((channels, (r1 - r0) * grid.pitch), BF16),
            pltpu.VMEM((channels, width), BF16),
            pltpu.SemaphoreType.DMA((-(-width // FLAT_LANES),)),
        ],
        compiler_params=params(
            (rows, sum(part.shape[1] for part in parts), 2),
            (*held, 2),
            (2 * channels, (r1 - r0) * grid.pitch, 2),
            (channels, 9 * rows, 2),
        ),
        cost_estimate=cost((80 if slow else 1) * channels * rows * width, width),
        name=f"input_{r0}",
    )(*operands)


def split_kernel(members, count, *refs):
    me = lax.axis_index("member")
    lanes = refs[count].shape[1]
    for d in range(members):
        span = pl.ds(pl.multiple_of((me ^ d) * lanes, LANES), lanes)
        total = refs[0][:, span]
        for ref in refs[1:count]:
            total += ref[:, span]
        refs[count + d][...] = total


def split_by_member(values, members):
    rows, lanes = values[0].shape
    return pl.pallas_call(
        functools.partial(split_kernel, members, len(values)),
        in_specs=[in_vmem()] * len(values),
        out_specs=[in_vmem()] * members,
        out_shape=[shape_of((rows, lanes // members), F32)] * members,
        compiler_params=params((rows, 3 * lanes, 4)),
        cost_estimate=cost(rows * lanes, 12 * rows * lanes),
        name="split",
    )(*values)


def join_kernel(members, *refs):
    me = lax.axis_index("member")
    lanes = refs[0].shape[1]
    for d in range(members):
        span = pl.ds(pl.multiple_of((me ^ d) * lanes, LANES), lanes)
        refs[members][:, span] = refs[d][...]


def join_members(pieces):
    members = len(pieces)
    rows, lanes = pieces[0].shape
    return pl.pallas_call(
        functools.partial(join_kernel, members),
        in_specs=[in_vmem()] * members,
        out_specs=in_vmem(),
        out_shape=shape_of((rows, members * lanes), F32),
        compiler_params=params((rows, 2 * members * lanes, 4)),
        cost_estimate=cost(rows * lanes, 12 * rows * lanes),
        name="join",
    )(*pieces)


def swap(value, axis, bits):
    return lax.ppermute(value, axis, [(i, i ^ bits) for i in range(lax.axis_size(axis))])


def sum_axis(value, axis, bit):
    size = lax.axis_size(axis)
    while bit < size:
        if 2 * bit < size:
            near, far, both = [swap(value, axis, k * bit) for k in (1, 2, 3)]
            value = (value + near) + (far + both)
        else:
            value = value + swap(value, axis, bit)
        bit *= 4
    return value


def sum_all(keep, send, upper, between):
    members = lax.axis_size("member")
    other = swap(send, "lat", 1)
    values = [keep, other]
    if lax.axis_size("lat") > 2:
        values = [sum_axis(keep + other, "lat", 2)]
    pieces = split_by_member(values, members)
    moved = [swap(pieces[d], "member", d) for d in range(1, members)]
    value = functools.reduce(jnp.add, moved, pieces[0])
    value = sum_axis(between(value), "lon", 1)
    value = between(value)
    half = join_members([value] + [swap(value, "member", d) for d in range(1, members)])
    other = swap(half, "lat", 1)
    total = jnp.where(
        upper,
        jnp.concatenate([other, half], axis=0),
        jnp.concatenate([half, other], axis=0),
    )
    return total


def weights_kernel(taps_ref, forward_ref, backward_ref):
    count, channels, fields = taps_ref.shape
    rows = backward_ref.shape[1] // count
    taps = [taps_ref[t] for t in range(count)]
    forward_ref[...] = jnp.concatenate(
        [tap.astype(F32).T for tap in taps], axis=1
    ).astype(BF16)
    none = [jnp.zeros((channels, rows - fields), BF16)] * (rows > fields)
    backward_ref[...] = jnp.concatenate([part for tap in taps for part in (tap, *none)], axis=1)


def prepare_weights(taps, rows):
    count, channels, fields = taps.shape
    return pl.pallas_call(
        weights_kernel,
        in_specs=[in_vmem()],
        out_specs=[in_vmem()] * 2,
        out_shape=[shape_of((fields, count * channels)), shape_of((channels, count * rows))],
        compiler_params=params((4 * channels, count * LANES, 4)),
        cost_estimate=cost(channels, 8 * count * channels * rows),
        name="weights",
    )(taps)


def chunks_of(grid, members):
    unit = members * LANES
    units = grid.padded // unit
    if units < 15 or grid.padded != grid.cells or members % 2:
        return [[(0, grid.padded)]]
    outer = (units // 2 + 2) // 2 * unit
    return [
        [(0, outer), (grid.cells - outer, outer)],
        [(outer, grid.cells - 2 * outer)],
    ]


def parts_of(grid, wanted):
    step = LAT_DEV // wanted
    if step * grid.columns % LANES:
        return [(0, LAT_DEV)]
    ranges = [(row, row + step) for row in range(0, LAT_DEV, step)]
    return ranges[1:-1] + [ranges[0], ranges[-1]]


def local(inputs, weight, bias, analysis, field_weight):
    channels, cells = inputs.shape[1], inputs.shape[4]
    fields = analysis.shape[0]
    members = lax.axis_size("member")
    grid = Grid(cells, members)
    x = inputs.reshape(channels, cells)
    target = analysis.reshape(fields, cells)
    if grid.padded != cells:
        target = jnp.pad(target, ((0, 0), (0, grid.padded - cells)))
    rows = round_up(fields, 16)
    taps = weight.reshape(9, channels, fields)
    forward_weight, backward_weight = prepare_weights(taps, rows)
    scale = jnp.broadcast_to(field_weight[:, None], (fields, LANES))
    shift = bias[:, None]
    upper = (lax.axis_index("lat") & 1) != 0
    odd = (lax.axis_index("lon") & 1) != 0
    x_edges, x_row = edges_of(grid, x)
    x_sides = lon_halo(x_edges)
    x_sides, forward_weight, backward_weight, scale, shift, upper, odd = (
        lax.optimization_barrier(
            (x_sides, forward_weight, backward_weight, scale, shift, upper, odd)
        )
    )
    first_lat = jnp.logical_not(upper)
    def to_members(pieces):
        moved = {0: pieces[0]}
        for d in range(members - 1, 0, -1):
            moved[d] = swap(pieces[d], "member", d)
        return [moved[d] for d in range(members)]

    chunks = chunks_of(grid, members)
    x_top, x_bottom = lat_halo(
        x[:, : grid.halo], x[:, cells - grid.halo :], x_sides, first_lat, x_row
    )
    received, targets, taken, held = [], [], [], None
    for ranges in chunks:
        out = forward(
            grid, ranges, members, x if held is None else held, held is None, x_sides, x_top,
            x_bottom, forward_weight, shift, target, [],
        )
        targets.append(out[members])
        taken.append(out[members + 1])
        held = out[members + 2] if held is None else held
        received.append(to_members(out[:members]))
    returned = []
    for ranges, pieces, goal in zip(chunks, received, targets):
        grads = score(ranges[0][0], goal, scale, pieces, targets[-1:])
        returned.append(to_members(grads))

    blocks = parts_of(grid, 4)
    parts, sums, grad_input = [], [None], None
    for number, ranges in enumerate(chunks):
        final = number == len(chunks) - 1
        after = [returned[-1][0]] if number == 0 else [kept_in_hbm(grad_input)]
        part, edge = gather(grid, ranges, rows, returned[number], after)
        sides = lon_halo(edge, odd)
        sums = weight_part(grid, ranges, members, taken[number], part, sums[0], [], final)
        sides, sums = lax.optimization_barrier((sides, list(sums)))
        parts.append(part)
        g_sides = sides if number == 0 else g_sides + sides
        if number == 0:
            end = part.shape[1] - grid.padded + cells
            outer_rows = (part[:, : grid.halo], part[:, end - grid.halo : end])
            g_top, g_bottom = lat_halo(*outer_rows, g_sides, first_lat)
        for _ in range(0 if final else 2):
            grad_input = input_part(
                grid, *blocks.pop(), chunks[:1], parts[:1], g_sides, g_top, g_bottom,
                backward_weight, grad_input, False,
            )

    def between(value):
        nonlocal grad_input
        for _ in range(min((len(blocks) + 1) // 2, len(blocks))):
            grad_input = input_part(
                grid, *blocks.pop(), chunks, parts, g_sides, g_top, g_bottom, backward_weight,
                grad_input, True,
            )
            value, grad_input = lax.optimization_barrier((value, grad_input))
        return value

    total = sum_all(*sums, upper, between)
    while blocks:
        grad_input = input_part(
            grid, *blocks.pop(), chunks, parts, g_sides, g_top, g_bottom, backward_weight,
            grad_input, True,
        )
    total = total / (cells * lax.axis_size("lat") * lax.axis_size("lon"))
    grad_weight = total[:fields, : 9 * channels].T.reshape(9, channels * fields)
    grad_bias = total[:fields, 9 * channels]
    return (grad_input.reshape(1, channels, 1, 1, cells), grad_weight, grad_bias)


def solution(mesh):
    placed = (P("member", None, "lat", "lon", None), P(), P(), P(None, "lat", "lon", None), P())
    return jax.shard_map(
        local,
        mesh=mesh,
        in_specs=placed,
        out_specs=(P("member", None, "lat", "lon", None), P(), P()),
        check_vma=False,
    )
```

```python
import functools

import jax
import jax.numpy as jnp
from jax import lax
from jax.experimental import pallas as pl
from jax.experimental.pallas import tpu as pltpu
from jax.sharding import PartitionSpec as P

LAT_DEV = 64
LANES = 128
ROW_GROUP = 2
FLAT_LANES = 1024
SLACK = 3 * 1024 * 1024
F32 = jnp.float32
BF16 = jnp.bfloat16


def round_up(value, step):
    return -(-value // step) * step


def params(*held):
    total = sum(round_up(rows, 16) * round_up(lanes, LANES) * size for rows, lanes, size in held)
    return pltpu.CompilerParams(vmem_limit_bytes=total + SLACK)


def kept_in_hbm(value):
    return pltpu.with_memory_space_constraint(value, pltpu.HBM)


def kept_in_vmem(value):
    return pltpu.with_memory_space_constraint(value, pltpu.VMEM)


def shape_of(dims, dtype=BF16):
    return jax.ShapeDtypeStruct(dims, dtype)


def cost(flops, moved):
    return pl.CostEstimate(flops=int(flops), bytes_accessed=int(moved), transcendentals=0)


def in_vmem():
    return pl.BlockSpec(memory_space=pltpu.VMEM)


def in_smem():
    return pl.BlockSpec(memory_space=pltpu.SMEM)


def in_hbm():
    return pl.BlockSpec(memory_space=pltpu.HBM)


def anywhere():
    return pl.BlockSpec(memory_space=pl.ANY)


def nt_dot(left, right):
    return lax.dot_general(left, right, (((1,), (1,)), ((), ())), preferred_element_type=F32)


class Grid:
    def __init__(self, cells, members):
        self.cells = cells
        self.columns = cells // LAT_DEV
        self.pitch = round_up(self.columns, LANES)
        self.halo = round_up(self.columns + 1, LANES)
        self.padded = round_up(cells, members * LANES)

    def rows(self, first, width):
        return first // self.columns, -(-min(first + width, self.cells) // self.columns)

    def layout(self, ranges):
        out, row, lane = [], 0, 0
        for first, width in ranges:
            r0, r1 = self.rows(first, width)
            out.append((first, width, r0, r1, row, lane))
            row, lane = row + r1 - r0 + 2, lane + width
        return out, row, lane


def take(ref, start, width):
    low = start // LANES * LANES
    off = start - low
    if off == 0:
        return ref[:, low : low + width]
    return ref[:, low : low + width + LANES][:, off : off + width]


def side_column(refs, grid, row, right):
    own, top, bottom = refs
    slot = LAT_DEV if right else 0
    if row < 0:
        ref, lane = top, grid.halo + slot + LAT_DEV - 1
    elif row >= LAT_DEV:
        ref, lane = bottom, grid.halo + slot
    else:
        ref, lane = own, slot + row
    return ref[:, lane : lane + 1]


def take_cells(sources, start, width):
    parts, at, end = [], start, start + width
    for ref, begin, last, lane in sorted(sources, key=lambda source: source[1]):
        shift = lane - begin
        base = (start + shift) // LANES * LANES
        if begin <= start and end <= last and base + width + LANES <= ref.shape[1]:
            return take(ref, start + shift, width)
        low, high = max(at, begin), min(end, last)
        if low < high:
            if low > at:
                parts.append(jnp.zeros((ref.shape[0], low - at), BF16))
            base = (low + shift) // LANES * LANES
            top = min(round_up(high + shift, LANES), ref.shape[1])
            parts.append(ref[:, base:top][:, low + shift - base : high + shift - base])
            at = high
    if at < end:
        parts.append(jnp.zeros((sources[0][0].shape[0], end - at), BF16))
    return jnp.concatenate(parts, axis=1) if len(parts) > 1 else parts[0]


def row_cells(grid, row, sources, top, bottom):
    if row < 0 and top is not None:
        return take_cells([(top, 0, top.shape[1], 0)], grid.halo - grid.columns, grid.pitch)
    if row >= LAT_DEV and bottom is not None:
        return take_cells([(bottom, 0, bottom.shape[1], 0)], 0, grid.pitch)
    return take_cells(sources, row * grid.columns, grid.pitch)


def build_taps(grid, origin, low, high, sources, sides, taps, backwards=False):
    rows = sources[0][0].shape[0]
    own, top, bottom = sides
    for row in range(low, high):
        base = (row - origin) * grid.pitch
        value = row_cells(grid, row, sources, top, bottom)
        left = side_column(sides, grid, row, False)
        right = side_column(sides, grid, row, True)
        before = jnp.concatenate([left, value[:, : grid.pitch - 1]], axis=1)
        after = [value[:, 1 : grid.columns], right]
        if grid.columns < grid.pitch:
            after.append(jnp.zeros((rows, grid.pitch - grid.columns), BF16))
        for b, part in enumerate((before, value, jnp.concatenate(after, axis=1))):
            block = pl.ds((2 - b if backwards else b) * rows, rows)
            taps[block, base : base + grid.pitch] = part


def stacked_rows(grid, taps, row, count, order=(0, 1, 2)):
    width = count * grid.pitch
    return jnp.concatenate(
        [taps[:, (row + a) * grid.pitch : (row + a) * grid.pitch + width] for a in order],
        axis=0,
    )


def groups_of(count, size=ROW_GROUP):
    return [(row, min(size, count - row)) for row in range(0, count, size)]


def flat_piece(grid, pitched, skip, low, high, count):
    parts, at = [], low
    while at < high:
        row, column = divmod(at + skip, grid.columns)
        if row >= count:
            parts.append(jnp.zeros((pitched.shape[0], high - at), BF16))
            break
        size = min(grid.columns - column, high - at)
        begin = row * grid.pitch + column
        parts.append(pitched[:, begin : begin + size])
        at += size
    return jnp.concatenate(parts, axis=1) if len(parts) > 1 else parts[0]


def convolve(grid, first, width, place, sources, sides, taps, weight, bias, pitched, flat,
             backwards=False, emit=None, fetch=None):
    r0, r1 = grid.rows(first, width)
    skip = first - r0 * grid.columns
    taps_row, lane = place
    built, done = r0 - 1, 0
    order = (2, 1, 0) if backwards else (0, 1, 2)
    for row, count in groups_of(r1 - r0):
        ready = min(r0 + row + count + 1 + ROW_GROUP, r1 + 1)
        if fetch is not None:
            fetch(ready)
        build_taps(
            grid, r0 - 1 - taps_row, built, ready, sources, sides, taps, backwards
        )
        built = ready
        stacked = stacked_rows(grid, taps, taps_row + row, count, order)
        value = jnp.dot(weight, stacked, preferred_element_type=F32)
        if bias is not None:
            value = value + bias
        pitched[:, row * grid.pitch : (row + count) * grid.pitch] = value.astype(BF16)
        last = row + count == r1 - r0
        while done < width:
            end = min(done + FLAT_LANES, width)
            if not last and end + skip > row * grid.columns:
                break
            piece = flat_piece(grid, pitched, skip, done, end, r1 - r0)
            flat[:, lane + done : lane + end] = piece
            if emit is not None:
                emit(done, end)
            done = end


def edges_kernel(grid, places, tiles, x_ref, out_ref, row_ref, held, sem, row_sem):
    last = jnp.where(lax.axis_index("lat") == 0, (grid.cells - grid.halo) // LANES, 0)
    row_copy = pltpu.make_async_copy(
        x_ref.at[:, pl.ds(pl.multiple_of(last * LANES, LANES), grid.halo)],
        row_ref,
        row_sem.at[0],
    )
    row_copy.start()
    copies = [
        pltpu.make_async_copy(
            x_ref.at[:, pl.ds(tile * LANES, LANES)],
            held.at[:, pl.ds(number * LANES, LANES)],
            sem.at[number],
        )
        for number, tile in enumerate(tiles)
    ]
    for copy in copies:
        copy.start()
    columns = {}
    for number, (tile, copy) in enumerate(zip(tiles, copies)):
        copy.wait()
        for cell in places:
            if cell // LANES == tile:
                at = number * LANES + cell % LANES
                columns[cell] = held[:, at : at + 1]
    out_ref[...] = jnp.concatenate([columns[cell] for cell in places], axis=1)
    row_copy.wait()


def edges_of(grid, field):
    rows = field.shape[0]
    places = [i for i in range(0, grid.cells, grid.columns)]
    places += [i for i in range(grid.columns - 1, grid.cells, grid.columns)]
    tiles = sorted({cell // LANES for cell in places})
    return pl.pallas_call(
        functools.partial(edges_kernel, grid, places, tiles),
        in_specs=[in_hbm()],
        out_specs=[in_vmem()] * 2,
        out_shape=[shape_of((rows, 2 * LAT_DEV)), shape_of((rows, grid.halo))],
        scratch_shapes=[
            pltpu.VMEM((rows, len(tiles) * LANES), BF16),
            pltpu.SemaphoreType.DMA((len(tiles),)),
            pltpu.SemaphoreType.DMA((1,)),
        ],
        compiler_params=params((rows, (len(tiles) + 1) * LANES + grid.halo, 2)),
        cost_estimate=cost(rows, rows),
        name="edges",
    )(kept_in_hbm(field))


def lon_halo(edges, odd=None):
    peers = lax.axis_size("lon")
    first, last = edges[:, :LAT_DEV], edges[:, LAT_DEV:]
    if peers % 2 or odd is None:
        right = [(i, (i + 1) % peers) for i in range(peers)]
        left = [(j, i) for i, j in right]
        before, after = lax.ppermute(last, "lon", right), lax.ppermute(first, "lon", left)
        return jnp.concatenate([before, after], axis=1)
    near = [(i, i ^ 1) for i in range(peers)]
    far = [(i, (i + 1 if i % 2 else i - 1) % peers) for i in range(peers)]
    inner = lax.ppermute(jnp.where(odd, first, last), "lon", near)
    outer = lax.ppermute(jnp.where(odd, last, first), "lon", far)
    return jnp.where(
        odd,
        jnp.concatenate([inner, outer], axis=1),
        jnp.concatenate([outer, inner], axis=1),
    )


def lat_halo(first_rows, last_rows, sides, upper, chosen=None):
    peers = lax.axis_size("lat")
    if peers == 2:
        if chosen is None:
            chosen = jnp.where(upper, last_rows, first_rows)
        sent = jnp.concatenate([chosen, sides], axis=1)
        other = lax.ppermute(sent, "lat", [(0, 1), (1, 0)])
        none = jnp.zeros_like(other)
        return jnp.where(upper, none, other), jnp.where(upper, other, none)
    up = [(i, i + 1) for i in range(peers - 1)]
    down = [(j, i) for i, j in up]
    top = lax.ppermute(jnp.concatenate([last_rows, sides], axis=1), "lat", up)
    bottom = lax.ppermute(jnp.concatenate([first_rows, sides], axis=1), "lat", down)
    return top, bottom


def stages_of(grid, ranges):
    stages, got = [], []
    for first, width in ranges:
        r0, r1 = grid.rows(first, width)
        low = max((r0 - 1) * grid.columns - 1, 0) // LANES * LANES
        high = min(round_up((r1 + 1) * grid.columns + 1, LANES), grid.cells)
        low = max([low] + [end for begin, end in got if begin <= low])
        step = round_up(max((high - low) // 3, LANES), LANES)
        stages += [(at, min(at + step, high)) for at in range(low, high, step)]
        got.append((low, high))
    at = 0
    for low, high in sorted(got) + [(grid.cells, grid.cells)]:
        if at < low:
            stages.append((at, low))
        at = max(at, high)
    return stages


def forward_kernel(grid, ranges, has_top, has_bottom, members, load, waits, *refs):
    refs = list(refs)
    x_ref, sides_ref = refs[:2]
    del refs[:2]
    top_ref = refs.pop(0) if has_top else None
    bottom_ref = refs.pop(0) if has_bottom else None
    weight_ref, bias_ref, analysis_ref = refs[:3]
    del refs[: 3 + waits]
    outs = refs[:members]
    target_ref, taps = refs[members : members + 2]
    pitched, pred, target_sem, load_sem = refs[-4:]
    me = lax.axis_index("member")
    places, _, width = grid.layout(ranges)
    piece = width // members
    pending = []
    if load:
        held = refs[members + 2]
        for begin, end in stages_of(grid, ranges):
            copies = []
            for low in range(0, x_ref.shape[0], 32):
                at = (pl.ds(low, min(32, x_ref.shape[0] - low)), pl.ds(begin, end - begin))
                sem = load_sem.at[len(pending), len(copies)]
                copies.append(pltpu.make_async_copy(x_ref.at[at], held.at[at], sem))
                copies[-1].start()
            pending.append((begin, end, copies))
        x_ref = held

    def fetch(low, high):
        for stage in list(pending):
            if stage[0] < high * grid.columns + 1 and stage[1] > low * grid.columns - 1:
                for copy in stage[2]:
                    copy.wait()
                pending.remove(stage)

    each = members // len(ranges)
    index = me // each
    begin = places[0][0] + me * piece
    if len(ranges) > 1:
        begin = jnp.where(index == 0, begin, places[1][0] + (me - each) * piece)
    begin = pl.multiple_of(begin, LANES)
    target_copy = pltpu.make_async_copy(
        analysis_ref.at[:, pl.ds(begin, piece)], target_ref, target_sem.at[0]
    )
    target_copy.start()
    sides = (sides_ref, top_ref, bottom_ref)
    weight, bias = weight_ref[...], bias_ref[...]
    for first, size, r0, r1, row, lane in places:
        convolve(
            grid, first, size, (row, lane), [(x_ref, 0, grid.cells, 0)], sides, taps, weight,
            bias, pitched, pred, fetch=lambda ready, r0=r0: fetch(r0 - 1, ready),
        )
    for d in range(members):
        begin = pl.multiple_of((me ^ d) * piece, LANES)
        outs[d][...] = pred[:, pl.ds(begin, piece)]
    target_copy.wait()
    fetch(0, LAT_DEV)


def forward(
    grid, ranges, members, x, load, sides, top, bottom, weight, bias, analysis, after
):
    channels = x.shape[0]
    fields = weight.shape[0]
    places, tap_rows, width = grid.layout(ranges)
    most = max(place[3] - place[2] for place in places)
    has_top = any(place[2] == 0 for place in places)
    has_bottom = any(place[3] == LAT_DEV for place in places)
    piece = width // members
    held = (3 * channels, tap_rows * grid.pitch)
    operands = [kept_in_hbm(x) if load else kept_in_vmem(x), sides]
    if has_top:
        operands.append(top)
    if has_bottom:
        operands.append(bottom)
    operands += [weight, bias]
    specs = [in_hbm() if load else in_vmem()] + [in_vmem()] * (len(operands) - 1) + [in_hbm()]
    operands += [kept_in_hbm(analysis), *after]
    specs += [anywhere()] * len(after)
    shapes = [shape_of((fields, piece))] * (members + 1) + [pltpu.VMEM(held, BF16)]
    if load:
        shapes.append(pltpu.VMEM((channels, grid.cells), BF16))
    return pl.pallas_call(
        functools.partial(
            forward_kernel, grid, ranges, has_top, has_bottom, members, load, len(after)
        ),
        in_specs=specs,
        out_specs=[in_vmem()] * len(shapes),
        out_shape=shapes,
        scratch_shapes=[
            pltpu.VMEM((fields, most * grid.pitch), BF16),
            pltpu.VMEM((fields, width), BF16),
            pltpu.SemaphoreType.DMA((1,)),
            pltpu.SemaphoreType.DMA((12, -(-channels // 32))),
        ],
        compiler_params=params(
            (2 * fields, most * grid.pitch, 2),
            (2 * fields, 2 * width, 2),
            (fields, 9 * channels, 2),
        ),
        cost_estimate=cost(81 * channels * fields * width, 0),
        name=f"forward_{ranges[0][0]}",
    )(*operands)


def slope(values):
    return values * lax.rsqrt(values * values + 1.0)


def score_kernel(members, target_ref, scale_ref, *refs):
    pieces = refs[:members]
    outs = refs[-members:]
    fields, piece = pieces[0].shape
    tiles = piece // LANES
    several = max(k for k in (1, 2, 3) if tiles % k == 0)

    def tile(index, carry):
        for part in range(several * -(-fields // 16)):
            low = part // several * 16
            at = (index * several + part % several) * LANES
            span = pl.ds(pl.multiple_of(at, LANES), LANES)
            rows = pl.ds(low, min(16, fields - low))
            values = [ref[rows, span].astype(F32) for ref in pieces]
            target = target_ref[rows, span].astype(F32)
            scale = scale_ref[rows, :]
            sums = [None] * members
            for i in range(members):
                for j in range(i + 1, members):
                    both = slope(values[i] - values[j])
                    sums[i] = both if sums[i] is None else sums[i] + both
                    sums[j] = -both if sums[j] is None else sums[j] - both
            for i in range(members):
                grad = slope(values[i] - target) * (1.0 / members) - sums[i] * (
                    1.0 / (members * (members - 1))
                )
                outs[i][rows, span] = (scale * grad).astype(BF16)
        return carry

    lax.fori_loop(0, tiles // several, tile, 0)


def score(first, target, scale, pieces, after):
    members = len(pieces)
    fields, piece = pieces[0].shape
    return pl.pallas_call(
        functools.partial(score_kernel, members),
        in_specs=[in_vmem()] * (2 + members) + [anywhere()] * len(after),
        out_specs=[in_vmem()] * members,
        out_shape=[shape_of((fields, piece))] * members,
        compiler_params=params((9 * round_up(fields, 16), piece, 2), (fields, LANES, 4)),
        cost_estimate=cost(13000 * fields * piece, 0),
        name=f"score_{first}",
    )(target, scale, *pieces, *after)


def gather_kernel(grid, ranges, members, *refs):
    me = lax.axis_index("member")
    pieces = refs[:members]
    out_ref, edge_ref = refs[members:]
    fields, piece = pieces[0].shape
    rows, width = out_ref.shape
    base = fields // 16 * 16
    if base < rows:
        out_ref[pl.ds(base, rows - base), :] = jnp.zeros((rows - base, width), BF16)
    for d in range(members):
        begin = pl.multiple_of((me ^ d) * piece, LANES)
        value = pieces[d][...]
        if grid.padded != grid.cells:
            cell = lax.broadcasted_iota(jnp.int32, (1, piece), 1) + begin
            value = jnp.where(cell < grid.cells, value.astype(F32), 0.0).astype(BF16)
        out_ref[pl.ds(0, fields), pl.ds(begin, piece)] = value
    columns = []
    for side in (0, grid.columns - 1):
        for row in range(LAT_DEV):
            cell = row * grid.columns + side
            for first, size, *_, lane in grid.layout(ranges)[0]:
                if first <= cell < first + size:
                    at = lane + cell - first
                    columns.append(out_ref[:, at : at + 1])
                    break
            else:
                columns.append(jnp.zeros((rows, 1), BF16))
    edge_ref[...] = jnp.concatenate(columns, axis=1)


def gather(grid, ranges, rows, pieces, after):
    members = len(pieces)
    width = members * pieces[0].shape[1]

    def kernel(*refs):
        gather_kernel(grid, ranges, members, *refs[:members], *refs[-2:])

    return pl.pallas_call(
        kernel,
        in_specs=[in_vmem()] * members + [anywhere()] * len(after),
        out_specs=[in_vmem()] * 2,
        out_shape=[shape_of((rows, width)), shape_of((rows, 2 * LAT_DEV))],
        compiler_params=params((rows, 2 * width + 2 * LAT_DEV, 2)),
        cost_estimate=cost(width, 0),
        name=f"gather_{ranges[0][0]}",
    )(*pieces, *after)


def weight_kernel(grid, ranges, chained, waits, halves, taps, part_ref, *refs):
    before_ref = refs[0] if chained else None
    refs = refs[chained + waits :]
    pitched, sum_ref = refs[-1], refs[-2]
    rows = part_ref.shape[0]
    keep = jnp.where(
        lax.broadcasted_iota(jnp.int32, (1, LANES), 1) < grid.columns % LANES, 1.0, 0.0
    ).astype(BF16)
    started = False
    for first, width, r0, r1, taps_row, place in grid.layout(ranges)[0]:
        source = [(part_ref, first, first + width, place)]
        for row, count in groups_of(r1 - r0):
            for at in range(row, row + count):
                value = take_cells(source, (r0 + at) * grid.columns, grid.pitch)
                to = at * grid.pitch
                for lane in range(0, grid.pitch, LANES):
                    part = value[:, lane : lane + LANES]
                    if lane + LANES > grid.columns:
                        part = part * keep
                    pitched[:, to + lane : to + lane + LANES] = part
            stacked = stacked_rows(grid, taps, taps_row + row, count)
            lanes = round_up(stacked.shape[0] + 1, LANES)
            ones = jnp.ones((lanes - stacked.shape[0], stacked.shape[1]), BF16)
            part = nt_dot(
                pitched[:, row * grid.pitch : (row + count) * grid.pitch],
                jnp.concatenate([stacked, ones], axis=0),
            )
            if started:
                sum_ref[:, :lanes] += part
            else:
                sum_ref[:, :lanes] = part + before_ref[:, :lanes] if chained else part
            started = True
    if lanes < sum_ref.shape[1]:
        sum_ref[:, lanes:] = jnp.zeros((rows, sum_ref.shape[1] - lanes), F32)
    if halves:
        keep_ref, send_ref = refs[:2]
        half = rows // 2
        upper = lax.axis_index("lat") & 1
        keep_ref[...] = sum_ref[pl.ds(pl.multiple_of(upper * half, 8), half), :]
        send_ref[...] = sum_ref[pl.ds(pl.multiple_of((1 - upper) * half, 8), half), :]


def weight_part(grid, ranges, members, taps, part, before, after, halves):
    rows = part.shape[0]
    channels = taps.shape[0] // 3
    places, _, width = grid.layout(ranges)
    most = max(place[3] - place[2] for place in places)
    sums = round_up(9 * channels + 1, members * LANES)
    chained = [] if before is None else [before]
    whole = []
    if halves:
        shapes = [shape_of((rows // 2, sums), F32)] * 2
        whole = [pltpu.VMEM((rows, sums), F32)]
    else:
        shapes = [shape_of((rows, sums), F32)]
    return pl.pallas_call(
        functools.partial(weight_kernel, grid, ranges, len(chained), len(after), halves),
        in_specs=[in_vmem()] * (2 + len(chained)) + [anywhere()] * len(after),
        out_specs=[in_vmem()] * len(shapes),
        out_shape=shapes,
        scratch_shapes=whole + [pltpu.VMEM((rows, most * grid.pitch), BF16)],
        compiler_params=params(
            (rows, width, 2),
            (rows, most * grid.pitch, 2),
            (rows, 3 * sums, 4),
        ),
        cost_estimate=cost(width, 0),
        name=f"weight_{ranges[0][0]}",
    )(kept_in_vmem(taps), part, *chained, *after)


def input_kernel(grid, r0, r1, chunks, aliased, *refs):
    refs = list(refs)
    parts = refs[: len(chunks)]
    del refs[: len(chunks)]
    sides_ref, weight_ref = refs[:2]
    del refs[:2]
    top_ref = refs.pop(0) if r0 == 0 else None
    bottom_ref = refs.pop(0) if r1 == LAT_DEV else None
    del refs[:aliased]
    out_ref, taps, pitched, flat, out_sem = refs
    sources = []
    for ref, ranges in zip(parts, chunks):
        for first, width, *_, lane in grid.layout(ranges)[0]:
            sources.append((ref, first, min(first + width, grid.cells), lane))
    sides = (sides_ref, top_ref, bottom_ref)
    copies = []

    def emit(low, high):
        at = r0 * grid.columns + low
        copies.append(
            pltpu.make_async_copy(
                flat.at[:, pl.ds(low, high - low)],
                out_ref.at[:, pl.ds(at, high - low)],
                out_sem.at[len(copies)],
            )
        )
        copies[-1].start()

    width = (r1 - r0) * grid.columns
    convolve(
        grid, r0 * grid.columns, width, (0, 0), sources, sides, taps, weight_ref[...], None,
        pitched, flat, backwards=True, emit=emit,
    )
    for copy in copies:
        copy.wait()


def input_part(grid, r0, r1, chunks, parts, sides, top, bottom, weight, before, slow):
    rows = parts[0].shape[0]
    channels = weight.shape[0]
    width = (r1 - r0) * grid.columns
    held = (3 * rows, (r1 - r0 + 2) * grid.pitch)
    begin, end = (r0 - 1) * grid.columns - 1, (r1 + 1) * grid.columns + 1
    near = [
        (ranges, part)
        for ranges, part in zip(chunks, parts)
        if any(first < end and first + size > begin for first, size in ranges)
    ]
    chunks, parts = [pair[0] for pair in near], [pair[1] for pair in near]
    operands = [*parts, sides, weight] + [top] * (r0 == 0) + [bottom] * (r1 == LAT_DEV)
    specs = [in_vmem()] * len(operands)
    alias = {}
    if before is not None:
        alias = {len(operands): 0}
        operands.append(before)
        specs.append(anywhere())
    return pl.pallas_call(
        functools.partial(input_kernel, grid, r0, r1, chunks, len(alias)),
        in_specs=specs,
        out_specs=anywhere(),
        out_shape=shape_of((channels, grid.cells)),
        input_output_aliases=alias,
        scratch_shapes=[
            pltpu.VMEM(held, BF16),
            pltpu.VMEM((channels, (r1 - r0) * grid.pitch), BF16),
            pltpu.VMEM((channels, width), BF16),
            pltpu.SemaphoreType.DMA((-(-width // FLAT_LANES),)),
        ],
        compiler_params=params(
            (rows, sum(part.shape[1] for part in parts), 2),
            (*held, 2),
            (2 * channels, (r1 - r0) * grid.pitch, 2),
            (channels, 9 * rows, 2),
        ),
        cost_estimate=cost((80 if slow else 1) * channels * rows * width, width),
        name=f"input_{r0}",
    )(*operands)


def split_kernel(members, count, *refs):
    me = lax.axis_index("member")
    lanes = refs[count].shape[1]
    for d in range(members):
        span = pl.ds(pl.multiple_of((me ^ d) * lanes, LANES), lanes)
        total = refs[0][:, span]
        for ref in refs[1:count]:
            total += ref[:, span]
        refs[count + d][...] = total


def split_by_member(values, members):
    rows, lanes = values[0].shape
    return pl.pallas_call(
        functools.partial(split_kernel, members, len(values)),
        in_specs=[in_vmem()] * len(values),
        out_specs=[in_vmem()] * members,
        out_shape=[shape_of((rows, lanes // members), F32)] * members,
        compiler_params=params((rows, 3 * lanes, 4)),
        cost_estimate=cost(rows * lanes, 12 * rows * lanes),
        name="split",
    )(*values)


def join_kernel(members, *refs):
    me = lax.axis_index("member")
    lanes = refs[0].shape[1]
    for d in range(members):
        span = pl.ds(pl.multiple_of((me ^ d) * lanes, LANES), lanes)
        refs[members][:, span] = refs[d][...]


def join_members(pieces):
    members = len(pieces)
    rows, lanes = pieces[0].shape
    return pl.pallas_call(
        functools.partial(join_kernel, members),
        in_specs=[in_vmem()] * members,
        out_specs=in_vmem(),
        out_shape=shape_of((rows, members * lanes), F32),
        compiler_params=params((rows, 2 * members * lanes, 4)),
        cost_estimate=cost(rows * lanes, 12 * rows * lanes),
        name="join",
    )(*pieces)


def swap(value, axis, bits):
    return lax.ppermute(value, axis, [(i, i ^ bits) for i in range(lax.axis_size(axis))])


def sum_axis(value, axis, bit):
    size = lax.axis_size(axis)
    while bit < size:
        if 2 * bit < size:
            near, far, both = [swap(value, axis, k * bit) for k in (1, 2, 3)]
            value = (value + near) + (far + both)
        else:
            value = value + swap(value, axis, bit)
        bit *= 4
    return value


def sum_all(keep, send, between):
    members = lax.axis_size("member")
    other = swap(send, "lat", 1)
    values = [keep, other]
    if lax.axis_size("lat") > 2:
        values = [sum_axis(keep + other, "lat", 2)]
    pieces = split_by_member(values, members)
    moved = [swap(pieces[d], "member", d) for d in range(1, members)]
    value = functools.reduce(jnp.add, moved, pieces[0])
    value = sum_axis(between(value), "lon", 1)
    value = between(value)
    moved = [swap(value, "member", d) for d in range(1, members)]
    moved[0] = between(moved[0])
    half = join_members([value, *moved])
    return half, swap(half, "lat", 1)


def finish_kernel(taps, channels, fields, scale, own_ref, other_ref, out_ref, bias_ref, rows_ref,
                  turned):
    upper = lax.axis_index("lat") & 1
    half = own_ref.shape[0]
    rows_ref[pl.ds(pl.multiple_of(upper * half, 8), half), :] = own_ref[...]
    rows_ref[pl.ds(pl.multiple_of((1 - upper) * half, 8), half), :] = other_ref[...]
    turned[...] = (rows_ref[:, : turned.shape[0]] * scale).T
    pieces = [
        turned[pl.ds(channel, taps, stride=channels), :][:, :fields]
        for channel in range(channels)
    ]
    out_ref[...] = jnp.concatenate(pieces, axis=1)
    bias_ref[...] = turned[pl.ds(taps * channels, 1), :][:, :fields]


def finish(own, other, taps, channels, fields, scale):
    half, lanes = own.shape
    used = round_up(taps * channels + 1, LANES)
    return pl.pallas_call(
        functools.partial(finish_kernel, taps, channels, fields, scale),
        in_specs=[in_vmem()] * 2,
        out_specs=[in_vmem()] * 2,
        out_shape=[shape_of((taps, channels * fields), F32), shape_of((1, fields), F32)],
        scratch_shapes=[
            pltpu.VMEM((2 * half, lanes), F32),
            pltpu.VMEM((used, 2 * half), F32),
        ],
        compiler_params=params((4 * half, lanes, 4), (used, LANES, 4), (16, channels * fields, 4)),
        cost_estimate=cost(lanes, 8 * half * lanes),
        name="finish",
    )(own, other)


def weights_kernel(taps_ref, forward_ref, backward_ref):
    count, channels, fields = taps_ref.shape
    rows = backward_ref.shape[1] // count
    taps = [taps_ref[t] for t in range(count)]
    forward_ref[...] = jnp.concatenate(
        [tap.astype(F32).T for tap in taps], axis=1
    ).astype(BF16)
    none = [jnp.zeros((channels, rows - fields), BF16)] * (rows > fields)
    backward_ref[...] = jnp.concatenate([part for tap in taps for part in (tap, *none)], axis=1)


def prepare_weights(taps, rows):
    count, channels, fields = taps.shape
    return pl.pallas_call(
        weights_kernel,
        in_specs=[in_vmem()],
        out_specs=[in_vmem()] * 2,
        out_shape=[shape_of((fields, count * channels)), shape_of((channels, count * rows))],
        compiler_params=params((4 * channels, count * LANES, 4)),
        cost_estimate=cost(channels, 8 * count * channels * rows),
        name="weights",
    )(taps)


def chunks_of(grid, members):
    unit = members * LANES
    units = grid.padded // unit
    if units < 15 or grid.padded != grid.cells or members % 2:
        return [[(0, grid.padded)]]
    outer = (units // 2 + 2) // 2 * unit
    return [
        [(0, outer), (grid.cells - outer, outer)],
        [(outer, grid.cells - 2 * outer)],
    ]


def parts_of(grid, wanted):
    step = LAT_DEV // wanted
    if step * grid.columns % LANES:
        return [(0, LAT_DEV)]
    ranges = [(row, row + step) for row in range(0, LAT_DEV, step)]
    return ranges[1:-1] + [ranges[0], ranges[-1]]


def local(inputs, weight, bias, analysis, field_weight):
    channels, cells = inputs.shape[1], inputs.shape[4]
    fields = analysis.shape[0]
    members = lax.axis_size("member")
    grid = Grid(cells, members)
    x = inputs.reshape(channels, cells)
    target = analysis.reshape(fields, cells)
    if grid.padded != cells:
        target = jnp.pad(target, ((0, 0), (0, grid.padded - cells)))
    rows = round_up(fields, 16)
    taps = weight.reshape(9, channels, fields)
    forward_weight, backward_weight = prepare_weights(taps, rows)
    scale = jnp.broadcast_to(field_weight[:, None], (fields, LANES))
    shift = bias[:, None]
    upper = (lax.axis_index("lat") & 1) != 0
    odd = (lax.axis_index("lon") & 1) != 0
    x_edges, x_row = edges_of(grid, x)
    x_sides = lon_halo(x_edges)
    x_sides, forward_weight, backward_weight, scale, shift, upper, odd = (
        lax.optimization_barrier(
            (x_sides, forward_weight, backward_weight, scale, shift, upper, odd)
        )
    )
    first_lat = jnp.logical_not(upper)
    def to_members(pieces):
        moved = {0: pieces[0]}
        for d in range(members - 1, 0, -1):
            moved[d] = swap(pieces[d], "member", d)
        return [moved[d] for d in range(members)]

    chunks = chunks_of(grid, members)
    x_top, x_bottom = lat_halo(
        x[:, : grid.halo], x[:, cells - grid.halo :], x_sides, first_lat, x_row
    )
    received, targets, taken, held = [], [], [], None
    for ranges in chunks:
        out = forward(
            grid, ranges, members, x if held is None else held, held is None, x_sides, x_top,
            x_bottom, forward_weight, shift, target, [],
        )
        targets.append(out[members])
        taken.append(out[members + 1])
        held = out[members + 2] if held is None else held
        received.append(to_members(out[:members]))
    returned = []
    for ranges, pieces, goal in zip(chunks, received, targets):
        grads = score(ranges[0][0], goal, scale, pieces, targets[-1:])
        returned.append(to_members(grads))

    blocks = parts_of(grid, 4)
    parts, sums, grad_input = [], [None], None
    for number, ranges in enumerate(chunks):
        final = number == len(chunks) - 1
        after = [returned[-1][0]] if number == 0 else [kept_in_hbm(grad_input)]
        part, edge = gather(grid, ranges, rows, returned[number], after)
        sides = lon_halo(edge, odd)
        sums = weight_part(grid, ranges, members, taken[number], part, sums[0], [], final)
        sides, sums = lax.optimization_barrier((sides, list(sums)))
        parts.append(part)
        g_sides = sides if number == 0 else g_sides + sides
        if number == 0:
            end = part.shape[1] - grid.padded + cells
            outer_rows = (part[:, : grid.halo], part[:, end - grid.halo : end])
            g_top, g_bottom = lat_halo(*outer_rows, g_sides, first_lat)
        for _ in range(0 if final else 1):
            grad_input = input_part(
                grid, *blocks.pop(), chunks[:1], parts[:1], g_sides, g_top, g_bottom,
                backward_weight, grad_input, False,
            )

    def between(value):
        nonlocal grad_input
        for _ in range(min(1, len(blocks))):
            grad_input = input_part(
                grid, *blocks.pop(), chunks, parts, g_sides, g_top, g_bottom, backward_weight,
                grad_input, True,
            )
            value, grad_input = lax.optimization_barrier((value, grad_input))
        return value

    own, other = sum_all(*sums, between)
    while blocks:
        grad_input = input_part(
            grid, *blocks.pop(), chunks, parts, g_sides, g_top, g_bottom, backward_weight,
            grad_input, True,
        )
    everywhere = cells * lax.axis_size("lat") * lax.axis_size("lon")
    grad_weight, grad_bias = finish(own, other, 9, channels, fields, 1.0 / everywhere)
    return (grad_input.reshape(1, channels, 1, 1, cells), grad_weight, grad_bias[0])


def solution(mesh):
    placed = (P("member", None, "lat", "lon", None), P(), P(), P(None, "lat", "lon", None), P())
    return jax.shard_map(
        local,
        mesh=mesh,
        in_specs=placed,
        out_specs=(P("member", None, "lat", "lon", None), P(), P()),
        check_vma=False,
    )
```

```python
import functools

import jax
import jax.numpy as jnp
from jax import lax
from jax.experimental import pallas as pl
from jax.experimental.pallas import tpu as pltpu
from jax.sharding import PartitionSpec as P

LAT_DEV = 64
LANES = 128
ROW_GROUP = 2
PRODUCT_ROWS = 4
FLAT_LANES = 1024
SLACK = 3 * 1024 * 1024
F32 = jnp.float32
BF16 = jnp.bfloat16


def round_up(value, step):
    return -(-value // step) * step


def params(*held):
    total = sum(round_up(rows, 16) * round_up(lanes, LANES) * size for rows, lanes, size in held)
    return pltpu.CompilerParams(vmem_limit_bytes=total + SLACK)


def kept_in_hbm(value):
    return pltpu.with_memory_space_constraint(value, pltpu.HBM)


def kept_in_vmem(value):
    return pltpu.with_memory_space_constraint(value, pltpu.VMEM)


def shape_of(dims, dtype=BF16):
    return jax.ShapeDtypeStruct(dims, dtype)


def cost(flops, moved):
    return pl.CostEstimate(flops=int(flops), bytes_accessed=int(moved), transcendentals=0)


def in_vmem():
    return pl.BlockSpec(memory_space=pltpu.VMEM)


def in_smem():
    return pl.BlockSpec(memory_space=pltpu.SMEM)


def in_hbm():
    return pl.BlockSpec(memory_space=pltpu.HBM)


def anywhere():
    return pl.BlockSpec(memory_space=pl.ANY)


def nt_dot(left, right):
    return lax.dot_general(left, right, (((1,), (1,)), ((), ())), preferred_element_type=F32)


class Grid:
    def __init__(self, cells, members):
        self.cells = cells
        self.columns = cells // LAT_DEV
        self.pitch = round_up(self.columns, LANES)
        self.halo = round_up(self.columns + 1, LANES)
        self.padded = round_up(cells, members * LANES)

    def rows(self, first, width):
        return first // self.columns, -(-min(first + width, self.cells) // self.columns)

    def layout(self, ranges):
        out, row, lane = [], 0, 0
        for first, width in ranges:
            r0, r1 = self.rows(first, width)
            out.append((first, width, r0, r1, row, lane))
            row, lane = row + r1 - r0 + 2, lane + width
        return out, row, lane


def take(ref, start, width):
    low = start // LANES * LANES
    off = start - low
    if off == 0:
        return ref[:, low : low + width]
    return ref[:, low : low + width + LANES][:, off : off + width]


def side_column(refs, grid, row, right):
    own, top, bottom = refs
    slot = LAT_DEV if right else 0
    if row < 0:
        ref, lane = top, grid.halo + slot + LAT_DEV - 1
    elif row >= LAT_DEV:
        ref, lane = bottom, grid.halo + slot
    else:
        ref, lane = own, slot + row
    return ref[:, lane : lane + 1]


def take_cells(sources, start, width):
    parts, at, end = [], start, start + width
    for ref, begin, last, lane in sorted(sources, key=lambda source: source[1]):
        shift = lane - begin
        base = (start + shift) // LANES * LANES
        if begin <= start and end <= last and base + width + LANES <= ref.shape[1]:
            return take(ref, start + shift, width)
        low, high = max(at, begin), min(end, last)
        if low < high:
            if low > at:
                parts.append(jnp.zeros((ref.shape[0], low - at), BF16))
            base = (low + shift) // LANES * LANES
            top = min(round_up(high + shift, LANES), ref.shape[1])
            parts.append(ref[:, base:top][:, low + shift - base : high + shift - base])
            at = high
    if at < end:
        parts.append(jnp.zeros((sources[0][0].shape[0], end - at), BF16))
    return jnp.concatenate(parts, axis=1) if len(parts) > 1 else parts[0]


def row_cells(grid, row, sources, top, bottom):
    if row < 0 and top is not None:
        return take_cells([(top, 0, top.shape[1], 0)], grid.halo - grid.columns, grid.pitch)
    if row >= LAT_DEV and bottom is not None:
        return take_cells([(bottom, 0, bottom.shape[1], 0)], 0, grid.pitch)
    return take_cells(sources, row * grid.columns, grid.pitch)


def build_taps(grid, origin, low, high, sources, sides, taps, backwards=False):
    rows = sources[0][0].shape[0]
    own, top, bottom = sides
    for row in range(low, high):
        base = (row - origin) * grid.pitch
        value = row_cells(grid, row, sources, top, bottom)
        left = side_column(sides, grid, row, False)
        right = side_column(sides, grid, row, True)
        before = jnp.concatenate([left, value[:, : grid.pitch - 1]], axis=1)
        after = [value[:, 1 : grid.columns], right]
        if grid.columns < grid.pitch:
            after.append(jnp.zeros((rows, grid.pitch - grid.columns), BF16))
        for b, part in enumerate((before, value, jnp.concatenate(after, axis=1))):
            block = pl.ds((2 - b if backwards else b) * rows, rows)
            taps[block, base : base + grid.pitch] = part


def stacked_rows(grid, taps, row, count, order=(0, 1, 2)):
    width = count * grid.pitch
    return jnp.concatenate(
        [taps[:, (row + a) * grid.pitch : (row + a) * grid.pitch + width] for a in order],
        axis=0,
    )


def groups_of(count, size=ROW_GROUP):
    return [(row, min(size, count - row)) for row in range(0, count, size)]


def flat_piece(grid, pitched, skip, low, high, count):
    parts, at = [], low
    while at < high:
        row, column = divmod(at + skip, grid.columns)
        if row >= count:
            parts.append(jnp.zeros((pitched.shape[0], high - at), BF16))
            break
        size = min(grid.columns - column, high - at)
        begin = row * grid.pitch + column
        parts.append(pitched[:, begin : begin + size])
        at += size
    return jnp.concatenate(parts, axis=1) if len(parts) > 1 else parts[0]


def convolve(grid, first, width, place, sources, sides, taps, weight, bias, pitched, flat,
             backwards=False, emit=None, fetch=None):
    r0, r1 = grid.rows(first, width)
    skip = first - r0 * grid.columns
    taps_row, lane = place
    built, done = r0 - 1, 0
    order = (2, 1, 0) if backwards else (0, 1, 2)
    for row, count in groups_of(r1 - r0, PRODUCT_ROWS):
        ready = min(r0 + row + count + 1 + ROW_GROUP, r1 + 1)
        if fetch is not None:
            fetch(ready)
        build_taps(
            grid, r0 - 1 - taps_row, built, ready, sources, sides, taps, backwards
        )
        built = ready
        stacked = stacked_rows(grid, taps, taps_row + row, count, order)
        value = jnp.dot(weight, stacked, preferred_element_type=F32)
        if bias is not None:
            value = value + bias
        pitched[:, row * grid.pitch : (row + count) * grid.pitch] = value.astype(BF16)
        last = row + count == r1 - r0
        while done < width:
            end = min(done + FLAT_LANES, width)
            if not last and end + skip > row * grid.columns:
                break
            piece = flat_piece(grid, pitched, skip, done, end, r1 - r0)
            flat[:, lane + done : lane + end] = piece
            if emit is not None:
                emit(done, end)
            done = end


def edges_kernel(grid, places, tiles, x_ref, out_ref, row_ref, held, sem, row_sem):
    last = jnp.where(lax.axis_index("lat") == 0, (grid.cells - grid.halo) // LANES, 0)
    row_copy = pltpu.make_async_copy(
        x_ref.at[:, pl.ds(pl.multiple_of(last * LANES, LANES), grid.halo)],
        row_ref,
        row_sem.at[0],
    )
    row_copy.start()
    copies = [
        pltpu.make_async_copy(
            x_ref.at[:, pl.ds(tile * LANES, LANES)],
            held.at[:, pl.ds(number * LANES, LANES)],
            sem.at[number],
        )
        for number, tile in enumerate(tiles)
    ]
    for copy in copies:
        copy.start()
    columns = {}
    for number, (tile, copy) in enumerate(zip(tiles, copies)):
        copy.wait()
        for cell in places:
            if cell // LANES == tile:
                at = number * LANES + cell % LANES
                columns[cell] = held[:, at : at + 1]
    out_ref[...] = jnp.concatenate([columns[cell] for cell in places], axis=1)
    row_copy.wait()


def edges_of(grid, field):
    rows = field.shape[0]
    places = [i for i in range(0, grid.cells, grid.columns)]
    places += [i for i in range(grid.columns - 1, grid.cells, grid.columns)]
    tiles = sorted({cell // LANES for cell in places})
    return pl.pallas_call(
        functools.partial(edges_kernel, grid, places, tiles),
        in_specs=[in_hbm()],
        out_specs=[in_vmem()] * 2,
        out_shape=[shape_of((rows, 2 * LAT_DEV)), shape_of((rows, grid.halo))],
        scratch_shapes=[
            pltpu.VMEM((rows, len(tiles) * LANES), BF16),
            pltpu.SemaphoreType.DMA((len(tiles),)),
            pltpu.SemaphoreType.DMA((1,)),
        ],
        compiler_params=params((rows, (len(tiles) + 1) * LANES + grid.halo, 2)),
        cost_estimate=cost(rows, rows),
        name="edges",
    )(kept_in_hbm(field))


def lon_halo(edges, odd=None):
    peers = lax.axis_size("lon")
    first, last = edges[:, :LAT_DEV], edges[:, LAT_DEV:]
    if peers % 2 or odd is None:
        right = [(i, (i + 1) % peers) for i in range(peers)]
        left = [(j, i) for i, j in right]
        before, after = lax.ppermute(last, "lon", right), lax.ppermute(first, "lon", left)
        return jnp.concatenate([before, after], axis=1)
    near = [(i, i ^ 1) for i in range(peers)]
    far = [(i, (i + 1 if i % 2 else i - 1) % peers) for i in range(peers)]
    inner = lax.ppermute(jnp.where(odd, first, last), "lon", near)
    outer = lax.ppermute(jnp.where(odd, last, first), "lon", far)
    return jnp.where(
        odd,
        jnp.concatenate([inner, outer], axis=1),
        jnp.concatenate([outer, inner], axis=1),
    )


def lat_halo(first_rows, last_rows, sides, upper, chosen=None):
    peers = lax.axis_size("lat")
    if peers == 2:
        if chosen is None:
            chosen = jnp.where(upper, last_rows, first_rows)
        sent = jnp.concatenate([chosen, sides], axis=1)
        other = lax.ppermute(sent, "lat", [(0, 1), (1, 0)])
        none = jnp.zeros_like(other)
        return jnp.where(upper, none, other), jnp.where(upper, other, none)
    up = [(i, i + 1) for i in range(peers - 1)]
    down = [(j, i) for i, j in up]
    top = lax.ppermute(jnp.concatenate([last_rows, sides], axis=1), "lat", up)
    bottom = lax.ppermute(jnp.concatenate([first_rows, sides], axis=1), "lat", down)
    return top, bottom


def stages_of(grid, ranges):
    stages, got = [], []
    for first, width in ranges:
        r0, r1 = grid.rows(first, width)
        low = max((r0 - 1) * grid.columns - 1, 0) // LANES * LANES
        high = min(round_up((r1 + 1) * grid.columns + 1, LANES), grid.cells)
        low = max([low] + [end for begin, end in got if begin <= low])
        step = round_up(max((high - low) // 3, LANES), LANES)
        stages += [(at, min(at + step, high)) for at in range(low, high, step)]
        got.append((low, high))
    at = 0
    for low, high in sorted(got) + [(grid.cells, grid.cells)]:
        if at < low:
            stages.append((at, low))
        at = max(at, high)
    return stages


def forward_kernel(grid, ranges, has_top, has_bottom, members, load, waits, *refs):
    refs = list(refs)
    x_ref, sides_ref = refs[:2]
    del refs[:2]
    top_ref = refs.pop(0) if has_top else None
    bottom_ref = refs.pop(0) if has_bottom else None
    weight_ref, bias_ref, analysis_ref = refs[:3]
    del refs[: 3 + waits]
    outs = refs[:members]
    target_ref, taps = refs[members : members + 2]
    pitched, pred, target_sem, load_sem = refs[-4:]
    me = lax.axis_index("member")
    places, _, width = grid.layout(ranges)
    piece = width // members
    pending = []
    if load:
        held = refs[members + 2]
        for begin, end in stages_of(grid, ranges):
            copies = []
            for low in range(0, x_ref.shape[0], 32):
                at = (pl.ds(low, min(32, x_ref.shape[0] - low)), pl.ds(begin, end - begin))
                sem = load_sem.at[len(pending), len(copies)]
                copies.append(pltpu.make_async_copy(x_ref.at[at], held.at[at], sem))
                copies[-1].start()
            pending.append((begin, end, copies))
        x_ref = held

    def fetch(low, high):
        for stage in list(pending):
            if stage[0] < high * grid.columns + 1 and stage[1] > low * grid.columns - 1:
                for copy in stage[2]:
                    copy.wait()
                pending.remove(stage)

    each = members // len(ranges)
    index = me // each
    begin = places[0][0] + me * piece
    if len(ranges) > 1:
        begin = jnp.where(index == 0, begin, places[1][0] + (me - each) * piece)
    begin = pl.multiple_of(begin, LANES)
    target_copy = pltpu.make_async_copy(
        analysis_ref.at[:, pl.ds(begin, piece)], target_ref, target_sem.at[0]
    )
    target_copy.start()
    sides = (sides_ref, top_ref, bottom_ref)
    weight, bias = weight_ref[...], bias_ref[...]
    for first, size, r0, r1, row, lane in places:
        convolve(
            grid, first, size, (row, lane), [(x_ref, 0, grid.cells, 0)], sides, taps, weight,
            bias, pitched, pred, fetch=lambda ready, r0=r0: fetch(r0 - 1, ready),
        )
    for d in range(members):
        begin = pl.multiple_of((me ^ d) * piece, LANES)
        outs[d][...] = pred[:, pl.ds(begin, piece)]
    target_copy.wait()
    fetch(0, LAT_DEV)


def forward(
    grid, ranges, members, x, load, sides, top, bottom, weight, bias, analysis, after
):
    channels = x.shape[0]
    fields = weight.shape[0]
    places, tap_rows, width = grid.layout(ranges)
    most = max(place[3] - place[2] for place in places)
    has_top = any(place[2] == 0 for place in places)
    has_bottom = any(place[3] == LAT_DEV for place in places)
    piece = width // members
    held = (3 * channels, tap_rows * grid.pitch)
    operands = [kept_in_hbm(x) if load else kept_in_vmem(x), sides]
    if has_top:
        operands.append(top)
    if has_bottom:
        operands.append(bottom)
    operands += [weight, bias]
    specs = [in_hbm() if load else in_vmem()] + [in_vmem()] * (len(operands) - 1) + [in_hbm()]
    operands += [kept_in_hbm(analysis), *after]
    specs += [anywhere()] * len(after)
    shapes = [shape_of((fields, piece))] * (members + 1) + [pltpu.VMEM(held, BF16)]
    if load:
        shapes.append(pltpu.VMEM((channels, grid.cells), BF16))
    return pl.pallas_call(
        functools.partial(
            forward_kernel, grid, ranges, has_top, has_bottom, members, load, len(after)
        ),
        in_specs=specs,
        out_specs=[in_vmem()] * len(shapes),
        out_shape=shapes,
        scratch_shapes=[
            pltpu.VMEM((fields, most * grid.pitch), BF16),
            pltpu.VMEM((fields, width), BF16),
            pltpu.SemaphoreType.DMA((1,)),
            pltpu.SemaphoreType.DMA((12, -(-channels // 32))),
        ],
        compiler_params=params(
            (2 * fields, most * grid.pitch, 2),
            (2 * fields, 2 * width, 2),
            (fields, 9 * channels, 2),
        ),
        cost_estimate=cost(81 * channels * fields * width, 0),
        name=f"forward_{ranges[0][0]}",
    )(*operands)


def slope(values):
    return values * lax.rsqrt(values * values + 1.0)


def score_kernel(members, target_ref, scale_ref, *refs):
    pieces = refs[:members]
    outs = refs[-members:]
    fields, piece = pieces[0].shape
    tiles = piece // LANES
    several = max(k for k in (1, 2, 3) if tiles % k == 0)

    def tile(index, carry):
        for part in range(several * -(-fields // 16)):
            low = part // several * 16
            at = (index * several + part % several) * LANES
            span = pl.ds(pl.multiple_of(at, LANES), LANES)
            rows = pl.ds(low, min(16, fields - low))
            values = [ref[rows, span].astype(F32) for ref in pieces]
            target = target_ref[rows, span].astype(F32)
            scale = scale_ref[rows, :]
            sums = [None] * members
            for i in range(members):
                for j in range(i + 1, members):
                    both = slope(values[i] - values[j])
                    sums[i] = both if sums[i] is None else sums[i] + both
                    sums[j] = -both if sums[j] is None else sums[j] - both
            for i in range(members):
                grad = slope(values[i] - target) * (1.0 / members) - sums[i] * (
                    1.0 / (members * (members - 1))
                )
                outs[i][rows, span] = (scale * grad).astype(BF16)
        return carry

    lax.fori_loop(0, tiles // several, tile, 0)


def score(first, target, scale, pieces, after):
    members = len(pieces)
    fields, piece = pieces[0].shape
    return pl.pallas_call(
        functools.partial(score_kernel, members),
        in_specs=[in_vmem()] * (2 + members) + [anywhere()] * len(after),
        out_specs=[in_vmem()] * members,
        out_shape=[shape_of((fields, piece))] * members,
        compiler_params=params((9 * round_up(fields, 16), piece, 2), (fields, LANES, 4)),
        cost_estimate=cost(13000 * fields * piece, 0),
        name=f"score_{first}",
    )(target, scale, *pieces, *after)


def gather_kernel(grid, ranges, members, *refs):
    me = lax.axis_index("member")
    pieces = refs[:members]
    out_ref, edge_ref = refs[members:]
    fields, piece = pieces[0].shape
    rows, width = out_ref.shape
    base = fields // 16 * 16
    if base < rows:
        out_ref[pl.ds(base, rows - base), :] = jnp.zeros((rows - base, width), BF16)
    for d in range(members):
        begin = pl.multiple_of((me ^ d) * piece, LANES)
        value = pieces[d][...]
        if grid.padded != grid.cells:
            cell = lax.broadcasted_iota(jnp.int32, (1, piece), 1) + begin
            value = jnp.where(cell < grid.cells, value.astype(F32), 0.0).astype(BF16)
        out_ref[pl.ds(0, fields), pl.ds(begin, piece)] = value
    columns = []
    for side in (0, grid.columns - 1):
        for row in range(LAT_DEV):
            cell = row * grid.columns + side
            for first, size, *_, lane in grid.layout(ranges)[0]:
                if first <= cell < first + size:
                    at = lane + cell - first
                    columns.append(out_ref[:, at : at + 1])
                    break
            else:
                columns.append(jnp.zeros((rows, 1), BF16))
    edge_ref[...] = jnp.concatenate(columns, axis=1)


def gather(grid, ranges, rows, pieces, after):
    members = len(pieces)
    width = members * pieces[0].shape[1]

    def kernel(*refs):
        gather_kernel(grid, ranges, members, *refs[:members], *refs[-2:])

    return pl.pallas_call(
        kernel,
        in_specs=[in_vmem()] * members + [anywhere()] * len(after),
        out_specs=[in_vmem()] * 2,
        out_shape=[shape_of((rows, width)), shape_of((rows, 2 * LAT_DEV))],
        compiler_params=params((rows, 2 * width + 2 * LAT_DEV, 2)),
        cost_estimate=cost(width, 0),
        name=f"gather_{ranges[0][0]}",
    )(*pieces, *after)


def weight_kernel(grid, ranges, chained, waits, halves, taps, part_ref, *refs):
    before_ref = refs[0] if chained else None
    refs = refs[chained + waits :]
    pitched, sum_ref = refs[-1], refs[-2]
    rows = part_ref.shape[0]
    keep = jnp.where(
        lax.broadcasted_iota(jnp.int32, (1, LANES), 1) < grid.columns % LANES, 1.0, 0.0
    ).astype(BF16)
    started = False
    for first, width, r0, r1, taps_row, place in grid.layout(ranges)[0]:
        source = [(part_ref, first, first + width, place)]
        for row, count in groups_of(r1 - r0):
            for at in range(row, row + count):
                value = take_cells(source, (r0 + at) * grid.columns, grid.pitch)
                to = at * grid.pitch
                for lane in range(0, grid.pitch, LANES):
                    part = value[:, lane : lane + LANES]
                    if lane + LANES > grid.columns:
                        part = part * keep
                    pitched[:, to + lane : to + lane + LANES] = part
            stacked = stacked_rows(grid, taps, taps_row + row, count)
            lanes = round_up(stacked.shape[0] + 1, LANES)
            ones = jnp.ones((lanes - stacked.shape[0], stacked.shape[1]), BF16)
            part = nt_dot(
                pitched[:, row * grid.pitch : (row + count) * grid.pitch],
                jnp.concatenate([stacked, ones], axis=0),
            )
            if started:
                sum_ref[:, :lanes] += part
            else:
                sum_ref[:, :lanes] = part + before_ref[:, :lanes] if chained else part
            started = True
    if lanes < sum_ref.shape[1]:
        sum_ref[:, lanes:] = jnp.zeros((rows, sum_ref.shape[1] - lanes), F32)
    if halves:
        keep_ref, send_ref = refs[:2]
        half = rows // 2
        upper = lax.axis_index("lat") & 1
        keep_ref[...] = sum_ref[pl.ds(pl.multiple_of(upper * half, 8), half), :]
        send_ref[...] = sum_ref[pl.ds(pl.multiple_of((1 - upper) * half, 8), half), :]


def weight_part(grid, ranges, members, taps, part, before, after, halves):
    rows = part.shape[0]
    channels = taps.shape[0] // 3
    places, _, width = grid.layout(ranges)
    most = max(place[3] - place[2] for place in places)
    sums = round_up(9 * channels + 1, members * LANES)
    chained = [] if before is None else [before]
    whole = []
    if halves:
        shapes = [shape_of((rows // 2, sums), F32)] * 2
        whole = [pltpu.VMEM((rows, sums), F32)]
    else:
        shapes = [shape_of((rows, sums), F32)]
    return pl.pallas_call(
        functools.partial(weight_kernel, grid, ranges, len(chained), len(after), halves),
        in_specs=[in_vmem()] * (2 + len(chained)) + [anywhere()] * len(after),
        out_specs=[in_vmem()] * len(shapes),
        out_shape=shapes,
        scratch_shapes=whole + [pltpu.VMEM((rows, most * grid.pitch), BF16)],
        compiler_params=params(
            (rows, width, 2),
            (rows, most * grid.pitch, 2),
            (rows, 3 * sums, 4),
        ),
        cost_estimate=cost(width, 0),
        name=f"weight_{ranges[0][0]}",
    )(kept_in_vmem(taps), part, *chained, *after)


def input_kernel(grid, r0, r1, chunks, aliased, *refs):
    refs = list(refs)
    parts = refs[: len(chunks)]
    del refs[: len(chunks)]
    sides_ref, weight_ref = refs[:2]
    del refs[:2]
    top_ref = refs.pop(0) if r0 == 0 else None
    bottom_ref = refs.pop(0) if r1 == LAT_DEV else None
    del refs[:aliased]
    out_ref, taps, pitched, flat, out_sem = refs
    sources = []
    for ref, ranges in zip(parts, chunks):
        for first, width, *_, lane in grid.layout(ranges)[0]:
            sources.append((ref, first, min(first + width, grid.cells), lane))
    sides = (sides_ref, top_ref, bottom_ref)
    copies = []

    def emit(low, high):
        at = r0 * grid.columns + low
        copies.append(
            pltpu.make_async_copy(
                flat.at[:, pl.ds(low, high - low)],
                out_ref.at[:, pl.ds(at, high - low)],
                out_sem.at[len(copies)],
            )
        )
        copies[-1].start()

    width = (r1 - r0) * grid.columns
    convolve(
        grid, r0 * grid.columns, width, (0, 0), sources, sides, taps, weight_ref[...], None,
        pitched, flat, backwards=True, emit=emit,
    )
    for copy in copies:
        copy.wait()


def input_part(grid, r0, r1, chunks, parts, sides, top, bottom, weight, before, slow):
    rows = parts[0].shape[0]
    channels = weight.shape[0]
    width = (r1 - r0) * grid.columns
    held = (3 * rows, (r1 - r0 + 2) * grid.pitch)
    begin, end = (r0 - 1) * grid.columns - 1, (r1 + 1) * grid.columns + 1
    near = [
        (ranges, part)
        for ranges, part in zip(chunks, parts)
        if any(first < end and first + size > begin for first, size in ranges)
    ]
    chunks, parts = [pair[0] for pair in near], [pair[1] for pair in near]
    operands = [*parts, sides, weight] + [top] * (r0 == 0) + [bottom] * (r1 == LAT_DEV)
    specs = [in_vmem()] * len(operands)
    alias = {}
    if before is not None:
        alias = {len(operands): 0}
        operands.append(before)
        specs.append(anywhere())
    return pl.pallas_call(
        functools.partial(input_kernel, grid, r0, r1, chunks, len(alias)),
        in_specs=specs,
        out_specs=anywhere(),
        out_shape=shape_of((channels, grid.cells)),
        input_output_aliases=alias,
        scratch_shapes=[
            pltpu.VMEM(held, BF16),
            pltpu.VMEM((channels, (r1 - r0) * grid.pitch), BF16),
            pltpu.VMEM((channels, width), BF16),
            pltpu.SemaphoreType.DMA((-(-width // FLAT_LANES),)),
        ],
        compiler_params=params(
            (rows, sum(part.shape[1] for part in parts), 2),
            (*held, 2),
            (2 * channels, (r1 - r0) * grid.pitch, 2),
            (channels, 9 * rows, 2),
        ),
        cost_estimate=cost((80 if slow else 1) * channels * rows * width, width),
        name=f"input_{r0}",
    )(*operands)


def split_kernel(members, count, *refs):
    me = lax.axis_index("member")
    lanes = refs[count].shape[1]
    for d in range(members):
        span = pl.ds(pl.multiple_of((me ^ d) * lanes, LANES), lanes)
        total = refs[0][:, span]
        for ref in refs[1:count]:
            total += ref[:, span]
        refs[count + d][...] = total


def split_by_member(values, members):
    rows, lanes = values[0].shape
    return pl.pallas_call(
        functools.partial(split_kernel, members, len(values)),
        in_specs=[in_vmem()] * len(values),
        out_specs=[in_vmem()] * members,
        out_shape=[shape_of((rows, lanes // members), F32)] * members,
        compiler_params=params((rows, 3 * lanes, 4)),
        cost_estimate=cost(rows * lanes, 12 * rows * lanes),
        name="split",
    )(*values)


def join_kernel(members, *refs):
    me = lax.axis_index("member")
    lanes = refs[0].shape[1]
    for d in range(members):
        span = pl.ds(pl.multiple_of((me ^ d) * lanes, LANES), lanes)
        refs[members][:, span] = refs[d][...]


def join_members(pieces):
    members = len(pieces)
    rows, lanes = pieces[0].shape
    return pl.pallas_call(
        functools.partial(join_kernel, members),
        in_specs=[in_vmem()] * members,
        out_specs=in_vmem(),
        out_shape=shape_of((rows, members * lanes), F32),
        compiler_params=params((rows, 2 * members * lanes, 4)),
        cost_estimate=cost(rows * lanes, 12 * rows * lanes),
        name="join",
    )(*pieces)


def swap(value, axis, bits):
    return lax.ppermute(value, axis, [(i, i ^ bits) for i in range(lax.axis_size(axis))])


def sum_axis(value, axis, bit):
    size = lax.axis_size(axis)
    while bit < size:
        if 2 * bit < size:
            near, far, both = [swap(value, axis, k * bit) for k in (1, 2, 3)]
            value = (value + near) + (far + both)
        else:
            value = value + swap(value, axis, bit)
        bit *= 4
    return value


def sum_all(keep, send, between):
    members = lax.axis_size("member")
    other = swap(send, "lat", 1)
    values = [keep, other]
    if lax.axis_size("lat") > 2:
        values = [sum_axis(keep + other, "lat", 2)]
    pieces = split_by_member(values, members)
    moved = [swap(pieces[d], "member", d) for d in range(1, members)]
    value = functools.reduce(jnp.add, moved, pieces[0])
    value = sum_axis(between(value), "lon", 1)
    value = between(value)
    moved = [swap(value, "member", d) for d in range(1, members)]
    moved[0] = between(moved[0])
    half = join_members([value, *moved])
    return half, swap(half, "lat", 1)


def finish_kernel(taps, channels, fields, scale, own_ref, other_ref, out_ref, bias_ref, rows_ref,
                  turned):
    upper = lax.axis_index("lat") & 1
    half = own_ref.shape[0]
    rows_ref[pl.ds(pl.multiple_of(upper * half, 8), half), :] = own_ref[...]
    rows_ref[pl.ds(pl.multiple_of((1 - upper) * half, 8), half), :] = other_ref[...]
    turned[...] = (rows_ref[:, : turned.shape[0]] * scale).T
    pieces = [
        turned[pl.ds(channel, taps, stride=channels), :][:, :fields]
        for channel in range(channels)
    ]
    out_ref[...] = jnp.concatenate(pieces, axis=1)
    bias_ref[...] = turned[pl.ds(taps * channels, 1), :][:, :fields]


def finish(own, other, taps, channels, fields, scale):
    half, lanes = own.shape
    used = round_up(taps * channels + 1, LANES)
    return pl.pallas_call(
        functools.partial(finish_kernel, taps, channels, fields, scale),
        in_specs=[in_vmem()] * 2,
        out_specs=[in_vmem()] * 2,
        out_shape=[shape_of((taps, channels * fields), F32), shape_of((1, fields), F32)],
        scratch_shapes=[
            pltpu.VMEM((2 * half, lanes), F32),
            pltpu.VMEM((used, 2 * half), F32),
        ],
        compiler_params=params((4 * half, lanes, 4), (used, LANES, 4), (16, channels * fields, 4)),
        cost_estimate=cost(lanes, 8 * half * lanes),
        name="finish",
    )(own, other)


def weights_kernel(taps_ref, forward_ref, backward_ref):
    count, channels, fields = taps_ref.shape
    rows = backward_ref.shape[1] // count
    taps = [taps_ref[t] for t in range(count)]
    forward_ref[...] = jnp.concatenate(
        [tap.astype(F32).T for tap in taps], axis=1
    ).astype(BF16)
    none = [jnp.zeros((channels, rows - fields), BF16)] * (rows > fields)
    backward_ref[...] = jnp.concatenate([part for tap in taps for part in (tap, *none)], axis=1)


def prepare_weights(taps, rows):
    count, channels, fields = taps.shape
    return pl.pallas_call(
        weights_kernel,
        in_specs=[in_vmem()],
        out_specs=[in_vmem()] * 2,
        out_shape=[shape_of((fields, count * channels)), shape_of((channels, count * rows))],
        compiler_params=params((4 * channels, count * LANES, 4)),
        cost_estimate=cost(channels, 8 * count * channels * rows),
        name="weights",
    )(taps)


def chunks_of(grid, members):
    unit = members * LANES
    units = grid.padded // unit
    if units < 15 or grid.padded != grid.cells or members % 2:
        return [[(0, grid.padded)]]
    outer = (units // 2 + 2) // 2 * unit
    return [
        [(0, outer), (grid.cells - outer, outer)],
        [(outer, grid.cells - 2 * outer)],
    ]


def parts_of(grid, wanted):
    step = LAT_DEV // wanted
    if step * grid.columns % LANES:
        return [(0, LAT_DEV)]
    ranges = [(row, row + step) for row in range(0, LAT_DEV, step)]
    return ranges[1:-1] + [ranges[0], ranges[-1]]


def local(inputs, weight, bias, analysis, field_weight):
    channels, cells = inputs.shape[1], inputs.shape[4]
    fields = analysis.shape[0]
    members = lax.axis_size("member")
    grid = Grid(cells, members)
    x = inputs.reshape(channels, cells)
    target = analysis.reshape(fields, cells)
    if grid.padded != cells:
        target = jnp.pad(target, ((0, 0), (0, grid.padded - cells)))
    rows = round_up(fields, 16)
    taps = weight.reshape(9, channels, fields)
    forward_weight, backward_weight = prepare_weights(taps, rows)
    scale = jnp.broadcast_to(field_weight[:, None], (fields, LANES))
    shift = bias[:, None]
    upper = (lax.axis_index("lat") & 1) != 0
    odd = (lax.axis_index("lon") & 1) != 0
    x_edges, x_row = edges_of(grid, x)
    x_sides = lon_halo(x_edges)
    x_sides, forward_weight, backward_weight, scale, shift, upper, odd = (
        lax.optimization_barrier(
            (x_sides, forward_weight, backward_weight, scale, shift, upper, odd)
        )
    )
    first_lat = jnp.logical_not(upper)
    def to_members(pieces):
        moved = {0: pieces[0]}
        for d in range(members - 1, 0, -1):
            moved[d] = swap(pieces[d], "member", d)
        return [moved[d] for d in range(members)]

    chunks = chunks_of(grid, members)
    x_top, x_bottom = lat_halo(
        x[:, : grid.halo], x[:, cells - grid.halo :], x_sides, first_lat, x_row
    )
    received, targets, taken, held = [], [], [], None
    for ranges in chunks:
        out = forward(
            grid, ranges, members, x if held is None else held, held is None, x_sides, x_top,
            x_bottom, forward_weight, shift, target, [],
        )
        targets.append(out[members])
        taken.append(out[members + 1])
        held = out[members + 2] if held is None else held
        received.append(to_members(out[:members]))
    returned = []
    for ranges, pieces, goal in zip(chunks, received, targets):
        grads = score(ranges[0][0], goal, scale, pieces, targets[-1:])
        returned.append(to_members(grads))

    blocks = parts_of(grid, 4)
    parts, sums, grad_input = [], [None], None
    for number, ranges in enumerate(chunks):
        final = number == len(chunks) - 1
        after = [returned[-1][0]] if number == 0 else [kept_in_hbm(grad_input)]
        part, edge = gather(grid, ranges, rows, returned[number], after)
        sides = lon_halo(edge, odd)
        sums = weight_part(grid, ranges, members, taken[number], part, sums[0], [], final)
        sides, sums = lax.optimization_barrier((sides, list(sums)))
        parts.append(part)
        g_sides = sides if number == 0 else g_sides + sides
        if number == 0:
            end = part.shape[1] - grid.padded + cells
            outer_rows = (part[:, : grid.halo], part[:, end - grid.halo : end])
            g_top, g_bottom = lat_halo(*outer_rows, g_sides, first_lat)
        for _ in range(0 if final else 1):
            grad_input = input_part(
                grid, *blocks.pop(), chunks[:1], parts[:1], g_sides, g_top, g_bottom,
                backward_weight, grad_input, False,
            )

    def between(value):
        nonlocal grad_input
        for _ in range(min(1, len(blocks))):
            grad_input = input_part(
                grid, *blocks.pop(), chunks, parts, g_sides, g_top, g_bottom, backward_weight,
                grad_input, True,
            )
            value, grad_input = lax.optimization_barrier((value, grad_input))
        return value

    own, other = sum_all(*sums, between)
    while blocks:
        grad_input = input_part(
            grid, *blocks.pop(), chunks, parts, g_sides, g_top, g_bottom, backward_weight,
            grad_input, True,
        )
    everywhere = cells * lax.axis_size("lat") * lax.axis_size("lon")
    grad_weight, grad_bias = finish(own, other, 9, channels, fields, 1.0 / everywhere)
    return (grad_input.reshape(1, channels, 1, 1, cells), grad_weight, grad_bias[0])


def solution(mesh):
    placed = (P("member", None, "lat", "lon", None), P(), P(), P(None, "lat", "lon", None), P())
    return jax.shard_map(
        local,
        mesh=mesh,
        in_specs=placed,
        out_specs=(P("member", None, "lat", "lon", None), P(), P()),
        check_vma=False,
    )
```

```python
import functools

import jax
import jax.numpy as jnp
from jax import lax
from jax.experimental import pallas as pl
from jax.experimental.pallas import tpu as pltpu
from jax.sharding import PartitionSpec as P

LAT_DEV = 64
LANES = 128
ROW_GROUP = 2
PRODUCT_ROWS = 4
FLAT_LANES = 1024
SLACK = 3 * 1024 * 1024
F32 = jnp.float32
BF16 = jnp.bfloat16


def round_up(value, step):
    return -(-value // step) * step


def params(*held):
    total = sum(round_up(rows, 16) * round_up(lanes, LANES) * size for rows, lanes, size in held)
    return pltpu.CompilerParams(vmem_limit_bytes=total + SLACK)


def kept_in_hbm(value):
    return pltpu.with_memory_space_constraint(value, pltpu.HBM)


def kept_in_vmem(value):
    return pltpu.with_memory_space_constraint(value, pltpu.VMEM)


def shape_of(dims, dtype=BF16):
    return jax.ShapeDtypeStruct(dims, dtype)


def cost(flops, moved):
    return pl.CostEstimate(flops=int(flops), bytes_accessed=int(moved), transcendentals=0)


def in_vmem():
    return pl.BlockSpec(memory_space=pltpu.VMEM)


def in_smem():
    return pl.BlockSpec(memory_space=pltpu.SMEM)


def in_hbm():
    return pl.BlockSpec(memory_space=pltpu.HBM)


def anywhere():
    return pl.BlockSpec(memory_space=pl.ANY)


def nt_dot(left, right):
    return lax.dot_general(left, right, (((1,), (1,)), ((), ())), preferred_element_type=F32)


class Grid:
    def __init__(self, cells, members):
        self.cells = cells
        self.columns = cells // LAT_DEV
        self.pitch = round_up(self.columns, LANES)
        self.halo = round_up(self.columns + 1, LANES)
        self.padded = round_up(cells, members * LANES)

    def rows(self, first, width):
        return first // self.columns, -(-min(first + width, self.cells) // self.columns)

    def layout(self, ranges):
        out, row, lane = [], 0, 0
        for first, width in ranges:
            r0, r1 = self.rows(first, width)
            out.append((first, width, r0, r1, row, lane))
            row, lane = row + r1 - r0 + 2, lane + width
        return out, row, lane


def take(ref, start, width):
    low = start // LANES * LANES
    off = start - low
    if off == 0:
        return ref[:, low : low + width]
    return ref[:, low : low + width + LANES][:, off : off + width]


def side_column(refs, grid, row, right):
    own, top, bottom = refs
    slot = LAT_DEV if right else 0
    if row < 0:
        ref, lane = top, grid.halo + slot + LAT_DEV - 1
    elif row >= LAT_DEV:
        ref, lane = bottom, grid.halo + slot
    else:
        ref, lane = own, slot + row
    return ref[:, lane : lane + 1]


def take_cells(sources, start, width):
    parts, at, end = [], start, start + width
    for ref, begin, last, lane in sorted(sources, key=lambda source: source[1]):
        shift = lane - begin
        base = (start + shift) // LANES * LANES
        if begin <= start and end <= last and base + width + LANES <= ref.shape[1]:
            return take(ref, start + shift, width)
        low, high = max(at, begin), min(end, last)
        if low < high:
            if low > at:
                parts.append(jnp.zeros((ref.shape[0], low - at), BF16))
            base = (low + shift) // LANES * LANES
            top = min(round_up(high + shift, LANES), ref.shape[1])
            parts.append(ref[:, base:top][:, low + shift - base : high + shift - base])
            at = high
    if at < end:
        parts.append(jnp.zeros((sources[0][0].shape[0], end - at), BF16))
    return jnp.concatenate(parts, axis=1) if len(parts) > 1 else parts[0]


def row_cells(grid, row, sources, top, bottom):
    if row < 0 and top is not None:
        return take_cells([(top, 0, top.shape[1], 0)], grid.halo - grid.columns, grid.pitch)
    if row >= LAT_DEV and bottom is not None:
        return take_cells([(bottom, 0, bottom.shape[1], 0)], 0, grid.pitch)
    return take_cells(sources, row * grid.columns, grid.pitch)


def build_taps(grid, origin, low, high, sources, sides, taps, backwards=False):
    rows = sources[0][0].shape[0]
    own, top, bottom = sides
    for row in range(low, high):
        base = (row - origin) * grid.pitch
        value = row_cells(grid, row, sources, top, bottom)
        left = side_column(sides, grid, row, False)
        right = side_column(sides, grid, row, True)
        before = jnp.concatenate([left, value[:, : grid.pitch - 1]], axis=1)
        after = [value[:, 1 : grid.columns], right]
        if grid.columns < grid.pitch:
            after.append(jnp.zeros((rows, grid.pitch - grid.columns), BF16))
        for b, part in enumerate((before, value, jnp.concatenate(after, axis=1))):
            block = pl.ds((2 - b if backwards else b) * rows, rows)
            taps[block, base : base + grid.pitch] = part


def stacked_rows(grid, taps, row, count, order=(0, 1, 2)):
    width = count * grid.pitch
    return jnp.concatenate(
        [taps[:, (row + a) * grid.pitch : (row + a) * grid.pitch + width] for a in order],
        axis=0,
    )


def groups_of(count, size=ROW_GROUP):
    return [(row, min(size, count - row)) for row in range(0, count, size)]


def flat_piece(grid, pitched, skip, low, high, count):
    parts, at = [], low
    while at < high:
        row, column = divmod(at + skip, grid.columns)
        if row >= count:
            parts.append(jnp.zeros((pitched.shape[0], high - at), BF16))
            break
        size = min(grid.columns - column, high - at)
        begin = row * grid.pitch + column
        parts.append(pitched[:, begin : begin + size])
        at += size
    return jnp.concatenate(parts, axis=1) if len(parts) > 1 else parts[0]


def convolve(grid, first, width, place, sources, sides, taps, weight, bias, pitched, flat,
             backwards=False, emit=None, fetch=None):
    r0, r1 = grid.rows(first, width)
    skip = first - r0 * grid.columns
    taps_row, lane = place
    built, done = r0 - 1, 0
    order = (2, 1, 0) if backwards else (0, 1, 2)
    for row, count in groups_of(r1 - r0, PRODUCT_ROWS):
        ready = min(r0 + row + count + 1 + ROW_GROUP, r1 + 1)
        if fetch is not None:
            fetch(ready)
        build_taps(
            grid, r0 - 1 - taps_row, built, ready, sources, sides, taps, backwards
        )
        built = ready
        stacked = stacked_rows(grid, taps, taps_row + row, count, order)
        value = jnp.dot(weight, stacked, preferred_element_type=F32)
        if bias is not None:
            value = value + bias
        pitched[:, row * grid.pitch : (row + count) * grid.pitch] = value.astype(BF16)
        last = row + count == r1 - r0
        while done < width:
            end = min(done + FLAT_LANES, width)
            if not last and end + skip > row * grid.columns:
                break
            piece = flat_piece(grid, pitched, skip, done, end, r1 - r0)
            flat[:, lane + done : lane + end] = piece
            if emit is not None:
                emit(done, end)
            done = end


def edges_kernel(grid, places, tiles, x_ref, out_ref, row_ref, held, sem, row_sem):
    last = jnp.where(lax.axis_index("lat") == 0, (grid.cells - grid.halo) // LANES, 0)
    row_copy = pltpu.make_async_copy(
        x_ref.at[:, pl.ds(pl.multiple_of(last * LANES, LANES), grid.halo)],
        row_ref,
        row_sem.at[0],
    )
    row_copy.start()
    copies = [
        pltpu.make_async_copy(
            x_ref.at[:, pl.ds(tile * LANES, LANES)],
            held.at[:, pl.ds(number * LANES, LANES)],
            sem.at[number],
        )
        for number, tile in enumerate(tiles)
    ]
    for copy in copies:
        copy.start()
    columns = {}
    for number, (tile, copy) in enumerate(zip(tiles, copies)):
        copy.wait()
        for cell in places:
            if cell // LANES == tile:
                at = number * LANES + cell % LANES
                columns[cell] = held[:, at : at + 1]
    out_ref[...] = jnp.concatenate([columns[cell] for cell in places], axis=1)
    row_copy.wait()


def edges_of(grid, field):
    rows = field.shape[0]
    places = [i for i in range(0, grid.cells, grid.columns)]
    places += [i for i in range(grid.columns - 1, grid.cells, grid.columns)]
    tiles = sorted({cell // LANES for cell in places})
    return pl.pallas_call(
        functools.partial(edges_kernel, grid, places, tiles),
        in_specs=[in_hbm()],
        out_specs=[in_vmem()] * 2,
        out_shape=[shape_of((rows, 2 * LAT_DEV)), shape_of((rows, grid.halo))],
        scratch_shapes=[
            pltpu.VMEM((rows, len(tiles) * LANES), BF16),
            pltpu.SemaphoreType.DMA((len(tiles),)),
            pltpu.SemaphoreType.DMA((1,)),
        ],
        compiler_params=params((rows, (len(tiles) + 1) * LANES + grid.halo, 2)),
        cost_estimate=cost(rows, rows),
        name="edges",
    )(kept_in_hbm(field))


def lon_halo(edges, odd=None):
    peers = lax.axis_size("lon")
    first, last = edges[:, :LAT_DEV], edges[:, LAT_DEV:]
    if peers % 2 or odd is None:
        right = [(i, (i + 1) % peers) for i in range(peers)]
        left = [(j, i) for i, j in right]
        before, after = lax.ppermute(last, "lon", right), lax.ppermute(first, "lon", left)
        return jnp.concatenate([before, after], axis=1)
    near = [(i, i ^ 1) for i in range(peers)]
    far = [(i, (i + 1 if i % 2 else i - 1) % peers) for i in range(peers)]
    inner = lax.ppermute(jnp.where(odd, first, last), "lon", near)
    outer = lax.ppermute(jnp.where(odd, last, first), "lon", far)
    return jnp.where(
        odd,
        jnp.concatenate([inner, outer], axis=1),
        jnp.concatenate([outer, inner], axis=1),
    )


def lat_halo(first_rows, last_rows, sides, upper, chosen=None):
    peers = lax.axis_size("lat")
    if peers == 2:
        if chosen is None:
            chosen = jnp.where(upper, last_rows, first_rows)
        sent = jnp.concatenate([chosen, sides], axis=1)
        other = lax.ppermute(sent, "lat", [(0, 1), (1, 0)])
        none = jnp.zeros_like(other)
        return jnp.where(upper, none, other), jnp.where(upper, other, none)
    up = [(i, i + 1) for i in range(peers - 1)]
    down = [(j, i) for i, j in up]
    top = lax.ppermute(jnp.concatenate([last_rows, sides], axis=1), "lat", up)
    bottom = lax.ppermute(jnp.concatenate([first_rows, sides], axis=1), "lat", down)
    return top, bottom


def stages_of(grid, ranges):
    stages, got = [], []
    for first, width in ranges:
        r0, r1 = grid.rows(first, width)
        low = max((r0 - 1) * grid.columns - 1, 0) // LANES * LANES
        high = min(round_up((r1 + 1) * grid.columns + 1, LANES), grid.cells)
        low = max([low] + [end for begin, end in got if begin <= low])
        step = round_up(max((high - low) // 3, LANES), LANES)
        stages += [(at, min(at + step, high)) for at in range(low, high, step)]
        got.append((low, high))
    at = 0
    for low, high in sorted(got) + [(grid.cells, grid.cells)]:
        if at < low:
            stages.append((at, low))
        at = max(at, high)
    return stages


def forward_kernel(grid, ranges, has_top, has_bottom, members, load, waits, *refs):
    refs = list(refs)
    x_ref, sides_ref = refs[:2]
    del refs[:2]
    top_ref = refs.pop(0) if has_top else None
    bottom_ref = refs.pop(0) if has_bottom else None
    weight_ref, bias_ref, analysis_ref = refs[:3]
    del refs[: 3 + waits]
    outs = refs[:members]
    target_ref, taps = refs[members : members + 2]
    pitched, pred, target_sem, load_sem = refs[-4:]
    me = lax.axis_index("member")
    places, _, width = grid.layout(ranges)
    piece = width // members
    pending = []
    if load:
        held = refs[members + 2]
        for begin, end in stages_of(grid, ranges):
            copies = []
            for low in range(0, x_ref.shape[0], 32):
                at = (pl.ds(low, min(32, x_ref.shape[0] - low)), pl.ds(begin, end - begin))
                sem = load_sem.at[len(pending), len(copies)]
                copies.append(pltpu.make_async_copy(x_ref.at[at], held.at[at], sem))
                copies[-1].start()
            pending.append((begin, end, copies))
        x_ref = held

    def fetch(low, high):
        for stage in list(pending):
            if stage[0] < high * grid.columns + 1 and stage[1] > low * grid.columns - 1:
                for copy in stage[2]:
                    copy.wait()
                pending.remove(stage)

    each = members // len(ranges)
    index = me // each
    begin = places[0][0] + me * piece
    if len(ranges) > 1:
        begin = jnp.where(index == 0, begin, places[1][0] + (me - each) * piece)
    begin = pl.multiple_of(begin, LANES)
    target_copy = pltpu.make_async_copy(
        analysis_ref.at[:, pl.ds(begin, piece)], target_ref, target_sem.at[0]
    )
    target_copy.start()
    sides = (sides_ref, top_ref, bottom_ref)
    weight, bias = weight_ref[...], bias_ref[...]
    for first, size, r0, r1, row, lane in places:
        convolve(
            grid, first, size, (row, lane), [(x_ref, 0, grid.cells, 0)], sides, taps, weight,
            bias, pitched, pred, fetch=lambda ready, r0=r0: fetch(r0 - 1, ready),
        )
    for d in range(members):
        begin = pl.multiple_of((me ^ d) * piece, LANES)
        outs[d][...] = pred[:, pl.ds(begin, piece)]
    target_copy.wait()
    fetch(0, LAT_DEV)


def forward(
    grid, ranges, members, x, load, sides, top, bottom, weight, bias, analysis, after
):
    channels = x.shape[0]
    fields = weight.shape[0]
    places, tap_rows, width = grid.layout(ranges)
    most = max(place[3] - place[2] for place in places)
    has_top = any(place[2] == 0 for place in places)
    has_bottom = any(place[3] == LAT_DEV for place in places)
    piece = width // members
    held = (3 * channels, tap_rows * grid.pitch)
    operands = [kept_in_hbm(x) if load else kept_in_vmem(x), sides]
    if has_top:
        operands.append(top)
    if has_bottom:
        operands.append(bottom)
    operands += [weight, bias]
    specs = [in_hbm() if load else in_vmem()] + [in_vmem()] * (len(operands) - 1) + [in_hbm()]
    operands += [kept_in_hbm(analysis), *after]
    specs += [anywhere()] * len(after)
    shapes = [shape_of((fields, piece))] * (members + 1) + [pltpu.VMEM(held, BF16)]
    if load:
        shapes.append(pltpu.VMEM((channels, grid.cells), BF16))
    return pl.pallas_call(
        functools.partial(
            forward_kernel, grid, ranges, has_top, has_bottom, members, load, len(after)
        ),
        in_specs=specs,
        out_specs=[in_vmem()] * len(shapes),
        out_shape=shapes,
        scratch_shapes=[
            pltpu.VMEM((fields, most * grid.pitch), BF16),
            pltpu.VMEM((fields, width), BF16),
            pltpu.SemaphoreType.DMA((1,)),
            pltpu.SemaphoreType.DMA((12, -(-channels // 32))),
        ],
        compiler_params=params(
            (2 * fields, most * grid.pitch, 2),
            (2 * fields, 2 * width, 2),
            (fields, 9 * channels, 2),
        ),
        cost_estimate=cost(81 * channels * fields * width, 0),
        name=f"forward_{ranges[0][0]}",
    )(*operands)


def slope(values):
    return values * lax.rsqrt(values * values + 1.0)


def score_kernel(members, target_ref, scale_ref, *refs):
    pieces = refs[:members]
    outs = refs[-members:]
    fields, piece = pieces[0].shape
    tiles = piece // LANES
    several = max(k for k in (1, 2, 3) if tiles % k == 0)

    def tile(index, carry):
        for part in range(several * -(-fields // 16)):
            low = part // several * 16
            at = (index * several + part % several) * LANES
            span = pl.ds(pl.multiple_of(at, LANES), LANES)
            rows = pl.ds(low, min(16, fields - low))
            values = [ref[rows, span].astype(F32) for ref in pieces]
            target = target_ref[rows, span].astype(F32)
            scale = scale_ref[rows, :]
            sums = [None] * members
            for i in range(members):
                for j in range(i + 1, members):
                    both = slope(values[i] - values[j])
                    sums[i] = both if sums[i] is None else sums[i] + both
                    sums[j] = -both if sums[j] is None else sums[j] - both
            for i in range(members):
                grad = slope(values[i] - target) * (1.0 / members) - sums[i] * (
                    1.0 / (members * (members - 1))
                )
                outs[i][rows, span] = (scale * grad).astype(BF16)
        return carry

    lax.fori_loop(0, tiles // several, tile, 0)


def score(first, target, scale, pieces, after):
    members = len(pieces)
    fields, piece = pieces[0].shape
    return pl.pallas_call(
        functools.partial(score_kernel, members),
        in_specs=[in_vmem()] * (2 + members) + [anywhere()] * len(after),
        out_specs=[in_vmem()] * members,
        out_shape=[shape_of((fields, piece))] * members,
        compiler_params=params((9 * round_up(fields, 16), piece, 2), (fields, LANES, 4)),
        cost_estimate=cost(13000 * fields * piece, 0),
        name=f"score_{first}",
    )(target, scale, *pieces, *after)


def gather_kernel(grid, ranges, members, *refs):
    me = lax.axis_index("member")
    pieces = refs[:members]
    out_ref, edge_ref = refs[members:]
    fields, piece = pieces[0].shape
    rows, width = out_ref.shape
    base = fields // 16 * 16
    if base < rows:
        out_ref[pl.ds(base, rows - base), :] = jnp.zeros((rows - base, width), BF16)
    for d in range(members):
        begin = pl.multiple_of((me ^ d) * piece, LANES)
        value = pieces[d][...]
        if grid.padded != grid.cells:
            cell = lax.broadcasted_iota(jnp.int32, (1, piece), 1) + begin
            value = jnp.where(cell < grid.cells, value.astype(F32), 0.0).astype(BF16)
        out_ref[pl.ds(0, fields), pl.ds(begin, piece)] = value
    columns = []
    for side in (0, grid.columns - 1):
        for row in range(LAT_DEV):
            cell = row * grid.columns + side
            for first, size, *_, lane in grid.layout(ranges)[0]:
                if first <= cell < first + size:
                    at = lane + cell - first
                    columns.append(out_ref[:, at : at + 1])
                    break
            else:
                columns.append(jnp.zeros((rows, 1), BF16))
    edge_ref[...] = jnp.concatenate(columns, axis=1)


def gather(grid, ranges, rows, pieces, after):
    members = len(pieces)
    width = members * pieces[0].shape[1]

    def kernel(*refs):
        gather_kernel(grid, ranges, members, *refs[:members], *refs[-2:])

    return pl.pallas_call(
        kernel,
        in_specs=[in_vmem()] * members + [anywhere()] * len(after),
        out_specs=[in_vmem()] * 2,
        out_shape=[shape_of((rows, width)), shape_of((rows, 2 * LAT_DEV))],
        compiler_params=params((rows, 2 * width + 2 * LAT_DEV, 2)),
        cost_estimate=cost(width, 0),
        name=f"gather_{ranges[0][0]}",
    )(*pieces, *after)


def weight_kernel(grid, ranges, chained, waits, halves, taps, part_ref, *refs):
    before_ref = refs[0] if chained else None
    refs = refs[chained + waits :]
    pitched, sum_ref = refs[-1], refs[-2]
    rows = part_ref.shape[0]
    keep = jnp.where(
        lax.broadcasted_iota(jnp.int32, (1, LANES), 1) < grid.columns % LANES, 1.0, 0.0
    ).astype(BF16)
    started = False
    for first, width, r0, r1, taps_row, place in grid.layout(ranges)[0]:
        source = [(part_ref, first, first + width, place)]
        for row, count in groups_of(r1 - r0):
            for at in range(row, row + count):
                value = take_cells(source, (r0 + at) * grid.columns, grid.pitch)
                to = at * grid.pitch
                for lane in range(0, grid.pitch, LANES):
                    part = value[:, lane : lane + LANES]
                    if lane + LANES > grid.columns:
                        part = part * keep
                    pitched[:, to + lane : to + lane + LANES] = part
            stacked = stacked_rows(grid, taps, taps_row + row, count)
            lanes = round_up(stacked.shape[0] + 1, LANES)
            ones = jnp.ones((lanes - stacked.shape[0], stacked.shape[1]), BF16)
            part = nt_dot(
                pitched[:, row * grid.pitch : (row + count) * grid.pitch],
                jnp.concatenate([stacked, ones], axis=0),
            )
            if started:
                sum_ref[:, :lanes] += part
            else:
                sum_ref[:, :lanes] = part + before_ref[:, :lanes] if chained else part
            started = True
    if lanes < sum_ref.shape[1]:
        sum_ref[:, lanes:] = jnp.zeros((rows, sum_ref.shape[1] - lanes), F32)
    if halves:
        keep_ref, send_ref = refs[:2]
        half = rows // 2
        upper = lax.axis_index("lat") & 1
        keep_ref[...] = sum_ref[pl.ds(pl.multiple_of(upper * half, 8), half), :]
        send_ref[...] = sum_ref[pl.ds(pl.multiple_of((1 - upper) * half, 8), half), :]


def weight_part(grid, ranges, members, taps, part, before, after, halves):
    rows = part.shape[0]
    channels = taps.shape[0] // 3
    places, _, width = grid.layout(ranges)
    most = max(place[3] - place[2] for place in places)
    sums = round_up(9 * channels + 1, members * LANES)
    chained = [] if before is None else [before]
    whole = []
    if halves:
        shapes = [shape_of((rows // 2, sums), F32)] * 2
        whole = [pltpu.VMEM((rows, sums), F32)]
    else:
        shapes = [shape_of((rows, sums), F32)]
    return pl.pallas_call(
        functools.partial(weight_kernel, grid, ranges, len(chained), len(after), halves),
        in_specs=[in_vmem()] * (2 + len(chained)) + [anywhere()] * len(after),
        out_specs=[in_vmem()] * len(shapes),
        out_shape=shapes,
        scratch_shapes=whole + [pltpu.VMEM((rows, most * grid.pitch), BF16)],
        compiler_params=params(
            (rows, width, 2),
            (rows, most * grid.pitch, 2),
            (rows, 3 * sums, 4),
        ),
        cost_estimate=cost(width, 0),
        name=f"weight_{ranges[0][0]}",
    )(kept_in_vmem(taps), part, *chained, *after)


def input_kernel(grid, r0, r1, chunks, aliased, *refs):
    refs = list(refs)
    parts = refs[: len(chunks)]
    del refs[: len(chunks)]
    sides_ref, weight_ref = refs[:2]
    del refs[:2]
    top_ref = refs.pop(0) if r0 == 0 else None
    bottom_ref = refs.pop(0) if r1 == LAT_DEV else None
    del refs[:aliased]
    out_ref, taps, pitched, flat, out_sem = refs
    sources = []
    for ref, ranges in zip(parts, chunks):
        for first, width, *_, lane in grid.layout(ranges)[0]:
            sources.append((ref, first, min(first + width, grid.cells), lane))
    sides = (sides_ref, top_ref, bottom_ref)
    copies = []

    def emit(low, high):
        at = r0 * grid.columns + low
        copies.append(
            pltpu.make_async_copy(
                flat.at[:, pl.ds(low, high - low)],
                out_ref.at[:, pl.ds(at, high - low)],
                out_sem.at[len(copies)],
            )
        )
        copies[-1].start()

    width = (r1 - r0) * grid.columns
    convolve(
        grid, r0 * grid.columns, width, (0, 0), sources, sides, taps, weight_ref[...], None,
        pitched, flat, backwards=True, emit=emit,
    )
    for copy in copies:
        copy.wait()


def input_part(grid, r0, r1, chunks, parts, sides, top, bottom, weight, before, slow):
    rows = parts[0].shape[0]
    channels = weight.shape[0]
    width = (r1 - r0) * grid.columns
    held = (3 * rows, (r1 - r0 + 2) * grid.pitch)
    begin, end = (r0 - 1) * grid.columns - 1, (r1 + 1) * grid.columns + 1
    near = [
        (ranges, part)
        for ranges, part in zip(chunks, parts)
        if any(first < end and first + size > begin for first, size in ranges)
    ]
    chunks, parts = [pair[0] for pair in near], [pair[1] for pair in near]
    operands = [*parts, sides, weight] + [top] * (r0 == 0) + [bottom] * (r1 == LAT_DEV)
    specs = [in_vmem()] * len(operands)
    alias = {}
    if before is not None:
        alias = {len(operands): 0}
        operands.append(before)
        specs.append(anywhere())
    return pl.pallas_call(
        functools.partial(input_kernel, grid, r0, r1, chunks, len(alias)),
        in_specs=specs,
        out_specs=anywhere(),
        out_shape=shape_of((channels, grid.cells)),
        input_output_aliases=alias,
        scratch_shapes=[
            pltpu.VMEM(held, BF16),
            pltpu.VMEM((channels, (r1 - r0) * grid.pitch), BF16),
            pltpu.VMEM((channels, width), BF16),
            pltpu.SemaphoreType.DMA((-(-width // FLAT_LANES),)),
        ],
        compiler_params=params(
            (rows, sum(part.shape[1] for part in parts), 2),
            (*held, 2),
            (2 * channels, (r1 - r0) * grid.pitch, 2),
            (channels, 9 * rows, 2),
        ),
        cost_estimate=cost((80 if slow else 1) * channels * rows * width, width),
        name=f"input_{r0}",
    )(*operands)


def split_kernel(members, count, *refs):
    me = lax.axis_index("member")
    lanes = refs[count].shape[1]
    for d in range(members):
        span = pl.ds(pl.multiple_of((me ^ d) * lanes, LANES), lanes)
        total = refs[0][:, span]
        for ref in refs[1:count]:
            total += ref[:, span]
        refs[count + d][...] = total


def split_by_member(values, members):
    rows, lanes = values[0].shape
    return pl.pallas_call(
        functools.partial(split_kernel, members, len(values)),
        in_specs=[in_vmem()] * len(values),
        out_specs=[in_vmem()] * members,
        out_shape=[shape_of((rows, lanes // members), F32)] * members,
        compiler_params=params((rows, 3 * lanes, 4)),
        cost_estimate=cost(rows * lanes, 12 * rows * lanes),
        name="split",
    )(*values)


def join_kernel(members, *refs):
    me = lax.axis_index("member")
    lanes = refs[0].shape[1]
    for d in range(members):
        span = pl.ds(pl.multiple_of((me ^ d) * lanes, LANES), lanes)
        refs[members][:, span] = refs[d][...]


def join_members(pieces):
    members = len(pieces)
    rows, lanes = pieces[0].shape
    return pl.pallas_call(
        functools.partial(join_kernel, members),
        in_specs=[in_vmem()] * members,
        out_specs=in_vmem(),
        out_shape=shape_of((rows, members * lanes), F32),
        compiler_params=params((rows, 2 * members * lanes, 4)),
        cost_estimate=cost(rows * lanes, 12 * rows * lanes),
        name="join",
    )(*pieces)


def swap(value, axis, bits):
    return lax.ppermute(value, axis, [(i, i ^ bits) for i in range(lax.axis_size(axis))])


def sum_axis(value, axis, bit):
    size = lax.axis_size(axis)
    while bit < size:
        if 2 * bit < size:
            near, far, both = [swap(value, axis, k * bit) for k in (1, 2, 3)]
            value = (value + near) + (far + both)
        else:
            value = value + swap(value, axis, bit)
        bit *= 4
    return value


def sum_all(keep, send, between):
    members = lax.axis_size("member")
    other = swap(send, "lat", 1)
    values = [keep, other]
    if lax.axis_size("lat") > 2:
        values = [sum_axis(keep + other, "lat", 2)]
    pieces = split_by_member(values, members)
    moved = [swap(pieces[d], "member", d) for d in range(1, members)]
    value = functools.reduce(jnp.add, moved, pieces[0])
    value = sum_axis(between(value), "lon", 1)
    value = between(value)
    moved = [swap(value, "member", d) for d in range(1, members)]
    moved[0] = between(moved[0])
    half = join_members([value, *moved])
    return half, swap(half, "lat", 1)


def finish_kernel(taps, channels, fields, scale, own_ref, other_ref, out_ref, bias_ref, rows_ref,
                  turned):
    upper = lax.axis_index("lat") & 1
    half = own_ref.shape[0]
    rows_ref[pl.ds(pl.multiple_of(upper * half, 8), half), :] = own_ref[...]
    rows_ref[pl.ds(pl.multiple_of((1 - upper) * half, 8), half), :] = other_ref[...]
    turned[...] = (rows_ref[:, : turned.shape[0]] * scale).T
    pieces = [
        turned[pl.ds(channel, taps, stride=channels), :][:, :fields]
        for channel in range(channels)
    ]
    out_ref[...] = jnp.concatenate(pieces, axis=1)
    bias_ref[...] = turned[pl.ds(taps * channels, 1), :][:, :fields]


def finish(own, other, taps, channels, fields, scale):
    half, lanes = own.shape
    used = round_up(taps * channels + 1, LANES)
    return pl.pallas_call(
        functools.partial(finish_kernel, taps, channels, fields, scale),
        in_specs=[in_vmem()] * 2,
        out_specs=[in_vmem()] * 2,
        out_shape=[shape_of((taps, channels * fields), F32), shape_of((1, fields), F32)],
        scratch_shapes=[
            pltpu.VMEM((2 * half, lanes), F32),
            pltpu.VMEM((used, 2 * half), F32),
        ],
        compiler_params=params((4 * half, lanes, 4), (used, LANES, 4), (16, channels * fields, 4)),
        cost_estimate=cost(lanes, 8 * half * lanes),
        name="finish",
    )(own, other)


def weights_kernel(taps_ref, forward_ref, backward_ref):
    count, channels, fields = taps_ref.shape
    rows = backward_ref.shape[1] // count
    taps = [taps_ref[t] for t in range(count)]
    forward_ref[...] = jnp.concatenate(
        [tap.astype(F32).T for tap in taps], axis=1
    ).astype(BF16)
    none = [jnp.zeros((channels, rows - fields), BF16)] * (rows > fields)
    backward_ref[...] = jnp.concatenate([part for tap in taps for part in (tap, *none)], axis=1)


def prepare_weights(taps, rows):
    count, channels, fields = taps.shape
    return pl.pallas_call(
        weights_kernel,
        in_specs=[in_vmem()],
        out_specs=[in_vmem()] * 2,
        out_shape=[shape_of((fields, count * channels)), shape_of((channels, count * rows))],
        compiler_params=params((4 * channels, count * LANES, 4)),
        cost_estimate=cost(channels, 8 * count * channels * rows),
        name="weights",
    )(taps)


def chunks_of(grid, members):
    unit = members * LANES
    units = grid.padded // unit
    if units < 15 or grid.padded != grid.cells or members % 2:
        return [[(0, grid.padded)]]
    outer = (units // 2 + 2) // 2 * unit
    return [
        [(0, outer), (grid.cells - outer, outer)],
        [(outer, grid.cells - 2 * outer)],
    ]


def parts_of(grid, wanted):
    step = LAT_DEV // wanted
    if step * grid.columns % LANES:
        return [(0, LAT_DEV)]
    ranges = [(row, row + step) for row in range(0, LAT_DEV, step)]
    return ranges[1:-1] + [ranges[0], ranges[-1]]


def local(inputs, weight, bias, analysis, field_weight):
    channels, cells = inputs.shape[1], inputs.shape[4]
    fields = analysis.shape[0]
    members = lax.axis_size("member")
    grid = Grid(cells, members)
    x = inputs.reshape(channels, cells)
    target = analysis.reshape(fields, cells)
    if grid.padded != cells:
        target = jnp.pad(target, ((0, 0), (0, grid.padded - cells)))
    rows = round_up(fields, 16)
    taps = weight.reshape(9, channels, fields)
    forward_weight, backward_weight = prepare_weights(taps, rows)
    scale = jnp.broadcast_to(field_weight[:, None], (fields, LANES))
    shift = bias[:, None]
    upper = (lax.axis_index("lat") & 1) != 0
    odd = (lax.axis_index("lon") & 1) != 0
    x_edges, x_row = edges_of(grid, x)
    x_sides = lon_halo(x_edges)
    x_sides, forward_weight, backward_weight, scale, shift, upper, odd = (
        lax.optimization_barrier(
            (x_sides, forward_weight, backward_weight, scale, shift, upper, odd)
        )
    )
    first_lat = jnp.logical_not(upper)
    def to_members(pieces):
        moved = {0: pieces[0]}
        for d in range(members - 1, 0, -1):
            moved[d] = swap(pieces[d], "member", d)
        return [moved[d] for d in range(members)]

    chunks = chunks_of(grid, members)
    x_top, x_bottom = lat_halo(
        x[:, : grid.halo], x[:, cells - grid.halo :], x_sides, first_lat, x_row
    )
    received, targets, taken, held = [], [], [], None
    for ranges in chunks:
        out = forward(
            grid, ranges, members, x if held is None else held, held is None, x_sides, x_top,
            x_bottom, forward_weight, shift, target, [],
        )
        targets.append(out[members])
        taken.append(out[members + 1])
        held = out[members + 2] if held is None else held
        received.append(to_members(out[:members]))
    returned = []
    for ranges, pieces, goal in zip(chunks, received, targets):
        grads = score(ranges[0][0], goal, scale, pieces, targets[-1:])
        returned.append(to_members(grads))

    blocks = parts_of(grid, 4)
    parts, sums, grad_input = [], [None], None
    for number, ranges in enumerate(chunks):
        final = number == len(chunks) - 1
        after = [returned[-1][0]] if number == 0 else [kept_in_hbm(grad_input)]
        part, edge = gather(grid, ranges, rows, returned[number], after)
        if final:
            sums = weight_part(grid, ranges, members, taken[number], part, sums[0], [], final)
            edge, sums = lax.optimization_barrier((edge, list(sums)))
        sides = lon_halo(edge, odd)
        if not final:
            sums = weight_part(grid, ranges, members, taken[number], part, sums[0], [], final)
            sides, sums = lax.optimization_barrier((sides, list(sums)))
        parts.append(part)
        g_sides = sides if number == 0 else g_sides + sides
        if number == 0:
            end = part.shape[1] - grid.padded + cells
            outer_rows = (part[:, : grid.halo], part[:, end - grid.halo : end])
            g_top, g_bottom = lat_halo(*outer_rows, g_sides, first_lat)
        for _ in range(0 if final else 1):
            grad_input = input_part(
                grid, *blocks.pop(), chunks[:1], parts[:1], g_sides, g_top, g_bottom,
                backward_weight, grad_input, False,
            )

    def between(value):
        nonlocal grad_input
        for _ in range(min(1, len(blocks))):
            grad_input = input_part(
                grid, *blocks.pop(), chunks, parts, g_sides, g_top, g_bottom, backward_weight,
                grad_input, True,
            )
            value, grad_input = lax.optimization_barrier((value, grad_input))
        return value

    own, other = sum_all(*sums, between)
    while blocks:
        grad_input = input_part(
            grid, *blocks.pop(), chunks, parts, g_sides, g_top, g_bottom, backward_weight,
            grad_input, True,
        )
    everywhere = cells * lax.axis_size("lat") * lax.axis_size("lon")
    grad_weight, grad_bias = finish(own, other, 9, channels, fields, 1.0 / everywhere)
    return (grad_input.reshape(1, channels, 1, 1, cells), grad_weight, grad_bias[0])


def solution(mesh):
    placed = (P("member", None, "lat", "lon", None), P(), P(), P(None, "lat", "lon", None), P())
    return jax.shard_map(
        local,
        mesh=mesh,
        in_specs=placed,
        out_specs=(P("member", None, "lat", "lon", None), P(), P()),
        check_vma=False,
    )
```
